32 devices in a mesh: dp: 16 (over z, y, x), tensor: 2 (over core).
Axes of the slice: x: 2, y: 2, z: 4, core: 2. Of those that a mesh axis runs over, the one named last changes fastest.
Arguments:
- content_in: bfloat16 [16, 512, 768], P('dp'), may hold values from -6 to 6
- query_in: bfloat16 [16, 512, 768], P('dp', 'tensor'), may hold values from -6 to 6
- memory: bfloat16 [16, 384, 768], P('dp'), may hold values from -6 to 6
- content_cot: bfloat16 [16, 512, 768], P('dp', 'tensor'), may hold values from -6 to 6
- query_cot: bfloat16 [16, 512, 768], P('dp', 'tensor'), may hold values from -6 to 6
- query_weight: bfloat16 [768, 768], replicated, may hold values from -0.21875 to 0.21875
- key_weight: bfloat16 [768, 768], replicated, may hold values from -0.21875 to 0.21875
- value_weight: bfloat16 [768, 768], replicated, may hold values from -0.21875 to 0.21875
- out_weight: bfloat16 [768, 768], replicated, may hold values from -0.875 to 0.875
- rel_weight: bfloat16 [768, 768], replicated, may hold values from -0.21875 to 0.21875
- content_bias: float32 [768], replicated, may hold values from -3 to 3
- position_bias: float32 [768], replicated, may hold values from -3 to 3
- segment_bias: float32 [768], replicated, may hold values from -3 to 3
- segment_embed: float32 [768, 2], replicated, may hold values from -4 to 4
- attn_gain: float32 [768], replicated, may hold values from 0.5 to 1.5
- attn_shift: float32 [768], replicated, may hold values from -1 to 1
- up_weight: bfloat16 [768, 3072], P(None, 'tensor'), may hold values from -0.21875 to 0.21875
- up_bias: float32 [3072], replicated, may hold values from -1.5 to 1.5
- down_weight: bfloat16 [3072, 768], P('tensor'), may hold values from -0.15625 to 0.15625
- down_bias: float32 [768], replicated, may hold values from -1.5 to 1.5
- ffn_gain: float32 [768], replicated, may hold values from 0.5 to 1.5
- ffn_shift: float32 [768], replicated, may hold values from -1 to 1
- lengths: int32 [16], P('dp'), may hold values from 64 to 512, as said below
- memory_lengths: int32 [16], P('dp'), may hold values from 1 to 384, as said below
- segment_ids: int32 [16, 512], P('dp'), may hold values from 0 to 1, as said below
- orders: int32 [16, 512], P('dp'), may hold values from 0 to 511, each once within a row
- targets: int32 [16, 512], P('dp'), may hold values 0 or 1
Outputs:
- content_out: bfloat16 [16, 512, 768], P('dp', 'tensor')
- query_out: bfloat16 [16, 512, 768], P('dp', 'tensor')
- content_grad: float32 [16, 512, 768], P('dp', 'tensor')
- query_grad: float32 [16, 512, 768], P('dp', 'tensor')
- query_weight_grad: float32 [768, 768], P(('dp', 'tensor'))
- key_weight_grad: float32 [768, 768], P(('dp', 'tensor'))
- value_weight_grad: float32 [768, 768], P(('dp', 'tensor'))
- out_weight_grad: float32 [768, 768], P(('dp', 'tensor'))
- rel_weight_grad: float32 [768, 768], P(('dp', 'tensor'))
- content_bias_grad: float32 [768], P(('dp', 'tensor'))
- position_bias_grad: float32 [768], P(('dp', 'tensor'))
- segment_bias_grad: float32 [768], P(('dp', 'tensor'))
- segment_embed_grad: float32 [768, 2], P(('dp', 'tensor'))
- attn_gain_grad: float32 [768], P(('dp', 'tensor'))
- attn_shift_grad: float32 [768], P(('dp', 'tensor'))
- up_weight_grad: float32 [768, 3072], P('dp', 'tensor')
- up_bias_grad: float32 [3072], P(('dp', 'tensor'))
- down_weight_grad: float32 [3072, 768], P('tensor', 'dp')
- down_bias_grad: float32 [768], P(('dp', 'tensor'))
- ffn_gain_grad: float32 [768], P(('dp', 'tensor'))
- ffn_shift_grad: float32 [768], P(('dp', 'tensor'))
The draws below stay inside these ranges and needn't reach their ends.
Inputs may be any that keep to these rules, and one draw needn't show every extreme that they name: `lengths`: the first slot and about one slot in eight have length 512; the others lie between 64 and 384. `memory_lengths`: 384 exactly where the length is 512, else at most 128. `segment_ids`: 0 before a split position between 1 and the slot's length, 1 from it on.
All inputs are finite; a program needn't handle non-finite values. No bound on the sum of `targets` on one device may be relied on, other than what follows from the above.
Results may differ from the reference program's by a relative error of at most 0.025.
Values may be sent and summed in bfloat16 or wider, within the bound.
No kernel may reach another device: no remote copies, remote signals or barrier semaphores. Data moves between devices by JAX's collectives and lax.ppermute only.
A program may use at most 320 MiB of HBM per device.

```python
import jax
import jax.numpy as jnp
from jax import lax

D = 768
HEADS = 12
HEAD_DIM = 64
FF = 3072
LEN = 512
MEM = 384
SLOTS = 16


def slot_plan(key):
    complete = jax.random.randint(jax.random.fold_in(key, 11), (SLOTS,), 0, 8) == 0
    complete = complete.at[0].set(True)
    shorter = jax.random.randint(jax.random.fold_in(key, 12), (SLOTS,), LEN // 8, 3 * LEN // 4 + 1)
    lengths = jnp.where(complete, LEN, shorter).astype(jnp.int32)
    mem_short = jax.random.randint(jax.random.fold_in(key, 13), (SLOTS,), 1, MEM // 3 + 1)
    memory_lengths = jnp.where(complete, MEM, mem_short).astype(jnp.int32)
    divider = jax.random.randint(jax.random.fold_in(key, 14), (SLOTS,), 1, lengths + 1).astype(jnp.int32)
    return (lengths, memory_lengths, divider)


def draw_lengths(key, part):
    plan = slot_plan(key)
    return plan[0]


def draw_memory_lengths(key, part):
    plan = slot_plan(key)
    return plan[1]


def draw_segment_ids(key, part):
    plan = slot_plan(key)
    return (jnp.arange(LEN, dtype=jnp.int32)[None, :] >= plan[2][:, None]).astype(jnp.int32)


def with_ends(entries, rng, least, largest):
    shape = entries.shape
    index_at = [jax.random.randint(jax.random.fold_in(rng, axis), (), 0, shape[axis]) for axis in range(len(shape))]
    entries = entries.at[tuple(index_at)].set(least)
    longest = shape.index(max(shape))
    index_at[longest] = (index_at[longest] + 1) % shape[longest]
    return entries.at[tuple(index_at)].set(largest)


def levels(rng, shape, shards, smallest, top_value):
    def one(dim, blocks):
        heights = jax.random.uniform(jax.random.fold_in(jax.random.fold_in(rng, 6), dim), (blocks,), jnp.float32, smallest / len(shards), top_value / len(shards))
        return jnp.repeat(jnp.exp(heights), shape[dim] // blocks).reshape((-1,) + (1,) * (len(shape) - dim - 1))

    gain = one(*shards[0])
    for cut in shards[1:]:
        gain = gain * one(*cut)
    return gain


def scatter_about(own_key, extent, scale, bound, shards=(), kind=jnp.bfloat16):
    values = scale * jax.random.normal(own_key, extent, jnp.float32)
    if shards:
        values = values * levels(own_key, extent, shards, -0.22, 0.18)
    return jnp.clip(values, -bound, bound).astype(kind)


def setup_inputs(seed: int = 0) -> dict:
    splits = jax.random.split(jax.random.key(seed), 28)
    return {
        "content_in": scatter_about(splits[0], (SLOTS, LEN, D), 1.0, 6.0, ((0, 16),)),
        "query_in": scatter_about(splits[1], (SLOTS, LEN, D), 1.0, 6.0, ((0, 16), (1, 2))),
        "memory": scatter_about(splits[2], (SLOTS, MEM, D), 1.0, 6.0, ((0, 16),)),
        "content_cot": scatter_about(splits[3], (SLOTS, LEN, D), 1.0, 6.0, ((0, 16), (1, 2))),
        "query_cot": scatter_about(splits[4], (SLOTS, LEN, D), 1.0, 6.0, ((0, 16), (1, 2))),
        "query_weight": scatter_about(splits[5], (D, D), D ** -0.5, 0.21875),
        "key_weight": scatter_about(splits[6], (D, D), D ** -0.5, 0.21875),
        "value_weight": scatter_about(splits[7], (D, D), D ** -0.5, 0.21875),
        "out_weight": scatter_about(splits[8], (D, D), (D // 16) ** -0.5, 0.875),
        "rel_weight": scatter_about(splits[9], (D, D), D ** -0.5, 0.21875),
        "content_bias": scatter_about(splits[10], (D,), 0.5, 3.0, (), jnp.float32),
        "position_bias": scatter_about(splits[11], (D,), 0.5, 3.0, (), jnp.float32),
        "segment_bias": scatter_about(splits[12], (D,), 0.5, 3.0, (), jnp.float32),
        "segment_embed": scatter_about(splits[13], (D, 2), 1.0, 4.0, (), jnp.float32),
        "attn_gain": jnp.clip(1.0 + 0.1 * jax.random.normal(splits[14], (D,), jnp.float32), 0.5, 1.5),
        "attn_shift": scatter_about(splits[15], (D,), 0.2, 1.0, (), jnp.float32),
        "up_weight": scatter_about(splits[16], (D, FF), D ** -0.5, 0.21875, ((1, 2),)),
        "up_bias": scatter_about(splits[17], (FF,), 0.3, 1.5, (), jnp.float32),
        "down_weight": scatter_about(splits[18], (FF, D), (FF // 2) ** -0.5, 0.15625, ((0, 2),)),
        "down_bias": scatter_about(splits[19], (D,), 0.3, 1.5, (), jnp.float32),
        "ffn_gain": jnp.clip(1.0 + 0.1 * jax.random.normal(splits[20], (D,), jnp.float32), 0.5, 1.5),
        "ffn_shift": scatter_about(splits[21], (D,), 0.2, 1.0, (), jnp.float32),
        "lengths": draw_lengths(jax.random.fold_in(splits[27], 71), 0),
        "memory_lengths": draw_memory_lengths(jax.random.fold_in(splits[27], 71), 0),
        "segment_ids": draw_segment_ids(jax.random.fold_in(splits[27], 71), 0),
        "orders": jax.vmap(lambda own: jax.random.permutation(own, LEN))(jax.random.split(splits[25], SLOTS)).reshape((SLOTS, LEN)).astype(jnp.int32),
        "targets": with_ends((jax.random.randint(splits[26], (SLOTS, LEN), 0, 6) < 1).astype(jnp.int32), jax.random.fold_in(splits[26], 1), 0, 1),
    }


precise = lax.Precision.HIGHEST

@jax.custom_vjp
def low(v):
    return lax.optimization_barrier(v.astype(jnp.bfloat16)).astype(jnp.float32)

@jax.custom_vjp
def low_back(v):
    return v

def low_keep(v):
    return (low(v), None)

def low_pass(kept, grad):
    return (grad,)

def back_keep(v):
    return (v, None)

def back_low(kept, grad):
    return (low(grad),)
low.defvjp(low_keep, low_pass)
low_back.defvjp(back_keep, back_low)

def matmul(left, right):
    return jnp.dot(left, right, precision=precise)

def layer_norm(summed, norm_gain, norm_shift):
    center = summed - lax.optimization_barrier(jnp.mean(summed, axis=-1, keepdims=True))
    spread = lax.optimization_barrier(jnp.mean(center * center, axis=-1, keepdims=True))
    return center * lax.rsqrt(spread + 1e-06) * norm_gain + norm_shift

def activate(inputs):
    return jax.nn.gelu(inputs, approximate=True)

def position_table():
    steps_back = MEM + LEN - jnp.arange(2 * LEN + MEM).astype(jnp.float32)
    inverse = 1.0 / 10000.0 ** (jnp.arange(0, D, 2).astype(jnp.float32) / D)
    angles = steps_back[:, None] * inverse[None, :]
    return jnp.concatenate([jnp.sin(angles), jnp.cos(angles)], axis=1).astype(jnp.bfloat16)

def split_heads(array):
    return array.reshape(array.shape[:-1] + (HEADS, HEAD_DIM))

def shift_index(positions):
    shift_at = (LEN - positions)[:, None] + jnp.arange(MEM + LEN, dtype=jnp.int32)[None, :]
    return jnp.concatenate([shift_at, shift_at], axis=0)

def visibility(positions, length, mem_len, seg_ids, ordering, target):
    key_tokens = jnp.arange(LEN, dtype=jnp.int32)
    live = (key_tokens < length)[None, :]
    query_order = ordering[positions]
    query_segment = seg_ids[positions]
    unmasked = (target == 0)[None, :]
    content_tokens = live & (unmasked | (ordering[None, :] <= query_order[:, None]))
    query_tokens = live & (unmasked | (ordering[None, :] < query_order[:, None])) & (key_tokens[None, :] != positions[:, None])
    count = positions.shape[0]
    memory_seen = jnp.broadcast_to((jnp.arange(MEM, dtype=jnp.int32) >= MEM - mem_len)[None, :], (count, MEM))
    visible = jnp.concatenate([jnp.concatenate([memory_seen, content_tokens], axis=1), jnp.concatenate([memory_seen, query_tokens], axis=1)], axis=0)
    memory_split = jnp.broadcast_to((query_segment != 0)[:, None], (count, MEM))
    split_rows = jnp.concatenate([memory_split, query_segment[:, None] != seg_ids[None, :]], axis=1)
    return (visible, jnp.concatenate([split_rows, split_rows], axis=0))

def slot_scores(head_content, head_position, head_segment, key_rows, rel_keys, segment_embed, positions, visible, different):
    scaling = HEAD_DIM ** (-0.5)
    direct = jnp.einsum('qhd,khd->hqk', split_heads(head_content), split_heads(key_rows), precision=precise)
    relative = jnp.einsum('qhd,phd->hqp', split_heads(head_position), split_heads(rel_keys), precision=precise)
    shifted = jnp.take_along_axis(relative, shift_index(positions)[None], axis=2)
    seg_terms = jnp.einsum('qhd,hdb->bhq', split_heads(head_segment), segment_embed.reshape(HEADS, HEAD_DIM, 2), precision=precise)
    segmental = jnp.where(different[None], seg_terms[1][:, :, None], seg_terms[0][:, :, None])
    return jnp.where(visible[None], scaling * (direct + shifted + segmental), -1e+30)

def slot_forward(weights, pos_table, slot_data):
    query_weight, key_weight, value_weight, out_weight, rel_weight, content_bias, position_bias, segment_bias, segment_embed, attn_gain, attn_shift, up_weight, up_bias, down_weight, down_bias, ffn_gain, ffn_shift = weights
    content, query_rows, memory, length, mem_len, seg_ids, ordering, target = slot_data
    key_rows = jnp.concatenate([low(matmul(memory, key_weight)), low_back(low(matmul(content, key_weight)))], axis=0)
    value_rows = jnp.concatenate([low(matmul(memory, value_weight)), low_back(low(matmul(content, value_weight)))], axis=0)
    rel_keys = low(matmul(pos_table, rel_weight))
    both_rows = jnp.concatenate([content, query_rows], axis=0)
    projection = low_back(matmul(both_rows, query_weight))
    head_content = low_back(low(projection + content_bias))
    head_position = low_back(low(projection + position_bias))
    head_segment = projection + segment_bias
    positions = jnp.arange(LEN, dtype=jnp.int32)
    visible, different = visibility(positions, length, mem_len, seg_ids, ordering, target)
    scores = low_back(slot_scores(head_content, head_position, head_segment, key_rows, rel_keys, segment_embed, positions, visible, different))
    norm_log = jax.scipy.special.logsumexp(scores, axis=-1)
    attention = jnp.exp(scores - norm_log[..., None])
    mixture = jnp.einsum('hqk,khd->qhd', low(attention), split_heads(value_rows), precision=precise)
    attended = low_back(low(mixture.reshape(mixture.shape[0], D)))
    projected = low_back(matmul(attended, out_weight))
    normed = layer_norm(projected + both_rows, attn_gain, attn_shift)
    pre_act = low_back(matmul(low(normed), up_weight) + up_bias)
    hidden = low(activate(pre_act))
    ffn_out = low_back(matmul(hidden, down_weight) + down_bias)
    return layer_norm(normed + ffn_out, ffn_gain, ffn_shift)

def reference(content_in, query_in, memory, content_cot, query_cot, query_weight, key_weight, value_weight, out_weight, rel_weight, content_bias, position_bias, segment_bias, segment_embed, attn_gain, attn_shift, up_weight, up_bias, down_weight, down_bias, ffn_gain, ffn_shift, lengths, memory_lengths, segment_ids, orders, targets):
    weights = tuple((argument.astype(jnp.float32) for argument in (query_weight, key_weight, value_weight, out_weight, rel_weight, content_bias, position_bias, segment_bias, segment_embed, attn_gain, attn_shift, up_weight, up_bias, down_weight, down_bias, ffn_gain, ffn_shift)))
    pos_table = position_table().astype(jnp.float32)
    memory_rows = memory.astype(jnp.float32)

    def forward(weights, content, query_rows):

        def one_slot(slot_data):
            return slot_forward(weights, pos_table, slot_data)
        return lax.map(jax.checkpoint(one_slot), (content, query_rows, memory_rows, lengths, memory_lengths, segment_ids, orders, targets))
    outputs, pullback = jax.vjp(forward, weights, content_in.astype(jnp.float32), query_in.astype(jnp.float32))
    cotangent = jnp.concatenate([content_cot, query_cot], axis=1).astype(jnp.float32)
    weight_grads, content_grad, query_grad = pullback(cotangent)
    return (outputs[:, :LEN].astype(jnp.bfloat16), outputs[:, LEN:].astype(jnp.bfloat16), content_grad, query_grad, weight_grads[0], weight_grads[1], weight_grads[2], weight_grads[3], weight_grads[4], weight_grads[5], weight_grads[6], weight_grads[7], weight_grads[8], weight_grads[9], weight_grads[10], weight_grads[11], weight_grads[12], weight_grads[13], weight_grads[14], weight_grads[15], weight_grads[16])
```

```python
import functools

import jax
import jax.numpy as jnp
from jax import lax
from jax.experimental import pallas as pl
from jax.experimental.pallas import tpu as pltpu
from jax.sharding import PartitionSpec as P

D = 768
HEADS = 12
HEAD_DIM = 64
FF = 3072
LEN = 512
MEM = 384
KEYS = MEM + LEN
QUAD = 4 * HEAD_DIM
QUADS = D // QUAD
PAIR = 2 * HEAD_DIM
SCALE = HEAD_DIM ** (-0.5)
VMEM_BYTES = 56 * 1024 * 1024

f32 = jnp.float32
bf16 = jnp.bfloat16
precise = lax.Precision.HIGHEST


def mm(left, right):
    return lax.dot_general(left, right, (((1,), (0,)), ((), ())), preferred_element_type=f32)


def mm_nt(left, right):
    return lax.dot_general(left, right, (((1,), (1,)), ((), ())), preferred_element_type=f32)


def lanes(shape):
    return lax.broadcasted_iota(jnp.int32, shape, 1)


def column_of(row):
    return jnp.broadcast_to(row.astype(f32), (128, row.shape[1])).T


def flip_rows(value):
    count, width = value.shape
    groups = value.reshape(count // 8, 8, width)
    index = 7 - lax.broadcasted_iota(jnp.int32, groups.shape, 1)
    turned = jnp.take_along_axis(groups, index, axis=1, mode="promise_in_bounds")
    return jnp.concatenate([turned[i] for i in range(count // 8 - 1, -1, -1)], axis=0)


def forward_kernel(
    half,
    scal_ref,
    seg_ref,
    ord_ref,
    tgt_ref,
    memory_ref,
    content_ref,
    query_ref,
    wq_ref,
    wk_ref,
    wv_ref,
    wr_ref,
    cb_ref,
    pb_ref,
    sb_ref,
    se_ref,
    att_ref,
    prob_ref,
    key_ref,
    val_ref,
    rel_ref,
    hc_ref,
    hp_ref,
    hs_ref,
    kaug_ref,
    scol_ref,
    both_t_ref,
    stack_t_ref,
    pos_t_ref,
    stack,
    both,
    pos,
    bias,
    fine,
    coarse,
):
    window = KEYS + half
    first = pl.multiple_of(scal_ref[0], half)

    @pl.when(pl.program_id(0) == 0)
    def _():
        stack[:MEM, :] = memory_ref[...]
        stack[MEM:, :] = content_ref[...]
        both[:half, :] = content_ref[pl.ds(first, half), :]
        both[half:, :] = query_ref[...]
        step = lax.broadcasted_iota(jnp.int32, (1, D // 2), 1).astype(f32) * (2.0 / D)
        inverse = 1.0 / jnp.power(jnp.full((1, D // 2), 10000.0, f32), step)
        coarse_rows = coarse.shape[1]
        top = (MEM + half + first).astype(f32)
        angle = (
            top - 32.0 * lax.broadcasted_iota(jnp.int32, (coarse_rows, 1), 0).astype(f32)
        ) * inverse
        coarse[0] = jnp.sin(angle)
        coarse[1] = jnp.cos(angle)
        small = lax.broadcasted_iota(jnp.int32, (32, 1), 0).astype(f32) * inverse
        fine[0] = jnp.sin(small)
        fine[1] = jnp.cos(small)

        def fill(a, carry):
            sa, ca = coarse[0, pl.ds(a, 1), :], coarse[1, pl.ds(a, 1), :]
            sb, cb = fine[0], fine[1]
            at = pl.ds(pl.multiple_of(a * 32, 32), 32)
            pos[at, : D // 2] = (sa * cb - ca * sb).astype(bf16)
            pos[at, D // 2 :] = (ca * cb + sa * sb).astype(bf16)
            return carry

        lax.fori_loop(0, window // 32, fill, 0)
        length, mem_len = scal_ref[1], scal_ref[2]
        never = float(LEN + 1)
        mem_at = lax.broadcasted_iota(jnp.int32, (1, MEM), 1)
        tok_at = lax.broadcasted_iota(jnp.int32, (1, LEN), 1)
        open_from = jnp.concatenate(
            [
                jnp.where(mem_at >= MEM - mem_len, -1.0, never),
                jnp.where(
                    tok_at < length,
                    jnp.where(tgt_ref[...] == 0, -1.0, ord_ref[...].astype(f32)),
                    never,
                ),
            ],
            axis=1,
        )
        order_col = column_of(ord_ref[...])
        seg_col = column_of(seg_ref[...])
        kaug_lane = lanes((LEN, PAIR)) % HEAD_DIM
        kaug_ref[:MEM, :] = (lanes((MEM, PAIR)) % HEAD_DIM < 2).astype(f32).astype(bf16)
        kaug_ref[MEM:, :] = jnp.where(
            kaug_lane < 2, 1.0, jnp.where(kaug_lane < 4, seg_col, 0.0)
        ).astype(bf16)
        bias[:LEN, :PAIR] = order_col
        own_order = bias[pl.ds(first, half), :PAIR][:, :1]
        bias[:LEN, :PAIR] = seg_col
        scol_ref[...] = bias[pl.ds(first, half), :PAIR]
        seen = open_from <= own_order
        bias[:half, :] = jnp.where(seen, 0.0, -1e30)
        key_at = lax.broadcasted_iota(jnp.int32, (half, KEYS), 1)
        row_at = lax.broadcasted_iota(jnp.int32, (half, KEYS), 0)
        seen_q = seen & (key_at - MEM != row_at + first)
        bias[half:, :] = jnp.where(seen_q, 0.0, -1e30)
        both_t_ref[...] = both[...].T
        stack_t_ref[...] = stack[...].T
        pos_t_ref[...] = pos[...].T

    keys = mm(stack[...], wk_ref[...]).astype(bf16)
    values = mm(stack[...], wv_ref[...]).astype(bf16)
    rel = mm(pos[...], wr_ref[...]).astype(bf16)
    projection = mm(both[...], wq_ref[...])
    head_content = (projection + cb_ref[...]).astype(bf16)
    head_position = (projection + pb_ref[...]).astype(bf16)
    head_segment = projection + sb_ref[...]
    key_ref[...] = keys
    val_ref[...] = values
    rel_ref[...] = rel
    hs_ref[...] = head_segment
    head_content = (head_content.astype(f32) * SCALE).astype(bf16)
    head_position = (head_position.astype(f32) * SCALE).astype(bf16)
    hc_ref[...] = head_content
    hp_ref[...] = head_position
    same, other = se_ref[:, 0:1], se_ref[:, 1:2]
    row_head = lax.broadcasted_iota(jnp.int32, (QUAD, QUAD), 0) // HEAD_DIM
    at = lanes((QUAD, QUAD)) - ((row_head // 2) * PAIR + (1 - row_head % 2) * HEAD_DIM)
    place_same = jnp.where((at >= 0) & (at < 2), same, 0.0)
    place_step = jnp.where((at >= 0) & (at < 4), other - same, 0.0)
    scol = scol_ref[...]
    scol = jnp.concatenate([scol, scol], axis=0)
    scol = jnp.concatenate([scol, scol], axis=1)
    lane4 = lanes((2 * half, QUAD)) % HEAD_DIM
    factor = jnp.where(lane4 < 2, scol, 1.0 - 2.0 * scol)
    terms = jnp.dot(head_segment, place_same, precision=precise, preferred_element_type=f32)
    steps = jnp.dot(head_segment, place_step, precision=precise, preferred_element_type=f32)
    terms = SCALE * (terms + steps * factor)
    high = terms.astype(bf16)
    low = (terms - high.astype(f32)).astype(bf16)
    qaug = jnp.where(lane4 % 2 == 0, high, low)
    kaug = kaug_ref[...]
    for pair in range(2):
        cols = slice(pair * PAIR, (pair + 1) * PAIR)
        mixtures = []
        for head in range(2):
            key_mine = (lanes((KEYS, PAIR)) < HEAD_DIM) == (head == 0)
            row_mine = (lanes((half, PAIR)) < HEAD_DIM) == (head == 0)
            key_x = jnp.where(key_mine, keys[:, cols], kaug)
            parts = []
            for part in range(2):
                rows = slice(part * half, (part + 1) * half)
                query_x = jnp.where(row_mine, head_content[rows, cols], qaug[rows, cols])
                place_x = jnp.where(row_mine, head_position[rows, cols], jnp.zeros((), bf16))
                score = mm_nt(query_x, key_x)
                relative = mm_nt(place_x, rel[:, cols])
                shifted = pltpu.roll(relative, KEYS, 1, stride=1, stride_axis=0)[:, :KEYS]
                score = score + shifted + bias[rows, :]
                score = score - jnp.max(score, axis=1, keepdims=True)
                prob = jnp.exp(score)
                prob = prob * (1.0 / jnp.sum(prob, axis=1, keepdims=True))
                prob = prob.astype(bf16)
                prob_ref[pair * 2 + head, rows, :] = prob
                parts.append(mm(prob, values[:, cols]))
            mixtures.append(jnp.concatenate(parts, axis=0))
        mine = lanes((2 * half, PAIR)) < HEAD_DIM
        att_ref[:, cols] = jnp.where(mine, mixtures[0], mixtures[1])


def norm_forward(summed, gain, shift):
    center = summed - jnp.mean(summed, axis=1, keepdims=True)
    inv = lax.rsqrt(jnp.mean(center * center, axis=1, keepdims=True) + 1e-06)
    unit = center * inv
    return unit, inv, unit * gain + shift


def norm_backward(grad, unit, inv, gain):
    scaled = grad * gain
    return inv * (
        scaled
        - jnp.mean(scaled, axis=1, keepdims=True)
        - unit * jnp.mean(scaled * unit, axis=1, keepdims=True)
    )


def row_sum(value):
    return jnp.sum(value, axis=0, keepdims=True)


def middle_kernel(
    half,
    chunk,
    scal_ref,
    att_ref,
    content_ref,
    query_ref,
    ccot_ref,
    qcot_ref,
    wo_ref,
    up_own_ref,
    up_oth_ref,
    down_own_ref,
    down_oth_ref,
    ubias_own_ref,
    ubias_oth_ref,
    dbias_ref,
    again_ref,
    ashift_ref,
    fgain_ref,
    fshift_ref,
    cout_ref,
    qout_ref,
    sgrad_ref,
    agrad_ref,
    wo_grad_ref,
    ffn_own_ref,
    ffn_oth_ref,
    small_ref,
    ub_own_ref,
    ub_oth_ref,
    hidden,
    slope,
):
    first = pl.multiple_of(scal_ref[0], half)
    part_cols = up_own_ref.shape[1]
    attended = att_ref[...].astype(bf16)
    rows_in = jnp.concatenate([content_ref[pl.ds(first, half), :], query_ref[...]], axis=0)
    summed = mm(attended, wo_ref[...]) + rows_in.astype(f32)
    unit1, inv1, normed = norm_forward(summed, again_ref[...], ashift_ref[...])
    low = normed.astype(bf16)
    sides = (
        (up_own_ref, down_own_ref, ubias_own_ref, ffn_own_ref, ub_own_ref),
        (up_oth_ref, down_oth_ref, ubias_oth_ref, ffn_oth_ref, ub_oth_ref),
    )
    residual = normed + dbias_ref[...]
    for side in range(2):
        up_ref, down_ref, ub_ref = sides[side][:3]
        for at in range(0, part_cols, chunk):
            cols = slice(at, at + chunk)
            x = mm(low, up_ref[:, cols]) + ub_ref[:, cols]
            square = x * x
            inner = (0.7978845608028654 * x) * (1.0 + 0.044715 * square)
            tanh = jnp.tanh(inner)
            act = (0.5 * x * (1.0 + tanh)).astype(bf16)
            grad = 0.5 * (1.0 + tanh) + (0.5 * x) * (1.0 - tanh * tanh) * (
                0.7978845608028654 * (1.0 + 0.134145 * square)
            )
            hidden[side, :, cols] = act
            slope[side, :, cols] = grad.astype(slope.dtype)
            residual = residual + mm(act, down_ref[cols, :])
    unit2, inv2, out = norm_forward(residual, fgain_ref[...], fshift_ref[...])
    cout_ref[...] = out[:half].astype(bf16)
    qout_ref[...] = out[half:].astype(bf16)
    cot = jnp.concatenate([ccot_ref[...], qcot_ref[...]], axis=0).astype(f32)
    small_ref[0:1, :] = row_sum(cot * unit2)
    small_ref[1:2, :] = row_sum(cot)
    residual_grad = norm_backward(cot, unit2, inv2, fgain_ref[...])
    down_grad = residual_grad.astype(bf16)
    small_ref[2:3, :] = row_sum(down_grad.astype(f32))
    down_grad_t = down_grad.T
    low_t = low.T
    grad = residual_grad
    for side in range(2):
        up_ref, down_ref, _, ffn_ref, ubg_ref = sides[side]
        for at in range(0, part_cols, chunk):
            cols = slice(at, at + chunk)
            hidden_grad = mm_nt(down_grad, down_ref[cols, :])
            pre_grad = (hidden_grad * slope[side, :, cols].astype(f32)).astype(bf16)
            ubg_ref[:, cols] = row_sum(pre_grad.astype(f32))
            grad = grad + mm_nt(pre_grad, up_ref[:, cols])
            ffn_ref[0, :, cols] = mm(low_t, pre_grad).astype(bf16)
            ffn_ref[1, :, cols] = mm(down_grad_t, hidden[side, :, cols]).astype(bf16)
    small_ref[3:4, :] = row_sum(grad * unit1)
    small_ref[4:5, :] = row_sum(grad)
    small_ref[5:8, :] = jnp.zeros((3, D), f32)
    summed_grad = norm_backward(grad, unit1, inv1, again_ref[...])
    sgrad_ref[...] = summed_grad
    out_grad = summed_grad.astype(bf16)
    wo_grad_ref[...] = mm(attended.T, out_grad).astype(bf16)
    agrad_ref[...] = mm_nt(out_grad, wo_ref[...]).astype(bf16)


def backward_kernel(
    half,
    prob_ref,
    key_ref,
    val_ref,
    rel_ref,
    hc_ref,
    hp_ref,
    hs_ref,
    kaug_ref,
    scol_ref,
    att_ref,
    agrad_ref,
    se_ref,
    wq_ref,
    wk_ref,
    wv_ref,
    both_t_ref,
    stack_t_ref,
    pos_t_ref,
    rows_in_ref,
    cont_in_ref,
    rows_ref,
    cont_ref,
    qk_ref,
    vr_ref,
    small_ref,
):
    count = 2 * half
    kaug = kaug_ref[...]
    scol = scol_ref[...]
    scol = jnp.concatenate([scol, scol], axis=0)
    swing = 1.0 - 2.0 * scol
    key_t, val_t, rel_t = [], [], []
    proj_grads = []
    hp_rev = jnp.concatenate(
        [
            flip_rows(hp_ref[:half, :].astype(f32)),
            flip_rows(hp_ref[half:, :].astype(f32)),
        ],
        axis=0,
    )
    hp_t = hp_rev.astype(bf16).T
    hc_t = hc_ref[...].T
    agrad_t = agrad_ref[...].T
    lane = lanes((count, PAIR))
    for pair in range(2):
        cols = slice(pair * PAIR, (pair + 1) * PAIR)
        agrad = agrad_ref[:, cols].astype(f32)
        products = agrad * att_ref[:, cols]
        content_heads, place_heads, term_same, term_other = [], [], [], []
        for head in range(2):
            base = (1 - head) * HEAD_DIM
            mine = (lane < HEAD_DIM) == (head == 0)
            key_mine = (lanes((KEYS, PAIR)) < HEAD_DIM) == (head == 0)
            key_x = jnp.where(key_mine, key_ref[:, cols], kaug)
            val_x = jnp.where(key_mine, val_ref[:, cols], kaug)
            weight = jnp.sum(jnp.where(mine, products, 0.0), axis=1, keepdims=True)
            high = weight.astype(bf16).astype(f32)
            grad_x = jnp.where(
                mine,
                agrad,
                jnp.where(lane == base, -high, jnp.where(lane == base + 1, high - weight, 0.0)),
            ).astype(bf16)
            which = pair * 2 + head
            score_grads, rolled, places = [], [], []
            for part in range(2):
                rows = slice(part * half, (part + 1) * half)
                spread = mm_nt(grad_x[rows], val_x)
                score_grad = prob_ref[which, rows, :].astype(f32) * spread
                score_grads.append(score_grad.astype(bf16))
                wide = jnp.concatenate(
                    [flip_rows(score_grad), jnp.zeros((half, half), f32)], axis=1
                )
                turned = pltpu.roll(wide, 1, 1, stride=1, stride_axis=0).astype(bf16)
                rolled.append(turned)
                places.append(flip_rows(mm(turned, rel_ref[:, cols])))
            score_grad = jnp.concatenate(score_grads, axis=0)
            rolled = jnp.concatenate(rolled, axis=0)
            head_rows = slice(which * HEAD_DIM, (which + 1) * HEAD_DIM)
            val_t.append(mm(agrad_t[head_rows], prob_ref[which]))
            key_t.append(mm(hc_t[head_rows], score_grad))
            rel_t.append(mm(hp_t[head_rows], rolled))
            content_head = mm(score_grad, key_x)
            content_heads.append(content_head)
            place_heads.append(jnp.concatenate(places, axis=0))
            total = content_head[:, base : base + 1]
            marked = content_head[:, base + 2 : base + 3]
            differ = SCALE * (scol * total + swing * marked)
            term_other.append(differ)
            term_same.append(SCALE * total - differ)
        first_head = lane < HEAD_DIM
        content_grad = (SCALE * jnp.where(first_head, *content_heads)).astype(bf16).astype(f32)
        place_grad = (SCALE * jnp.where(first_head, *place_heads)).astype(bf16).astype(f32)
        same = jnp.where(first_head, *term_same)
        other = jnp.where(first_head, *term_other)
        segment_grad = same * se_ref[0:1, cols] + other * se_ref[1:2, cols]
        proj_grads.append((content_grad + place_grad + segment_grad).astype(bf16))
        small_ref[0:1, cols] = row_sum(content_grad)
        small_ref[1:2, cols] = row_sum(place_grad)
        small_ref[2:3, cols] = row_sum(segment_grad)
        head_segment = hs_ref[:, cols]
        small_ref[3:4, cols] = row_sum(same * head_segment)
        small_ref[4:5, cols] = row_sum(other * head_segment)
    small_ref[5:8, :] = jnp.zeros((3, QUAD), f32)
    proj_grad = jnp.concatenate(proj_grads, axis=1)
    key_t = jnp.concatenate(key_t, axis=0).astype(bf16)
    val_t = jnp.concatenate(val_t, axis=0).astype(bf16)
    rel_t = jnp.concatenate(rel_t, axis=0).astype(bf16)
    qk_ref[:, :QUAD] = mm(both_t_ref[...], proj_grad).astype(bf16)
    qk_ref[:, QUAD:] = mm_nt(stack_t_ref[...], key_t).astype(bf16)
    vr_ref[:, :QUAD] = mm_nt(stack_t_ref[...], val_t).astype(bf16)
    vr_ref[:, QUAD:] = mm_nt(pos_t_ref[...], rel_t).astype(bf16)
    rows_ref[...] = rows_in_ref[...] + mm_nt(proj_grad, wq_ref[...])
    cont_ref[...] = (
        cont_in_ref[...]
        + mm_nt(key_t[:, MEM:].T, wk_ref[...])
        + mm_nt(val_t[:, MEM:].T, wv_ref[...])
    )


def whole(shape):
    return pl.BlockSpec(shape, lambda i: (0,) * len(shape))


def columns(rows, width, at=None):
    if at is None:
        return pl.BlockSpec((rows, width), lambda i: (0, i))
    return pl.BlockSpec((rows, width), lambda i: (0, at))


def scalars():
    return pl.BlockSpec(memory_space=pltpu.SMEM)


def params():
    return pltpu.CompilerParams(vmem_limit_bytes=VMEM_BYTES)


def cost(flops, bytes_accessed):
    return pl.CostEstimate(flops=flops, bytes_accessed=bytes_accessed, transcendentals=0)


def attention_forward(
    half, scal, seg, order, target, memory, content, query, weights, biases, segment_embed
):
    count, window = 2 * half, KEYS + half
    coarse_rows = -(-(window // 32) // 8) * 8
    outs = (
        ((count, D), f32, columns(count, QUAD)),
        ((HEADS, count, KEYS), bf16, pl.BlockSpec((4, count, KEYS), lambda i: (i, 0, 0))),
        ((KEYS, D), bf16, columns(KEYS, QUAD)),
        ((KEYS, D), bf16, columns(KEYS, QUAD)),
        ((window, D), bf16, columns(window, QUAD)),
        ((count, D), bf16, columns(count, QUAD)),
        ((count, D), bf16, columns(count, QUAD)),
        ((count, D), f32, columns(count, QUAD)),
        ((KEYS, PAIR), bf16, whole((KEYS, PAIR))),
        ((half, PAIR), f32, whole((half, PAIR))),
        ((D, count), bf16, whole((D, count))),
        ((D, KEYS), bf16, whole((D, KEYS))),
        ((D, window), bf16, whole((D, window))),
    )
    return pl.pallas_call(
        functools.partial(forward_kernel, half),
        grid=(QUADS,),
        out_shape=[jax.ShapeDtypeStruct(shape, kind) for shape, kind, _ in outs],
        in_specs=[
            scalars(),
            whole((1, LEN)),
            whole((1, LEN)),
            whole((1, LEN)),
            whole((MEM, D)),
            whole((LEN, D)),
            whole((half, D)),
        ]
        + [columns(D, QUAD)] * 4
        + [columns(1, QUAD)] * 3
        + [pl.BlockSpec((QUAD, 2), lambda i: (i, 0))],
        out_specs=[spec for _, _, spec in outs],
        scratch_shapes=[
            pltpu.VMEM((KEYS, D), bf16),
            pltpu.VMEM((count, D), bf16),
            pltpu.VMEM((window, D), bf16),
            pltpu.VMEM((count, KEYS), f32),
            pltpu.VMEM((2, 32, D // 2), f32),
            pltpu.VMEM((2, coarse_rows, D // 2), f32),
        ],
        compiler_params=params(),
        cost_estimate=cost(10_000_000_000, 40_000_000),
        name="attention_forward",
    )(scal, seg, order, target, memory, content, query, *weights, *biases, segment_embed)


def middle(half, scal, arrays, hidden_cols):
    count = 2 * half
    chunk = min(hidden_cols, 768)
    outs = (
        ((half, D), bf16),
        ((half, D), bf16),
        ((count, D), f32),
        ((count, D), bf16),
        ((D, D), bf16),
        ((2, D, hidden_cols), bf16),
        ((2, D, hidden_cols), bf16),
        ((8, D), f32),
        ((1, hidden_cols), f32),
        ((1, hidden_cols), f32),
    )
    return pl.pallas_call(
        functools.partial(middle_kernel, half, chunk),
        grid=(1,),
        out_shape=[jax.ShapeDtypeStruct(shape, kind) for shape, kind in outs],
        in_specs=[scalars()] + [whole(array.shape) for array in arrays],
        out_specs=[whole(shape) for shape, _ in outs],
        scratch_shapes=[
            pltpu.VMEM((2, count, hidden_cols), bf16),
            pltpu.VMEM((2, count, hidden_cols), bf16),
        ],
        compiler_params=params(),
        cost_estimate=cost(16_000_000_000, 40_000_000),
        name="feed_forward",
    )(scal, *arrays)


def attention_backward(half, at, saved, agrad, segment_rows, weights, rows_grad, content_part):
    count, window = 2 * half, KEYS + half
    att, prob, keys, values, rel, hc, hp, hs, kaug, scol, both_t, stack_t, pos_t = saved
    wq, wk, wv = weights
    operands = (
        (prob, pl.BlockSpec((4, count, KEYS), lambda i: (at, 0, 0))),
        (keys, columns(KEYS, QUAD, at)),
        (values, columns(KEYS, QUAD, at)),
        (rel, columns(window, QUAD, at)),
        (hc, columns(count, QUAD, at)),
        (hp, columns(count, QUAD, at)),
        (hs, columns(count, QUAD, at)),
        (kaug, whole((KEYS, PAIR))),
        (scol, whole((half, PAIR))),
        (att, columns(count, QUAD, at)),
        (agrad, columns(count, QUAD, at)),
        (segment_rows, columns(2, QUAD, at)),
        (wq, columns(D, QUAD, at)),
        (wk, columns(D, QUAD, at)),
        (wv, columns(D, QUAD, at)),
        (both_t, whole((D, count))),
        (stack_t, whole((D, KEYS))),
        (pos_t, whole((D, window))),
        (rows_grad, whole((count, D))),
        (content_part, whole((LEN, D))),
    )
    outs = (
        ((count, D), f32),
        ((LEN, D), f32),
        ((D, 2 * QUAD), bf16),
        ((D, 2 * QUAD), bf16),
        ((8, QUAD), f32),
    )
    return pl.pallas_call(
        functools.partial(backward_kernel, half),
        grid=(1,),
        out_shape=[jax.ShapeDtypeStruct(shape, kind) for shape, kind in outs],
        in_specs=[spec for _, spec in operands],
        out_specs=[whole(shape) for shape, _ in outs],
        input_output_aliases={18: 0, 19: 1},
        compiler_params=params(),
        cost_estimate=cost(7_000_000_000, 16_000_000),
        name="attention_backward",
    )(*[array for array, _ in operands])


def swap(array):
    groups = lax.axis_size("tensor")
    return lax.ppermute(array, "tensor", [(i, (i + 1) % groups) for i in range(groups)])


def pick(array, index, axis):
    return lax.dynamic_index_in_dim(array, index, axis, keepdims=False)


def scatter_rows(array, order):
    size = lax.axis_size("dp")
    me = lax.axis_index("dp")
    bits = size.bit_length() - 1
    array = array.reshape((2,) * bits + array.shape[1:])
    left = list(range(bits - 1, -1, -1))
    for bit in order:
        axis = left.index(bit)
        left.remove(bit)
        mine = (me >> bit) & 1
        pairs = [(i, i ^ (1 << bit)) for i in range(size)]
        keep = pick(array, mine, axis)
        got = lax.ppermute(pick(array, 1 - mine, axis), "dp", pairs)
        array = keep.astype(f32) + got.astype(f32)
        if left:
            array = array.astype(bf16)
    return array


def orders_for(size):
    bits = size.bit_length() - 1
    plain = list(range(bits))
    turned = plain[1:2] + plain[:1] + plain[2:]
    return plain, turned


def by_owner(array, member):
    size, groups = lax.axis_size("dp"), lax.axis_size("tensor")
    blocks = array.reshape(size, groups, -1, array.shape[1])
    return pick(blocks, member, 1), pick(blocks, 1 - member, 1)


def reduce_rows(array, member, order):
    own, other = by_owner(array, member)
    total = (own.astype(f32) + swap(other).astype(f32)).astype(bf16)
    return scatter_rows(total, order)


def all_sum(array):
    array = array + swap(array)
    size = lax.axis_size("dp")
    for bit in range(size.bit_length() - 1):
        array = array + lax.ppermute(array, "dp", [(i, i ^ (1 << bit)) for i in range(size)])
    return array


def body(
    content_in,
    query_in,
    memory,
    content_cot,
    query_cot,
    query_weight,
    key_weight,
    value_weight,
    out_weight,
    rel_weight,
    content_bias,
    position_bias,
    segment_bias,
    segment_embed,
    attn_gain,
    attn_shift,
    up_weight,
    up_bias,
    down_weight,
    down_bias,
    ffn_gain,
    ffn_shift,
    lengths,
    memory_lengths,
    segment_ids,
    orders,
    targets,
):
    groups = lax.axis_size("tensor")
    size = lax.axis_size("dp")
    member = lax.axis_index("tensor")
    place = lax.axis_index("dp") * groups + member
    half = LEN // groups
    hidden_cols = up_weight.shape[1]
    plain, turned = orders_for(size)
    first_row = member * half
    up_other, down_other = swap(up_weight), swap(down_weight)
    scal = jnp.stack([first_row.astype(jnp.int32), lengths[0], memory_lengths[0]])
    content, query = content_in[0], query_in[0]

    def row(vector):
        return vector.reshape(1, -1)

    saved = attention_forward(
        half,
        scal,
        segment_ids,
        orders,
        targets,
        memory[0],
        content,
        query,
        (query_weight, key_weight, value_weight, rel_weight),
        (row(content_bias), row(position_bias), row(segment_bias)),
        segment_embed,
    )
    bias_parts = up_bias.reshape(groups, 1, hidden_cols)
    (
        content_out,
        query_out,
        summed_grad,
        attended_grad,
        out_part,
        ffn_own,
        ffn_other,
        early_small,
        up_bias_own,
        up_bias_other,
    ) = middle(
        half,
        scal,
        (
            saved[0],
            content,
            query,
            content_cot[0],
            query_cot[0],
            out_weight,
            up_weight,
            up_other,
            down_weight,
            down_other,
            pick(bias_parts, member, 0),
            pick(bias_parts, 1 - member, 0),
            row(down_bias),
            row(attn_gain),
            row(attn_shift),
            row(ffn_gain),
            row(ffn_shift),
        ),
        hidden_cols,
    )
    got = swap(ffn_other)
    ffn = (ffn_own.astype(f32) + got.astype(f32)).astype(bf16)
    up_grad = scatter_rows(ffn[0].reshape(size, -1, hidden_cols), plain)
    down_grad = scatter_rows(ffn[1].reshape(size, -1, hidden_cols), turned)
    out_grad = reduce_rows(out_part, member, plain)
    rows_grad = summed_grad
    content_part = jnp.zeros((LEN, D), f32)
    pieces, late_small = [], []
    for at in range(QUADS):
        rows_grad, content_part, qk_part, vr_part, small = attention_backward(
            half,
            at,
            saved,
            attended_grad,
            segment_embed.T,
            (query_weight, key_weight, value_weight),
            rows_grad,
            content_part,
        )
        late_small.append(small)
        pieces.append(
            (reduce_rows(qk_part, member, plain), reduce_rows(vr_part, member, turned))
        )
    content_halves = content_part.reshape(groups, half, D)
    content_got = swap(pick(content_halves, 1 - member, 0).astype(bf16))
    content_grad = rows_grad[:half] + pick(content_halves, member, 0) + content_got.astype(f32)
    query_grad = rows_grad[half:]
    up_bias_rows = jnp.where(
        member == 0,
        jnp.concatenate([up_bias_own, up_bias_other], axis=0),
        jnp.concatenate([up_bias_other, up_bias_own], axis=0),
    )
    small = jnp.concatenate(
        [early_small[:5], jnp.concatenate(late_small, axis=1)[:5], up_bias_rows.reshape(-1, D)],
        axis=0,
    )
    small = all_sum(small)
    share = D // (size * groups)
    vectors = lax.dynamic_slice_in_dim(small[:10], place * share, share, 1)
    up_bias_grad = lax.dynamic_slice_in_dim(
        small[10:].reshape(-1), place * (FF // (size * groups)), FF // (size * groups), 0
    )

    def joined(pick_one):
        return jnp.concatenate([pick_one(piece) for piece in pieces], axis=1)

    query_weight_grad = joined(lambda piece: piece[0][:, :QUAD])
    key_weight_grad = joined(lambda piece: piece[0][:, QUAD:])
    value_weight_grad = joined(lambda piece: piece[1][:, :QUAD])
    rel_weight_grad = joined(lambda piece: piece[1][:, QUAD:])
    return (
        content_out[None],
        query_out[None],
        content_grad[None],
        query_grad[None],
        query_weight_grad,
        key_weight_grad,
        value_weight_grad,
        out_grad,
        rel_weight_grad,
        vectors[5],
        vectors[6],
        vectors[7],
        vectors[8:10].T,
        vectors[3],
        vectors[4],
        up_grad,
        up_bias_grad,
        down_grad.T,
        vectors[2],
        vectors[0],
        vectors[1],
    )


def solution(mesh):
    in_specs = (
        P("dp", None, None),
        P("dp", "tensor", None),
        P("dp", None, None),
        P("dp", "tensor", None),
        P("dp", "tensor", None),
        P(),
        P(),
        P(),
        P(),
        P(),
        P(),
        P(),
        P(),
        P(),
        P(),
        P(),
        P(None, "tensor"),
        P(),
        P("tensor", None),
        P(),
        P(),
        P(),
        P("dp"),
        P("dp"),
        P("dp", None),
        P("dp", None),
        P("dp", None),
    )
    out_specs = (
        P("dp", "tensor", None),
        P("dp", "tensor", None),
        P("dp", "tensor", None),
        P("dp", "tensor", None),
        P(("dp", "tensor"), None),
        P(("dp", "tensor"), None),
        P(("dp", "tensor"), None),
        P(("dp", "tensor"), None),
        P(("dp", "tensor"), None),
        P(("dp", "tensor")),
        P(("dp", "tensor")),
        P(("dp", "tensor")),
        P(("dp", "tensor"), None),
        P(("dp", "tensor")),
        P(("dp", "tensor")),
        P("dp", "tensor"),
        P(("dp", "tensor")),
        P("tensor", "dp"),
        P(("dp", "tensor")),
        P(("dp", "tensor")),
        P(("dp", "tensor")),
    )
    return jax.shard_map(body, mesh=mesh, in_specs=in_specs, out_specs=out_specs, check_vma=False)
```

```python
import functools

import jax
import jax.numpy as jnp
from jax import lax
from jax.experimental import pallas as pl
from jax.experimental.pallas import tpu as pltpu
from jax.sharding import PartitionSpec as P

D = 768
HEADS = 12
HEAD_DIM = 64
FF = 3072
LEN = 512
MEM = 384
KEYS = MEM + LEN
QUAD = 4 * HEAD_DIM
QUADS = D // QUAD
PAIR = 2 * HEAD_DIM
SCALE = HEAD_DIM ** (-0.5)
VMEM_BYTES = 56 * 1024 * 1024
BLOCK = 32
TILE = 128

f32 = jnp.float32
bf16 = jnp.bfloat16
precise = lax.Precision.HIGHEST


def mm(left, right):
    return lax.dot_general(left, right, (((1,), (0,)), ((), ())), preferred_element_type=f32)


def mm_nt(left, right):
    return lax.dot_general(left, right, (((1,), (1,)), ((), ())), preferred_element_type=f32)


def lanes(shape):
    return lax.broadcasted_iota(jnp.int32, shape, 1)


def column_of(row):
    return jnp.broadcast_to(row.astype(f32), (128, row.shape[1])).T


def flip_rows(value):
    count, width = value.shape
    groups = value.reshape(count // 8, 8, width)
    index = 7 - lax.broadcasted_iota(jnp.int32, groups.shape, 1)
    turned = jnp.take_along_axis(groups, index, axis=1, mode="promise_in_bounds")
    return jnp.concatenate([turned[i] for i in range(count // 8 - 1, -1, -1)], axis=0)


def lane_tiles(value, combine):
    tiles = [value[:, at : at + TILE] for at in range(0, value.shape[1], TILE)]
    return functools.reduce(combine, tiles)


def order_of(core, bits):
    plain = list(range(bits))
    return plain[1:2] + plain[:1] + plain[2:] if core == 1 and bits > 1 else plain


def block_owner(place, core, bits):
    owner = jnp.zeros_like(place)
    for step in range(bits):
        owner = owner | (((place >> (bits - 1 - step)) & 1) << step)
    if bits > 1:
        swapped = (owner & ~3) | ((owner & 1) << 1) | ((owner >> 1) & 1)
        owner = jnp.where(core == 1, swapped, owner)
    return owner ^ lax.axis_index("dp")


def one_hot(source):
    return jnp.where(lanes((source.shape[0], D)) == source, 1.0, 0.0).astype(bf16)


def owner_rows(size, groups):
    share = D // (size * groups)
    row = lax.broadcasted_iota(jnp.int32, (D, 1), 0)
    side, rest = lax.div(row, size * share), lax.rem(row, size * share)
    core = lax.rem(lax.axis_index("tensor") + side, groups)
    owner = block_owner(lax.div(rest, share), core, size.bit_length() - 1)
    return one_hot((owner * groups + core) * share + lax.rem(rest, share))


def shared_rows(size, core):
    share = D // size
    row = lax.broadcasted_iota(jnp.int32, (D, 1), 0)
    owner = block_owner(lax.div(row, share), core, size.bit_length() - 1)
    return one_hot(owner * share + lax.rem(row, share))


def forward_kernel(
    half,
    size,
    groups,
    length_ref,
    mem_length_ref,
    seg_ref,
    ord_ref,
    tgt_ref,
    memory_ref,
    content_ref,
    query_ref,
    wq_ref,
    wk_ref,
    wv_ref,
    wr_ref,
    cb_ref,
    pb_ref,
    sb_ref,
    se_ref,
    att_ref,
    prob_ref,
    key_ref,
    val_ref,
    rel_ref,
    hc_ref,
    hp_ref,
    hs_ref,
    linv_ref,
    kaug_ref,
    scol_ref,
    both_t_ref,
    stack_t_ref,
    pos_t_ref,
    stack,
    both,
    pos,
    bias,
    fine,
    coarse,
    vectors,
    scores,
    places,
):
    window = KEYS + half
    first = pl.multiple_of(lax.axis_index("tensor") * half, half)
    step_id = pl.program_id(0)

    @pl.when(step_id == 0)
    def _():
        stack[:MEM, :] = memory_ref[...]
        stack[MEM:, :] = content_ref[...]
        both[:half, :] = content_ref[pl.ds(first, half), :]
        both[half:, :] = query_ref[...]
        vectors[0:1, :] = cb_ref[...][None, :]
        vectors[1:2, :] = pb_ref[...][None, :]
        vectors[2:3, :] = sb_ref[...][None, :]
        step = lax.broadcasted_iota(jnp.int32, (1, D // 2), 1).astype(f32) * (2.0 / D)
        inverse = 1.0 / jnp.power(jnp.full((1, D // 2), 10000.0, f32), step)
        coarse_rows = coarse.shape[1]
        top = (MEM + half + first).astype(f32)
        angle = (
            top - 32.0 * lax.broadcasted_iota(jnp.int32, (coarse_rows, 1), 0).astype(f32)
        ) * inverse
        coarse[0] = jnp.sin(angle)
        coarse[1] = jnp.cos(angle)
        small = lax.broadcasted_iota(jnp.int32, (32, 1), 0).astype(f32) * inverse
        fine[0] = jnp.sin(small)
        fine[1] = jnp.cos(small)
        for a in range(window // 32):
            sa, ca = coarse[0, a : a + 1, :], coarse[1, a : a + 1, :]
            sb, cb = fine[0], fine[1]
            pos[a * 32 : (a + 1) * 32, : D // 2] = (sa * cb - ca * sb).astype(bf16)
            pos[a * 32 : (a + 1) * 32, D // 2 :] = (ca * cb + sa * sb).astype(bf16)
        never = float(LEN + 1)
        mem_at = lax.broadcasted_iota(jnp.int32, (1, MEM), 1)
        tok_at = lax.broadcasted_iota(jnp.int32, (1, LEN), 1)
        open_from = jnp.concatenate(
            [
                jnp.where(mem_at >= MEM - mem_length_ref[0], -1.0, never),
                jnp.where(
                    tok_at < length_ref[0],
                    jnp.where(tgt_ref[...] == 0, -1.0, ord_ref[...].astype(f32)),
                    never,
                ),
            ],
            axis=1,
        )
        order_col = column_of(ord_ref[...])
        seg_col = column_of(seg_ref[...])
        kaug_lane = lanes((LEN, PAIR)) % HEAD_DIM
        kaug_ref[:MEM, :] = (lanes((MEM, PAIR)) % HEAD_DIM < 4).astype(f32).astype(bf16)
        kaug_ref[MEM:, :] = jnp.where(
            kaug_lane < 4, 1.0, jnp.where(kaug_lane < 6, seg_col, 0.0)
        ).astype(bf16)
        bias[:LEN, :PAIR] = order_col
        own_order = bias[pl.ds(first, half), :PAIR][:, :1]
        bias[:LEN, :PAIR] = seg_col
        scol_ref[...] = bias[pl.ds(first, half), :PAIR]
        seen = open_from <= own_order
        bias[:half, :] = jnp.where(seen, 0.0, -1e30)
        key_at = lax.broadcasted_iota(jnp.int32, (half, KEYS), 1)
        row_at = lax.broadcasted_iota(jnp.int32, (half, KEYS), 0)
        seen_q = seen & (key_at - MEM != row_at + first)
        bias[half:, :] = jnp.where(seen_q, 0.0, -1e30)
        chosen = owner_rows(size, groups)
        both_t_ref[...] = mm_nt(chosen, both[...]).astype(bf16)
        stack_t_ref[...] = mm_nt(chosen, stack[...]).astype(bf16)
        pos_t_ref[...] = mm_nt(chosen, pos[...]).astype(bf16)

    here = pl.ds(pl.multiple_of(step_id * QUAD, QUAD), QUAD)
    keys = mm(stack[...], wk_ref[...]).astype(bf16)
    values = mm(stack[...], wv_ref[...]).astype(bf16)
    rel = mm(pos[...], wr_ref[...]).astype(bf16)
    projection = mm(both[...], wq_ref[...])
    head_content = (projection + vectors[0:1, here]).astype(bf16)
    head_position = (projection + vectors[1:2, here]).astype(bf16)
    head_segment = projection + vectors[2:3, here]
    key_ref[...] = keys
    val_ref[...] = values
    rel_ref[...] = rel
    hs_ref[...] = head_segment
    head_content = (head_content.astype(f32) * SCALE).astype(bf16)
    head_position = (head_position.astype(f32) * SCALE).astype(bf16)
    hc_ref[...] = head_content
    hp_ref[...] = head_position
    same = column_of(se_ref[0:1, :])
    differ = column_of(se_ref[1:2, :] - se_ref[0:1, :])
    same = jnp.concatenate([same, same], axis=1)
    differ = jnp.concatenate([differ, differ], axis=1)
    row_head = lax.broadcasted_iota(jnp.int32, (QUAD, QUAD), 0) // HEAD_DIM
    at = lanes((QUAD, QUAD)) - ((row_head // 2) * PAIR + (1 - row_head % 2) * HEAD_DIM)
    embed = jnp.where(
        (at >= 0) & (at < 2), same, jnp.where((at >= 2) & (at < 6), differ, 0.0)
    )
    embed_high = embed.astype(bf16)
    embed_low = (embed - embed_high.astype(f32)).astype(bf16)
    segment_high = head_segment.astype(bf16)
    segment_low = (head_segment - segment_high.astype(f32)).astype(bf16)
    terms = (
        mm(segment_high, embed_high) + mm(segment_high, embed_low) + mm(segment_low, embed_high)
    )
    scol = scol_ref[...]
    scol = jnp.concatenate([scol, scol], axis=0)
    scol = jnp.concatenate([scol, scol], axis=1)
    lane6 = lanes((2 * half, QUAD)) % HEAD_DIM
    factor = jnp.where(lane6 < 2, 1.0, jnp.where(lane6 < 4, scol, 1.0 - 2.0 * scol))
    terms = SCALE * (terms * factor)
    high = terms.astype(bf16)
    low = (terms - high.astype(f32)).astype(bf16)
    qaug = jnp.where(lane6 % 2 == 0, high, low)
    kaug = kaug_ref[...]
    sums = []
    turn = 0
    for pair in range(2):
        cols = slice(pair * PAIR, (pair + 1) * PAIR)
        mixtures = []
        for head in range(2):
            key_mine = (lanes((KEYS, PAIR)) < HEAD_DIM) == (head == 0)
            row_mine = (lanes((half, PAIR)) < HEAD_DIM) == (head == 0)
            key_x = jnp.where(key_mine, keys[:, cols], kaug)
            which = pair * 2 + head
            parts, totals = [], []
            for part in range(2):
                rows = slice(part * half, (part + 1) * half)
                query_x = jnp.where(row_mine, head_content[rows, cols], qaug[rows, cols])
                place_x = jnp.where(row_mine, head_position[rows, cols], jnp.zeros((), bf16))
                slot, turn = turn % 2, turn + 1
                scores[slot] = mm_nt(query_x, key_x)
                places[slot] = mm_nt(place_x, rel[:, cols])
                peaks = []
                for b in range(0, half, BLOCK):
                    block = slice(b, b + BLOCK)
                    shifted = pltpu.roll(
                        places[slot, block, :], (KEYS + b) % window, 1, stride=1, stride_axis=0
                    )[:, :KEYS]
                    score = (
                        scores[slot, block, :]
                        + shifted
                        + bias[part * half + b : part * half + b + BLOCK, :]
                    )
                    scores[slot, block, :] = score
                    peaks.append(lane_tiles(score, jnp.maximum))
                peak = jnp.max(jnp.concatenate(peaks, axis=0), axis=1, keepdims=True)
                pieces = []
                for b in range(0, half, BLOCK):
                    block = slice(b, b + BLOCK)
                    prob = jnp.exp(scores[slot, block, :] - peak[block])
                    pieces.append(lane_tiles(prob, jnp.add))
                    prob_ref[which, part * half + b : part * half + b + BLOCK, :] = prob.astype(
                        bf16
                    )
                total = 1.0 / jnp.sum(jnp.concatenate(pieces, axis=0), axis=1, keepdims=True)
                totals.append(total)
                parts.append(mm(prob_ref[which, rows, :], values[:, cols]) * total)
            mixtures.append(jnp.concatenate(parts, axis=0))
            sums.append(jnp.concatenate(totals, axis=0))
        mine = lanes((2 * half, PAIR)) < HEAD_DIM
        att_ref[:, cols] = jnp.where(mine, mixtures[0], mixtures[1])
    lane = lanes((2 * half, TILE))
    linv_ref[...] = jnp.where(
        lane == 0, sums[0], jnp.where(lane == 1, sums[1], jnp.where(lane == 2, sums[2], sums[3]))
    )


def norm_forward(summed, gain, shift):
    center = summed - jnp.mean(summed, axis=1, keepdims=True)
    inv = lax.rsqrt(jnp.mean(center * center, axis=1, keepdims=True) + 1e-06)
    unit = center * inv
    return unit, inv, unit * gain + shift


def norm_backward(grad, unit, inv, gain):
    scaled = grad * gain
    return inv * (
        scaled
        - jnp.mean(scaled, axis=1, keepdims=True)
        - unit * jnp.mean(scaled * unit, axis=1, keepdims=True)
    )


def row_sum(value):
    return jnp.sum(value, axis=0, keepdims=True)


def gelu_parts(x):
    square = x * x
    tanh = jnp.tanh((0.7978845608028654 * x) * (1.0 + 0.044715 * square))
    rise = 0.5 * (1.0 + tanh)
    grad = rise + (0.5 * x) * (1.0 - tanh * tanh) * (
        0.7978845608028654 * (1.0 + 0.134145 * square)
    )
    return x * rise, grad


def upper_kernel(
    half,
    size,
    chunk,
    att_ref,
    content_ref,
    query_ref,
    ccot_ref,
    qcot_ref,
    wo_ref,
    up_own_hbm,
    up_oth_hbm,
    down_own_hbm,
    down_oth_hbm,
    ubias_ref,
    dbias_ref,
    again_ref,
    ashift_ref,
    fgain_ref,
    fshift_ref,
    cout_ref,
    qout_ref,
    ffn_oth_hbm,
    hid_ref,
    slope_ref,
    dgrad_ref,
    grad_ref,
    unit_ref,
    inv_ref,
    small_ref,
    ub_oth_ref,
    ups,
    downs,
    hidden,
    slope,
    ffn,
    vectors,
    sems,
    out_sems,
):
    first = pl.multiple_of(lax.axis_index("tensor") * half, half)
    member = lax.axis_index("tensor")
    part_cols = ups.shape[2]
    chunks = part_cols // chunk
    sources = ((up_own_hbm, down_own_hbm), (up_oth_hbm, down_oth_hbm))

    def loads(side, at):
        cols = pl.ds(at * chunk, chunk)
        return (
            pltpu.make_async_copy(
                sources[side][0].at[:, cols], ups.at[side, :, cols], sems.at[0, side, at]
            ),
            pltpu.make_async_copy(
                sources[side][1].at[cols, :], downs.at[side, cols, :], sems.at[1, side, at]
            ),
        )

    for side in range(2):
        for at in range(chunks):
            for copy in loads(side, at):
                copy.start()
    vectors[0:1, :] = ubias_ref[...][None, :]
    attended = att_ref[...].astype(bf16)
    rows_in = jnp.concatenate([content_ref[pl.ds(first, half), :], query_ref[...]], axis=0)
    summed = mm(attended, wo_ref[...]) + rows_in.astype(f32)
    unit1, inv1, normed = norm_forward(summed, again_ref[...][None, :], ashift_ref[...][None, :])
    unit_ref[...] = unit1
    inv_ref[...] = jnp.broadcast_to(inv1, inv_ref.shape)
    low = normed.astype(bf16)
    residual = normed + dbias_ref[...][None, :]
    for side in range(2):
        start = lax.rem(member + side, 2) * part_cols
        for at in range(chunks):
            cols = slice(at * chunk, (at + 1) * chunk)
            for copy in loads(side, at):
                copy.wait()
            bias = vectors[0:1, pl.ds(pl.multiple_of(start + at * chunk, TILE), chunk)]
            act, grad = gelu_parts(mm(low, ups[side, :, cols]) + bias)
            act, grad = act.astype(bf16), grad.astype(bf16)
            if side == 0:
                hid_ref[:, cols] = act
                slope_ref[:, cols] = grad
            else:
                hidden[:, cols] = act
                slope[:, cols] = grad
            residual = residual + mm(act, downs[side, cols, :])
    unit2, inv2, out = norm_forward(residual, fgain_ref[...][None, :], fshift_ref[...][None, :])
    cout_ref[...] = out[:half].astype(bf16)
    qout_ref[...] = out[half:].astype(bf16)
    cot = jnp.concatenate([ccot_ref[...], qcot_ref[...]], axis=0).astype(f32)
    small_ref[0:1, :] = row_sum(cot * unit2)
    small_ref[1:2, :] = row_sum(cot)
    residual_grad = norm_backward(cot, unit2, inv2, fgain_ref[...][None, :])
    down_grad = residual_grad.astype(bf16)
    dgrad_ref[...] = down_grad
    small_ref[2:3, :] = row_sum(down_grad.astype(f32))
    small_ref[3:8, :] = jnp.zeros((5, D), f32)
    chosen = shared_rows(size, 1 - member)
    down_grad_t = mm_nt(chosen, down_grad).astype(bf16)
    low_t = mm_nt(chosen, low).astype(bf16)
    grad = residual_grad
    copies = []
    for at in range(chunks):
        cols = slice(at * chunk, (at + 1) * chunk)
        hidden_grad = mm_nt(down_grad, downs[1, cols, :])
        pre_grad = (hidden_grad * slope[:, cols].astype(f32)).astype(bf16)
        ub_oth_ref[:, cols] = row_sum(pre_grad.astype(f32))
        ffn[0, :, cols] = mm(low_t, pre_grad).astype(bf16)
        ffn[1, :, cols] = mm(down_grad_t, hidden[:, cols]).astype(bf16)
        window = (slice(None), slice(None), pl.ds(at * chunk, chunk))
        copy = pltpu.make_async_copy(ffn.at[window], ffn_oth_hbm.at[window], out_sems.at[at])
        copy.start()
        copies.append(copy)
        grad = grad + mm_nt(pre_grad, ups[1, :, cols])
    grad_ref[...] = grad
    for copy in copies:
        copy.wait()


def lower_kernel(
    half,
    size,
    groups,
    chunk,
    att_ref,
    hid_hbm,
    slope_ref,
    dgrad_ref,
    grad_in_ref,
    unit_hbm,
    inv_ref,
    wo_hbm,
    up_hbm,
    down_ref,
    again_ref,
    ashift_ref,
    ffn_own_hbm,
    sgrad_ref,
    agrad_ref,
    out_own_ref,
    out_oth_ref,
    small_ref,
    ub_own_ref,
    hidden,
    unit,
    wo,
    up,
    ffn,
    sems,
    out_sems,
):
    member = lax.axis_index("tensor")
    part_cols = up.shape[1]
    fetches = [
        pltpu.make_async_copy(source, target, sems.at[index])
        for index, (source, target) in enumerate(
            ((hid_hbm, hidden), (up_hbm, up), (unit_hbm, unit), (wo_hbm, wo))
        )
    ]
    for fetch in fetches:
        fetch.start()
    down_grad = dgrad_ref[...]
    gain, shift = again_ref[...][None, :], ashift_ref[...][None, :]
    chosen = shared_rows(size, member)
    down_grad_t = mm_nt(chosen, down_grad).astype(bf16)
    fetches[2].wait()
    low = (unit[...] * gain + shift).astype(bf16)
    low_t = mm_nt(chosen, low).astype(bf16)
    grad = grad_in_ref[...]
    copies = []
    for at in range(part_cols // chunk):
        cols = slice(at * chunk, (at + 1) * chunk)
        hidden_grad = mm_nt(down_grad, down_ref[cols, :])
        pre_grad = (hidden_grad * slope_ref[:, cols].astype(f32)).astype(bf16)
        ub_own_ref[:, cols] = row_sum(pre_grad.astype(f32))
        ffn[0, :, cols] = mm(low_t, pre_grad).astype(bf16)
        if at == 0:
            fetches[0].wait()
            fetches[1].wait()
        ffn[1, :, cols] = mm(down_grad_t, hidden[:, cols]).astype(bf16)
        window = (slice(None), slice(None), pl.ds(at * chunk, chunk))
        copy = pltpu.make_async_copy(ffn.at[window], ffn_own_hbm.at[window], out_sems.at[at])
        copy.start()
        copies.append(copy)
        grad = grad + mm_nt(pre_grad, up[:, cols])
    unit1, inv1 = unit[...], inv_ref[:, :1]
    small_ref[0:1, :] = row_sum(grad * unit1)
    small_ref[1:2, :] = row_sum(grad)
    small_ref[2:8, :] = jnp.zeros((6, D), f32)
    summed_grad = norm_backward(grad, unit1, inv1, gain)
    sgrad_ref[...] = summed_grad
    out_grad = summed_grad.astype(bf16)
    fetches[3].wait()
    agrad_ref[...] = mm_nt(out_grad, wo[...]).astype(bf16)
    attended_t = mm_nt(owner_rows(size, groups), att_ref[...].astype(bf16)).astype(bf16)
    out_part = mm(attended_t, out_grad).astype(bf16)
    out_own_ref[...] = out_part[: D // groups]
    out_oth_ref[...] = out_part[D // groups : 2 * (D // groups)]
    for copy in copies:
        copy.wait()


def backward_kernel(
    half,
    groups,
    at,
    extra,
    prob_hbm,
    key_ref,
    val_ref,
    rel_ref,
    hc_ref,
    hp_ref,
    hs_ref,
    linv_ref,
    kaug_ref,
    scol_ref,
    att_ref,
    agrad_ref,
    se_ref,
    both_t_hbm,
    stack_t_hbm,
    pos_t_hbm,
    *rest,
):
    more = rest[:2] if extra else ()
    (
        own_ref,
        oth_ref,
        proj_ref,
        tok_key_ref,
        tok_val_ref,
        small_ref,
        prob,
        both_t,
        stack_t,
        pos_t,
        spread,
        grads,
        turned,
        sems,
    ) = rest[len(more) :]
    count, window = 2 * half, KEYS + half
    heads = 4
    prob_copies = [
        pltpu.make_async_copy(prob_hbm.at[at * heads + h], prob.at[h], sems.at[h])
        for h in range(heads)
    ]
    fetches = [
        pltpu.make_async_copy(source, target, sems.at[heads + index])
        for index, (source, target) in enumerate(
            ((both_t_hbm, both_t), (stack_t_hbm, stack_t), (pos_t_hbm, pos_t))
        )
    ]
    for copy in prob_copies + fetches:
        copy.start()
    share = D // groups
    if extra:
        own_ref[:, 4 * QUAD :] = more[0][...]
        oth_ref[:, 4 * QUAD :] = more[1][...]
    kaug = kaug_ref[...]
    scol = scol_ref[...]
    scol = jnp.concatenate([scol, scol], axis=0)
    swing = 1.0 - 2.0 * scol
    key_t, val_t, rel_t = [], [], []
    proj_grads = []
    hp_rev = jnp.concatenate(
        [
            flip_rows(hp_ref[:half, :].astype(f32)),
            flip_rows(hp_ref[half:, :].astype(f32)),
        ],
        axis=0,
    )
    hp_t = hp_rev.astype(bf16).T
    hc_t = hc_ref[...].T
    lane = lanes((count, PAIR))
    turn = 0
    for pair in range(2):
        cols = slice(pair * PAIR, (pair + 1) * PAIR)
        plain_grad = agrad_ref[:, cols].astype(f32)
        linv = jnp.where(
            lane < HEAD_DIM,
            linv_ref[:, 2 * pair : 2 * pair + 1],
            linv_ref[:, 2 * pair + 1 : 2 * pair + 2],
        )
        agrad = (plain_grad * linv).astype(bf16).astype(f32)
        products = agrad * att_ref[:, cols]
        agrad_t = agrad.astype(bf16).T
        content_heads, place_heads, term_same, term_other = [], [], [], []
        for head in range(2):
            base = (1 - head) * HEAD_DIM
            mine = (lane < HEAD_DIM) == (head == 0)
            key_mine = (lanes((KEYS, PAIR)) < HEAD_DIM) == (head == 0)
            key_x = jnp.where(key_mine, key_ref[:, cols], kaug)
            val_x = jnp.where(key_mine, val_ref[:, cols], kaug)
            weight = jnp.sum(jnp.where(mine, products, 0.0), axis=1, keepdims=True)
            high = weight.astype(bf16).astype(f32)
            grad_x = jnp.where(
                mine,
                agrad,
                jnp.where(lane == base, -high, jnp.where(lane == base + 1, high - weight, 0.0)),
            ).astype(bf16)
            which = pair * 2 + head
            prob_copies[which].wait()
            buffer, turn = turn % 2, turn + 1
            for part in range(2):
                spread[part] = mm_nt(grad_x[part * half : (part + 1) * half], val_x)
                for b in range(0, half, BLOCK):
                    at_row = part * half + b
                    block = slice(at_row, at_row + BLOCK)
                    score_grad = prob[which, block, :].astype(f32) * spread[part, b : b + BLOCK, :]
                    grads[buffer, block, :] = score_grad.astype(bf16)
                    back = half - BLOCK - b
                    wide = jnp.concatenate(
                        [flip_rows(score_grad), jnp.zeros((BLOCK, half), f32)], axis=1
                    )
                    turned[buffer, part * half + back : part * half + back + BLOCK, :] = pltpu.roll(
                        wide, 1 + back, 1, stride=1, stride_axis=0
                    ).astype(bf16)
            head_rows = slice(which * HEAD_DIM, (which + 1) * HEAD_DIM)
            side = slice(head * HEAD_DIM, (head + 1) * HEAD_DIM)
            val_t.append(mm(agrad_t[side], prob[which]))
            key_t.append(mm(hc_t[head_rows], grads[buffer]))
            rel_t.append(mm(hp_t[head_rows], turned[buffer]))
            content_head = mm(grads[buffer], key_x)
            place_head = mm(turned[buffer], rel_ref[:, cols])
            content_heads.append(content_head)
            place_heads.append(place_head)
            total = content_head[:, base : base + 1]
            marked = content_head[:, base + 4 : base + 5]
            differ = SCALE * (scol * total + swing * marked)
            term_other.append(differ)
            term_same.append(SCALE * total - differ)
        first_head = lane < HEAD_DIM
        content_grad = (SCALE * jnp.where(first_head, *content_heads)).astype(bf16).astype(f32)
        place = SCALE * jnp.where(first_head, *place_heads)
        place = jnp.concatenate([flip_rows(place[:half]), flip_rows(place[half:])], axis=0)
        place_grad = place.astype(bf16).astype(f32)
        same = jnp.where(first_head, *term_same)
        other = jnp.where(first_head, *term_other)
        segment_grad = same * se_ref[0:1, cols] + other * se_ref[1:2, cols]
        proj_grads.append((content_grad + place_grad + segment_grad).astype(bf16))
        small_ref[0:1, cols] = row_sum(content_grad)
        small_ref[1:2, cols] = row_sum(place_grad)
        small_ref[2:3, cols] = row_sum(segment_grad)
        head_segment = hs_ref[:, cols]
        small_ref[3:4, cols] = row_sum(same * head_segment)
        small_ref[4:5, cols] = row_sum(other * head_segment)
    small_ref[5:8, :] = jnp.zeros((3, QUAD), f32)
    proj_grad = jnp.concatenate(proj_grads, axis=1)
    key_t = jnp.concatenate(key_t, axis=0).astype(bf16)
    val_t = jnp.concatenate(val_t, axis=0).astype(bf16)
    rel_t = jnp.concatenate(rel_t, axis=0).astype(bf16)
    proj_ref[...] = proj_grad
    tok_key_ref[...] = key_t[:, MEM:].T
    tok_val_ref[...] = val_t[:, MEM:].T
    for fetch in fetches:
        fetch.wait()
    parts = (
        mm(both_t[...], proj_grad),
        mm_nt(stack_t[...], key_t),
        mm_nt(stack_t[...], val_t),
        mm_nt(pos_t[...], rel_t),
    )
    for index, value in enumerate(parts):
        cols = slice(index * QUAD, (index + 1) * QUAD)
        own_ref[:, cols] = value[:share].astype(bf16)
        oth_ref[:, cols] = value[share : 2 * share].astype(bf16)


def rows_kernel(half, groups, sgrad_ref, *rest):
    proj, keys, vals = rest[:QUADS], rest[QUADS : 2 * QUADS], rest[2 * QUADS : 3 * QUADS]
    wq_ref, wk_ref, wv_ref, own_ref, query_ref, send_ref, both = rest[3 * QUADS :]
    member = lax.axis_index("tensor")
    wide = [jnp.concatenate([ref[...] for ref in refs], axis=1) for refs in (proj, keys, vals)]
    both[...] = mm_nt(wide[1], wk_ref[...]) + mm_nt(wide[2], wv_ref[...])
    rows = sgrad_ref[...] + mm_nt(wide[0], wq_ref[...])
    own = pl.multiple_of(member * half, half)
    other = pl.multiple_of(lax.rem(member + 1, groups) * half, half)
    send_ref[...] = both[pl.ds(other, half), :].astype(bf16)
    own_ref[...] = rows[:half] + both[pl.ds(own, half), :]
    query_ref[...] = rows[half:]


def whole(shape):
    return pl.BlockSpec(shape, lambda i: (0,) * len(shape))


def columns(rows, width, at=None):
    if at is None:
        return pl.BlockSpec((rows, width), lambda i: (0, i))
    return pl.BlockSpec((rows, width), lambda i: (0, at))


def scalars():
    return pl.BlockSpec(memory_space=pltpu.SMEM)


def params():
    return pltpu.CompilerParams(vmem_limit_bytes=VMEM_BYTES)


def cost(flops, bytes_accessed):
    return pl.CostEstimate(flops=flops, bytes_accessed=bytes_accessed, transcendentals=0)


def in_hbm():
    return pl.BlockSpec(memory_space=pl.ANY)


def attention_forward(
    half, size, groups, ints, memory, content, query, weights, biases, segment_rows
):
    count, window = 2 * half, KEYS + half
    coarse_rows = -(-(window // 32) // 8) * 8
    outs = (
        ((count, D), f32, columns(count, QUAD)),
        ((HEADS, count, KEYS), bf16, pl.BlockSpec((4, count, KEYS), lambda i: (i, 0, 0))),
        ((KEYS, D), bf16, columns(KEYS, QUAD)),
        ((KEYS, D), bf16, columns(KEYS, QUAD)),
        ((window, D), bf16, columns(window, QUAD)),
        ((count, D), bf16, columns(count, QUAD)),
        ((count, D), bf16, columns(count, QUAD)),
        ((count, D), f32, columns(count, QUAD)),
        ((count, QUADS * TILE), f32, columns(count, TILE)),
        ((KEYS, PAIR), bf16, whole((KEYS, PAIR))),
        ((half, PAIR), f32, whole((half, PAIR))),
        ((D, count), bf16, whole((D, count))),
        ((D, KEYS), bf16, whole((D, KEYS))),
        ((D, window), bf16, whole((D, window))),
    )
    return pl.pallas_call(
        functools.partial(forward_kernel, half, size, groups),
        grid=(QUADS,),
        out_shape=[jax.ShapeDtypeStruct(shape, kind) for shape, kind, _ in outs],
        in_specs=[
            scalars(),
            scalars(),
            whole((1, LEN)),
            whole((1, LEN)),
            whole((1, LEN)),
            whole((MEM, D)),
            whole((LEN, D)),
            whole((half, D)),
        ]
        + [columns(D, QUAD)] * 4
        + [whole((D,))] * 3
        + [columns(2, QUAD)],
        out_specs=[spec for _, _, spec in outs],
        scratch_shapes=[
            pltpu.VMEM((KEYS, D), bf16),
            pltpu.VMEM((count, D), bf16),
            pltpu.VMEM((window, D), bf16),
            pltpu.VMEM((count, KEYS), f32),
            pltpu.VMEM((2, 32, D // 2), f32),
            pltpu.VMEM((2, coarse_rows, D // 2), f32),
            pltpu.VMEM((8, D), f32),
            pltpu.VMEM((2, half, KEYS), f32),
            pltpu.VMEM((2, half, window), f32),
        ],
        compiler_params=params(),
        cost_estimate=cost(30_000_000_000, 40_000_000),
        name="attention_forward",
    )(*ints, memory, content, query, *weights, *biases, segment_rows)


def upper(half, size, arrays, hidden_cols):
    count = 2 * half
    chunk = min(hidden_cols, 768)
    chunks = hidden_cols // chunk
    outs = (
        ((half, D), bf16),
        ((half, D), bf16),
        ((2, D, hidden_cols), bf16),
        ((count, hidden_cols), bf16),
        ((count, hidden_cols), bf16),
        ((count, D), bf16),
        ((count, D), f32),
        ((count, D), f32),
        ((count, TILE), f32),
        ((8, D), f32),
        ((1, hidden_cols), f32),
    )
    far_in, far_out = (6, 7, 8, 9), (2,)
    return pl.pallas_call(
        functools.partial(upper_kernel, half, size, chunk),
        grid=(1,),
        out_shape=[jax.ShapeDtypeStruct(shape, kind) for shape, kind in outs],
        in_specs=[
            in_hbm() if i in far_in else whole(array.shape) for i, array in enumerate(arrays)
        ],
        out_specs=[in_hbm() if i in far_out else whole(s) for i, (s, _) in enumerate(outs)],
        scratch_shapes=[
            pltpu.VMEM((2, D, hidden_cols), bf16),
            pltpu.VMEM((2, hidden_cols, D), bf16),
            pltpu.VMEM((count, hidden_cols), bf16),
            pltpu.VMEM((count, hidden_cols), bf16),
            pltpu.VMEM((2, D, hidden_cols), bf16),
            pltpu.VMEM((8, FF), f32),
            pltpu.SemaphoreType.DMA((2, 2, chunks)),
            pltpu.SemaphoreType.DMA((chunks,)),
        ],
        compiler_params=params(),
        cost_estimate=cost(20_000_000_000, 30_000_000),
        name="feed_forward",
    )(*arrays)


def lower(half, size, groups, arrays, hidden_cols):
    count, share = 2 * half, D // groups
    chunk = min(hidden_cols, 768)
    outs = (
        ((2, D, hidden_cols), bf16),
        ((count, D), f32),
        ((count, D), bf16),
        ((share, D), bf16),
        ((share, D), bf16),
        ((8, D), f32),
        ((1, hidden_cols), f32),
    )
    far_in, far_out = (1, 5, 7, 8), (0,)
    return pl.pallas_call(
        functools.partial(lower_kernel, half, size, groups, chunk),
        grid=(1,),
        out_shape=[jax.ShapeDtypeStruct(shape, kind) for shape, kind in outs],
        in_specs=[
            in_hbm() if i in far_in else whole(array.shape) for i, array in enumerate(arrays)
        ],
        out_specs=[in_hbm() if i in far_out else whole(s) for i, (s, _) in enumerate(outs)],
        scratch_shapes=[
            pltpu.VMEM((count, hidden_cols), bf16),
            pltpu.VMEM((count, D), f32),
            pltpu.VMEM((D, D), bf16),
            pltpu.VMEM((D, hidden_cols), bf16),
            pltpu.VMEM((2, D, hidden_cols), bf16),
            pltpu.SemaphoreType.DMA((4,)),
            pltpu.SemaphoreType.DMA((hidden_cols // chunk,)),
        ],
        compiler_params=params(),
        cost_estimate=cost(10_000_000_000, 20_000_000),
        name="feed_forward_back",
    )(*arrays)


def attention_backward(half, groups, at, saved, agrad, segment_rows, extra):
    count, window, share = 2 * half, KEYS + half, D // groups
    att, prob, keys, values, rel, hc, hp, hs, linv, kaug, scol, both_t, stack_t, pos_t = saved
    width = 4 * QUAD + (D if extra else 0)
    operands = (
        (prob, in_hbm()),
        (keys, columns(KEYS, QUAD, at)),
        (values, columns(KEYS, QUAD, at)),
        (rel, columns(window, QUAD, at)),
        (hc, columns(count, QUAD, at)),
        (hp, columns(count, QUAD, at)),
        (hs, columns(count, QUAD, at)),
        (linv, columns(count, TILE, at)),
        (kaug, whole((KEYS, PAIR))),
        (scol, whole((half, PAIR))),
        (att, columns(count, QUAD, at)),
        (agrad, columns(count, QUAD, at)),
        (segment_rows, columns(2, QUAD, at)),
        (both_t, in_hbm()),
        (stack_t, in_hbm()),
        (pos_t, in_hbm()),
    ) + tuple((array, whole(array.shape)) for array in extra)
    outs = (
        ((share, width), bf16),
        ((share, width), bf16),
        ((count, QUAD), bf16),
        ((LEN, QUAD), bf16),
        ((LEN, QUAD), bf16),
        ((8, QUAD), f32),
    )
    return pl.pallas_call(
        functools.partial(backward_kernel, half, groups, at, bool(extra)),
        grid=(1,),
        out_shape=[jax.ShapeDtypeStruct(shape, kind) for shape, kind in outs],
        in_specs=[spec for _, spec in operands],
        out_specs=[whole(shape) for shape, _ in outs],
        scratch_shapes=[
            pltpu.VMEM((4, count, KEYS), bf16),
            pltpu.VMEM((D, count), bf16),
            pltpu.VMEM((D, KEYS), bf16),
            pltpu.VMEM((D, window), bf16),
            pltpu.VMEM((2, half, KEYS), f32),
            pltpu.VMEM((2, count, KEYS), bf16),
            pltpu.VMEM((2, count, window), bf16),
            pltpu.SemaphoreType.DMA((7,)),
        ],
        compiler_params=params(),
        cost_estimate=cost(16_000_000_000, 16_000_000),
        name="attention_backward",
    )(*[array for array, _ in operands])


def row_gradients(half, groups, summed_grad, proj, keys, vals, weights):
    count = 2 * half
    arrays = (summed_grad, *proj, *keys, *vals, *weights)
    outs = (((half, D), f32), ((half, D), f32), ((half, D), bf16))
    return pl.pallas_call(
        functools.partial(rows_kernel, half, groups),
        grid=(1,),
        out_shape=[jax.ShapeDtypeStruct(shape, kind) for shape, kind in outs],
        in_specs=[whole(array.shape) for array in arrays],
        out_specs=[whole(shape) for shape, _ in outs],
        scratch_shapes=[pltpu.VMEM((LEN, D), f32)],
        compiler_params=params(),
        cost_estimate=cost(4_000_000_000, 10_000_000),
        name="row_gradients",
    )(*arrays)


def swap(array):
    groups = lax.axis_size("tensor")
    return lax.ppermute(array, "tensor", [(i, (i + 1) % groups) for i in range(groups)])


def across(array, step):
    size, groups = lax.axis_size("dp"), lax.axis_size("tensor")
    bits = size.bit_length() - 1
    pairs = [
        (place * groups + core, (place ^ (1 << order_of(core, bits)[step])) * groups + core)
        for place in range(size)
        for core in range(groups)
    ]
    return lax.ppermute(array, ("dp", "tensor"), pairs)


def total(terms):
    return functools.reduce(jnp.add, [term.astype(f32) for term in terms])


class Chain:
    def __init__(self, terms):
        self.terms = terms
        self.step = 0
        self.message = None

    def load(self):
        kept = self.terms[0].shape[0] // 2
        self.message = total([term[kept:] for term in self.terms]).astype(bf16)
        self.terms = [term[:kept] for term in self.terms]
        return self

    def send(self):
        self.terms.append(across(self.message, self.step))
        self.message = None
        self.step += 1
        return self

    def result(self):
        return total(self.terms)


def hold(value, chains):
    value, messages = lax.optimization_barrier((value, [chain.message for chain in chains]))
    for chain, message in zip(chains, messages):
        chain.message = message
    return value


def all_sum(array):
    array = array + swap(array)
    size = lax.axis_size("dp")
    for bit in range(size.bit_length() - 1):
        array = array + lax.ppermute(array, "dp", [(i, i ^ (1 << bit)) for i in range(size)])
    return array


def body(
    content_in,
    query_in,
    memory,
    content_cot,
    query_cot,
    query_weight,
    key_weight,
    value_weight,
    out_weight,
    rel_weight,
    content_bias,
    position_bias,
    segment_bias,
    segment_embed,
    attn_gain,
    attn_shift,
    up_weight,
    up_bias,
    down_weight,
    down_bias,
    ffn_gain,
    ffn_shift,
    lengths,
    memory_lengths,
    segment_ids,
    orders,
    targets,
):
    groups = lax.axis_size("tensor")
    size = lax.axis_size("dp")
    steps = size.bit_length() - 1
    member = lax.axis_index("tensor")
    place = lax.axis_index("dp") * groups + member
    half = LEN // groups
    hidden_cols = up_weight.shape[1]
    up_other, down_other = swap(up_weight), swap(down_weight)
    content, query = content_in[0], query_in[0]
    segment_rows = segment_embed.T
    saved = attention_forward(
        half,
        size,
        groups,
        (lengths, memory_lengths, segment_ids, orders, targets),
        memory[0],
        content,
        query,
        (query_weight, key_weight, value_weight, rel_weight),
        (content_bias, position_bias, segment_bias),
        segment_rows,
    )
    att = saved[0]
    (
        content_out,
        query_out,
        ffn_other,
        hidden,
        slope,
        down_grad,
        grad_part,
        unit,
        inv,
        small_upper,
        up_bias_other,
    ) = upper(
        half,
        size,
        (
            att,
            content,
            query,
            content_cot[0],
            query_cot[0],
            out_weight,
            up_weight,
            up_other,
            down_weight,
            down_other,
            up_bias,
            down_bias,
            attn_gain,
            attn_shift,
            ffn_gain,
            ffn_shift,
        ),
        hidden_cols,
    )
    ffn_got = swap(ffn_other)
    ffn_own, summed_grad, attended_grad, out_own, out_other, small_lower, up_bias_own = lower(
        half,
        size,
        groups,
        (
            att,
            hidden,
            slope,
            down_grad,
            grad_part,
            unit,
            inv,
            out_weight,
            up_weight,
            down_weight,
            attn_gain,
            attn_shift,
        ),
        hidden_cols,
    )
    up_chain = Chain([ffn_own[0], ffn_got[0]]).load()
    down_chain = Chain([ffn_own[1], ffn_got[1]])
    chains = [up_chain, down_chain]
    held = hold(attended_grad, [up_chain])
    up_chain.send()
    proj, tok_keys, tok_vals, late_small = [], [], [], []
    late = []
    for at in range(QUADS):
        own, other, proj_part, key_part, val_part, small = attention_backward(
            half,
            groups,
            at,
            saved,
            held,
            segment_rows,
            (out_own, out_other) if at == 0 else (),
        )
        proj.append(proj_part)
        tok_keys.append(key_part)
        tok_vals.append(val_part)
        late_small.append(small)
        got = swap(other)
        if at < QUADS - 1:
            ready = [chain.load() for chain in chains if chain.step < steps]
            held = hold(held, ready)
            for chain in ready:
                chain.send()
        late.append(Chain([own, got]))
        chains.append(late[-1])
    own_rows, query_grad, row_send = row_gradients(
        half, groups, summed_grad, proj, tok_keys, tok_vals, (query_weight, key_weight, value_weight)
    )
    content_grad = own_rows + swap(row_send).astype(f32)
    while any(chain.step < steps for chain in chains):
        for chain in chains:
            if chain.step < steps:
                chain.load().send()
    up_bias_rows = jnp.where(
        member == 0,
        jnp.concatenate([up_bias_own, up_bias_other], axis=0),
        jnp.concatenate([up_bias_other, up_bias_own], axis=0),
    )
    small = jnp.concatenate(
        [
            small_upper[:3],
            small_lower[:2],
            jnp.concatenate(late_small, axis=1)[:5],
            up_bias_rows.reshape(-1, D),
        ],
        axis=0,
    )
    small = all_sum(small)
    share = D // (size * groups)
    vectors = lax.dynamic_slice_in_dim(small[:10], place * share, share, 1)
    up_bias_grad = lax.dynamic_slice_in_dim(
        small[10:].reshape(-1), place * (FF // (size * groups)), FF // (size * groups), 0
    )
    up_grad, down_grad_own = up_chain.result(), down_chain.result()
    blocks = [chain.result() for chain in late]

    def joined(index):
        return jnp.concatenate(
            [block[:, index * QUAD : (index + 1) * QUAD] for block in blocks], axis=1
        )

    return (
        content_out[None],
        query_out[None],
        content_grad[None],
        query_grad[None],
        joined(0),
        joined(1),
        joined(2),
        blocks[0][:, 4 * QUAD :],
        joined(3),
        vectors[5],
        vectors[6],
        vectors[7],
        vectors[8:10].T,
        vectors[3],
        vectors[4],
        up_grad,
        up_bias_grad,
        down_grad_own.T,
        vectors[2],
        vectors[0],
        vectors[1],
    )


def solution(mesh):
    in_specs = (
        P("dp", None, None),
        P("dp", "tensor", None),
        P("dp", None, None),
        P("dp", "tensor", None),
        P("dp", "tensor", None),
        P(),
        P(),
        P(),
        P(),
        P(),
        P(),
        P(),
        P(),
        P(),
        P(),
        P(),
        P(None, "tensor"),
        P(),
        P("tensor", None),
        P(),
        P(),
        P(),
        P("dp"),
        P("dp"),
        P("dp", None),
        P("dp", None),
        P("dp", None),
    )
    out_specs = (
        P("dp", "tensor", None),
        P("dp", "tensor", None),
        P("dp", "tensor", None),
        P("dp", "tensor", None),
        P(("dp", "tensor"), None),
        P(("dp", "tensor"), None),
        P(("dp", "tensor"), None),
        P(("dp", "tensor"), None),
        P(("dp", "tensor"), None),
        P(("dp", "tensor")),
        P(("dp", "tensor")),
        P(("dp", "tensor")),
        P(("dp", "tensor"), None),
        P(("dp", "tensor")),
        P(("dp", "tensor")),
        P("dp", "tensor"),
        P(("dp", "tensor")),
        P("tensor", "dp"),
        P(("dp", "tensor")),
        P(("dp", "tensor")),
        P(("dp", "tensor")),
    )
    return jax.shard_map(body, mesh=mesh, in_specs=in_specs, out_specs=out_specs, check_vma=False)
```

```python
import functools

import jax
import jax.numpy as jnp
from jax import lax
from jax.experimental import pallas as pl
from jax.experimental.pallas import tpu as pltpu
from jax.sharding import PartitionSpec as P

D = 768
HEADS = 12
HEAD_DIM = 64
FF = 3072
LEN = 512
MEM = 384
KEYS = MEM + LEN
QUAD = 4 * HEAD_DIM
QUADS = D // QUAD
PAIR = 2 * HEAD_DIM
SCALE = HEAD_DIM ** (-0.5)
VMEM_BYTES = 56 * 1024 * 1024
BLOCK = 32
TILE = 128
WIDE = 256

f32 = jnp.float32
bf16 = jnp.bfloat16
precise = lax.Precision.HIGHEST


def mm(left, right):
    return lax.dot_general(left, right, (((1,), (0,)), ((), ())), preferred_element_type=f32)


def mm_nt(left, right):
    return lax.dot_general(left, right, (((1,), (1,)), ((), ())), preferred_element_type=f32)


def lanes(shape):
    return lax.broadcasted_iota(jnp.int32, shape, 1)


def column_of(row):
    return jnp.broadcast_to(row.astype(f32), (128, row.shape[1])).T


def flip_rows(value):
    count, width = value.shape
    groups = value.reshape(count // 8, 8, width)
    index = 7 - lax.broadcasted_iota(jnp.int32, groups.shape, 1)
    turned = jnp.take_along_axis(groups, index, axis=1, mode="promise_in_bounds")
    return jnp.concatenate([turned[i] for i in range(count // 8 - 1, -1, -1)], axis=0)


def lane_tiles(value, combine):
    tiles = [value[:, at : at + TILE] for at in range(0, value.shape[1], TILE)]
    return functools.reduce(combine, tiles)


def interleave(steps, tasks):
    done = 0
    for index, step in enumerate(steps):
        step()
        while done * len(steps) < (index + 1) * len(tasks) and done < len(tasks):
            tasks[done]()
            done += 1
    for task in tasks[done:]:
        task()


def order_of(core, bits):
    plain = list(range(bits))
    return plain[1:2] + plain[:1] + plain[2:] if core == 1 and bits > 1 else plain


def block_owner(place, core, bits):
    owner = jnp.zeros_like(place)
    for step in range(bits):
        owner = owner | (((place >> (bits - 1 - step)) & 1) << step)
    if bits > 1:
        swapped = (owner & ~3) | ((owner & 1) << 1) | ((owner >> 1) & 1)
        owner = jnp.where(core == 1, swapped, owner)
    return owner ^ lax.axis_index("dp")


def one_hot(source):
    return jnp.where(lanes((source.shape[0], D)) == source, 1.0, 0.0).astype(bf16)


def owner_rows(size, groups):
    share = D // (size * groups)
    row = lax.broadcasted_iota(jnp.int32, (D, 1), 0)
    side, rest = lax.div(row, size * share), lax.rem(row, size * share)
    core = lax.rem(lax.axis_index("tensor") + side, groups)
    owner = block_owner(lax.div(rest, share), core, size.bit_length() - 1)
    return one_hot((owner * groups + core) * share + lax.rem(rest, share))


def shared_rows(size, core):
    share = D // size
    row = lax.broadcasted_iota(jnp.int32, (D, 1), 0)
    owner = block_owner(lax.div(row, share), core, size.bit_length() - 1)
    return one_hot(owner * share + lax.rem(row, share))


def forward_kernel(
    half,
    size,
    groups,
    length_ref,
    mem_length_ref,
    seg_ref,
    ord_ref,
    tgt_ref,
    memory_ref,
    content_ref,
    query_ref,
    wq_ref,
    wk_ref,
    wv_ref,
    wr_ref,
    cb_ref,
    pb_ref,
    sb_ref,
    se_ref,
    att_ref,
    prob_ref,
    key_ref,
    val_ref,
    rel_ref,
    hc_ref,
    hp_ref,
    hs_ref,
    linv_ref,
    kaug_ref,
    scol_ref,
    both_t_ref,
    stack_t_ref,
    pos_t_ref,
    stack,
    both,
    pos,
    bias,
    fine,
    coarse,
    vectors,
    scores,
    places,
):
    window = KEYS + half
    first = pl.multiple_of(lax.axis_index("tensor") * half, half)
    step_id = pl.program_id(0)

    @pl.when(step_id == 0)
    def _():
        stack[:MEM, :] = memory_ref[...]
        stack[MEM:, :] = content_ref[...]
        both[:half, :] = content_ref[pl.ds(first, half), :]
        both[half:, :] = query_ref[...]
        vectors[0:1, :] = cb_ref[...][None, :]
        vectors[1:2, :] = pb_ref[...][None, :]
        vectors[2:3, :] = sb_ref[...][None, :]
        step = lax.broadcasted_iota(jnp.int32, (1, D // 2), 1).astype(f32) * (2.0 / D)
        inverse = 1.0 / jnp.power(jnp.full((1, D // 2), 10000.0, f32), step)
        coarse_rows = coarse.shape[1]
        top = (MEM + half + first).astype(f32)
        angle = (
            top - 32.0 * lax.broadcasted_iota(jnp.int32, (coarse_rows, 1), 0).astype(f32)
        ) * inverse
        coarse[0] = jnp.sin(angle)
        coarse[1] = jnp.cos(angle)
        small = lax.broadcasted_iota(jnp.int32, (32, 1), 0).astype(f32) * inverse
        fine[0] = jnp.sin(small)
        fine[1] = jnp.cos(small)
        for a in range(window // 32):
            sa, ca = coarse[0, a : a + 1, :], coarse[1, a : a + 1, :]
            sb, cb = fine[0], fine[1]
            pos[a * 32 : (a + 1) * 32, : D // 2] = (sa * cb - ca * sb).astype(bf16)
            pos[a * 32 : (a + 1) * 32, D // 2 :] = (ca * cb + sa * sb).astype(bf16)
        never = float(LEN + 1)
        mem_at = lax.broadcasted_iota(jnp.int32, (1, MEM), 1)
        tok_at = lax.broadcasted_iota(jnp.int32, (1, LEN), 1)
        open_from = jnp.concatenate(
            [
                jnp.where(mem_at >= MEM - mem_length_ref[0], -1.0, never),
                jnp.where(
                    tok_at < length_ref[0],
                    jnp.where(tgt_ref[...] == 0, -1.0, ord_ref[...].astype(f32)),
                    never,
                ),
            ],
            axis=1,
        )
        order_col = column_of(ord_ref[...])
        seg_col = column_of(seg_ref[...])
        kaug_lane = lanes((LEN, PAIR)) % HEAD_DIM
        kaug_ref[:MEM, :] = (lanes((MEM, PAIR)) % HEAD_DIM < 4).astype(f32).astype(bf16)
        kaug_ref[MEM:, :] = jnp.where(
            kaug_lane < 4, 1.0, jnp.where(kaug_lane < 6, seg_col, 0.0)
        ).astype(bf16)
        bias[:LEN, :PAIR] = order_col
        own_order = bias[pl.ds(first, half), :PAIR][:, :1]
        bias[:LEN, :PAIR] = seg_col
        scol_ref[...] = bias[pl.ds(first, half), :PAIR]
        seen = open_from <= own_order
        bias[:half, :] = jnp.where(seen, 0.0, -1e30)
        key_at = lax.broadcasted_iota(jnp.int32, (half, KEYS), 1)
        row_at = lax.broadcasted_iota(jnp.int32, (half, KEYS), 0)
        seen_q = seen & (key_at - MEM != row_at + first)
        bias[half:, :] = jnp.where(seen_q, 0.0, -1e30)
        chosen = owner_rows(size, groups)
        both_t_ref[...] = mm_nt(chosen, both[...]).astype(bf16)
        stack_t_ref[...] = mm_nt(chosen, stack[...]).astype(bf16)
        pos_t_ref[...] = mm_nt(chosen, pos[...]).astype(bf16)

    here = pl.ds(pl.multiple_of(step_id * QUAD, QUAD), QUAD)
    keys = mm(stack[...], wk_ref[...]).astype(bf16)
    values = mm(stack[...], wv_ref[...]).astype(bf16)
    rel = mm(pos[...], wr_ref[...]).astype(bf16)
    projection = mm(both[...], wq_ref[...])
    head_content = (projection + vectors[0:1, here]).astype(bf16)
    head_position = (projection + vectors[1:2, here]).astype(bf16)
    head_segment = projection + vectors[2:3, here]
    key_ref[...] = keys
    val_ref[...] = values
    rel_ref[...] = rel
    hs_ref[...] = head_segment
    head_content = (head_content.astype(f32) * SCALE).astype(bf16)
    head_position = (head_position.astype(f32) * SCALE).astype(bf16)
    hc_ref[...] = head_content
    hp_ref[...] = head_position
    same = column_of(se_ref[0:1, :])
    differ = column_of(se_ref[1:2, :] - se_ref[0:1, :])
    same = jnp.concatenate([same, same], axis=1)
    differ = jnp.concatenate([differ, differ], axis=1)
    row_head = lax.broadcasted_iota(jnp.int32, (QUAD, QUAD), 0) // HEAD_DIM
    at = lanes((QUAD, QUAD)) - ((row_head // 2) * PAIR + (1 - row_head % 2) * HEAD_DIM)
    embed = jnp.where(
        (at >= 0) & (at < 2), same, jnp.where((at >= 2) & (at < 6), differ, 0.0)
    )
    embed_high = embed.astype(bf16)
    embed_low = (embed - embed_high.astype(f32)).astype(bf16)
    segment_high = head_segment.astype(bf16)
    segment_low = (head_segment - segment_high.astype(f32)).astype(bf16)
    terms = (
        mm(segment_high, embed_high) + mm(segment_high, embed_low) + mm(segment_low, embed_high)
    )
    scol = scol_ref[...]
    scol = jnp.concatenate([scol, scol], axis=0)
    scol = jnp.concatenate([scol, scol], axis=1)
    lane6 = lanes((2 * half, QUAD)) % HEAD_DIM
    factor = jnp.where(lane6 < 2, 1.0, jnp.where(lane6 < 4, scol, 1.0 - 2.0 * scol))
    terms = SCALE * (terms * factor)
    high = terms.astype(bf16)
    low = (terms - high.astype(f32)).astype(bf16)
    qaug = jnp.where(lane6 % 2 == 0, high, low)
    kaug = kaug_ref[...]
    units = [(pair, head, part) for pair in range(2) for head in range(2) for part in range(2)]
    key_x = [
        jnp.where(
            (lanes((KEYS, PAIR)) < HEAD_DIM) == (which % 2 == 0),
            keys[:, which // 2 * PAIR : (which // 2 + 1) * PAIR],
            kaug,
        )
        for which in range(4)
    ]
    peaks, totals, outs = {}, {}, {}

    def products(index):
        pair, head, part = units[index]
        cols, rows = slice(pair * PAIR, (pair + 1) * PAIR), slice(part * half, (part + 1) * half)
        slot, which = index % 2, pair * 2 + head
        row_mine = (lanes((half, PAIR)) < HEAD_DIM) == (head == 0)
        query_x = jnp.where(row_mine, head_content[rows, cols], qaug[rows, cols])
        place_x = jnp.where(row_mine, head_position[rows, cols], jnp.zeros((), bf16))

        def score(n, stop):
            scores[slot, :, n:stop] = mm_nt(query_x, key_x[which][n:stop])

        def placed(n, stop):
            places[slot, :, n:stop] = mm_nt(place_x, rel[n:stop, cols])

        return [functools.partial(placed, n, min(n + WIDE, window)) for n in range(0, window, WIDE)] + [
            functools.partial(score, n, min(n + WIDE, KEYS)) for n in range(0, KEYS, WIDE)
        ]

    def softmax(index):
        pair, head, part = units[index]
        slot, which = index % 2, pair * 2 + head
        tops, pieces = [], []

        def join(b):
            block = slice(b, b + BLOCK)
            shifted = pltpu.roll(
                places[slot, block, :], (KEYS + b) % window, 1, stride=1, stride_axis=0
            )[:, :KEYS]
            score = (
                scores[slot, block, :]
                + shifted
                + bias[part * half + b : part * half + b + BLOCK, :]
            )
            scores[slot, block, :] = score
            tops.append(lane_tiles(score, jnp.maximum))

        def peak():
            peaks[index] = jnp.max(jnp.concatenate(tops, axis=0), axis=1, keepdims=True)

        def power(b):
            block = slice(b, b + BLOCK)
            prob = jnp.exp(scores[slot, block, :] - peaks[index][block])
            pieces.append(lane_tiles(prob, jnp.add))
            prob_ref[which, part * half + b : part * half + b + BLOCK, :] = prob.astype(bf16)

        def finish():
            totals[index] = 1.0 / jnp.sum(
                jnp.concatenate(pieces, axis=0), axis=1, keepdims=True
            )

        blocks = range(0, half, BLOCK)
        return (
            [functools.partial(join, b) for b in blocks]
            + [peak]
            + [functools.partial(power, b) for b in blocks]
            + [finish]
        )

    def mixture(index):
        pair, head, part = units[index]
        cols, rows = slice(pair * PAIR, (pair + 1) * PAIR), slice(part * half, (part + 1) * half)
        outs[index] = mm(prob_ref[pair * 2 + head, rows, :], values[:, cols]) * totals[index]

    interleave([], products(0))
    for index in range(len(units)):
        tasks = products(index + 1) if index + 1 < len(units) else []
        if index:
            tasks.append(functools.partial(mixture, index - 1))
        interleave(softmax(index), tasks)
    mixture(len(units) - 1)
    for pair in range(2):
        cols = slice(pair * PAIR, (pair + 1) * PAIR)
        mixtures = [
            jnp.concatenate([outs[pair * 4 + head * 2], outs[pair * 4 + head * 2 + 1]], axis=0)
            for head in range(2)
        ]
        mine = lanes((2 * half, PAIR)) < HEAD_DIM
        att_ref[:, cols] = jnp.where(mine, mixtures[0], mixtures[1])
    sums = [
        jnp.concatenate([totals[2 * which], totals[2 * which + 1]], axis=0) for which in range(4)
    ]
    lane = lanes((2 * half, TILE))
    linv_ref[...] = jnp.where(
        lane == 0, sums[0], jnp.where(lane == 1, sums[1], jnp.where(lane == 2, sums[2], sums[3]))
    )


def norm_forward(summed, gain, shift):
    center = summed - jnp.mean(summed, axis=1, keepdims=True)
    inv = lax.rsqrt(jnp.mean(center * center, axis=1, keepdims=True) + 1e-06)
    unit = center * inv
    return unit, inv, unit * gain + shift


def norm_backward(grad, unit, inv, gain):
    scaled = grad * gain
    return inv * (
        scaled
        - jnp.mean(scaled, axis=1, keepdims=True)
        - unit * jnp.mean(scaled * unit, axis=1, keepdims=True)
    )


def row_sum(value):
    return jnp.sum(value, axis=0, keepdims=True)


def gelu_parts(x):
    square = x * x
    tanh = jnp.tanh((0.7978845608028654 * x) * (1.0 + 0.044715 * square))
    rise = 0.5 * (1.0 + tanh)
    grad = rise + (0.5 * x) * (1.0 - tanh * tanh) * (
        0.7978845608028654 * (1.0 + 0.134145 * square)
    )
    return x * rise, grad


def upper_kernel(
    half,
    size,
    chunk,
    att_ref,
    content_ref,
    query_ref,
    ccot_ref,
    qcot_ref,
    wo_ref,
    up_own_hbm,
    up_oth_hbm,
    down_own_hbm,
    down_oth_hbm,
    ubias_ref,
    dbias_ref,
    again_ref,
    ashift_ref,
    fgain_ref,
    fshift_ref,
    cout_ref,
    qout_ref,
    ffn_ref,
    hid_ref,
    slope_ref,
    dgrad_ref,
    grad_ref,
    unit_ref,
    inv_ref,
    small_ref,
    ub_oth_ref,
    ups,
    downs,
    hidden,
    slope,
    pre,
    residual,
    vectors,
    sems,
):
    first = pl.multiple_of(lax.axis_index("tensor") * half, half)
    member = lax.axis_index("tensor")
    part_cols = ups.shape[2]
    chunks = part_cols // chunk
    fetches = [
        pltpu.make_async_copy(source, target.at[side], sems.at[kind, side])
        for kind, side, source, target in (
            (0, 0, up_own_hbm, ups),
            (1, 0, down_own_hbm, downs),
            (0, 1, up_oth_hbm, ups),
            (1, 1, down_oth_hbm, downs),
        )
    ]
    for fetch in fetches:
        fetch.start()
    vectors[0:1, :] = ubias_ref[...][None, :]
    attended = att_ref[...].astype(bf16)
    rows_in = jnp.concatenate([content_ref[pl.ds(first, half), :], query_ref[...]], axis=0)
    summed = mm(attended, wo_ref[...]) + rows_in.astype(f32)
    unit1, inv1, normed = norm_forward(summed, again_ref[...][None, :], ashift_ref[...][None, :])
    unit_ref[...] = unit1
    inv_ref[...] = jnp.broadcast_to(inv1, inv_ref.shape)
    low = normed.astype(bf16)
    residual[...] = normed + dbias_ref[...][None, :]
    for fetch in fetches:
        fetch.wait()
    pieces = [(side, at) for side in range(2) for at in range(chunks)]

    def rise(index):
        side, at = pieces[index]

        def task(n):
            pre[index % 2, :, n : n + WIDE] = mm(
                low, ups[side, :, at * chunk + n : at * chunk + n + WIDE]
            )

        return [functools.partial(task, n) for n in range(0, chunk, WIDE)]

    def bend(index):
        side, at = pieces[index]
        cols = slice(at * chunk, (at + 1) * chunk)
        start = lax.rem(member + side, 2) * part_cols + at * chunk
        bias = vectors[0:1, pl.ds(pl.multiple_of(start, TILE), chunk)]

        def step(b):
            block = slice(b, b + BLOCK)
            act, grad = gelu_parts(pre[index % 2, block, :] + bias)
            if side == 0:
                hid_ref[block, cols] = act.astype(bf16)
                slope_ref[block, cols] = grad.astype(bf16)
            else:
                hidden[block, cols] = act.astype(bf16)
                slope[block, cols] = grad.astype(bf16)

        return [functools.partial(step, b) for b in range(0, 2 * half, BLOCK)]

    def fall(index):
        side, at = pieces[index]
        cols = slice(at * chunk, (at + 1) * chunk)
        act = hid_ref if side == 0 else hidden

        def task(n):
            residual[:, n : n + WIDE] += mm(act[:, cols], downs[side, cols, n : n + WIDE])

        return [functools.partial(task, n) for n in range(0, D, WIDE)]

    interleave([], rise(0))
    for index in range(len(pieces)):
        tasks = rise(index + 1) if index + 1 < len(pieces) else []
        if index:
            tasks += fall(index - 1)
        interleave(bend(index), tasks)
    interleave([], fall(len(pieces) - 1))
    unit2, inv2, out = norm_forward(
        residual[...], fgain_ref[...][None, :], fshift_ref[...][None, :]
    )
    cout_ref[...] = out[:half].astype(bf16)
    qout_ref[...] = out[half:].astype(bf16)
    cot = jnp.concatenate([ccot_ref[...], qcot_ref[...]], axis=0).astype(f32)
    small_ref[0:1, :] = row_sum(cot * unit2)
    small_ref[1:2, :] = row_sum(cot)
    residual_grad = norm_backward(cot, unit2, inv2, fgain_ref[...][None, :])
    down_grad = residual_grad.astype(bf16)
    dgrad_ref[...] = down_grad
    small_ref[2:3, :] = row_sum(down_grad.astype(f32))
    small_ref[3:8, :] = jnp.zeros((5, D), f32)
    chosen = shared_rows(size, 1 - member)
    down_grad_t = mm_nt(chosen, down_grad).astype(bf16)
    low_t = mm_nt(chosen, low).astype(bf16)
    grad = residual_grad
    for at in range(chunks):
        cols = slice(at * chunk, (at + 1) * chunk)
        hidden_grad = mm_nt(down_grad, downs[1, cols, :])
        pre_grad = (hidden_grad * slope[:, cols].astype(f32)).astype(bf16)
        ub_oth_ref[:, cols] = row_sum(pre_grad.astype(f32))
        ffn_ref[1, :, cols] = mm(down_grad_t, hidden[:, cols]).astype(bf16)
        ffn_ref[0, :, cols] = mm(low_t, pre_grad).astype(bf16)
        grad = grad + mm_nt(pre_grad, ups[1, :, cols])
    grad_ref[...] = grad


def lower_kernel(
    half,
    size,
    groups,
    chunk,
    att_ref,
    hid_hbm,
    slope_ref,
    dgrad_ref,
    grad_in_ref,
    unit_hbm,
    inv_ref,
    wo_hbm,
    up_hbm,
    down_ref,
    again_ref,
    ashift_ref,
    ffn_own_hbm,
    sgrad_ref,
    agrad_ref,
    out_own_ref,
    out_oth_ref,
    small_ref,
    ub_own_ref,
    hidden,
    unit,
    wo,
    up,
    ffn,
    sems,
    out_sems,
):
    member = lax.axis_index("tensor")
    part_cols = up.shape[1]
    fetches = [
        pltpu.make_async_copy(source, target, sems.at[index])
        for index, (source, target) in enumerate(
            ((hid_hbm, hidden), (up_hbm, up), (unit_hbm, unit), (wo_hbm, wo))
        )
    ]
    for fetch in fetches:
        fetch.start()
    down_grad = dgrad_ref[...]
    gain, shift = again_ref[...][None, :], ashift_ref[...][None, :]
    chosen = shared_rows(size, member)
    down_grad_t = mm_nt(chosen, down_grad).astype(bf16)
    for fetch in fetches:
        fetch.wait()
    low = (unit[...] * gain + shift).astype(bf16)
    low_t = mm_nt(chosen, low).astype(bf16)
    grad = grad_in_ref[...]
    for at in range(part_cols // chunk):
        cols = slice(at * chunk, (at + 1) * chunk)
        hidden_grad = mm_nt(down_grad, down_ref[cols, :])
        pre_grad = (hidden_grad * slope_ref[:, cols].astype(f32)).astype(bf16)
        ub_own_ref[:, cols] = row_sum(pre_grad.astype(f32))
        ffn[1, :, cols] = mm(down_grad_t, hidden[:, cols]).astype(bf16)
        ffn[0, :, cols] = mm(low_t, pre_grad).astype(bf16)
        grad = grad + mm_nt(pre_grad, up[:, cols])
    copy = pltpu.make_async_copy(ffn, ffn_own_hbm, out_sems.at[0])
    copy.start()
    unit1, inv1 = unit[...], inv_ref[:, :1]
    small_ref[0:1, :] = row_sum(grad * unit1)
    small_ref[1:2, :] = row_sum(grad)
    small_ref[2:8, :] = jnp.zeros((6, D), f32)
    summed_grad = norm_backward(grad, unit1, inv1, gain)
    sgrad_ref[...] = summed_grad
    out_grad = summed_grad.astype(bf16)
    agrad_ref[...] = mm_nt(out_grad, wo[...]).astype(bf16)
    attended_t = mm_nt(owner_rows(size, groups), att_ref[...].astype(bf16)).astype(bf16)
    out_part = mm(attended_t, out_grad).astype(bf16)
    out_own_ref[...] = out_part[: D // groups]
    out_oth_ref[...] = out_part[D // groups : 2 * (D // groups)]
    copy.wait()


def backward_kernel(
    half,
    groups,
    at,
    extra,
    prob_hbm,
    key_ref,
    val_ref,
    rel_ref,
    hc_ref,
    hp_ref,
    hs_ref,
    linv_ref,
    kaug_ref,
    scol_ref,
    att_ref,
    agrad_ref,
    se_ref,
    both_t_hbm,
    stack_t_hbm,
    pos_t_hbm,
    *rest,
):
    more = rest[:2] if extra else ()
    (
        own_ref,
        oth_ref,
        proj_ref,
        tok_key_ref,
        tok_val_ref,
        small_ref,
        prob,
        both_t,
        stack_t,
        pos_t,
        spread,
        grads,
        turned,
        sems,
    ) = rest[len(more) :]
    count, window = 2 * half, KEYS + half
    heads = 4
    prob_copies = [
        pltpu.make_async_copy(prob_hbm.at[at * heads + h], prob.at[h], sems.at[h])
        for h in range(heads)
    ]
    fetches = [
        pltpu.make_async_copy(source, target, sems.at[heads + index])
        for index, (source, target) in enumerate(
            ((both_t_hbm, both_t), (stack_t_hbm, stack_t), (pos_t_hbm, pos_t))
        )
    ]
    for copy in prob_copies + fetches:
        copy.start()
    share = D // groups
    if extra:
        own_ref[:, 4 * QUAD :] = more[0][...]
        oth_ref[:, 4 * QUAD :] = more[1][...]
    kaug = kaug_ref[...]
    scol = scol_ref[...]
    scol = jnp.concatenate([scol, scol], axis=0)
    swing = 1.0 - 2.0 * scol
    key_t, val_t, rel_t = [], [], []
    proj_grads = []
    hp_rev = jnp.concatenate(
        [
            flip_rows(hp_ref[:half, :].astype(f32)),
            flip_rows(hp_ref[half:, :].astype(f32)),
        ],
        axis=0,
    )
    hp_t = hp_rev.astype(bf16).T
    hc_t = hc_ref[...].T
    lane = lanes((count, PAIR))
    for copy in prob_copies:
        copy.wait()
    agrads, grad_x, agrad_t = [], [], []
    for pair in range(2):
        cols = slice(pair * PAIR, (pair + 1) * PAIR)
        linv = jnp.where(
            lane < HEAD_DIM,
            linv_ref[:, 2 * pair : 2 * pair + 1],
            linv_ref[:, 2 * pair + 1 : 2 * pair + 2],
        )
        agrad = (agrad_ref[:, cols].astype(f32) * linv).astype(bf16).astype(f32)
        products = agrad * att_ref[:, cols]
        agrad_t.append(agrad.astype(bf16).T)
        for head in range(2):
            base = (1 - head) * HEAD_DIM
            mine = (lane < HEAD_DIM) == (head == 0)
            weight = jnp.sum(jnp.where(mine, products, 0.0), axis=1, keepdims=True)
            high = weight.astype(bf16).astype(f32)
            grad_x.append(
                jnp.where(
                    mine,
                    agrad,
                    jnp.where(
                        lane == base, -high, jnp.where(lane == base + 1, high - weight, 0.0)
                    ),
                ).astype(bf16)
            )
    key_mine = lanes((KEYS, PAIR)) < HEAD_DIM
    found = {}

    def columns_of(which):
        return slice(which // 2 * PAIR, (which // 2 + 1) * PAIR)

    def extended(ref, which):
        return jnp.where(key_mine == (which % 2 == 0), ref[:, columns_of(which)], kaug)

    def spreads(which):
        val_x = extended(val_ref, which)

        def task(n, stop):
            spread[which % 2, :, n:stop] = mm_nt(grad_x[which], val_x[n:stop])

        return [functools.partial(task, n, min(n + WIDE, KEYS)) for n in range(0, KEYS, WIDE)]

    def score_grads(which):
        buffer = which % 2

        def step(part, b):
            at_row = part * half + b
            block = slice(at_row, at_row + BLOCK)
            score_grad = prob[which, block, :].astype(f32) * spread[buffer, block, :]
            grads[buffer, block, :] = score_grad.astype(bf16)
            back = half - BLOCK - b
            wide = jnp.concatenate([flip_rows(score_grad), jnp.zeros((BLOCK, half), f32)], axis=1)
            turned[buffer, part * half + back : part * half + back + BLOCK, :] = pltpu.roll(
                wide, 1 + back, 1, stride=1, stride_axis=0
            ).astype(bf16)

        return [
            functools.partial(step, part, b) for part in range(2) for b in range(0, half, BLOCK)
        ]

    def gathers(which):
        buffer = which % 2
        head_rows = slice(which * HEAD_DIM, (which + 1) * HEAD_DIM)
        side = slice(which % 2 * HEAD_DIM, (which % 2 + 1) * HEAD_DIM)
        key_x = extended(key_ref, which)
        found[which] = {"value": [], "key": [], "rel": [], "content": [], "place": []}

        def down_rows(name, left, ref, n, stop):
            found[which][name].append(mm(left, ref[:, n:stop]))

        tasks = []
        for name, left, ref, end in (
            ("value", agrad_t[which // 2][side], prob.at[which], KEYS),
            ("key", hc_t[head_rows], grads.at[buffer], KEYS),
            ("rel", hp_t[head_rows], turned.at[buffer], window),
        ):
            tasks += [
                functools.partial(down_rows, name, left, ref, n, min(n + WIDE, end))
                for n in range(0, end, WIDE)
            ]

        def content(n):
            found[which]["content"].append(mm(grads[buffer, n : n + half, :], key_x))

        def placed(n):
            found[which]["place"].append(
                mm(turned[buffer, n : n + half, :], rel_ref[:, columns_of(which)])
            )

        for n in (0, half):
            tasks += [functools.partial(content, n), functools.partial(placed, n)]
        return tasks

    interleave([], spreads(0))
    for which in range(heads):
        tasks = spreads(which + 1) if which + 1 < heads else []
        if which:
            tasks += gathers(which - 1)
        interleave(score_grads(which), tasks)
    interleave([], gathers(heads - 1))
    for which in range(heads):
        val_t.append(jnp.concatenate(found[which]["value"], axis=1))
        key_t.append(jnp.concatenate(found[which]["key"], axis=1))
        rel_t.append(jnp.concatenate(found[which]["rel"], axis=1))
    for pair in range(2):
        cols = slice(pair * PAIR, (pair + 1) * PAIR)
        content_heads, place_heads, term_same, term_other = [], [], [], []
        for head in range(2):
            base = (1 - head) * HEAD_DIM
            content_head = jnp.concatenate(found[pair * 2 + head]["content"], axis=0)
            content_heads.append(content_head)
            place_heads.append(jnp.concatenate(found[pair * 2 + head]["place"], axis=0))
            total = content_head[:, base : base + 1]
            marked = content_head[:, base + 4 : base + 5]
            differ = SCALE * (scol * total + swing * marked)
            term_other.append(differ)
            term_same.append(SCALE * total - differ)
        first_head = lane < HEAD_DIM
        content_grad = (SCALE * jnp.where(first_head, *content_heads)).astype(bf16).astype(f32)
        place = SCALE * jnp.where(first_head, *place_heads)
        place = jnp.concatenate([flip_rows(place[:half]), flip_rows(place[half:])], axis=0)
        place_grad = place.astype(bf16).astype(f32)
        same = jnp.where(first_head, *term_same)
        other = jnp.where(first_head, *term_other)
        segment_grad = same * se_ref[0:1, cols] + other * se_ref[1:2, cols]
        proj_grads.append((content_grad + place_grad + segment_grad).astype(bf16))
        small_ref[0:1, cols] = row_sum(content_grad)
        small_ref[1:2, cols] = row_sum(place_grad)
        small_ref[2:3, cols] = row_sum(segment_grad)
        head_segment = hs_ref[:, cols]
        small_ref[3:4, cols] = row_sum(same * head_segment)
        small_ref[4:5, cols] = row_sum(other * head_segment)
    small_ref[5:8, :] = jnp.zeros((3, QUAD), f32)
    proj_grad = jnp.concatenate(proj_grads, axis=1)
    key_t = jnp.concatenate(key_t, axis=0).astype(bf16)
    val_t = jnp.concatenate(val_t, axis=0).astype(bf16)
    rel_t = jnp.concatenate(rel_t, axis=0).astype(bf16)
    proj_ref[...] = proj_grad
    tok_key_ref[...] = key_t[:, MEM:].T
    tok_val_ref[...] = val_t[:, MEM:].T
    for fetch in fetches:
        fetch.wait()
    parts = (
        mm(both_t[...], proj_grad),
        mm_nt(stack_t[...], key_t),
        mm_nt(stack_t[...], val_t),
        mm_nt(pos_t[...], rel_t),
    )
    for index, value in enumerate(parts):
        cols = slice(index * QUAD, (index + 1) * QUAD)
        own_ref[:, cols] = value[:share].astype(bf16)
        oth_ref[:, cols] = value[share : 2 * share].astype(bf16)


def rows_kernel(half, groups, sgrad_ref, *rest):
    proj, keys, vals = rest[:QUADS], rest[QUADS : 2 * QUADS], rest[2 * QUADS : 3 * QUADS]
    wq_ref, wk_ref, wv_ref, own_ref, query_ref, send_ref, both = rest[3 * QUADS :]
    member = lax.axis_index("tensor")
    wide = [jnp.concatenate([ref[...] for ref in refs], axis=1) for refs in (proj, keys, vals)]
    both[...] = mm_nt(wide[1], wk_ref[...]) + mm_nt(wide[2], wv_ref[...])
    rows = sgrad_ref[...] + mm_nt(wide[0], wq_ref[...])
    own = pl.multiple_of(member * half, half)
    other = pl.multiple_of(lax.rem(member + 1, groups) * half, half)
    send_ref[...] = both[pl.ds(other, half), :].astype(bf16)
    own_ref[...] = rows[:half] + both[pl.ds(own, half), :]
    query_ref[...] = rows[half:]


def whole(shape):
    return pl.BlockSpec(shape, lambda i: (0,) * len(shape))


def columns(rows, width, at=None):
    if at is None:
        return pl.BlockSpec((rows, width), lambda i: (0, i))
    return pl.BlockSpec((rows, width), lambda i: (0, at))


def scalars():
    return pl.BlockSpec(memory_space=pltpu.SMEM)


def params():
    return pltpu.CompilerParams(vmem_limit_bytes=VMEM_BYTES)


def cost(flops, bytes_accessed):
    return pl.CostEstimate(flops=flops, bytes_accessed=bytes_accessed, transcendentals=0)


def in_hbm():
    return pl.BlockSpec(memory_space=pl.ANY)


def attention_forward(
    half, size, groups, ints, memory, content, query, weights, biases, segment_rows
):
    count, window = 2 * half, KEYS + half
    coarse_rows = -(-(window // 32) // 8) * 8
    outs = (
        ((count, D), f32, columns(count, QUAD)),
        ((HEADS, count, KEYS), bf16, pl.BlockSpec((4, count, KEYS), lambda i: (i, 0, 0))),
        ((KEYS, D), bf16, columns(KEYS, QUAD)),
        ((KEYS, D), bf16, columns(KEYS, QUAD)),
        ((window, D), bf16, columns(window, QUAD)),
        ((count, D), bf16, columns(count, QUAD)),
        ((count, D), bf16, columns(count, QUAD)),
        ((count, D), f32, columns(count, QUAD)),
        ((count, QUADS * TILE), f32, columns(count, TILE)),
        ((KEYS, PAIR), bf16, whole((KEYS, PAIR))),
        ((half, PAIR), f32, whole((half, PAIR))),
        ((D, count), bf16, whole((D, count))),
        ((D, KEYS), bf16, whole((D, KEYS))),
        ((D, window), bf16, whole((D, window))),
    )
    return pl.pallas_call(
        functools.partial(forward_kernel, half, size, groups),
        grid=(QUADS,),
        out_shape=[jax.ShapeDtypeStruct(shape, kind) for shape, kind, _ in outs],
        in_specs=[
            scalars(),
            scalars(),
            whole((1, LEN)),
            whole((1, LEN)),
            whole((1, LEN)),
            whole((MEM, D)),
            whole((LEN, D)),
            whole((half, D)),
        ]
        + [columns(D, QUAD)] * 4
        + [whole((D,))] * 3
        + [columns(2, QUAD)],
        out_specs=[spec for _, _, spec in outs],
        scratch_shapes=[
            pltpu.VMEM((KEYS, D), bf16),
            pltpu.VMEM((count, D), bf16),
            pltpu.VMEM((window, D), bf16),
            pltpu.VMEM((count, KEYS), f32),
            pltpu.VMEM((2, 32, D // 2), f32),
            pltpu.VMEM((2, coarse_rows, D // 2), f32),
            pltpu.VMEM((8, D), f32),
            pltpu.VMEM((2, half, KEYS), f32),
            pltpu.VMEM((2, half, window), f32),
        ],
        compiler_params=params(),
        cost_estimate=cost(30_000_000_000, 40_000_000),
        name="attention_forward",
    )(*ints, memory, content, query, *weights, *biases, segment_rows)


def upper(half, size, arrays, hidden_cols):
    count = 2 * half
    chunk = min(hidden_cols, 768)
    outs = (
        ((half, D), bf16),
        ((half, D), bf16),
        ((2, D, hidden_cols), bf16),
        ((count, hidden_cols), bf16),
        ((count, hidden_cols), bf16),
        ((count, D), bf16),
        ((count, D), f32),
        ((count, D), f32),
        ((count, TILE), f32),
        ((8, D), f32),
        ((1, hidden_cols), f32),
    )
    far_in = (6, 7, 8, 9)
    return pl.pallas_call(
        functools.partial(upper_kernel, half, size, chunk),
        grid=(1,),
        out_shape=[jax.ShapeDtypeStruct(shape, kind) for shape, kind in outs],
        in_specs=[
            in_hbm() if i in far_in else whole(array.shape) for i, array in enumerate(arrays)
        ],
        out_specs=[whole(shape) for shape, _ in outs],
        scratch_shapes=[
            pltpu.VMEM((2, D, hidden_cols), bf16),
            pltpu.VMEM((2, hidden_cols, D), bf16),
            pltpu.VMEM((count, hidden_cols), bf16),
            pltpu.VMEM((count, hidden_cols), bf16),
            pltpu.VMEM((2, count, chunk), f32),
            pltpu.VMEM((count, D), f32),
            pltpu.VMEM((8, FF), f32),
            pltpu.SemaphoreType.DMA((2, 2)),
        ],
        compiler_params=params(),
        cost_estimate=cost(20_000_000_000, 30_000_000),
        name="feed_forward",
    )(*arrays)


def lower(half, size, groups, arrays, hidden_cols):
    count, share = 2 * half, D // groups
    chunk = min(hidden_cols, 768)
    outs = (
        ((2, D, hidden_cols), bf16),
        ((count, D), f32),
        ((count, D), bf16),
        ((share, D), bf16),
        ((share, D), bf16),
        ((8, D), f32),
        ((1, hidden_cols), f32),
    )
    far_in, far_out = (1, 5, 7, 8), (0,)
    return pl.pallas_call(
        functools.partial(lower_kernel, half, size, groups, chunk),
        grid=(1,),
        out_shape=[jax.ShapeDtypeStruct(shape, kind) for shape, kind in outs],
        in_specs=[
            in_hbm() if i in far_in else whole(array.shape) for i, array in enumerate(arrays)
        ],
        out_specs=[in_hbm() if i in far_out else whole(s) for i, (s, _) in enumerate(outs)],
        scratch_shapes=[
            pltpu.VMEM((count, hidden_cols), bf16),
            pltpu.VMEM((count, D), f32),
            pltpu.VMEM((D, D), bf16),
            pltpu.VMEM((D, hidden_cols), bf16),
            pltpu.VMEM((2, D, hidden_cols), bf16),
            pltpu.SemaphoreType.DMA((4,)),
            pltpu.SemaphoreType.DMA((1,)),
        ],
        compiler_params=params(),
        cost_estimate=cost(10_000_000_000, 20_000_000),
        name="feed_forward_back",
    )(*arrays)


def attention_backward(half, groups, at, saved, agrad, segment_rows, extra):
    count, window, share = 2 * half, KEYS + half, D // groups
    att, prob, keys, values, rel, hc, hp, hs, linv, kaug, scol, both_t, stack_t, pos_t = saved
    width = 4 * QUAD + (D if extra else 0)
    operands = (
        (prob, in_hbm()),
        (keys, columns(KEYS, QUAD, at)),
        (values, columns(KEYS, QUAD, at)),
        (rel, columns(window, QUAD, at)),
        (hc, columns(count, QUAD, at)),
        (hp, columns(count, QUAD, at)),
        (hs, columns(count, QUAD, at)),
        (linv, columns(count, TILE, at)),
        (kaug, whole((KEYS, PAIR))),
        (scol, whole((half, PAIR))),
        (att, columns(count, QUAD, at)),
        (agrad, columns(count, QUAD, at)),
        (segment_rows, columns(2, QUAD, at)),
        (both_t, in_hbm()),
        (stack_t, in_hbm()),
        (pos_t, in_hbm()),
    ) + tuple((array, whole(array.shape)) for array in extra)
    outs = (
        ((share, width), bf16),
        ((share, width), bf16),
        ((count, QUAD), bf16),
        ((LEN, QUAD), bf16),
        ((LEN, QUAD), bf16),
        ((8, QUAD), f32),
    )
    return pl.pallas_call(
        functools.partial(backward_kernel, half, groups, at, bool(extra)),
        grid=(1,),
        out_shape=[jax.ShapeDtypeStruct(shape, kind) for shape, kind in outs],
        in_specs=[spec for _, spec in operands],
        out_specs=[whole(shape) for shape, _ in outs],
        scratch_shapes=[
            pltpu.VMEM((4, count, KEYS), bf16),
            pltpu.VMEM((D, count), bf16),
            pltpu.VMEM((D, KEYS), bf16),
            pltpu.VMEM((D, window), bf16),
            pltpu.VMEM((2, count, KEYS), f32),
            pltpu.VMEM((2, count, KEYS), bf16),
            pltpu.VMEM((2, count, window), bf16),
            pltpu.SemaphoreType.DMA((7,)),
        ],
        compiler_params=params(),
        cost_estimate=cost(16_000_000_000, 16_000_000),
        name="attention_backward",
    )(*[array for array, _ in operands])


def row_gradients(half, groups, summed_grad, proj, keys, vals, weights):
    count = 2 * half
    arrays = (summed_grad, *proj, *keys, *vals, *weights)
    outs = (((half, D), f32), ((half, D), f32), ((half, D), bf16))
    return pl.pallas_call(
        functools.partial(rows_kernel, half, groups),
        grid=(1,),
        out_shape=[jax.ShapeDtypeStruct(shape, kind) for shape, kind in outs],
        in_specs=[whole(array.shape) for array in arrays],
        out_specs=[whole(shape) for shape, _ in outs],
        scratch_shapes=[pltpu.VMEM((LEN, D), f32)],
        compiler_params=params(),
        cost_estimate=cost(4_000_000_000, 10_000_000),
        name="row_gradients",
    )(*arrays)


def swap(array):
    groups = lax.axis_size("tensor")
    return lax.ppermute(array, "tensor", [(i, (i + 1) % groups) for i in range(groups)])


def across(array, step):
    size, groups = lax.axis_size("dp"), lax.axis_size("tensor")
    bits = size.bit_length() - 1
    pairs = [
        (place * groups + core, (place ^ (1 << order_of(core, bits)[step])) * groups + core)
        for place in range(size)
        for core in range(groups)
    ]
    return lax.ppermute(array, ("dp", "tensor"), pairs)


def total(terms):
    return functools.reduce(jnp.add, [term.astype(f32) for term in terms])


class Chain:
    def __init__(self, own, other, vectors=None):
        self.rows = own.shape[0]
        self.terms = [own]
        self.vectors = None if vectors is None else [vectors]
        self.step = -1
        self.message = self.with_vectors(other)

    def with_vectors(self, message):
        if self.vectors is None:
            return message
        vectors = total(self.vectors).astype(bf16)
        pad = (0, -vectors.shape[0] % 16), (0, message.shape[1] - vectors.shape[1])
        return jnp.concatenate([message, jnp.pad(vectors, pad)], axis=0)

    def load(self):
        self.rows //= 2
        kept = self.rows
        message = total([term[kept : 2 * kept] for term in self.terms]).astype(bf16)
        self.message = self.with_vectors(message)
        self.terms = [term[:kept] for term in self.terms]

    def send(self):
        got = swap(self.message) if self.step < 0 else across(self.message, self.step)
        self.terms.append(got[: self.rows])
        if self.vectors is not None:
            count, width = self.vectors[0].shape
            self.vectors.append(got[self.rows : self.rows + count, :width])
        self.message = None
        self.step += 1

    def result(self):
        return total(self.terms)


def launch(chains, value):
    arrived = [chain for chain in chains if chain.message is None]
    value, gots = lax.optimization_barrier((value, [chain.terms[-1] for chain in arrived]))
    for chain, got in zip(arrived, gots):
        chain.terms[-1] = got
        chain.load()
    value, messages = lax.optimization_barrier((value, [chain.message for chain in chains]))
    for chain, message in zip(chains, messages):
        chain.message = message
        chain.send()
    return value


def body(
    content_in,
    query_in,
    memory,
    content_cot,
    query_cot,
    query_weight,
    key_weight,
    value_weight,
    out_weight,
    rel_weight,
    content_bias,
    position_bias,
    segment_bias,
    segment_embed,
    attn_gain,
    attn_shift,
    up_weight,
    up_bias,
    down_weight,
    down_bias,
    ffn_gain,
    ffn_shift,
    lengths,
    memory_lengths,
    segment_ids,
    orders,
    targets,
):
    groups = lax.axis_size("tensor")
    size = lax.axis_size("dp")
    steps = size.bit_length() - 1
    member = lax.axis_index("tensor")
    place = lax.axis_index("dp") * groups + member
    half = LEN // groups
    hidden_cols = up_weight.shape[1]
    up_other, down_other = swap(up_weight), swap(down_weight)
    content, query = content_in[0], query_in[0]
    segment_rows = segment_embed.T
    saved = attention_forward(
        half,
        size,
        groups,
        (lengths, memory_lengths, segment_ids, orders, targets),
        memory[0],
        content,
        query,
        (query_weight, key_weight, value_weight, rel_weight),
        (content_bias, position_bias, segment_bias),
        segment_rows,
    )
    att = saved[0]
    (
        content_out,
        query_out,
        ffn_other,
        hidden,
        slope,
        down_grad,
        grad_part,
        unit,
        inv,
        small_upper,
        up_bias_other,
    ) = upper(
        half,
        size,
        (
            att,
            content,
            query,
            content_cot[0],
            query_cot[0],
            out_weight,
            up_weight,
            up_other,
            down_weight,
            down_other,
            up_bias,
            down_bias,
            attn_gain,
            attn_shift,
            ffn_gain,
            ffn_shift,
        ),
        hidden_cols,
    )
    ffn_got = swap(ffn_other)
    ffn_own, summed_grad, attended_grad, out_own, out_other, small_lower, up_bias_own = lower(
        half,
        size,
        groups,
        (
            att,
            hidden,
            slope,
            down_grad,
            grad_part,
            unit,
            inv,
            out_weight,
            up_weight,
            down_weight,
            attn_gain,
            attn_shift,
        ),
        hidden_cols,
    )
    ffn_chains = []
    for part in range(2):
        chain = Chain(ffn_own[part], None)
        chain.terms.append(ffn_got[part])
        chain.step = 0
        ffn_chains.append(chain)
    up_bias_rows = jnp.where(
        member == 0,
        jnp.concatenate([up_bias_own, up_bias_other], axis=0),
        jnp.concatenate([up_bias_other, up_bias_own], axis=0),
    )
    early_small = jnp.concatenate(
        [small_upper[:3], small_lower[:2], up_bias_rows.reshape(-1, D)], axis=0
    )
    proj, tok_keys, tok_vals, late_small, late = [], [], [], [], []
    active = list(ffn_chains)
    held = attended_grad
    for at in range(QUADS):
        held = launch(active, held)
        active = [chain for chain in active if chain.step < steps]
        own, other, proj_part, key_part, val_part, small = attention_backward(
            half,
            groups,
            at,
            saved,
            held,
            segment_rows,
            (out_own, out_other) if at == 0 else (),
        )
        proj.append(proj_part)
        tok_keys.append(key_part)
        tok_vals.append(val_part)
        late_small.append(small)
        vectors = None
        if at == QUADS - 1:
            vectors = jnp.concatenate(
                [early_small, jnp.concatenate(late_small, axis=1)[:5]], axis=0
            )
        late.append(Chain(own, other, vectors))
        active.append(late[-1])
    last = late[-1]
    proj[-1] = launch(active, proj[-1])
    active = [chain for chain in active if chain.step < steps]
    own_rows, query_grad, row_send = row_gradients(
        half, groups, summed_grad, proj, tok_keys, tok_vals, (query_weight, key_weight, value_weight)
    )
    row_send = launch(active, row_send)
    row_got = swap(row_send)
    while active:
        active = [chain for chain in active if chain.step < steps]
        if active:
            launch(active, own_rows[:1, :1])
    content_grad = own_rows + row_got.astype(f32)
    up_chain, down_chain = ffn_chains
    small = total(last.vectors)
    share = D // (size * groups)
    vectors = lax.dynamic_slice_in_dim(small, place * share, share, 1)
    up_bias_grad = lax.dynamic_slice_in_dim(
        small[5:9].reshape(-1), place * (FF // (size * groups)), FF // (size * groups), 0
    )
    up_grad, down_grad_own = up_chain.result(), down_chain.result()
    blocks = [chain.result() for chain in late]

    def joined(index):
        return jnp.concatenate(
            [block[:, index * QUAD : (index + 1) * QUAD] for block in blocks], axis=1
        )

    return (
        content_out[None],
        query_out[None],
        content_grad[None],
        query_grad[None],
        joined(0),
        joined(1),
        joined(2),
        blocks[0][:, 4 * QUAD :],
        joined(3),
        vectors[9],
        vectors[10],
        vectors[11],
        vectors[12:14].T,
        vectors[3],
        vectors[4],
        up_grad,
        up_bias_grad,
        down_grad_own.T,
        vectors[2],
        vectors[0],
        vectors[1],
    )


def solution(mesh):
    in_specs = (
        P("dp", None, None),
        P("dp", "tensor", None),
        P("dp", None, None),
        P("dp", "tensor", None),
        P("dp", "tensor", None),
        P(),
        P(),
        P(),
        P(),
        P(),
        P(),
        P(),
        P(),
        P(),
        P(),
        P(),
        P(None, "tensor"),
        P(),
        P("tensor", None),
        P(),
        P(),
        P(),
        P("dp"),
        P("dp"),
        P("dp", None),
        P("dp", None),
        P("dp", None),
    )
    out_specs = (
        P("dp", "tensor", None),
        P("dp", "tensor", None),
        P("dp", "tensor", None),
        P("dp", "tensor", None),
        P(("dp", "tensor"), None),
        P(("dp", "tensor"), None),
        P(("dp", "tensor"), None),
        P(("dp", "tensor"), None),
        P(("dp", "tensor"), None),
        P(("dp", "tensor")),
        P(("dp", "tensor")),
        P(("dp", "tensor")),
        P(("dp", "tensor"), None),
        P(("dp", "tensor")),
        P(("dp", "tensor")),
        P("dp", "tensor"),
        P(("dp", "tensor")),
        P("tensor", "dp"),
        P(("dp", "tensor")),
        P(("dp", "tensor")),
        P(("dp", "tensor")),
    )
    return jax.shard_map(body, mesh=mesh, in_specs=in_specs, out_specs=out_specs, check_vma=False)
```

```python
import functools

import jax
import jax.numpy as jnp
from jax import lax
from jax.experimental import pallas as pl
from jax.experimental.pallas import tpu as pltpu
from jax.sharding import PartitionSpec as P

D = 768
HEADS = 12
HEAD_DIM = 64
FF = 3072
LEN = 512
MEM = 384
KEYS = MEM + LEN
QUAD = 4 * HEAD_DIM
QUADS = D // QUAD
PAIR = 2 * HEAD_DIM
SCALE = HEAD_DIM ** (-0.5)
VMEM_BYTES = 61 * 1024 * 1024
COMBINE_BYTES = 58 * 1024 * 1024
BLOCK = 32
TILE = 128
WIDE = 256
VECTORS = 16

f32 = jnp.float32
bf16 = jnp.bfloat16
precise = lax.Precision.HIGHEST


def mm(left, right):
    return lax.dot_general(left, right, (((1,), (0,)), ((), ())), preferred_element_type=f32)


def mm_nt(left, right):
    return lax.dot_general(left, right, (((1,), (1,)), ((), ())), preferred_element_type=f32)


def lanes(shape):
    return lax.broadcasted_iota(jnp.int32, shape, 1)


def column_of(row):
    return jnp.broadcast_to(row.astype(f32), (128, row.shape[1])).T


def lane_tiles(value, combine):
    tiles = [value[:, at : at + TILE] for at in range(0, value.shape[1], TILE)]
    return functools.reduce(combine, tiles)


def interleave(steps, tasks):
    done = 0
    for index, step in enumerate(steps):
        step()
        while done * len(steps) < (index + 1) * len(tasks) and done < len(tasks):
            tasks[done]()
            done += 1
    for task in tasks[done:]:
        task()


def order_of(core, bits):
    plain = list(range(bits))
    return plain[1:2] + plain[:1] + plain[2:] if core == 1 and bits > 1 else plain


def block_owner(place, core, bits):
    owner = jnp.zeros_like(place)
    for step in range(bits):
        owner = owner | (((place >> (bits - 1 - step)) & 1) << step)
    if bits > 1:
        swapped = (owner & ~3) | ((owner & 1) << 1) | ((owner >> 1) & 1)
        owner = jnp.where(core == 1, swapped, owner)
    return owner ^ lax.axis_index("dp")


def one_hot(source):
    return jnp.where(lanes((source.shape[0], D)) == source, 1.0, 0.0).astype(bf16)


def owner_rows(size, groups):
    share = D // (size * groups)
    row = lax.broadcasted_iota(jnp.int32, (D, 1), 0)
    side, rest = lax.div(row, size * share), lax.rem(row, size * share)
    core = lax.rem(lax.axis_index("tensor") + side, groups)
    owner = block_owner(lax.div(rest, share), core, size.bit_length() - 1)
    return one_hot((owner * groups + core) * share + lax.rem(rest, share))


def shared_rows(size, core):
    share = D // size
    row = lax.broadcasted_iota(jnp.int32, (D, 1), 0)
    owner = block_owner(lax.div(row, share), core, size.bit_length() - 1)
    return one_hot(owner * share + lax.rem(row, share))


def forward_kernel(
    half,
    size,
    groups,
    length_ref,
    mem_length_ref,
    seg_ref,
    ord_ref,
    tgt_ref,
    memory_ref,
    content_ref,
    query_ref,
    wq_ref,
    wk_ref,
    wv_ref,
    wr_ref,
    cb_ref,
    pb_ref,
    sb_ref,
    se_ref,
    att_ref,
    prob_ref,
    key_ref,
    val_ref,
    rel_ref,
    hc_ref,
    hp_ref,
    hs_ref,
    linv_ref,
    kaug_ref,
    scol_ref,
    both_t_ref,
    stack_t_ref,
    pos_t_ref,
    stack,
    both,
    pos,
    bias,
    fine,
    coarse,
    vectors,
    scores,
    places,
):
    window = KEYS + half
    first = pl.multiple_of(lax.axis_index("tensor") * half, half)
    step_id = pl.program_id(0)

    @pl.when(step_id == 0)
    def _():
        stack[:MEM, :] = memory_ref[...]
        stack[MEM:, :] = content_ref[...]
        both[:half, :] = content_ref[pl.ds(first, half), :]
        both[half:, :] = query_ref[...]
        vectors[0:1, :] = cb_ref[...][None, :]
        vectors[1:2, :] = pb_ref[...][None, :]
        vectors[2:3, :] = sb_ref[...][None, :]
        step = lax.broadcasted_iota(jnp.int32, (1, D // 2), 1).astype(f32) * (2.0 / D)
        inverse = 1.0 / jnp.power(jnp.full((1, D // 2), 10000.0, f32), step)
        coarse_rows = coarse.shape[1]
        top = (MEM + half + first).astype(f32)
        angle = (
            top - 32.0 * lax.broadcasted_iota(jnp.int32, (coarse_rows, 1), 0).astype(f32)
        ) * inverse
        coarse[0] = jnp.sin(angle)
        coarse[1] = jnp.cos(angle)
        small = lax.broadcasted_iota(jnp.int32, (32, 1), 0).astype(f32) * inverse
        fine[0] = jnp.sin(small)
        fine[1] = jnp.cos(small)
        for a in range(window // 32):
            sa, ca = coarse[0, a : a + 1, :], coarse[1, a : a + 1, :]
            sb, cb = fine[0], fine[1]
            pos[a * 32 : (a + 1) * 32, : D // 2] = (sa * cb - ca * sb).astype(bf16)
            pos[a * 32 : (a + 1) * 32, D // 2 :] = (ca * cb + sa * sb).astype(bf16)
        never = float(LEN + 1)
        mem_at = lax.broadcasted_iota(jnp.int32, (1, MEM), 1)
        tok_at = lax.broadcasted_iota(jnp.int32, (1, LEN), 1)
        open_from = jnp.concatenate(
            [
                jnp.where(mem_at >= MEM - mem_length_ref[0], -1.0, never),
                jnp.where(
                    tok_at < length_ref[0],
                    jnp.where(tgt_ref[...] == 0, -1.0, ord_ref[...].astype(f32)),
                    never,
                ),
            ],
            axis=1,
        )
        order_col = column_of(ord_ref[...])
        seg_col = column_of(seg_ref[...])
        kaug_lane = lanes((LEN, PAIR)) % HEAD_DIM
        kaug_ref[:MEM, :] = (lanes((MEM, PAIR)) % HEAD_DIM < 4).astype(f32).astype(bf16)
        kaug_ref[MEM:, :] = jnp.where(
            kaug_lane < 4, 1.0, jnp.where(kaug_lane < 6, seg_col, 0.0)
        ).astype(bf16)
        bias[:LEN, :PAIR] = order_col
        own_order = bias[pl.ds(first, half), :PAIR][:, :1]
        bias[:LEN, :PAIR] = seg_col
        scol_ref[...] = bias[pl.ds(first, half), :PAIR]
        seen = open_from <= own_order
        bias[:half, :] = jnp.where(seen, 0.0, -1e30)
        key_at = lax.broadcasted_iota(jnp.int32, (half, KEYS), 1)
        row_at = lax.broadcasted_iota(jnp.int32, (half, KEYS), 0)
        seen_q = seen & (key_at - MEM != row_at + first)
        bias[half:, :] = jnp.where(seen_q, 0.0, -1e30)
        chosen = owner_rows(size, groups)
        both_t_ref[...] = mm_nt(chosen, both[...]).astype(bf16)
        stack_t_ref[...] = mm_nt(chosen, stack[...]).astype(bf16)
        pos_t_ref[...] = mm_nt(chosen, pos[...]).astype(bf16)

    here = pl.ds(pl.multiple_of(step_id * QUAD, QUAD), QUAD)
    keys = mm(stack[...], wk_ref[...]).astype(bf16)
    values = mm(stack[...], wv_ref[...]).astype(bf16)
    rel = mm(pos[...], wr_ref[...]).astype(bf16)
    projection = mm(both[...], wq_ref[...])
    head_content = (projection + vectors[0:1, here]).astype(bf16)
    head_position = (projection + vectors[1:2, here]).astype(bf16)
    head_segment = projection + vectors[2:3, here]
    key_ref[...] = keys
    val_ref[...] = values
    rel_ref[...] = rel
    hs_ref[...] = head_segment
    head_content = (head_content.astype(f32) * SCALE).astype(bf16)
    head_position = (head_position.astype(f32) * SCALE).astype(bf16)
    hc_ref[...] = head_content
    hp_ref[...] = head_position
    same = column_of(se_ref[0:1, :])
    differ = column_of(se_ref[1:2, :] - se_ref[0:1, :])
    same = jnp.concatenate([same, same], axis=1)
    differ = jnp.concatenate([differ, differ], axis=1)
    row_head = lax.broadcasted_iota(jnp.int32, (QUAD, QUAD), 0) // HEAD_DIM
    at = lanes((QUAD, QUAD)) - ((row_head // 2) * PAIR + (1 - row_head % 2) * HEAD_DIM)
    embed = jnp.where(
        (at >= 0) & (at < 2), same, jnp.where((at >= 2) & (at < 6), differ, 0.0)
    )
    embed_high = embed.astype(bf16)
    embed_low = (embed - embed_high.astype(f32)).astype(bf16)
    segment_high = head_segment.astype(bf16)
    segment_low = (head_segment - segment_high.astype(f32)).astype(bf16)
    terms = (
        mm(segment_high, embed_high) + mm(segment_high, embed_low) + mm(segment_low, embed_high)
    )
    scol = scol_ref[...]
    scol = jnp.concatenate([scol, scol], axis=0)
    scol = jnp.concatenate([scol, scol], axis=1)
    lane6 = lanes((2 * half, QUAD)) % HEAD_DIM
    factor = jnp.where(lane6 < 2, 1.0, jnp.where(lane6 < 4, scol, 1.0 - 2.0 * scol))
    terms = SCALE * (terms * factor)
    high = terms.astype(bf16)
    low = (terms - high.astype(f32)).astype(bf16)
    qaug = jnp.where(lane6 % 2 == 0, high, low)
    kaug = kaug_ref[...]
    units = [(pair, head, part) for pair in range(2) for head in range(2) for part in range(2)]
    key_x = [
        jnp.where(
            (lanes((KEYS, PAIR)) < HEAD_DIM) == (which % 2 == 0),
            keys[:, which // 2 * PAIR : (which // 2 + 1) * PAIR],
            kaug,
        )
        for which in range(4)
    ]
    peaks, totals, outs = {}, {}, {}

    def products(index):
        pair, head, part = units[index]
        cols, rows = slice(pair * PAIR, (pair + 1) * PAIR), slice(part * half, (part + 1) * half)
        slot, which = index % 2, pair * 2 + head
        row_mine = (lanes((half, PAIR)) < HEAD_DIM) == (head == 0)
        query_x = jnp.where(row_mine, head_content[rows, cols], qaug[rows, cols])
        place_x = jnp.where(row_mine, head_position[rows, cols], jnp.zeros((), bf16))

        def score(n, stop):
            scores[slot, :, n:stop] = mm_nt(query_x, key_x[which][n:stop])

        def placed(n, stop):
            places[slot, :, n:stop] = mm_nt(place_x, rel[n:stop, cols])

        return [functools.partial(placed, n, min(n + WIDE, window)) for n in range(0, window, WIDE)] + [
            functools.partial(score, n, min(n + WIDE, KEYS)) for n in range(0, KEYS, WIDE)
        ]

    def softmax(index):
        pair, head, part = units[index]
        slot, which = index % 2, pair * 2 + head
        tops, pieces = [], []

        def join(b):
            block = slice(b, b + BLOCK)
            shifted = pltpu.roll(
                places[slot, block, :], (KEYS + b) % window, 1, stride=1, stride_axis=0
            )[:, :KEYS]
            score = (
                scores[slot, block, :]
                + shifted
                + bias[part * half + b : part * half + b + BLOCK, :]
            )
            scores[slot, block, :] = score
            tops.append(lane_tiles(score, jnp.maximum))

        def peak():
            peaks[index] = jnp.max(jnp.concatenate(tops, axis=0), axis=1, keepdims=True)

        def power(b):
            block = slice(b, b + BLOCK)
            prob = jnp.exp(scores[slot, block, :] - peaks[index][block])
            pieces.append(lane_tiles(prob, jnp.add))
            prob_ref[which, part * half + b : part * half + b + BLOCK, :] = prob.astype(bf16)

        def finish():
            totals[index] = 1.0 / jnp.sum(
                jnp.concatenate(pieces, axis=0), axis=1, keepdims=True
            )

        blocks = range(0, half, BLOCK)
        return (
            [functools.partial(join, b) for b in blocks]
            + [peak]
            + [functools.partial(power, b) for b in blocks]
            + [finish]
        )

    def mixture(index):
        pair, head, part = units[index]
        cols, rows = slice(pair * PAIR, (pair + 1) * PAIR), slice(part * half, (part + 1) * half)
        outs[index] = mm(prob_ref[pair * 2 + head, rows, :], values[:, cols]) * totals[index]

    interleave([], products(0))
    for index in range(len(units)):
        tasks = products(index + 1) if index + 1 < len(units) else []
        if index:
            tasks.append(functools.partial(mixture, index - 1))
        interleave(softmax(index), tasks)
    mixture(len(units) - 1)
    for pair in range(2):
        cols = slice(pair * PAIR, (pair + 1) * PAIR)
        mixtures = [
            jnp.concatenate([outs[pair * 4 + head * 2], outs[pair * 4 + head * 2 + 1]], axis=0)
            for head in range(2)
        ]
        mine = lanes((2 * half, PAIR)) < HEAD_DIM
        att_ref[:, cols] = jnp.where(mine, mixtures[0], mixtures[1])
    sums = [
        jnp.concatenate([totals[2 * which], totals[2 * which + 1]], axis=0) for which in range(4)
    ]
    lane = lanes((2 * half, TILE))
    linv_ref[...] = jnp.where(
        lane == 0, sums[0], jnp.where(lane == 1, sums[1], jnp.where(lane == 2, sums[2], sums[3]))
    )


def norm_forward(summed, gain, shift):
    center = summed - jnp.mean(summed, axis=1, keepdims=True)
    inv = lax.rsqrt(jnp.mean(center * center, axis=1, keepdims=True) + 1e-06)
    unit = center * inv
    return unit, inv, unit * gain + shift


def norm_backward(grad, unit, inv, gain):
    scaled = grad * gain
    return inv * (
        scaled
        - jnp.mean(scaled, axis=1, keepdims=True)
        - unit * jnp.mean(scaled * unit, axis=1, keepdims=True)
    )


def row_sum(value):
    return jnp.sum(value, axis=0, keepdims=True)


def gelu_parts(x):
    square = x * x
    tanh = jnp.tanh((0.7978845608028654 * x) * (1.0 + 0.044715 * square))
    rise = 0.5 * (1.0 + tanh)
    grad = rise + (0.5 * x) * (1.0 - tanh * tanh) * (
        0.7978845608028654 * (1.0 + 0.134145 * square)
    )
    return x * rise, grad


def fold_rows(value):
    return functools.reduce(jnp.add, [value[r : r + 8] for r in range(0, value.shape[0], 8)])


def middle_kernel(
    half,
    size,
    groups,
    chunk,
    att_ref,
    content_ref,
    query_ref,
    ccot_ref,
    qcot_ref,
    wo_ref,
    up_own_hbm,
    up_oth_hbm,
    down_own_hbm,
    down_oth_hbm,
    ubias_ref,
    dbias_ref,
    again_ref,
    ashift_ref,
    fgain_ref,
    fshift_ref,
    cout_ref,
    qout_ref,
    ffn_own_ref,
    ffn_oth_ref,
    sgrad_ref,
    agrad_ref,
    out_own_ref,
    out_oth_ref,
    small_ref,
    ubg_ref,
    hidden,
    slope,
    pre,
    work,
    unit,
    low,
    down_grad,
    vectors,
    up,
    down,
    sems,
):
    count = 2 * half
    member = lax.axis_index("tensor")
    first = pl.multiple_of(member * half, half)
    fetches = [
        pltpu.make_async_copy(source, target.at[side], sems.at[kind, side])
        for kind, side, source, target in (
            (0, 0, up_own_hbm, up),
            (1, 0, down_own_hbm, down),
            (0, 1, up_oth_hbm, up),
            (1, 1, down_oth_hbm, down),
        )
    ]
    for fetch in fetches:
        fetch.start()
    ups, downs = (up.at[0], up.at[1]), (down.at[0], down.at[1])
    part_cols = up.shape[2]
    chunks = part_cols // chunk
    vectors[0:1, :] = ubias_ref[...][None, :]
    attended = att_ref[...].astype(bf16)
    work[...] = mm(attended, wo_ref[...])
    attn_gain, attn_shift = again_ref[...][None, :], ashift_ref[...][None, :]
    ffn_gain, ffn_shift = fgain_ref[...][None, :], fshift_ref[...][None, :]
    down_bias = dbias_ref[...][None, :]
    inverse = []
    for b in range(0, count, BLOCK):
        block = slice(b, b + BLOCK)
        if b < half:
            rows_in = content_ref[pl.ds(pl.multiple_of(first + b, BLOCK), BLOCK), :]
        else:
            rows_in = query_ref[b - half : b - half + BLOCK, :]
        found, inv, normed = norm_forward(
            work[block, :] + rows_in.astype(f32), attn_gain, attn_shift
        )
        unit[block, :] = found
        inverse.append(inv)
        low[block, :] = normed.astype(bf16)
        work[block, :] = normed + down_bias
    for fetch in fetches:
        fetch.wait()
    pieces = [(side, at) for side in range(2) for at in range(chunks)]

    def rise(index):
        side, at = pieces[index]

        def task(n):
            pre[index % 2, :, n : n + WIDE] = mm(
                low[...], ups[side][:, at * chunk + n : at * chunk + n + WIDE]
            )

        return [functools.partial(task, n) for n in range(0, chunk, WIDE)]

    def bend(index):
        side, at = pieces[index]
        cols = slice(at * chunk, (at + 1) * chunk)
        start = lax.rem(member + side, 2) * part_cols + at * chunk
        bias = vectors[0:1, pl.ds(pl.multiple_of(start, TILE), chunk)]

        def step(b):
            block = slice(b, b + BLOCK)
            act, grad = gelu_parts(pre[index % 2, block, :] + bias)
            hidden[side, block, cols] = act.astype(bf16)
            slope[side, block, cols] = grad.astype(bf16)

        return [functools.partial(step, b) for b in range(0, count, BLOCK)]

    def fall(index):
        side, at = pieces[index]
        cols = slice(at * chunk, (at + 1) * chunk)

        def task(n):
            work[:, n : n + WIDE] += mm(hidden[side, :, cols], downs[side][cols, n : n + WIDE])

        return [functools.partial(task, n) for n in range(0, D, WIDE)]

    interleave([], rise(0))
    for index in range(len(pieces)):
        tasks = rise(index + 1) if index + 1 < len(pieces) else []
        if index:
            tasks += fall(index - 1)
        interleave(bend(index), tasks)
    interleave([], fall(len(pieces) - 1))
    sums = [jnp.zeros((8, D), f32) for _ in range(5)]
    for b in range(0, count, BLOCK):
        block = slice(b, b + BLOCK)
        found, inv, out = norm_forward(work[block, :], ffn_gain, ffn_shift)
        if b < half:
            cout_ref[block, :] = out.astype(bf16)
            cot = ccot_ref[block, :].astype(f32)
        else:
            block_q = slice(b - half, b - half + BLOCK)
            qout_ref[block_q, :] = out.astype(bf16)
            cot = qcot_ref[block_q, :].astype(f32)
        residual_grad = norm_backward(cot, found, inv, ffn_gain)
        rounded = residual_grad.astype(bf16)
        down_grad[block, :] = rounded
        work[block, :] = residual_grad
        for index, value in enumerate((cot * found, cot, rounded.astype(f32))):
            sums[index] = sums[index] + fold_rows(value)
    chosen = shared_rows(size, member)
    low_t = mm_nt(chosen, low[...]).astype(bf16)
    down_grad_t = mm_nt(chosen, down_grad[...]).astype(bf16)
    for side in range(2):
        for at in range(chunks):
            cols = slice(at * chunk, (at + 1) * chunk)
            hidden_grad = mm_nt(down_grad[...], downs[side][cols, :])
            pre_grad = (hidden_grad * slope[side, :, cols].astype(f32)).astype(bf16)
            slope[side, :, cols] = pre_grad
            ubg_ref[side : side + 1, cols] = row_sum(pre_grad.astype(f32))
            work[...] += mm_nt(pre_grad, ups[side][:, cols])

    def settle(b):
        block = slice(b, b + BLOCK)
        grad, found = work[block, :], unit[block, :]
        summed_grad = norm_backward(grad, found, inverse[b // BLOCK], attn_gain)
        sgrad_ref[block, :] = summed_grad
        down_grad[block, :] = summed_grad.astype(bf16)
        sums[3] = sums[3] + fold_rows(grad * found)
        sums[4] = sums[4] + fold_rows(grad)

    quarter = D // 4

    def weigh(side, kind, n):
        left, right = ((low_t, slope), (down_grad_t, hidden))[kind]
        value = mm(left, right[side, :, n : n + WIDE]).astype(bf16)
        target = (ffn_own_ref, ffn_oth_ref)[side]
        cols = slice(kind * part_cols + n, kind * part_cols + n + WIDE)
        places = (0, 2, 1, 3) if side == 1 and size > 2 else (0, 1, 2, 3)
        for q, place in enumerate(places):
            target[place * quarter : (place + 1) * quarter, cols] = value[
                q * quarter : (q + 1) * quarter
            ]

    tasks = [
        functools.partial(weigh, side, kind, n)
        for side in (1, 0)
        for kind in range(2)
        for n in range(0, part_cols, WIDE)
    ]
    interleave([functools.partial(settle, b) for b in range(0, count, BLOCK)], tasks)
    for index, value in enumerate(sums):
        small_ref[index : index + 1, :] = row_sum(value)
    small_ref[5:8, :] = jnp.zeros((3, D), f32)
    agrad_ref[...] = mm_nt(down_grad[...], wo_ref[...]).astype(bf16)
    attended_t = mm_nt(owner_rows(size, groups), attended).astype(bf16)
    out_part = mm(attended_t, down_grad[...]).astype(bf16)
    share = D // groups
    out_own_ref[...] = out_part[:share]
    out_oth_ref[...] = out_part[share : 2 * share]


def unshift(value, shift, window):
    whole, rest = shift // TILE, shift % TILE
    row = lax.broadcasted_iota(jnp.int32, (BLOCK, TILE), 0)
    lane = lanes((BLOCK, TILE))
    index = (lane + row - rest) & (TILE - 1)
    tiles = [
        jnp.take_along_axis(
            value[:, n : n + TILE], index, axis=1, mode="promise_in_bounds"
        )
        for n in range(0, value.shape[1], TILE)
    ]
    zero = jnp.zeros((BLOCK, TILE), f32)

    def tile(n):
        return tiles[n] if 0 <= n < len(tiles) else zero

    if rest:
        here = lane >= rest - row
        found = [
            jnp.where(here, tile(n - whole), tile(n - whole - 1)) for n in range(window // TILE)
        ]
    else:
        here = lane + row < TILE
        found = [
            jnp.where(here, tile(n - whole), tile(n - whole + 1)) for n in range(window // TILE)
        ]
    return jnp.concatenate(found, axis=1)


def backward_kernel(
    half,
    groups,
    at,
    mode,
    prob_hbm,
    key_ref,
    val_ref,
    rel_ref,
    hc_ref,
    hp_ref,
    hs_ref,
    linv_ref,
    kaug_ref,
    scol_ref,
    att_ref,
    agrad_ref,
    se_ref,
    both_t_hbm,
    stack_t_hbm,
    pos_t_hbm,
    *rest,
):
    more = rest[: {"first": 2, "middle": 0, "last": 4}[mode]]
    own_ref, oth_ref, proj_ref, tok_key_ref, tok_val_ref, small_ref = rest[len(more) :][:6]
    prob, both_t, stack_t, pos_t, spread, grads, turned, sems = rest[-8:]
    count, window = 2 * half, KEYS + half
    heads = 4
    prob_copies = [
        pltpu.make_async_copy(prob_hbm.at[at * heads + h], prob.at[h], sems.at[h])
        for h in range(heads)
    ]
    fetches = [
        pltpu.make_async_copy(source, target, sems.at[heads + index])
        for index, (source, target) in enumerate(
            ((both_t_hbm, both_t), (stack_t_hbm, stack_t), (pos_t_hbm, pos_t))
        )
    ]
    for copy in prob_copies + fetches:
        copy.start()
    share = D // groups
    if mode == "first":
        own_ref[:, 4 * QUAD :] = more[0][...]
        oth_ref[:, 4 * QUAD :] = more[1][...]
    kaug = kaug_ref[...]
    scol = scol_ref[...]
    scol = jnp.concatenate([scol, scol], axis=0)
    swing = 1.0 - 2.0 * scol
    key_t, val_t, rel_t = [], [], []
    proj_grads = []
    hp_t = hp_ref[...].T
    hc_t = hc_ref[...].T
    lane = lanes((count, PAIR))
    agrads, grad_x, agrad_t = [], [], []
    for pair in range(2):
        cols = slice(pair * PAIR, (pair + 1) * PAIR)
        linv = jnp.where(
            lane < HEAD_DIM,
            linv_ref[:, 2 * pair : 2 * pair + 1],
            linv_ref[:, 2 * pair + 1 : 2 * pair + 2],
        )
        agrad = (agrad_ref[:, cols].astype(f32) * linv).astype(bf16).astype(f32)
        products = agrad * att_ref[:, cols]
        agrad_t.append(agrad.astype(bf16).T)
        for head in range(2):
            base = (1 - head) * HEAD_DIM
            mine = (lane < HEAD_DIM) == (head == 0)
            weight = jnp.sum(jnp.where(mine, products, 0.0), axis=1, keepdims=True)
            high = weight.astype(bf16).astype(f32)
            grad_x.append(
                jnp.where(
                    mine,
                    agrad,
                    jnp.where(
                        lane == base, -high, jnp.where(lane == base + 1, high - weight, 0.0)
                    ),
                ).astype(bf16)
            )
    key_mine = lanes((KEYS, PAIR)) < HEAD_DIM
    found = {}

    def columns_of(which):
        return slice(which // 2 * PAIR, (which // 2 + 1) * PAIR)

    def extended(ref, which):
        return jnp.where(key_mine == (which % 2 == 0), ref[:, columns_of(which)], kaug)

    def spreads(which):
        val_x = extended(val_ref, which)
        prob_copies[which].wait()

        def task(n, stop):
            spread[which % 2, :, n:stop] = mm_nt(grad_x[which], val_x[n:stop])

        return [functools.partial(task, n, min(n + WIDE, KEYS)) for n in range(0, KEYS, WIDE)]

    def score_grads(which):
        buffer = which % 2

        def step(part, b):
            at_row = part * half + b
            block = slice(at_row, at_row + BLOCK)
            score_grad = prob[which, block, :].astype(f32) * spread[buffer, block, :]
            grads[buffer, block, :] = score_grad.astype(bf16)
            turned[buffer, block, :] = unshift(score_grad, half - b, window).astype(bf16)

        return [
            functools.partial(step, part, b) for part in range(2) for b in range(0, half, BLOCK)
        ]

    def gathers(which):
        buffer = which % 2
        head_rows = slice(which * HEAD_DIM, (which + 1) * HEAD_DIM)
        side = slice(which % 2 * HEAD_DIM, (which % 2 + 1) * HEAD_DIM)
        key_x = extended(key_ref, which)
        found[which] = {"value": [], "key": [], "rel": [], "content": [], "place": []}

        def down_rows(name, left, ref, n, stop):
            found[which][name].append(mm(left, ref[:, n:stop]))

        tasks = []
        for name, left, ref, end in (
            ("value", agrad_t[which // 2][side], prob.at[which], KEYS),
            ("key", hc_t[head_rows], grads.at[buffer], KEYS),
            ("rel", hp_t[head_rows], turned.at[buffer], window),
        ):
            tasks += [
                functools.partial(down_rows, name, left, ref, n, min(n + WIDE, end))
                for n in range(0, end, WIDE)
            ]

        def content(n):
            found[which]["content"].append(mm(grads[buffer, n : n + half, :], key_x))

        def placed(n):
            found[which]["place"].append(
                mm(turned[buffer, n : n + half, :], rel_ref[:, columns_of(which)])
            )

        for n in (0, half):
            tasks += [functools.partial(content, n), functools.partial(placed, n)]
        return tasks

    interleave([], spreads(0))
    for which in range(heads):
        tasks = spreads(which + 1) if which + 1 < heads else []
        if which:
            tasks += gathers(which - 1)
        interleave(score_grads(which), tasks)
    interleave([], gathers(heads - 1))
    for which in range(heads):
        val_t.append(jnp.concatenate(found[which]["value"], axis=1))
        key_t.append(jnp.concatenate(found[which]["key"], axis=1))
        rel_t.append(jnp.concatenate(found[which]["rel"], axis=1))
    for pair in range(2):
        cols = slice(pair * PAIR, (pair + 1) * PAIR)
        content_heads, place_heads, term_same, term_other = [], [], [], []
        for head in range(2):
            base = (1 - head) * HEAD_DIM
            content_head = jnp.concatenate(found[pair * 2 + head]["content"], axis=0)
            content_heads.append(content_head)
            place_heads.append(jnp.concatenate(found[pair * 2 + head]["place"], axis=0))
            total = content_head[:, base : base + 1]
            marked = content_head[:, base + 4 : base + 5]
            differ = SCALE * (scol * total + swing * marked)
            term_other.append(differ)
            term_same.append(SCALE * total - differ)
        first_head = lane < HEAD_DIM
        content_grad = (SCALE * jnp.where(first_head, *content_heads)).astype(bf16).astype(f32)
        place_grad = (SCALE * jnp.where(first_head, *place_heads)).astype(bf16).astype(f32)
        same = jnp.where(first_head, *term_same)
        other = jnp.where(first_head, *term_other)
        segment_grad = same * se_ref[0:1, cols] + other * se_ref[1:2, cols]
        proj_grads.append((content_grad + place_grad + segment_grad).astype(bf16))
        small_ref[0:1, cols] = row_sum(content_grad)
        small_ref[1:2, cols] = row_sum(place_grad)
        small_ref[2:3, cols] = row_sum(segment_grad)
        head_segment = hs_ref[:, cols]
        small_ref[3:4, cols] = row_sum(same * head_segment)
        small_ref[4:5, cols] = row_sum(other * head_segment)
    small_ref[5:8, :] = jnp.zeros((3, QUAD), f32)
    proj_grad = jnp.concatenate(proj_grads, axis=1)
    key_t = jnp.concatenate(key_t, axis=0).astype(bf16)
    val_t = jnp.concatenate(val_t, axis=0).astype(bf16)
    rel_t = jnp.concatenate(rel_t, axis=0).astype(bf16)
    proj_ref[...] = proj_grad
    tok_key_ref[...] = key_t[:, MEM:].T
    tok_val_ref[...] = val_t[:, MEM:].T
    for fetch in fetches:
        fetch.wait()
    parts = (
        mm(both_t[...], proj_grad),
        mm_nt(stack_t[...], key_t),
        mm_nt(stack_t[...], val_t),
        mm_nt(pos_t[...], rel_t),
    )
    for index, value in enumerate(parts):
        cols = slice(index * QUAD, (index + 1) * QUAD)
        own_ref[:, cols] = value[:share].astype(bf16)
        oth_ref[:share, cols] = value[share : 2 * share].astype(bf16)
    if mode == "last":
        vec_ref = rest[len(more) + 6]
        early, ubias, before, between = more
        core = lax.axis_index("tensor")
        rows = [early[0:5, :]]
        mine = [ubias[0:1, n : n + D] for n in range(0, ubias.shape[1], D)]
        theirs = [ubias[1:2, n : n + D] for n in range(0, ubias.shape[1], D)]
        for left, right in ((mine, theirs), (theirs, mine)):
            rows += [jnp.where(core == 0, a, b) for a, b in zip(left, right)]
        rows.append(
            jnp.concatenate([before[0:5, :], between[0:5, :], small_ref[0:5, :]], axis=1)
        )
        rows = jnp.concatenate(rows, axis=0)
        vec_ref[...] = jnp.concatenate(
            [rows, jnp.zeros((VECTORS - rows.shape[0], D), f32)], axis=0
        )
        oth_ref[share:, :D] = vec_ref[...].astype(bf16)
        oth_ref[share:, D:] = jnp.zeros((VECTORS, oth_ref.shape[1] - D), bf16)


def rows_kernel(half, groups, sgrad_ref, *rest):
    proj, keys, vals = rest[:QUADS], rest[QUADS : 2 * QUADS], rest[2 * QUADS : 3 * QUADS]
    wq_ref, wk_ref, wv_ref, own_ref, query_ref, send_ref, both = rest[3 * QUADS :]
    member = lax.axis_index("tensor")
    wide = [jnp.concatenate([ref[...] for ref in refs], axis=1) for refs in (proj, keys, vals)]
    both[...] = mm_nt(wide[1], wk_ref[...]) + mm_nt(wide[2], wv_ref[...])
    rows = sgrad_ref[...] + mm_nt(wide[0], wq_ref[...])
    own = pl.multiple_of(member * half, half)
    other = pl.multiple_of(lax.rem(member + 1, groups) * half, half)
    send_ref[...] = both[pl.ds(other, half), :].astype(bf16)
    own_ref[...] = rows[:half] + both[pl.ds(own, half), :]
    query_ref[...] = rows[half:]


def combine_kernel(plans, *refs):
    operands, outs = refs[: -len(plans)], refs[-len(plans) :]
    for (rows, first, parts, vectors), out_ref in zip(plans, outs):
        column = 0
        for width, terms in parts:
            value = functools.reduce(
                jnp.add,
                [
                    operands[index][...].astype(f32)[skip : skip + rows, at : at + width]
                    for index, at, skip in terms
                ],
            )
            out_ref[:rows, column : column + width] = value.astype(out_ref.dtype)
            column += width
        if vectors:
            value = functools.reduce(
                jnp.add,
                [
                    operands[index][...].astype(f32)[skip : skip + VECTORS, :D]
                    for index, skip in vectors
                ],
            )
            out_ref[rows:, :D] = value.astype(out_ref.dtype)
            out_ref[rows:, D:] = jnp.zeros((VECTORS, out_ref.shape[1] - D), out_ref.dtype)


def finish_kernel(size, groups, count, plan, up_rows, *refs):
    operands, outs = refs[:count], refs[count:]
    weights, vec_out = outs[:-1], outs[-1]
    place = lax.axis_index("dp") * groups + lax.axis_index("tensor")
    share = D // (size * groups)
    for target, at, width, terms in plan[0]:
        value = functools.reduce(
            jnp.add,
            [operands[index][...].astype(f32)[:share, c : c + width] for index, c in terms],
        )
        weights[target][:, at : at + width] = value
    value = functools.reduce(
        jnp.add,
        [
            operands[index][...].astype(f32)[skip : skip + VECTORS, :D]
            for index, skip in plan[1]
        ],
    )
    vec_out[...] = pltpu.roll(value, lax.rem(D - place * share, D), 1)[:, :TILE]
    wide = up_rows * share
    each = D // wide
    line = lax.div(place, each)
    chosen = functools.reduce(
        jnp.add,
        [jnp.where(line == r, value[5 + r : 6 + r], 0.0) for r in range(up_rows)],
    )
    chosen = jnp.broadcast_to(chosen, (8, D))
    turned = pltpu.roll(chosen, lax.rem(D - lax.rem(place, each) * wide, D), 1)[:, :TILE]
    vec_out[VECTORS - 1 : VECTORS, :] = turned[0:1, :]


def whole(shape):
    return pl.BlockSpec(shape, lambda i: (0,) * len(shape))


def columns(rows, width, at=None):
    if at is None:
        return pl.BlockSpec((rows, width), lambda i: (0, i))
    return pl.BlockSpec((rows, width), lambda i: (0, at))


def scalars():
    return pl.BlockSpec(memory_space=pltpu.SMEM)


def params(size=VMEM_BYTES):
    return pltpu.CompilerParams(vmem_limit_bytes=size)


def cost(flops, bytes_accessed):
    return pl.CostEstimate(flops=flops, bytes_accessed=bytes_accessed, transcendentals=0)


def in_hbm():
    return pl.BlockSpec(memory_space=pl.ANY)


def attention_forward(
    half, size, groups, ints, memory, content, query, weights, biases, segment_rows
):
    count, window = 2 * half, KEYS + half
    coarse_rows = -(-(window // 32) // 8) * 8
    outs = (
        ((count, D), f32, columns(count, QUAD)),
        ((HEADS, count, KEYS), bf16, pl.BlockSpec((4, count, KEYS), lambda i: (i, 0, 0))),
        ((KEYS, D), bf16, columns(KEYS, QUAD)),
        ((KEYS, D), bf16, columns(KEYS, QUAD)),
        ((window, D), bf16, columns(window, QUAD)),
        ((count, D), bf16, columns(count, QUAD)),
        ((count, D), bf16, columns(count, QUAD)),
        ((count, D), f32, columns(count, QUAD)),
        ((count, QUADS * TILE), f32, columns(count, TILE)),
        ((KEYS, PAIR), bf16, whole((KEYS, PAIR))),
        ((half, PAIR), f32, whole((half, PAIR))),
        ((D, count), bf16, whole((D, count))),
        ((D, KEYS), bf16, whole((D, KEYS))),
        ((D, window), bf16, whole((D, window))),
    )
    return pl.pallas_call(
        functools.partial(forward_kernel, half, size, groups),
        grid=(QUADS,),
        out_shape=[jax.ShapeDtypeStruct(shape, kind) for shape, kind, _ in outs],
        in_specs=[
            scalars(),
            scalars(),
            whole((1, LEN)),
            whole((1, LEN)),
            whole((1, LEN)),
            whole((MEM, D)),
            whole((LEN, D)),
            whole((half, D)),
        ]
        + [columns(D, QUAD)] * 4
        + [whole((D,))] * 3
        + [columns(2, QUAD)],
        out_specs=[spec for _, _, spec in outs],
        scratch_shapes=[
            pltpu.VMEM((KEYS, D), bf16),
            pltpu.VMEM((count, D), bf16),
            pltpu.VMEM((window, D), bf16),
            pltpu.VMEM((count, KEYS), f32),
            pltpu.VMEM((2, 32, D // 2), f32),
            pltpu.VMEM((2, coarse_rows, D // 2), f32),
            pltpu.VMEM((8, D), f32),
            pltpu.VMEM((2, half, KEYS), f32),
            pltpu.VMEM((2, half, window), f32),
        ],
        compiler_params=params(),
        cost_estimate=cost(30_000_000_000, 40_000_000),
        name="attention_forward",
    )(*ints, memory, content, query, *weights, *biases, segment_rows)


def middle(half, size, groups, arrays, hidden_cols):
    count, share = 2 * half, D // groups
    chunk = min(hidden_cols, 768)
    outs = (
        ((half, D), bf16),
        ((half, D), bf16),
        ((D, 2 * hidden_cols), bf16),
        ((D, 2 * hidden_cols), bf16),
        ((count, D), f32),
        ((count, D), bf16),
        ((share, D), bf16),
        ((share, D), bf16),
        ((8, D), f32),
        ((2, hidden_cols), f32),
    )
    weights = (6, 7, 8, 9)
    return pl.pallas_call(
        functools.partial(middle_kernel, half, size, groups, chunk),
        grid=(1,),
        out_shape=[jax.ShapeDtypeStruct(shape, kind) for shape, kind in outs],
        in_specs=[
            in_hbm() if i in weights else whole(array.shape) for i, array in enumerate(arrays)
        ],
        out_specs=[whole(shape) for shape, _ in outs],
        scratch_shapes=[
            pltpu.VMEM((2, count, hidden_cols), bf16),
            pltpu.VMEM((2, count, hidden_cols), bf16),
            pltpu.VMEM((2, count, chunk), f32),
            pltpu.VMEM((count, D), f32),
            pltpu.VMEM((count, D), f32),
            pltpu.VMEM((count, D), bf16),
            pltpu.VMEM((count, D), bf16),
            pltpu.VMEM((8, FF), f32),
            pltpu.VMEM((2, D, hidden_cols), bf16),
            pltpu.VMEM((2, hidden_cols, D), bf16),
            pltpu.SemaphoreType.DMA((2, 2)),
        ],
        compiler_params=params(),
        cost_estimate=cost(30_000_000_000, 30_000_000),
        name="feed_forward",
    )(*arrays)


def attention_backward(half, groups, at, mode, saved, agrad, segment_rows, extra):
    count, window, share = 2 * half, KEYS + half, D // groups
    att, prob, keys, values, rel, hc, hp, hs, linv, kaug, scol, both_t, stack_t, pos_t = saved
    width = 4 * QUAD + (D if mode == "first" else 0)
    more_rows = VECTORS if mode == "last" else 0
    operands = (
        (prob, in_hbm()),
        (keys, columns(KEYS, QUAD, at)),
        (values, columns(KEYS, QUAD, at)),
        (rel, columns(window, QUAD, at)),
        (hc, columns(count, QUAD, at)),
        (hp, columns(count, QUAD, at)),
        (hs, columns(count, QUAD, at)),
        (linv, columns(count, TILE, at)),
        (kaug, whole((KEYS, PAIR))),
        (scol, whole((half, PAIR))),
        (att, columns(count, QUAD, at)),
        (agrad, columns(count, QUAD, at)),
        (segment_rows, columns(2, QUAD, at)),
        (both_t, in_hbm()),
        (stack_t, in_hbm()),
        (pos_t, in_hbm()),
    ) + tuple((array, whole(array.shape)) for array in extra)
    outs = (
        ((share, width), bf16),
        ((share + more_rows, width), bf16),
        ((count, QUAD), bf16),
        ((LEN, QUAD), bf16),
        ((LEN, QUAD), bf16),
        ((8, QUAD), f32),
    )
    if mode == "last":
        outs += (((VECTORS, D), f32),)
    return pl.pallas_call(
        functools.partial(backward_kernel, half, groups, at, mode),
        grid=(1,),
        out_shape=[jax.ShapeDtypeStruct(shape, kind) for shape, kind in outs],
        in_specs=[spec for _, spec in operands],
        out_specs=[whole(shape) for shape, _ in outs],
        scratch_shapes=[
            pltpu.VMEM((4, count, KEYS), bf16),
            pltpu.VMEM((D, count), bf16),
            pltpu.VMEM((D, KEYS), bf16),
            pltpu.VMEM((D, window), bf16),
            pltpu.VMEM((2, count, KEYS), f32),
            pltpu.VMEM((2, count, KEYS), bf16),
            pltpu.VMEM((2, count, window), bf16),
            pltpu.SemaphoreType.DMA((7,)),
        ],
        compiler_params=params(),
        cost_estimate=cost(16_000_000_000, 16_000_000),
        name="attention_backward",
    )(*[array for array, _ in operands])


def row_gradients(half, groups, summed_grad, proj, keys, vals, weights):
    count = 2 * half
    arrays = (summed_grad, *proj, *keys, *vals, *weights)
    outs = (((half, D), f32), ((half, D), f32), ((half, D), bf16))
    return pl.pallas_call(
        functools.partial(rows_kernel, half, groups),
        grid=(1,),
        out_shape=[jax.ShapeDtypeStruct(shape, kind) for shape, kind in outs],
        in_specs=[whole(array.shape) for array in arrays],
        out_specs=[whole(shape) for shape, _ in outs],
        scratch_shapes=[pltpu.VMEM((LEN, D), f32)],
        compiler_params=params(),
        cost_estimate=cost(4_000_000_000, 10_000_000),
        name="row_gradients",
    )(*arrays)


def swap(array):
    groups = lax.axis_size("tensor")
    return lax.ppermute(array, "tensor", [(i, (i + 1) % groups) for i in range(groups)])


def across(array, step):
    size, groups = lax.axis_size("dp"), lax.axis_size("tensor")
    bits = size.bit_length() - 1
    pairs = [
        (place * groups + core, (place ^ (1 << order_of(core, bits)[step])) * groups + core)
        for place in range(size)
        for core in range(groups)
    ]
    return lax.ppermute(array, ("dp", "tensor"), pairs)


def total(terms):
    return functools.reduce(jnp.add, [term.astype(f32) for term in terms])


class Chain:
    def __init__(self, parts, rows, step, vectors=()):
        self.parts, self.rows, self.step = parts, rows, step
        self.vectors = list(vectors)
        self.message = None

    def shape(self):
        rows = self.rows + (VECTORS if self.vectors else 0)
        return rows, sum(width for width, _ in self.parts)

    def send(self):
        got = swap(self.message) if self.step < 0 else across(self.message, self.step)
        column = 0
        for width, terms in self.parts:
            terms.append((got, column))
            column += width
        if self.vectors:
            self.vectors.append((got, self.rows))
        self.step += 1
        self.message = None

    def arrays(self):
        found = []
        for _, terms in self.parts:
            found += [array for array, _ in terms]
        return found + [array for array, _ in self.vectors]

    def replace(self, old, new):
        for index, (width, terms) in enumerate(self.parts):
            self.parts[index] = (
                width,
                [(new if array is old else array, at) for array, at in terms],
            )
        self.vectors = [(new if array is old else array, at) for array, at in self.vectors]

    def latest(self):
        return self.parts[0][1][-1][0]


def merged(one, two):
    return Chain(one.parts + two.parts, one.rows, one.step, one.vectors + two.vectors)


class Operands:
    def __init__(self):
        self.arrays, self.specs = [], []

    def rows(self, array, first, rows):
        if rows % 16 == 0 and first % rows == 0:
            spec, skip = pl.BlockSpec((rows, array.shape[1]), lambda i: (first // rows, 0)), 0
        elif (first + rows) % 16 == 0 and first + rows < array.shape[0]:
            spec, skip = pl.BlockSpec((first + rows, array.shape[1]), lambda i: (0, 0)), first
        else:
            spec, skip = whole(array.shape), first
        self.arrays.append(array)
        self.specs.append(spec)
        return len(self.arrays) - 1, skip


def load(chains):
    if any(chain.rows % 16 for chain in chains):
        for chain in chains:
            chain.rows //= 2
            kept = chain.rows
            message = jnp.concatenate(
                [
                    total([array[kept : 2 * kept, at : at + width] for array, at in terms])
                    for width, terms in chain.parts
                ],
                axis=1,
            )
            if chain.vectors:
                vectors = total([array[at : at + VECTORS, :D] for array, at in chain.vectors])
                vectors = jnp.pad(vectors, ((0, 0), (0, message.shape[1] - D)))
                message = jnp.concatenate([message, vectors], axis=0)
            chain.message = message.astype(bf16)
        return
    operands, plans, outs = Operands(), [], []
    for chain in chains:
        chain.rows //= 2
        kept = chain.rows
        index_of = {}
        parts = []
        for width, terms in chain.parts:
            found = []
            for array, at in terms:
                if id(array) not in index_of:
                    index_of[id(array)] = operands.rows(array, kept, kept)
                index, skip = index_of[id(array)]
                found.append((index, at, skip))
            parts.append((width, found))
        vectors = [operands.rows(array, at, VECTORS) for array, at in chain.vectors]
        plans.append((kept, 0, parts, vectors))
        outs.append(chain.shape())
    messages = pl.pallas_call(
        functools.partial(combine_kernel, plans),
        grid=(1,),
        out_shape=[jax.ShapeDtypeStruct(shape, bf16) for shape in outs],
        in_specs=operands.specs,
        out_specs=[whole(shape) for shape in outs],
        compiler_params=params(COMBINE_BYTES),
        cost_estimate=cost(1_000_000_000, 8_000_000),
        name="combine",
    )(*operands.arrays)
    for chain, message in zip(chains, messages):
        chain.message = message


def launch(chains, value):
    arrived = [chain for chain in chains if chain.message is None]
    if arrived:
        latest = [chain.latest() for chain in arrived]
        value, gots = lax.optimization_barrier((value, latest))
        for chain, old, got in zip(arrived, latest, gots):
            chain.replace(old, got)
    steps = lax.axis_size("dp").bit_length() - 1
    chains = [chain for chain in chains if chain.step < steps]
    arrived = [chain for chain in chains if chain.message is None]
    if arrived:
        load(arrived)
    value, messages = lax.optimization_barrier((value, [chain.message for chain in chains]))
    for chain, message in zip(chains, messages):
        chain.message = message
        chain.send()
    return value


def finish(size, groups, chains):
    share = D // (size * groups)
    first, second = chains
    parts = list(first.parts) + list(second.parts)
    sums = (list(range(4)) + [4], list(range(4)), list(range(4)))
    up_rows = FF // D
    pieces = []
    for quad, (width, terms) in enumerate(parts):
        for index in range(4):
            pieces.append((index, quad * QUAD, QUAD, [(a, at + index * QUAD) for a, at in terms]))
        if width > 4 * QUAD:
            pieces.append((4, 0, D, [(a, at + 4 * QUAD) for a, at in terms]))
    if share % 8:
        blocks = {}
        for target, at, width, terms in pieces:
            blocks.setdefault(target, []).append(
                total([array[:share, c : c + width] for array, c in terms])
            )
        weights = [jnp.concatenate(blocks[target], axis=1) for target in range(5)]
        vectors = total([array[at : at + VECTORS, :D] for array, at in second.vectors])
        place = lax.axis_index("dp") * groups + lax.axis_index("tensor")
        mine = lax.dynamic_slice_in_dim(vectors, place * share, share, 1)
        ups = lax.dynamic_slice_in_dim(
            vectors[5 : 5 + up_rows].reshape(-1), place * up_rows * share, up_rows * share, 0
        )
        return weights, mine, ups
    operands = Operands()
    index_of = {}

    def operand(array):
        if id(array) not in index_of:
            index_of[id(array)] = operands.rows(array, 0, min(-(-share // 16) * 16, array.shape[0]))
        return index_of[id(array)][0]

    plan = [
        (target, at, width, [(operand(a), c) for a, c in terms])
        for target, at, width, terms in pieces
    ]
    vectors = [operands.rows(array, at, VECTORS) for array, at in second.vectors]
    outs = [(share, D)] * 5 + [(VECTORS, TILE)]
    *weights, vec = pl.pallas_call(
        functools.partial(
            finish_kernel, size, groups, len(operands.arrays), (plan, vectors), up_rows
        ),
        grid=(1,),
        out_shape=[jax.ShapeDtypeStruct(shape, f32) for shape in outs],
        in_specs=operands.specs,
        out_specs=[whole(shape) for shape in outs],
        compiler_params=params(COMBINE_BYTES),
        name="finish",
    )(*operands.arrays)
    return weights, vec[:, :share], vec[VECTORS - 1, : up_rows * share]


def body(
    content_in,
    query_in,
    memory,
    content_cot,
    query_cot,
    query_weight,
    key_weight,
    value_weight,
    out_weight,
    rel_weight,
    content_bias,
    position_bias,
    segment_bias,
    segment_embed,
    attn_gain,
    attn_shift,
    up_weight,
    up_bias,
    down_weight,
    down_bias,
    ffn_gain,
    ffn_shift,
    lengths,
    memory_lengths,
    segment_ids,
    orders,
    targets,
):
    groups = lax.axis_size("tensor")
    size = lax.axis_size("dp")
    steps = size.bit_length() - 1
    half = LEN // groups
    hidden_cols = up_weight.shape[1]
    up_other, down_other = swap(up_weight), swap(down_weight)
    content, query = content_in[0], query_in[0]
    segment_rows = segment_embed.T
    saved = attention_forward(
        half,
        size,
        groups,
        (lengths, memory_lengths, segment_ids, orders, targets),
        memory[0],
        content,
        query,
        (query_weight, key_weight, value_weight, rel_weight),
        (content_bias, position_bias, segment_bias),
        segment_rows,
    )
    (
        content_out,
        query_out,
        ffn_own,
        ffn_other,
        summed_grad,
        attended_grad,
        out_own,
        out_other,
        early_small,
        up_bias_part,
    ) = middle(
        half,
        size,
        groups,
        (
            saved[0],
            content,
            query,
            content_cot[0],
            query_cot[0],
            out_weight,
            up_weight,
            up_other,
            down_weight,
            down_other,
            up_bias,
            down_bias,
            attn_gain,
            attn_shift,
            ffn_gain,
            ffn_shift,
        ),
        hidden_cols,
    )
    ffn = Chain([(2 * hidden_cols, [(ffn_own, 0)])], D, -1)
    ffn.message = ffn_other
    proj, tok_keys, tok_vals, small, late = [], [], [], [], []
    active = [ffn]
    held = attended_grad
    modes = ("first", "middle", "last")
    extras = ((out_own, out_other), (), None)
    for at in range(QUADS):
        held = launch(active, held)
        extra = extras[at]
        if extra is None:
            extra = (early_small, up_bias_part, *small)
        own, other, proj_part, key_part, val_part, small_part, *vectors = attention_backward(
            half, groups, at, modes[at], saved, held, segment_rows, extra
        )
        proj.append(proj_part)
        tok_keys.append(key_part)
        tok_vals.append(val_part)
        small.append(small_part)
        chain = Chain(
            [(own.shape[1], [(own, 0)])], own.shape[0], -1, [(array, 0) for array in vectors]
        )
        chain.message = other
        late.append(chain)
        if at < QUADS - 1:
            held, proj[-1] = lax.optimization_barrier((held, proj[-1]))
            active.append(chain)
    proj[-1] = launch([ffn, late[0], late[2]], proj[-1])
    own_rows, query_grad, row_send = row_gradients(
        half, groups, summed_grad, proj, tok_keys, tok_vals, (query_weight, key_weight, value_weight)
    )
    pair = merged(late[1], late[2])
    active = [ffn, late[0], pair]
    row_send = launch(active, row_send)
    row_got = swap(row_send)
    content_grad = own_rows + row_got.astype(f32)
    while pair.step < steps:
        content_grad = launch(active, content_grad)
    ffn_sum = total([array[: ffn.rows] for array, _ in ffn.parts[0][1]])
    up_grad, down_grad_own = ffn_sum[:, :hidden_cols], ffn_sum[:, hidden_cols:].T
    weights, vectors, up_bias_grad = finish(size, groups, (late[0], pair))
    return (
        content_out[None],
        query_out[None],
        content_grad[None],
        query_grad[None],
        weights[0],
        weights[1],
        weights[2],
        weights[4],
        weights[3],
        vectors[9],
        vectors[10],
        vectors[11],
        vectors[12:14].T,
        vectors[3],
        vectors[4],
        up_grad,
        up_bias_grad,
        down_grad_own,
        vectors[2],
        vectors[0],
        vectors[1],
    )


def solution(mesh):
    in_specs = (
        P("dp", None, None),
        P("dp", "tensor", None),
        P("dp", None, None),
        P("dp", "tensor", None),
        P("dp", "tensor", None),
        P(),
        P(),
        P(),
        P(),
        P(),
        P(),
        P(),
        P(),
        P(),
        P(),
        P(),
        P(None, "tensor"),
        P(),
        P("tensor", None),
        P(),
        P(),
        P(),
        P("dp"),
        P("dp"),
        P("dp", None),
        P("dp", None),
        P("dp", None),
    )
    out_specs = (
        P("dp", "tensor", None),
        P("dp", "tensor", None),
        P("dp", "tensor", None),
        P("dp", "tensor", None),
        P(("dp", "tensor"), None),
        P(("dp", "tensor"), None),
        P(("dp", "tensor"), None),
        P(("dp", "tensor"), None),
        P(("dp", "tensor"), None),
        P(("dp", "tensor")),
        P(("dp", "tensor")),
        P(("dp", "tensor")),
        P(("dp", "tensor"), None),
        P(("dp", "tensor")),
        P(("dp", "tensor")),
        P("dp", "tensor"),
        P(("dp", "tensor")),
        P("tensor", "dp"),
        P(("dp", "tensor")),
        P(("dp", "tensor")),
        P(("dp", "tensor")),
    )
    return jax.shard_map(body, mesh=mesh, in_specs=in_specs, out_specs=out_specs, check_vma=False)
```

```python
import functools

import jax
import jax.numpy as jnp
from jax import lax
from jax.experimental import pallas as pl
from jax.experimental.pallas import tpu as pltpu
from jax.sharding import PartitionSpec as P

D = 768
HEADS = 12
HEAD_DIM = 64
FF = 3072
LEN = 512
MEM = 384
KEYS = MEM + LEN
QUAD = 4 * HEAD_DIM
QUADS = D // QUAD
PAIR = 2 * HEAD_DIM
SCALE = HEAD_DIM ** (-0.5)
VMEM_BYTES = 61 * 1024 * 1024
COMBINE_BYTES = 58 * 1024 * 1024
BLOCK = 32
TILE = 128
WIDE = 256
VECTORS = 16

VECTOR_ROWS = VECTORS * D // TILE

f32 = jnp.float32
bf16 = jnp.bfloat16
precise = lax.Precision.HIGHEST


def mm(left, right):
    return lax.dot_general(left, right, (((1,), (0,)), ((), ())), preferred_element_type=f32)


def mm_nt(left, right):
    return lax.dot_general(left, right, (((1,), (1,)), ((), ())), preferred_element_type=f32)


def lanes(shape):
    return lax.broadcasted_iota(jnp.int32, shape, 1)


def column_of(row):
    return jnp.broadcast_to(row.astype(f32), (128, row.shape[1])).T


def lane_tiles(value, combine):
    tiles = [value[:, at : at + TILE] for at in range(0, value.shape[1], TILE)]
    return functools.reduce(combine, tiles)


def interleave(steps, tasks):
    done = 0
    for index, step in enumerate(steps):
        step()
        while done * len(steps) < (index + 1) * len(tasks) and done < len(tasks):
            tasks[done]()
            done += 1
    for task in tasks[done:]:
        task()


def order_of(core, bits):
    plain = list(range(bits))
    return plain[1:2] + plain[:1] + plain[2:] if core == 1 and bits > 1 else plain


def block_owner(place, core, bits):
    owner = jnp.zeros_like(place)
    for step in range(bits):
        owner = owner | (((place >> (bits - 1 - step)) & 1) << step)
    if bits > 1:
        swapped = (owner & ~3) | ((owner & 1) << 1) | ((owner >> 1) & 1)
        owner = jnp.where(core == 1, swapped, owner)
    return owner ^ lax.axis_index("dp")


def one_hot(source):
    return jnp.where(lanes((source.shape[0], D)) == source, 1.0, 0.0).astype(bf16)


def owner_rows(size, groups):
    share = D // (size * groups)
    row = lax.broadcasted_iota(jnp.int32, (D, 1), 0)
    side, rest = lax.div(row, size * share), lax.rem(row, size * share)
    core = lax.rem(lax.axis_index("tensor") + side, groups)
    owner = block_owner(lax.div(rest, share), core, size.bit_length() - 1)
    return one_hot((owner * groups + core) * share + lax.rem(rest, share))


def shared_rows(size, core):
    share = D // size
    row = lax.broadcasted_iota(jnp.int32, (D, 1), 0)
    owner = block_owner(lax.div(row, share), core, size.bit_length() - 1)
    return one_hot(owner * share + lax.rem(row, share))


def forward_kernel(
    half,
    size,
    groups,
    length_ref,
    mem_length_ref,
    seg_ref,
    ord_ref,
    tgt_ref,
    memory_ref,
    content_ref,
    query_ref,
    wq_ref,
    wk_ref,
    wv_ref,
    wr_ref,
    cb_ref,
    pb_ref,
    sb_ref,
    se_ref,
    att_ref,
    prob_ref,
    key_ref,
    val_ref,
    rel_ref,
    hc_ref,
    hp_ref,
    hs_ref,
    linv_ref,
    kaug_ref,
    scol_ref,
    both_t_ref,
    stack_t_ref,
    pos_t_ref,
    stack,
    both,
    pos,
    bias,
    fine,
    coarse,
    vectors,
    scores,
    places,
    kaug_t,
):
    window = KEYS + half
    first = pl.multiple_of(lax.axis_index("tensor") * half, half)
    step_id = pl.program_id(0)

    @pl.when(step_id == 0)
    def _():
        stack[:MEM, :] = memory_ref[...]
        stack[MEM:, :] = content_ref[...]
        both[:half, :] = content_ref[pl.ds(first, half), :]
        both[half:, :] = query_ref[...]
        vectors[0:1, :] = cb_ref[...][None, :]
        vectors[1:2, :] = pb_ref[...][None, :]
        vectors[2:3, :] = sb_ref[...][None, :]
        step = lax.broadcasted_iota(jnp.int32, (1, D // 2), 1).astype(f32) * (2.0 / D)
        inverse = 1.0 / jnp.power(jnp.full((1, D // 2), 10000.0, f32), step)
        coarse_rows = coarse.shape[1]
        top = (MEM + half + first).astype(f32)
        angle = (
            top - 32.0 * lax.broadcasted_iota(jnp.int32, (coarse_rows, 1), 0).astype(f32)
        ) * inverse
        coarse[0] = jnp.sin(angle)
        coarse[1] = jnp.cos(angle)
        small = lax.broadcasted_iota(jnp.int32, (32, 1), 0).astype(f32) * inverse
        fine[0] = jnp.sin(small)
        fine[1] = jnp.cos(small)
        for a in range(window // 32):
            sa, ca = coarse[0, a : a + 1, :], coarse[1, a : a + 1, :]
            sb, cb = fine[0], fine[1]
            pos[a * 32 : (a + 1) * 32, : D // 2] = (sa * cb - ca * sb).astype(bf16)
            pos[a * 32 : (a + 1) * 32, D // 2 :] = (ca * cb + sa * sb).astype(bf16)
        never = float(LEN + 1)
        mem_at = lax.broadcasted_iota(jnp.int32, (1, MEM), 1)
        tok_at = lax.broadcasted_iota(jnp.int32, (1, LEN), 1)
        open_from = jnp.concatenate(
            [
                jnp.where(mem_at >= MEM - mem_length_ref[0], -1.0, never),
                jnp.where(
                    tok_at < length_ref[0],
                    jnp.where(tgt_ref[...] == 0, -1.0, ord_ref[...].astype(f32)),
                    never,
                ),
            ],
            axis=1,
        )
        order_col = column_of(ord_ref[...])
        seg_col = column_of(seg_ref[...])
        kaug_lane = lanes((LEN, PAIR)) % HEAD_DIM
        kaug_ref[:MEM, :] = (lanes((MEM, PAIR)) % HEAD_DIM < 4).astype(f32).astype(bf16)
        kaug_ref[MEM:, :] = jnp.where(
            kaug_lane < 4, 1.0, jnp.where(kaug_lane < 6, seg_col, 0.0)
        ).astype(bf16)
        kaug_t[...] = kaug_ref[...].T[:HEAD_DIM]
        bias[:LEN, :PAIR] = order_col
        own_order = bias[pl.ds(first, half), :PAIR][:, :1]
        bias[:LEN, :PAIR] = seg_col
        scol_ref[...] = bias[pl.ds(first, half), :PAIR]
        seen = open_from <= own_order
        bias[:half, :] = jnp.where(seen, 0.0, -1e30)
        key_at = lax.broadcasted_iota(jnp.int32, (half, KEYS), 1)
        row_at = lax.broadcasted_iota(jnp.int32, (half, KEYS), 0)
        seen_q = seen & (key_at - MEM != row_at + first)
        bias[half:, :] = jnp.where(seen_q, 0.0, -1e30)
        chosen = owner_rows(size, groups)
        both_t_ref[...] = mm_nt(chosen, both[...]).astype(bf16)
        stack_t_ref[...] = mm_nt(chosen, stack[...]).astype(bf16)
        pos_t_ref[...] = mm_nt(chosen, pos[...]).astype(bf16)

    here = pl.ds(pl.multiple_of(step_id * QUAD, QUAD), QUAD)
    keys = mm(stack[...], wk_ref[...]).astype(bf16)
    values = mm(stack[...], wv_ref[...]).astype(bf16)
    rel = mm(pos[...], wr_ref[...]).astype(bf16)
    projection = mm(both[...], wq_ref[...])
    head_content = (projection + vectors[0:1, here]).astype(bf16)
    head_position = (projection + vectors[1:2, here]).astype(bf16)
    head_segment = projection + vectors[2:3, here]
    key_ref[...] = keys
    val_ref[...] = values
    rel_ref[...] = rel
    hs_ref[...] = head_segment
    head_content = (head_content.astype(f32) * SCALE).astype(bf16)
    head_position = (head_position.astype(f32) * SCALE).astype(bf16)
    hc_ref[...] = head_content
    hp_ref[...] = head_position
    same = column_of(se_ref[0:1, :])
    differ = column_of(se_ref[1:2, :] - se_ref[0:1, :])
    same = jnp.concatenate([same, same], axis=1)
    differ = jnp.concatenate([differ, differ], axis=1)
    row_head = lax.broadcasted_iota(jnp.int32, (QUAD, QUAD), 0) // HEAD_DIM
    at = lanes((QUAD, QUAD)) - ((row_head // 2) * PAIR + (1 - row_head % 2) * HEAD_DIM)
    embed = jnp.where(
        (at >= 0) & (at < 2), same, jnp.where((at >= 2) & (at < 6), differ, 0.0)
    )
    embed_high = embed.astype(bf16)
    embed_low = (embed - embed_high.astype(f32)).astype(bf16)
    segment_high = head_segment.astype(bf16)
    segment_low = (head_segment - segment_high.astype(f32)).astype(bf16)
    terms = (
        mm(segment_high, embed_high) + mm(segment_high, embed_low) + mm(segment_low, embed_high)
    )
    scol = scol_ref[...]
    scol = jnp.concatenate([scol, scol], axis=0)
    scol = jnp.concatenate([scol, scol], axis=1)
    lane6 = lanes((2 * half, QUAD)) % HEAD_DIM
    factor = jnp.where(lane6 < 2, 1.0, jnp.where(lane6 < 4, scol, 1.0 - 2.0 * scol))
    terms = SCALE * (terms * factor)
    high = terms.astype(bf16)
    low = (terms - high.astype(f32)).astype(bf16)
    qaug = jnp.where(lane6 % 2 == 0, high, low)
    keys_t, rel_t = keys.T, rel.T
    units = [(pair, head, part) for pair in range(2) for head in range(2) for part in range(2)]
    key_x = []
    for which in range(4):
        own = keys_t[which * HEAD_DIM : (which + 1) * HEAD_DIM]
        sides = [own, kaug_t[...]] if which % 2 == 0 else [kaug_t[...], own]
        key_x.append(jnp.concatenate(sides, axis=0))
    peaks, totals, outs = {}, {}, {}

    def products(index):
        pair, head, part = units[index]
        cols, rows = slice(pair * PAIR, (pair + 1) * PAIR), slice(part * half, (part + 1) * half)
        slot, which = index % 2, pair * 2 + head
        row_mine = (lanes((half, PAIR)) < HEAD_DIM) == (head == 0)
        query_x = jnp.where(row_mine, head_content[rows, cols], qaug[rows, cols])
        place_x = jnp.where(row_mine, head_position[rows, cols], jnp.zeros((), bf16))

        def score(n, stop):
            scores[slot, :, n:stop] = mm(query_x, key_x[which][:, n:stop])

        def placed(n, stop):
            places[slot, :, n:stop] = mm(place_x, rel_t[cols, n:stop])

        return [functools.partial(placed, n, min(n + WIDE, window)) for n in range(0, window, WIDE)] + [
            functools.partial(score, n, min(n + WIDE, KEYS)) for n in range(0, KEYS, WIDE)
        ]

    def softmax(index):
        pair, head, part = units[index]
        slot, which = index % 2, pair * 2 + head
        tops, pieces = [], []

        def join(b):
            block = slice(b, b + BLOCK)
            shifted = pltpu.roll(
                places[slot, block, :], (KEYS + b) % window, 1, stride=1, stride_axis=0
            )[:, :KEYS]
            score = (
                scores[slot, block, :]
                + shifted
                + bias[part * half + b : part * half + b + BLOCK, :]
            )
            scores[slot, block, :] = score
            tops.append(lane_tiles(score, jnp.maximum))

        def peak():
            peaks[index] = jnp.max(jnp.concatenate(tops, axis=0), axis=1, keepdims=True)

        def power(b):
            block = slice(b, b + BLOCK)
            prob = jnp.exp(scores[slot, block, :] - peaks[index][block])
            pieces.append(lane_tiles(prob, jnp.add))
            prob_ref[which, part * half + b : part * half + b + BLOCK, :] = prob.astype(bf16)

        def finish():
            totals[index] = 1.0 / jnp.sum(
                jnp.concatenate(pieces, axis=0), axis=1, keepdims=True
            )

        blocks = range(0, half, BLOCK)
        return (
            [functools.partial(join, b) for b in blocks]
            + [peak]
            + [functools.partial(power, b) for b in blocks]
            + [finish]
        )

    def mixture(index):
        pair, head, part = units[index]
        cols, rows = slice(pair * PAIR, (pair + 1) * PAIR), slice(part * half, (part + 1) * half)
        outs[index] = mm(prob_ref[pair * 2 + head, rows, :], values[:, cols]) * totals[index]

    interleave([], products(0))
    for index in range(len(units)):
        tasks = products(index + 1) if index + 1 < len(units) else []
        if index:
            tasks.append(functools.partial(mixture, index - 1))
        interleave(softmax(index), tasks)
    mixture(len(units) - 1)
    for pair in range(2):
        cols = slice(pair * PAIR, (pair + 1) * PAIR)
        mixtures = [
            jnp.concatenate([outs[pair * 4 + head * 2], outs[pair * 4 + head * 2 + 1]], axis=0)
            for head in range(2)
        ]
        mine = lanes((2 * half, PAIR)) < HEAD_DIM
        att_ref[:, cols] = jnp.where(mine, mixtures[0], mixtures[1])
    sums = [
        jnp.concatenate([totals[2 * which], totals[2 * which + 1]], axis=0) for which in range(4)
    ]
    lane = lanes((2 * half, TILE))
    linv_ref[...] = jnp.where(
        lane == 0, sums[0], jnp.where(lane == 1, sums[1], jnp.where(lane == 2, sums[2], sums[3]))
    )


def norm_forward(summed, gain, shift):
    center = summed - jnp.mean(summed, axis=1, keepdims=True)
    inv = lax.rsqrt(jnp.mean(center * center, axis=1, keepdims=True) + 1e-06)
    unit = center * inv
    return unit, inv, unit * gain + shift


def norm_backward(grad, unit, inv, gain):
    scaled = grad * gain
    return inv * (
        scaled
        - jnp.mean(scaled, axis=1, keepdims=True)
        - unit * jnp.mean(scaled * unit, axis=1, keepdims=True)
    )


def row_sum(value):
    return jnp.sum(value, axis=0, keepdims=True)


def gelu_parts(x):
    square = x * x
    tanh = jnp.tanh((0.7978845608028654 * x) * (1.0 + 0.044715 * square))
    rise = 0.5 * (1.0 + tanh)
    grad = rise + (0.5 * x) * (1.0 - tanh * tanh) * (
        0.7978845608028654 * (1.0 + 0.134145 * square)
    )
    return x * rise, grad


def fold_rows(value):
    return functools.reduce(jnp.add, [value[r : r + 8] for r in range(0, value.shape[0], 8)])


def middle_kernel(
    half,
    size,
    groups,
    chunk,
    att_ref,
    content_ref,
    query_ref,
    ccot_ref,
    qcot_ref,
    wo_ref,
    up_own_hbm,
    up_oth_hbm,
    down_own_hbm,
    down_oth_hbm,
    ubias_ref,
    dbias_ref,
    again_ref,
    ashift_ref,
    fgain_ref,
    fshift_ref,
    cout_ref,
    qout_ref,
    ffn_hbm,
    hid_hbm,
    pre_hbm,
    low_t_ref,
    down_t_ref,
    sgrad_ref,
    agrad_ref,
    out_own_ref,
    out_oth_ref,
    small_ref,
    ubg_ref,
    hidden,
    slope,
    ffn,
    pre,
    work,
    unit,
    low,
    down_grad,
    vectors,
    up,
    down,
    sems,
    out_sems,
):
    count = 2 * half
    member = lax.axis_index("tensor")
    first = pl.multiple_of(member * half, half)
    fetches = [
        pltpu.make_async_copy(source, target.at[side], sems.at[kind, side])
        for kind, side, source, target in (
            (0, 0, up_own_hbm, up),
            (1, 0, down_own_hbm, down),
            (0, 1, up_oth_hbm, up),
            (1, 1, down_oth_hbm, down),
        )
    ]
    for fetch in fetches:
        fetch.start()
    ups, downs = (up.at[0], up.at[1]), (down.at[0], down.at[1])
    part_cols = up.shape[2]
    chunks = part_cols // chunk
    vectors[0:1, :] = ubias_ref[...][None, :]
    attended = att_ref[...].astype(bf16)
    work[...] = mm(attended, wo_ref[...])
    attn_gain, attn_shift = again_ref[...][None, :], ashift_ref[...][None, :]
    ffn_gain, ffn_shift = fgain_ref[...][None, :], fshift_ref[...][None, :]
    down_bias = dbias_ref[...][None, :]
    inverse = []
    for b in range(0, count, BLOCK):
        block = slice(b, b + BLOCK)
        if b < half:
            rows_in = content_ref[pl.ds(pl.multiple_of(first + b, BLOCK), BLOCK), :]
        else:
            rows_in = query_ref[b - half : b - half + BLOCK, :]
        found, inv, normed = norm_forward(
            work[block, :] + rows_in.astype(f32), attn_gain, attn_shift
        )
        unit[block, :] = found
        inverse.append(inv)
        low[block, :] = normed.astype(bf16)
        work[block, :] = normed + down_bias
    for fetch in fetches:
        fetch.wait()
    pieces = [(side, at) for side in range(2) for at in range(chunks)]

    def rise(index):
        side, at = pieces[index]

        def task(n):
            pre[index % 2, :, n : n + WIDE] = mm(
                low[...], ups[side][:, at * chunk + n : at * chunk + n + WIDE]
            )

        return [functools.partial(task, n) for n in range(0, chunk, WIDE)]

    def bend(index):
        side, at = pieces[index]
        cols = slice(at * chunk, (at + 1) * chunk)
        start = lax.rem(member + side, 2) * part_cols + at * chunk
        bias = vectors[0:1, pl.ds(pl.multiple_of(start, TILE), chunk)]

        def step(b):
            block = slice(b, b + BLOCK)
            act, grad = gelu_parts(pre[index % 2, block, :] + bias)
            hidden[side, block, cols] = act.astype(bf16)
            slope[side, block, cols] = grad.astype(bf16)

        return [functools.partial(step, b) for b in range(0, count, BLOCK)]

    def fall(index):
        side, at = pieces[index]
        cols = slice(at * chunk, (at + 1) * chunk)

        def task(n):
            work[:, n : n + WIDE] += mm(hidden[side, :, cols], downs[side][cols, n : n + WIDE])

        return [functools.partial(task, n) for n in range(0, D, WIDE)]

    interleave([], rise(0))
    for index in range(len(pieces)):
        tasks = rise(index + 1) if index + 1 < len(pieces) else []
        if index:
            tasks += fall(index - 1)
        interleave(bend(index), tasks)
    interleave([], fall(len(pieces) - 1))
    stores = [
        pltpu.make_async_copy(source, target, out_sems.at[index])
        for index, (source, target) in enumerate(
            (
                (hidden.at[0], hid_hbm),
                (slope.at[0], pre_hbm),
                (ffn.at[:, :part_cols], ffn_hbm.at[:, :part_cols]),
                (ffn.at[:, part_cols:], ffn_hbm.at[:, part_cols:]),
            )
        )
    ]
    stores[0].start()
    sums = [jnp.zeros((8, D), f32) for _ in range(5)]
    for b in range(0, count, BLOCK):
        block = slice(b, b + BLOCK)
        found, inv, out = norm_forward(work[block, :], ffn_gain, ffn_shift)
        if b < half:
            cout_ref[block, :] = out.astype(bf16)
            cot = ccot_ref[block, :].astype(f32)
        else:
            block_q = slice(b - half, b - half + BLOCK)
            qout_ref[block_q, :] = out.astype(bf16)
            cot = qcot_ref[block_q, :].astype(f32)
        residual_grad = norm_backward(cot, found, inv, ffn_gain)
        rounded = residual_grad.astype(bf16)
        down_grad[block, :] = rounded
        work[block, :] = residual_grad
        for index, value in enumerate((cot * found, cot, rounded.astype(f32))):
            sums[index] = sums[index] + fold_rows(value)
    chosen = shared_rows(size, member)
    low_t_ref[...] = mm_nt(chosen, low[...]).astype(bf16)
    down_t_ref[...] = mm_nt(chosen, down_grad[...]).astype(bf16)
    for side in range(2):
        for at in range(chunks):
            cols = slice(at * chunk, (at + 1) * chunk)
            hidden_grad = mm_nt(down_grad[...], downs[side][cols, :])
            pre_grad = (hidden_grad * slope[side, :, cols].astype(f32)).astype(bf16)
            slope[side, :, cols] = pre_grad
            ubg_ref[side : side + 1, cols] = row_sum(pre_grad.astype(f32))
            work[...] += mm_nt(pre_grad, ups[side][:, cols])

    def settle(b):
        block = slice(b, b + BLOCK)
        grad, found = work[block, :], unit[block, :]
        summed_grad = norm_backward(grad, found, inverse[b // BLOCK], attn_gain)
        sgrad_ref[block, :] = summed_grad
        down_grad[block, :] = summed_grad.astype(bf16)
        sums[3] = sums[3] + fold_rows(grad * found)
        sums[4] = sums[4] + fold_rows(grad)

    quarter = D // 4

    def weigh(kind, n):
        left, right = ((low_t_ref, slope), (down_t_ref, hidden))[kind]
        value = mm(left[...], right[1, :, n : n + WIDE]).astype(bf16)
        cols = slice(kind * part_cols + n, kind * part_cols + n + WIDE)
        places = (0, 2, 1, 3) if size > 2 else (0, 1, 2, 3)
        for q, place in enumerate(places):
            ffn[place * quarter : (place + 1) * quarter, cols] = value[
                q * quarter : (q + 1) * quarter
            ]

    stores[1].start()
    tasks = [
        functools.partial(weigh, kind, n)
        for kind in range(2)
        for n in range(0, part_cols, WIDE)
    ]
    tasks.insert(len(tasks) // 2, stores[2].start)
    interleave([functools.partial(settle, b) for b in range(0, count, BLOCK)], tasks)
    stores[3].start()
    for index, value in enumerate(sums):
        small_ref[index : index + 1, :] = row_sum(value)
    small_ref[5:8, :] = jnp.zeros((3, D), f32)
    agrad_ref[...] = mm_nt(down_grad[...], wo_ref[...]).astype(bf16)
    attended_t = mm_nt(owner_rows(size, groups), attended).astype(bf16)
    out_part = mm(attended_t, down_grad[...]).astype(bf16)
    share = D // groups
    out_own_ref[...] = out_part[:share]
    out_oth_ref[...] = out_part[share : 2 * share]
    for store in stores:
        store.wait()


def weights_kernel(steps, low_t_ref, down_t_ref, pre_ref, hid_ref, out_ref):
    @pl.when(pl.program_id(0) < steps)
    def _():
        out_ref[...] = mm(low_t_ref[...], pre_ref[...]).astype(bf16)

    @pl.when(pl.program_id(0) >= steps)
    def _():
        out_ref[...] = mm(down_t_ref[...], hid_ref[...]).astype(bf16)


def unshift(value, shift, window):
    whole, rest = shift // TILE, shift % TILE
    row = lax.broadcasted_iota(jnp.int32, (BLOCK, TILE), 0)
    lane = lanes((BLOCK, TILE))
    index = (lane + row - rest) & (TILE - 1)
    tiles = [
        jnp.take_along_axis(
            value[:, n : n + TILE], index, axis=1, mode="promise_in_bounds"
        )
        for n in range(0, value.shape[1], TILE)
    ]
    zero = jnp.zeros((BLOCK, TILE), f32)

    def tile(n):
        return tiles[n] if 0 <= n < len(tiles) else zero

    if rest:
        here = lane >= rest - row
        found = [
            jnp.where(here, tile(n - whole), tile(n - whole - 1)) for n in range(window // TILE)
        ]
    else:
        here = lane + row < TILE
        found = [
            jnp.where(here, tile(n - whole), tile(n - whole + 1)) for n in range(window // TILE)
        ]
    return jnp.concatenate(found, axis=1)


def backward_kernel(
    half,
    groups,
    at,
    mode,
    prob_hbm,
    key_ref,
    val_ref,
    rel_ref,
    hc_ref,
    hp_ref,
    hs_ref,
    linv_ref,
    kaug_ref,
    scol_ref,
    att_ref,
    agrad_ref,
    se_ref,
    both_t_hbm,
    stack_t_hbm,
    pos_t_hbm,
    *rest,
):
    more = rest[: {"first": 2, "middle": 0, "last": 4}[mode]]
    own_ref, oth_ref, proj_ref, tok_key_ref, tok_val_ref, small_ref = rest[len(more) :][:6]
    prob, both_t, stack_t, pos_t, spread, grads, turned, sems = rest[-8:]
    count, window = 2 * half, KEYS + half
    heads = 4
    prob_copies = [
        pltpu.make_async_copy(prob_hbm.at[at * heads + h], prob.at[h], sems.at[h])
        for h in range(heads)
    ]
    fetches = [
        pltpu.make_async_copy(source, target, sems.at[heads + index])
        for index, (source, target) in enumerate(
            ((both_t_hbm, both_t), (stack_t_hbm, stack_t), (pos_t_hbm, pos_t))
        )
    ]
    for copy in prob_copies + fetches:
        copy.start()
    share = D // groups
    if mode == "first":
        own_ref[:, 4 * QUAD :] = more[0][...]
        oth_ref[:, 4 * QUAD :] = more[1][...]
    kaug = kaug_ref[...]
    scol = scol_ref[...]
    scol = jnp.concatenate([scol, scol], axis=0)
    swing = 1.0 - 2.0 * scol
    key_t, val_t, rel_t = [], [], []
    proj_grads = []
    hp_t = hp_ref[...].T
    hc_t = hc_ref[...].T
    lane = lanes((count, PAIR))
    agrads, grad_x, agrad_t = [], [], []
    for pair in range(2):
        cols = slice(pair * PAIR, (pair + 1) * PAIR)
        linv = jnp.where(
            lane < HEAD_DIM,
            linv_ref[:, 2 * pair : 2 * pair + 1],
            linv_ref[:, 2 * pair + 1 : 2 * pair + 2],
        )
        agrad = (agrad_ref[:, cols].astype(f32) * linv).astype(bf16).astype(f32)
        products = agrad * att_ref[:, cols]
        agrad_t.append(agrad.astype(bf16).T)
        for head in range(2):
            base = (1 - head) * HEAD_DIM
            mine = (lane < HEAD_DIM) == (head == 0)
            weight = jnp.sum(jnp.where(mine, products, 0.0), axis=1, keepdims=True)
            high = weight.astype(bf16).astype(f32)
            grad_x.append(
                jnp.where(
                    mine,
                    agrad,
                    jnp.where(
                        lane == base, -high, jnp.where(lane == base + 1, high - weight, 0.0)
                    ),
                ).astype(bf16)
            )
    key_mine = lanes((KEYS, PAIR)) < HEAD_DIM
    found = {}

    def columns_of(which):
        return slice(which // 2 * PAIR, (which // 2 + 1) * PAIR)

    def extended(ref, which):
        return jnp.where(key_mine == (which % 2 == 0), ref[:, columns_of(which)], kaug)

    values_t, kaug_t = val_ref[...].T, kaug.T[:HEAD_DIM]

    def spreads(which):
        own = values_t[which * HEAD_DIM : (which + 1) * HEAD_DIM]
        val_x = jnp.concatenate([own, kaug_t] if which % 2 == 0 else [kaug_t, own], axis=0)
        prob_copies[which].wait()

        def task(n, stop):
            spread[which % 2, :, n:stop] = mm(grad_x[which], val_x[:, n:stop])

        return [functools.partial(task, n, min(n + WIDE, KEYS)) for n in range(0, KEYS, WIDE)]

    def score_grads(which):
        buffer = which % 2

        def step(part, b):
            at_row = part * half + b
            block = slice(at_row, at_row + BLOCK)
            score_grad = prob[which, block, :].astype(f32) * spread[buffer, block, :]
            grads[buffer, block, :] = score_grad.astype(bf16)
            turned[buffer, block, :] = unshift(score_grad, half - b, window).astype(bf16)

        return [
            functools.partial(step, part, b) for part in range(2) for b in range(0, half, BLOCK)
        ]

    def gathers(which):
        buffer = which % 2
        head_rows = slice(which * HEAD_DIM, (which + 1) * HEAD_DIM)
        side = slice(which % 2 * HEAD_DIM, (which % 2 + 1) * HEAD_DIM)
        key_x = extended(key_ref, which)
        found[which] = {"value": [], "key": [], "rel": [], "content": [], "place": []}

        def down_rows(name, left, ref, n, stop):
            found[which][name].append(mm(left, ref[:, n:stop]))

        tasks = []
        for name, left, ref, end in (
            ("value", agrad_t[which // 2][side], prob.at[which], KEYS),
            ("key", hc_t[head_rows], grads.at[buffer], KEYS),
            ("rel", hp_t[head_rows], turned.at[buffer], window),
        ):
            tasks += [
                functools.partial(down_rows, name, left, ref, n, min(n + WIDE, end))
                for n in range(0, end, WIDE)
            ]

        def content(n):
            found[which]["content"].append(mm(grads[buffer, n : n + half, :], key_x))

        def placed(n):
            found[which]["place"].append(
                mm(turned[buffer, n : n + half, :], rel_ref[:, columns_of(which)])
            )

        for n in (0, half):
            tasks += [functools.partial(content, n), functools.partial(placed, n)]
        return tasks

    interleave([], spreads(0))
    for which in range(heads):
        tasks = spreads(which + 1) if which + 1 < heads else []
        if which:
            tasks += gathers(which - 1)
        interleave(score_grads(which), tasks)
    interleave([], gathers(heads - 1))
    for which in range(heads):
        val_t.append(jnp.concatenate(found[which]["value"], axis=1))
        key_t.append(jnp.concatenate(found[which]["key"], axis=1))
        rel_t.append(jnp.concatenate(found[which]["rel"], axis=1))
    for pair in range(2):
        cols = slice(pair * PAIR, (pair + 1) * PAIR)
        content_heads, place_heads, term_same, term_other = [], [], [], []
        for head in range(2):
            base = (1 - head) * HEAD_DIM
            content_head = jnp.concatenate(found[pair * 2 + head]["content"], axis=0)
            content_heads.append(content_head)
            place_heads.append(jnp.concatenate(found[pair * 2 + head]["place"], axis=0))
            total = content_head[:, base : base + 1]
            marked = content_head[:, base + 4 : base + 5]
            differ = SCALE * (scol * total + swing * marked)
            term_other.append(differ)
            term_same.append(SCALE * total - differ)
        first_head = lane < HEAD_DIM
        content_grad = (SCALE * jnp.where(first_head, *content_heads)).astype(bf16).astype(f32)
        place_grad = (SCALE * jnp.where(first_head, *place_heads)).astype(bf16).astype(f32)
        same = jnp.where(first_head, *term_same)
        other = jnp.where(first_head, *term_other)
        segment_grad = same * se_ref[0:1, cols] + other * se_ref[1:2, cols]
        proj_grads.append((content_grad + place_grad + segment_grad).astype(bf16))
        small_ref[0:1, cols] = row_sum(content_grad)
        small_ref[1:2, cols] = row_sum(place_grad)
        small_ref[2:3, cols] = row_sum(segment_grad)
        head_segment = hs_ref[:, cols]
        small_ref[3:4, cols] = row_sum(same * head_segment)
        small_ref[4:5, cols] = row_sum(other * head_segment)
    small_ref[5:8, :] = jnp.zeros((3, QUAD), f32)
    proj_grad = jnp.concatenate(proj_grads, axis=1)
    key_t = jnp.concatenate(key_t, axis=0).astype(bf16)
    val_t = jnp.concatenate(val_t, axis=0).astype(bf16)
    rel_t = jnp.concatenate(rel_t, axis=0).astype(bf16)
    proj_ref[...] = proj_grad
    tok_key_ref[...] = key_t[:, MEM:].T
    tok_val_ref[...] = val_t[:, MEM:].T
    for fetch in fetches:
        fetch.wait()
    parts = (
        mm(both_t[...], proj_grad),
        mm_nt(stack_t[...], key_t),
        mm_nt(stack_t[...], val_t),
        mm_nt(pos_t[...], rel_t),
    )
    for index, value in enumerate(parts):
        cols = slice(index * QUAD, (index + 1) * QUAD)
        own_ref[:, cols] = value[:share].astype(bf16)
        oth_ref[:, cols] = value[share : 2 * share].astype(bf16)
    if mode == "last":
        vec_ref = rest[len(more) + 6]
        early, ubias, before, between = more
        core = lax.axis_index("tensor")
        rows = [early[0:5, :]]
        mine = [ubias[0:1, n : n + D] for n in range(0, ubias.shape[1], D)]
        theirs = [ubias[1:2, n : n + D] for n in range(0, ubias.shape[1], D)]
        for left, right in ((mine, theirs), (theirs, mine)):
            rows += [jnp.where(core == 0, a, b) for a, b in zip(left, right)]
        rows.append(
            jnp.concatenate([before[0:5, :], between[0:5, :], small_ref[0:5, :]], axis=1)
        )
        rows = jnp.concatenate(rows, axis=0)
        spare = jnp.zeros((VECTORS - rows.shape[0], D), f32)
        rows = jnp.concatenate([rows, spare], axis=0)
        packed = jnp.concatenate([rows[:, n : n + TILE] for n in range(0, D, TILE)], axis=0)
        vec_ref[...] = packed
        oth_ref[:VECTOR_ROWS, 4 * QUAD :] = packed.astype(bf16)
        oth_ref[VECTOR_ROWS:, 4 * QUAD :] = jnp.zeros((share - VECTOR_ROWS, TILE), bf16)


def rows_kernel(half, groups, sgrad_ref, *rest):
    proj, keys, vals = rest[:QUADS], rest[QUADS : 2 * QUADS], rest[2 * QUADS : 3 * QUADS]
    wq_ref, wk_ref, wv_ref, own_ref, query_ref, send_ref, both = rest[3 * QUADS :]
    member = lax.axis_index("tensor")
    wide = [jnp.concatenate([ref[...] for ref in refs], axis=1) for refs in (proj, keys, vals)]
    both[...] = mm_nt(wide[1], wk_ref[...]) + mm_nt(wide[2], wv_ref[...])
    rows = sgrad_ref[...] + mm_nt(wide[0], wq_ref[...])
    own = pl.multiple_of(member * half, half)
    other = pl.multiple_of(lax.rem(member + 1, groups) * half, half)
    send_ref[...] = both[pl.ds(other, half), :].astype(bf16)
    own_ref[...] = rows[:half] + both[pl.ds(own, half), :]
    query_ref[...] = rows[half:]


def summed(operands, terms, rows, width):
    return functools.reduce(
        jnp.add,
        [
            operands[index][...].astype(f32)[skip : skip + rows, at : at + width]
            for index, at, skip in terms
        ],
    )


def vector_width(rows):
    return TILE * max(1, VECTOR_ROWS // rows)


def fold_vectors(packed, rows):
    if rows > VECTOR_ROWS:
        return jnp.concatenate([packed, jnp.zeros((rows - VECTOR_ROWS, TILE), f32)], axis=0)
    return jnp.concatenate(
        [packed[n : n + rows] for n in range(0, VECTOR_ROWS, rows)], axis=1
    )


def unfold_vectors(block, rows):
    if rows >= VECTOR_ROWS:
        return block[:VECTOR_ROWS]
    return jnp.concatenate(
        [block[:, n : n + TILE] for n in range(0, vector_width(rows), TILE)], axis=0
    )


def summed_vectors(values, terms):
    return functools.reduce(
        jnp.add,
        [
            unfold_vectors(
                values(index)[:rows, at : at + vector_width(rows)].astype(f32), rows
            )
            for index, at, rows in terms
        ],
    )


def combine_kernel(plans, *refs):
    operands, outs = refs[: -len(plans)], refs[-len(plans) :]
    for (rows, parts, vectors), out_ref in zip(plans, outs):
        column = 0
        for width, terms in parts:
            value = summed(operands, terms, rows, width)
            out_ref[:, column : column + width] = value.astype(out_ref.dtype)
            column += width
        if vectors:
            packed = summed_vectors(lambda index: operands[index][...].astype(f32), vectors)
            out_ref[:, column:] = fold_vectors(packed, rows).astype(out_ref.dtype)


def unpack_vectors(packed):
    return jnp.concatenate(
        [packed[n : n + VECTORS] for n in range(0, VECTOR_ROWS, VECTORS)], axis=1
    )


def finish_kernel(size, groups, count, plan, up_rows, *refs):
    operands, outs = refs[:count], refs[count:]
    weights, vec_outs, embed_out, up_out = outs[:5], outs[5:-2], outs[-2], outs[-1]
    place = lax.axis_index("dp") * groups + lax.axis_index("tensor")
    share = D // (size * groups)
    for target, at, width, terms in plan[0]:
        weights[target][:, at : at + width] = summed(operands, terms, share, width)
    value = unpack_vectors(
        summed_vectors(lambda index: operands[index][...].astype(f32), plan[1])
    )
    mine = pltpu.roll(value, lax.rem(D - place * share, D), 1)[:, :TILE]
    rows = [row for row in range(5 + up_rows + 3) if not 5 <= row < 5 + up_rows]
    for row, out_ref in zip(rows, vec_outs):
        out_ref[...] = mine[row, :share]
    embed = jnp.concatenate([mine[5 + up_rows + 3 : 5 + up_rows + 5], jnp.zeros((6, TILE), f32)], axis=0)
    embed_out[...] = embed.T[:share, :2]
    wide = up_rows * share
    each = D // wide
    line = lax.div(place, each)
    chosen = functools.reduce(
        jnp.add,
        [jnp.where(line == r, value[5 + r : 6 + r], 0.0) for r in range(up_rows)],
    )
    chosen = jnp.broadcast_to(chosen, (8, D))
    turned = pltpu.roll(chosen, lax.rem(D - lax.rem(place, each) * wide, D), 1)[:, :TILE]
    up_out[...] = turned[0, :wide]


def whole(shape):
    return pl.BlockSpec(shape, lambda i: (0,) * len(shape))


def columns(rows, width, at=None):
    if at is None:
        return pl.BlockSpec((rows, width), lambda i: (0, i))
    return pl.BlockSpec((rows, width), lambda i: (0, at))


def scalars():
    return pl.BlockSpec(memory_space=pltpu.SMEM)


def params(size=VMEM_BYTES):
    return pltpu.CompilerParams(vmem_limit_bytes=size)


def cost(flops, bytes_accessed):
    return pl.CostEstimate(flops=flops, bytes_accessed=bytes_accessed, transcendentals=0)


def in_hbm():
    return pl.BlockSpec(memory_space=pl.ANY)


def attention_forward(
    half, size, groups, ints, memory, content, query, weights, biases, segment_rows
):
    count, window = 2 * half, KEYS + half
    coarse_rows = -(-(window // 32) // 8) * 8
    outs = (
        ((count, D), f32, columns(count, QUAD)),
        ((HEADS, count, KEYS), bf16, pl.BlockSpec((4, count, KEYS), lambda i: (i, 0, 0))),
        ((KEYS, D), bf16, columns(KEYS, QUAD)),
        ((KEYS, D), bf16, columns(KEYS, QUAD)),
        ((window, D), bf16, columns(window, QUAD)),
        ((count, D), bf16, columns(count, QUAD)),
        ((count, D), bf16, columns(count, QUAD)),
        ((count, D), f32, columns(count, QUAD)),
        ((count, QUADS * TILE), f32, columns(count, TILE)),
        ((KEYS, PAIR), bf16, whole((KEYS, PAIR))),
        ((half, PAIR), f32, whole((half, PAIR))),
        ((D, count), bf16, whole((D, count))),
        ((D, KEYS), bf16, whole((D, KEYS))),
        ((D, window), bf16, whole((D, window))),
    )
    return pl.pallas_call(
        functools.partial(forward_kernel, half, size, groups),
        grid=(QUADS,),
        out_shape=[jax.ShapeDtypeStruct(shape, kind) for shape, kind, _ in outs],
        in_specs=[
            scalars(),
            scalars(),
            whole((1, LEN)),
            whole((1, LEN)),
            whole((1, LEN)),
            whole((MEM, D)),
            whole((LEN, D)),
            whole((half, D)),
        ]
        + [columns(D, QUAD)] * 4
        + [whole((D,))] * 3
        + [columns(2, QUAD)],
        out_specs=[spec for _, _, spec in outs],
        scratch_shapes=[
            pltpu.VMEM((KEYS, D), bf16),
            pltpu.VMEM((count, D), bf16),
            pltpu.VMEM((window, D), bf16),
            pltpu.VMEM((count, KEYS), f32),
            pltpu.VMEM((2, 32, D // 2), f32),
            pltpu.VMEM((2, coarse_rows, D // 2), f32),
            pltpu.VMEM((8, D), f32),
            pltpu.VMEM((2, half, KEYS), f32),
            pltpu.VMEM((2, half, window), f32),
            pltpu.VMEM((HEAD_DIM, KEYS), bf16),
        ],
        compiler_params=params(),
        cost_estimate=cost(30_000_000_000, 40_000_000),
        name="attention_forward",
    )(*ints, memory, content, query, *weights, *biases, segment_rows)


def middle(half, size, groups, arrays, hidden_cols):
    count, share = 2 * half, D // groups
    chunk = min(hidden_cols, 768)
    outs = (
        ((half, D), bf16),
        ((half, D), bf16),
        ((D, 2 * hidden_cols), bf16),
        ((count, hidden_cols), bf16),
        ((count, hidden_cols), bf16),
        ((D, count), bf16),
        ((D, count), bf16),
        ((count, D), f32),
        ((count, D), bf16),
        ((share, D), bf16),
        ((share, D), bf16),
        ((8, D), f32),
        ((2, hidden_cols), f32),
    )
    weights = (6, 7, 8, 9)
    return pl.pallas_call(
        functools.partial(middle_kernel, half, size, groups, chunk),
        grid=(1,),
        out_shape=[jax.ShapeDtypeStruct(shape, kind) for shape, kind in outs],
        in_specs=[
            in_hbm() if i in weights else whole(array.shape) for i, array in enumerate(arrays)
        ],
        out_specs=[in_hbm() if i in (2, 3, 4) else whole(shape) for i, (shape, _) in enumerate(outs)],
        scratch_shapes=[
            pltpu.VMEM((2, count, hidden_cols), bf16),
            pltpu.VMEM((2, count, hidden_cols), bf16),
            pltpu.VMEM((D, 2 * hidden_cols), bf16),
            pltpu.VMEM((2, count, chunk), f32),
            pltpu.VMEM((count, D), f32),
            pltpu.VMEM((count, D), f32),
            pltpu.VMEM((count, D), bf16),
            pltpu.VMEM((count, D), bf16),
            pltpu.VMEM((8, FF), f32),
            pltpu.VMEM((2, D, hidden_cols), bf16),
            pltpu.VMEM((2, hidden_cols, D), bf16),
            pltpu.SemaphoreType.DMA((2, 2)),
            pltpu.SemaphoreType.DMA((4,)),
        ],
        compiler_params=params(),
        cost_estimate=cost(30_000_000_000, 30_000_000),
        name="feed_forward",
    )(*arrays)


def own_weights(low_t, down_t, pre, hid):
    count, hidden_cols = pre.shape
    width = 512
    steps = hidden_cols // width
    return pl.pallas_call(
        functools.partial(weights_kernel, steps),
        grid=(2 * steps,),
        out_shape=jax.ShapeDtypeStruct((D, 2 * hidden_cols), bf16),
        in_specs=[
            whole((D, count)),
            whole((D, count)),
            pl.BlockSpec((count, width), lambda i: (0, jnp.minimum(i, steps - 1))),
            pl.BlockSpec((count, width), lambda i: (0, jnp.maximum(i - steps, 0))),
        ],
        out_specs=columns(D, width),
        compiler_params=params(),
        cost_estimate=cost(5_000_000_000, 10_000_000),
        name="own_weights",
    )(low_t, down_t, pre, hid)


def attention_backward(half, groups, at, mode, saved, agrad, segment_rows, extra):
    count, window, share = 2 * half, KEYS + half, D // groups
    att, prob, keys, values, rel, hc, hp, hs, linv, kaug, scol, both_t, stack_t, pos_t = saved
    width = 4 * QUAD + (D if mode == "first" else 0)
    operands = (
        (prob, in_hbm()),
        (keys, columns(KEYS, QUAD, at)),
        (values, columns(KEYS, QUAD, at)),
        (rel, columns(window, QUAD, at)),
        (hc, columns(count, QUAD, at)),
        (hp, columns(count, QUAD, at)),
        (hs, columns(count, QUAD, at)),
        (linv, columns(count, TILE, at)),
        (kaug, whole((KEYS, PAIR))),
        (scol, whole((half, PAIR))),
        (att, columns(count, QUAD, at)),
        (agrad, columns(count, QUAD, at)),
        (segment_rows, columns(2, QUAD, at)),
        (both_t, in_hbm()),
        (stack_t, in_hbm()),
        (pos_t, in_hbm()),
    ) + tuple((array, whole(array.shape)) for array in extra)
    outs = (
        ((share, width), bf16),
        ((share, width + (TILE if mode == "last" else 0)), bf16),
        ((count, QUAD), bf16),
        ((LEN, QUAD), bf16),
        ((LEN, QUAD), bf16),
        ((8, QUAD), f32),
    )
    if mode == "last":
        outs += (((VECTOR_ROWS, TILE), f32),)
    return pl.pallas_call(
        functools.partial(backward_kernel, half, groups, at, mode),
        grid=(1,),
        out_shape=[jax.ShapeDtypeStruct(shape, kind) for shape, kind in outs],
        in_specs=[spec for _, spec in operands],
        out_specs=[whole(shape) for shape, _ in outs],
        scratch_shapes=[
            pltpu.VMEM((4, count, KEYS), bf16),
            pltpu.VMEM((D, count), bf16),
            pltpu.VMEM((D, KEYS), bf16),
            pltpu.VMEM((D, window), bf16),
            pltpu.VMEM((2, count, KEYS), f32),
            pltpu.VMEM((2, count, KEYS), bf16),
            pltpu.VMEM((2, count, window), bf16),
            pltpu.SemaphoreType.DMA((7,)),
        ],
        compiler_params=params(),
        cost_estimate=cost(16_000_000_000, 16_000_000),
        name="attention_backward",
    )(*[array for array, _ in operands])


def row_gradients(half, groups, summed_grad, proj, keys, vals, weights):
    count = 2 * half
    arrays = (summed_grad, *proj, *keys, *vals, *weights)
    outs = (((half, D), f32), ((half, D), f32), ((half, D), bf16))
    return pl.pallas_call(
        functools.partial(rows_kernel, half, groups),
        grid=(1,),
        out_shape=[jax.ShapeDtypeStruct(shape, kind) for shape, kind in outs],
        in_specs=[whole(array.shape) for array in arrays],
        out_specs=[whole(shape) for shape, _ in outs],
        scratch_shapes=[pltpu.VMEM((LEN, D), f32)],
        compiler_params=params(),
        cost_estimate=cost(4_000_000_000, 10_000_000),
        name="row_gradients",
    )(*arrays)


def swap(array):
    groups = lax.axis_size("tensor")
    return lax.ppermute(array, "tensor", [(i, (i + 1) % groups) for i in range(groups)])


def across(array, masks):
    size, groups = lax.axis_size("dp"), lax.axis_size("tensor")
    pairs = [
        (place * groups + core, (place ^ masks[core]) * groups + core)
        for place in range(size)
        for core in range(groups)
    ]
    return lax.ppermute(array, ("dp", "tensor"), pairs)


def total(terms):
    return functools.reduce(jnp.add, [term.astype(f32) for term in terms])


class Chain:
    def __init__(self, parts, rows, vectors=()):
        self.parts, self.rows = parts, rows
        self.vectors = list(vectors)
        self.messages = None
        self.done = 0

    def masks(self, part, bits):
        size, groups = lax.axis_size("dp"), lax.axis_size("tensor")
        found = []
        for core in range(groups):
            order = order_of(core, size.bit_length() - 1)[self.done : self.done + bits]
            found.append(
                sum(((part >> (bits - 1 - j)) & 1) << bit for j, bit in enumerate(order))
            )
        return found

    def send(self):
        if not self.bits:
            gots = [swap(self.messages[0])]
        else:
            gots = [
                across(message, self.masks(part + 1, self.bits))
                for part, message in enumerate(self.messages)
            ]
        for got in gots:
            column = 0
            for width, terms in self.parts:
                terms.append((got, column))
                column += width
            if self.vectors:
                self.vectors.append((got, column, self.rows))
        self.pending = gots
        self.done += self.bits
        self.messages = None

    def replace(self, old, new):
        for index, (width, terms) in enumerate(self.parts):
            self.parts[index] = (
                width,
                [(new if array is old else array, at) for array, at in terms],
            )
        self.vectors = [(new if a is old else a, at, rows) for a, at, rows in self.vectors]


def merged(chains):
    chain = Chain(
        [part for chain in chains for part in chain.parts],
        chains[0].rows,
        [term for chain in chains for term in chain.vectors],
    )
    chain.done = chains[0].done
    chain.pending = []
    return chain


class Operands:
    def __init__(self):
        self.arrays, self.specs = [], []

    def rows(self, array, first, rows):
        if rows % 16 == 0 and first % rows == 0:
            at = first // rows
            spec, skip = pl.BlockSpec((rows, array.shape[1]), lambda i: (at, 0)), 0
        else:
            spec, skip = whole(array.shape), first
        for index, (held, kept) in enumerate(zip(self.arrays, self.specs)):
            if held is array and kept[1] == (spec.block_shape, first - skip):
                return index, skip
        self.arrays.append(array)
        self.specs.append((spec, (spec.block_shape, first - skip)))
        return len(self.arrays) - 1, skip

    def in_specs(self):
        return [spec for spec, _ in self.specs]


def room_for(arrays):
    return COMBINE_BYTES if any(array.size > 2 * D * D for array in arrays) else COMBINE_BYTES // 2


def prepare(requests):
    operands, plans, outs = Operands(), [], []
    plain = False
    for chain, bits in requests:
        parts = 1 << bits
        plain = plain or chain.rows % (8 * parts) != 0
    for chain, bits in requests:
        chain.bits = bits
        chain.rows >>= bits
        kept = chain.rows
        messages = []
        for part in range(1, 1 << bits):
            if plain:
                message = jnp.concatenate(
                    [
                        total(
                            [
                                array[part * kept : (part + 1) * kept, at : at + width]
                                for array, at in terms
                            ]
                        )
                        for width, terms in chain.parts
                    ],
                    axis=1,
                )
                if chain.vectors:
                    packed = summed_vectors(lambda array: array, chain.vectors)
                    message = jnp.concatenate([message, fold_vectors(packed, kept)], axis=1)
                messages.append(message.astype(bf16))
                continue
            found = []
            for width, terms in chain.parts:
                places = []
                for array, at in terms:
                    index, skip = operands.rows(array, part * kept, kept)
                    places.append((index, at, skip))
                found.append((width, places))
            vectors = [
                (operands.rows(array, 0, min(rows, VECTOR_ROWS))[0], at, rows)
                for array, at, rows in chain.vectors
            ]
            plans.append((kept, found, vectors))
            width = sum(width for width, _ in chain.parts)
            outs.append((kept, width + (vector_width(kept) if vectors else 0)))
        chain.messages = messages
    if plain:
        return
    results = pl.pallas_call(
        functools.partial(combine_kernel, plans),
        grid=(1,),
        out_shape=[jax.ShapeDtypeStruct(shape, bf16) for shape in outs],
        in_specs=operands.in_specs(),
        out_specs=[whole(shape) for shape in outs],
        compiler_params=params(room_for(operands.arrays)),
        cost_estimate=cost(1_000_000_000, 8_000_000),
        name="combine",
    )(*operands.arrays)
    results = list(results)
    for chain, bits in requests:
        chain.messages = [results.pop(0) for _ in range((1 << bits) - 1)]


def launch(requests, value, waits=()):
    chains = [chain for chain, bits in requests if bits is not None] + list(waits)
    olds = [got for chain in chains for got in chain.pending]
    if olds:
        value, news = lax.optimization_barrier((value, olds))
        for chain in chains + [chain for chain, _ in requests]:
            for old, new in zip(olds, news):
                chain.replace(old, new)
        for chain in chains:
            chain.pending = []
    sums = [(chain, bits) for chain, bits in requests if bits is not None]
    if sums:
        prepare(sums)
    messages = [chain.messages for chain, _ in requests]
    value, messages = lax.optimization_barrier((value, messages))
    for (chain, bits), message in zip(requests, messages):
        chain.messages = message
        if bits is None:
            chain.bits = 0
        chain.send()
    return value


def finish(size, groups, chain):
    share = D // (size * groups)
    up_rows = FF // D
    pieces = []
    for quad, (width, terms) in enumerate(chain.parts):
        for index in range(4):
            pieces.append((index, quad * QUAD, QUAD, [(a, at + index * QUAD) for a, at in terms]))
        if width > 4 * QUAD:
            pieces.append((4, 0, D, [(a, at + 4 * QUAD) for a, at in terms]))
    if share % 8:
        blocks = {}
        for target, at, width, terms in pieces:
            blocks.setdefault(target, []).append(
                total([array[:share, c : c + width] for array, c in terms])
            )
        weights = [jnp.concatenate(blocks[target], axis=1) for target in range(5)]
        vectors = unpack_vectors(summed_vectors(lambda array: array, chain.vectors))
        place = lax.axis_index("dp") * groups + lax.axis_index("tensor")
        mine = lax.dynamic_slice_in_dim(vectors, place * share, share, 1)
        ups = lax.dynamic_slice_in_dim(
            vectors[5 : 5 + up_rows].reshape(-1), place * up_rows * share, up_rows * share, 0
        )
        late = 5 + up_rows
        return weights, [mine[r] for r in (0, 1, 2, 3, 4, late, late + 1, late + 2)], mine[
            late + 3 : late + 5
        ].T, ups
    operands = Operands()
    plan = []
    for target, at, width, terms in pieces:
        places = []
        for array, c in terms:
            index, skip = operands.rows(array, 0, min(-(-share // 16) * 16, array.shape[0]))
            places.append((index, c, skip))
        plan.append((target, at, width, places))
    vectors = [
        (operands.rows(array, 0, min(rows, VECTOR_ROWS))[0], at, rows)
        for array, at, rows in chain.vectors
    ]
    outs = [(share, D)] * 5 + [(share,)] * 8 + [(share, 2), (up_rows * share,)]
    found = pl.pallas_call(
        functools.partial(
            finish_kernel, size, groups, len(operands.arrays), (plan, vectors), up_rows
        ),
        grid=(1,),
        out_shape=[jax.ShapeDtypeStruct(shape, f32) for shape in outs],
        in_specs=operands.in_specs(),
        out_specs=[whole(shape) for shape in outs],
        compiler_params=params(room_for(operands.arrays)),
        name="finish",
    )(*operands.arrays)
    return found[:5], found[5:13], found[13], found[14]


def body(
    content_in,
    query_in,
    memory,
    content_cot,
    query_cot,
    query_weight,
    key_weight,
    value_weight,
    out_weight,
    rel_weight,
    content_bias,
    position_bias,
    segment_bias,
    segment_embed,
    attn_gain,
    attn_shift,
    up_weight,
    up_bias,
    down_weight,
    down_bias,
    ffn_gain,
    ffn_shift,
    lengths,
    memory_lengths,
    segment_ids,
    orders,
    targets,
):
    groups = lax.axis_size("tensor")
    size = lax.axis_size("dp")
    steps = size.bit_length() - 1
    half = LEN // groups
    hidden_cols = up_weight.shape[1]
    up_other, down_other = swap(up_weight), swap(down_weight)
    content, query = content_in[0], query_in[0]
    segment_rows = segment_embed.T
    saved = attention_forward(
        half,
        size,
        groups,
        (lengths, memory_lengths, segment_ids, orders, targets),
        memory[0],
        content,
        query,
        (query_weight, key_weight, value_weight, rel_weight),
        (content_bias, position_bias, segment_bias),
        segment_rows,
    )
    (
        content_out,
        query_out,
        ffn_other,
        hidden,
        pre_grad,
        low_t,
        down_t,
        summed_grad,
        attended_grad,
        out_own,
        out_other,
        early_small,
        up_bias_part,
    ) = middle(
        half,
        size,
        groups,
        (
            saved[0],
            content,
            query,
            content_cot[0],
            query_cot[0],
            out_weight,
            up_weight,
            up_other,
            down_weight,
            down_other,
            up_bias,
            down_bias,
            attn_gain,
            attn_shift,
            ffn_gain,
            ffn_shift,
        ),
        hidden_cols,
    )
    ffn = Chain([(2 * hidden_cols, [])], D)
    ffn.messages = [ffn_other]
    launch([(ffn, None)], summed_grad[:1, :1])
    ffn_own = own_weights(low_t, down_t, pre_grad, hidden)
    ffn.parts[0][1].append((ffn_own, 0))
    proj, tok_keys, tok_vals, small, late = [], [], [], [], []

    def backward(at, mode, grad, extra):
        own, other, proj_part, key_part, val_part, small_part, *vectors = attention_backward(
            half, groups, at, mode, saved, grad, segment_rows, extra
        )
        proj.append(proj_part)
        tok_keys.append(key_part)
        tok_vals.append(val_part)
        small.append(small_part)
        chain = Chain(
            [(own.shape[1], [(own, 0)])],
            own.shape[0],
            [(array, 0, VECTOR_ROWS) for array in vectors],
        )
        chain.messages = [other]
        late.append(chain)

    held = launch([(ffn, 1)], attended_grad)
    backward(0, "first", held, (out_own, out_other))
    held, proj[0] = launch([(late[0], None)], (attended_grad, proj[0]))
    backward(1, "middle", held, ())
    held, proj[1] = launch(
        [(ffn, 1), (late[0], 1), (late[1], None)], (attended_grad, proj[1])
    )
    backward(2, "last", held, (early_small, up_bias_part, *small))
    xy = min(2, steps)
    proj[2] = launch([(ffn, steps - ffn.done if steps < 5 else 2), (late[0], 1), (late[1], xy), (late[2], None)], proj[2])
    own_rows, query_grad, row_send = row_gradients(
        half, groups, summed_grad, proj, tok_keys, tok_vals, (query_weight, key_weight, value_weight)
    )
    row_send = launch([(late[2], xy)], row_send)
    row_got = swap(row_send)
    content_grad = own_rows + row_got.astype(f32)
    final = merged(late)
    while final.done < steps:
        content_grad = launch([(final, min(2, steps - final.done))], content_grad, late)
    while ffn.done < steps:
        content_grad = launch([(ffn, min(2, steps - ffn.done))], content_grad)
    ffn_sum = total([array[: ffn.rows] for array, _ in ffn.parts[0][1]])
    up_grad, down_grad_own = ffn_sum[:, :hidden_cols], ffn_sum[:, hidden_cols:].T
    weights, vectors, segment_grad, up_bias_grad = finish(size, groups, final)
    return (
        content_out[None],
        query_out[None],
        content_grad[None],
        query_grad[None],
        weights[0],
        weights[1],
        weights[2],
        weights[4],
        weights[3],
        vectors[5],
        vectors[6],
        vectors[7],
        segment_grad,
        vectors[3],
        vectors[4],
        up_grad,
        up_bias_grad,
        down_grad_own,
        vectors[2],
        vectors[0],
        vectors[1],
    )


def solution(mesh):
    in_specs = (
        P("dp", None, None),
        P("dp", "tensor", None),
        P("dp", None, None),
        P("dp", "tensor", None),
        P("dp", "tensor", None),
        P(),
        P(),
        P(),
        P(),
        P(),
        P(),
        P(),
        P(),
        P(),
        P(),
        P(),
        P(None, "tensor"),
        P(),
        P("tensor", None),
        P(),
        P(),
        P(),
        P("dp"),
        P("dp"),
        P("dp", None),
        P("dp", None),
        P("dp", None),
    )
    out_specs = (
        P("dp", "tensor", None),
        P("dp", "tensor", None),
        P("dp", "tensor", None),
        P("dp", "tensor", None),
        P(("dp", "tensor"), None),
        P(("dp", "tensor"), None),
        P(("dp", "tensor"), None),
        P(("dp", "tensor"), None),
        P(("dp", "tensor"), None),
        P(("dp", "tensor")),
        P(("dp", "tensor")),
        P(("dp", "tensor")),
        P(("dp", "tensor"), None),
        P(("dp", "tensor")),
        P(("dp", "tensor")),
        P("dp", "tensor"),
        P(("dp", "tensor")),
        P("tensor", "dp"),
        P(("dp", "tensor")),
        P(("dp", "tensor")),
        P(("dp", "tensor")),
    )
    return jax.shard_map(body, mesh=mesh, in_specs=in_specs, out_specs=out_specs, check_vma=False)
```

```python
import functools

import jax
import jax.numpy as jnp
from jax import lax
from jax.experimental import pallas as pl
from jax.experimental.pallas import tpu as pltpu
from jax.sharding import PartitionSpec as P

D = 768
HEADS = 12
HEAD_DIM = 64
FF = 3072
LEN = 512
MEM = 384
KEYS = MEM + LEN
QUAD = 4 * HEAD_DIM
QUADS = D // QUAD
PAIR = 2 * HEAD_DIM
SCALE = HEAD_DIM ** (-0.5)
VMEM_BYTES = 61 * 1024 * 1024
COMBINE_BYTES = 28 * 1024 * 1024
BLOCK = 32
TILE = 128
WIDE = 256
PART = 128
VECTORS = 16

VECTOR_ROWS = VECTORS * D // TILE

f32 = jnp.float32
bf16 = jnp.bfloat16
precise = lax.Precision.HIGHEST


def mm(left, right):
    return lax.dot_general(left, right, (((1,), (0,)), ((), ())), preferred_element_type=f32)


def mm_nt(left, right):
    return lax.dot_general(left, right, (((1,), (1,)), ((), ())), preferred_element_type=f32)


def lanes(shape):
    return lax.broadcasted_iota(jnp.int32, shape, 1)


def column_of(row):
    return jnp.broadcast_to(row.astype(f32), (128, row.shape[1])).T


def lane_tiles(value, combine):
    tiles = [value[:, at : at + TILE] for at in range(0, value.shape[1], TILE)]
    return functools.reduce(combine, tiles)


def interleave(steps, tasks):
    done = 0
    for index, step in enumerate(steps):
        step()
        while done * len(steps) < (index + 1) * len(tasks) and done < len(tasks):
            tasks[done]()
            done += 1
    for task in tasks[done:]:
        task()


def order_of(core, bits):
    plain = list(range(bits))
    return plain[1:2] + plain[:1] + plain[2:] if core == 1 and bits > 1 else plain


def block_owner(place, core, bits):
    owner = jnp.zeros_like(place)
    for step in range(bits):
        owner = owner | (((place >> (bits - 1 - step)) & 1) << step)
    if bits > 1:
        swapped = (owner & ~3) | ((owner & 1) << 1) | ((owner >> 1) & 1)
        owner = jnp.where(core == 1, swapped, owner)
    return owner ^ lax.axis_index("dp")


def one_hot(source):
    return jnp.where(lanes((source.shape[0], D)) == source, 1.0, 0.0).astype(bf16)


def owner_rows(size, groups):
    share = D // (size * groups)
    row = lax.broadcasted_iota(jnp.int32, (D, 1), 0)
    side, rest = lax.div(row, size * share), lax.rem(row, size * share)
    core = lax.rem(lax.axis_index("tensor") + side, groups)
    owner = block_owner(lax.div(rest, share), core, size.bit_length() - 1)
    return one_hot((owner * groups + core) * share + lax.rem(rest, share))


def shared_rows(size, core):
    share = D // size
    row = lax.broadcasted_iota(jnp.int32, (D, 1), 0)
    owner = block_owner(lax.div(row, share), core, size.bit_length() - 1)
    return one_hot(owner * share + lax.rem(row, share))


def transpose_by_owner(out_ref, value, work, size, groups):
    share = D // (size * groups)
    if share % 8 or (2 * share) % 16:
        out_ref[...] = mm_nt(owner_rows(size, groups), value).astype(bf16)
        return
    width = value.shape[0]
    work[:, :width] = value.T.astype(f32)
    bits = size.bit_length() - 1
    blocks = []
    for block in range(size * groups):
        core = lax.rem(lax.axis_index("tensor") + block // size, groups)
        owner = block_owner(jnp.int32(block % size), core, bits)
        at = pl.multiple_of((owner * groups + core) * share, 8)
        blocks.append(work[pl.ds(at, share), :width])
        if block % 2:
            out_ref[(block - 1) * share : (block + 1) * share, :] = jnp.concatenate(
                blocks, axis=0
            ).astype(bf16)
            blocks = []


def transpose_by_dp(out_ref, value, work, size):
    share = D // size
    core = lax.axis_index("tensor")
    if share % 16:
        out_ref[...] = mm_nt(shared_rows(size, core), value).astype(bf16)
        return
    work[...] = value.T
    for block in range(size):
        owner = block_owner(jnp.int32(block), core, size.bit_length() - 1)
        at = pl.multiple_of(owner * share, 16)
        out_ref[block * share : (block + 1) * share, :] = work[pl.ds(at, share), :]


def forward_kernel(
    half,
    size,
    groups,
    length_ref,
    mem_length_ref,
    seg_ref,
    ord_ref,
    tgt_ref,
    memory_ref,
    content_ref,
    query_ref,
    wq_ref,
    wk_ref,
    wv_ref,
    wr_ref,
    cb_ref,
    pb_ref,
    sb_ref,
    se_ref,
    att_ref,
    prob_ref,
    key_ref,
    val_ref,
    rel_ref,
    hc_ref,
    hp_ref,
    hs_ref,
    linv_ref,
    kaug_ref,
    srow_ref,
    both_t_ref,
    stack_t_ref,
    pos_t_ref,
    stack,
    both,
    pos,
    bias,
    fine,
    coarse,
    vectors,
    scores,
    places,
    kaug_t,
    scol,
    seg_row,
    turn_work,
    kaug_work,
):
    window, reach = KEYS + half, KEYS + PART
    first = pl.multiple_of(lax.axis_index("tensor") * half, half)
    step_id = pl.program_id(0)

    @pl.when(step_id == 0)
    def _():
        stack[:MEM, :] = memory_ref[...]
        stack[MEM:, :] = content_ref[...]
        both[:half, :] = content_ref[pl.ds(first, half), :]
        both[half:, :] = query_ref[...]
        vectors[0:1, :] = cb_ref[...][None, :]
        vectors[1:2, :] = pb_ref[...][None, :]
        vectors[2:3, :] = sb_ref[...][None, :]
        step = lax.broadcasted_iota(jnp.int32, (1, D // 2), 1).astype(f32) * (2.0 / D)
        inverse = 1.0 / jnp.power(jnp.full((1, D // 2), 10000.0, f32), step)
        coarse_rows = coarse.shape[1]
        top = (MEM + half + first).astype(f32)
        angle = (
            top - 32.0 * lax.broadcasted_iota(jnp.int32, (coarse_rows, 1), 0).astype(f32)
        ) * inverse
        coarse[0] = jnp.sin(angle)
        coarse[1] = jnp.cos(angle)
        small = lax.broadcasted_iota(jnp.int32, (32, 1), 0).astype(f32) * inverse
        fine[0] = jnp.sin(small)
        fine[1] = jnp.cos(small)
        for a in range(window // 32):
            sa, ca = coarse[0, a : a + 1, :], coarse[1, a : a + 1, :]
            sb, cb = fine[0], fine[1]
            pos[a * 32 : (a + 1) * 32, : D // 2] = (sa * cb - ca * sb).astype(bf16)
            pos[a * 32 : (a + 1) * 32, D // 2 :] = (ca * cb + sa * sb).astype(bf16)
        never = float(LEN + 1)
        mem_at = lax.broadcasted_iota(jnp.int32, (1, MEM), 1)
        tok_at = lax.broadcasted_iota(jnp.int32, (1, LEN), 1)
        open_from = jnp.concatenate(
            [
                jnp.where(mem_at >= MEM - mem_length_ref[0], -1.0, never),
                jnp.where(
                    tok_at < length_ref[0],
                    jnp.where(tgt_ref[...] == 0, -1.0, ord_ref[...].astype(f32)),
                    never,
                ),
            ],
            axis=1,
        )
        order_col = column_of(ord_ref[...])
        seg_col = column_of(seg_ref[...])
        kaug_lane = lanes((LEN, PAIR)) % HEAD_DIM
        kaug_work[:MEM, :] = (lanes((MEM, PAIR)) % HEAD_DIM < 4).astype(f32).astype(bf16)
        kaug_work[MEM:, :] = jnp.where(
            kaug_lane < 4, 1.0, jnp.where(kaug_lane < 6, seg_col, 0.0)
        ).astype(bf16)
        kaug_t[...] = kaug_work[...].T[:HEAD_DIM]
        kaug_ref[...] = kaug_t[:16, :]
        bias[:LEN, :PAIR] = order_col
        own_order = bias[pl.ds(first, half), :PAIR][:, :1]
        bias[:LEN, :PAIR] = seg_col
        scol[...] = bias[pl.ds(first, half), :PAIR]
        seen = open_from <= own_order
        bias[:half, :] = jnp.where(seen, 0.0, -1e30)
        key_at = lax.broadcasted_iota(jnp.int32, (half, KEYS), 1)
        row_at = lax.broadcasted_iota(jnp.int32, (half, KEYS), 0)
        seen_q = seen & (key_at - MEM != row_at + first)
        bias[half:, :] = jnp.where(seen_q, 0.0, -1e30)
        seg_row[0:1, :] = seg_ref[...].astype(f32)
        srow_ref[...] = jnp.broadcast_to(seg_row[0:1, pl.ds(first, half)], srow_ref.shape)
        transpose_by_owner(both_t_ref, both[...], turn_work, size, groups)
        transpose_by_owner(stack_t_ref, stack[...], turn_work, size, groups)
        transpose_by_owner(pos_t_ref, pos[...], turn_work, size, groups)

    here = pl.ds(pl.multiple_of(step_id * QUAD, QUAD), QUAD)
    keys = mm(stack[...], wk_ref[...]).astype(bf16)
    values = mm(stack[...], wv_ref[...]).astype(bf16)
    rel = mm(pos[...], wr_ref[...]).astype(bf16)
    projection = mm(both[...], wq_ref[...])
    head_content = (projection + vectors[0:1, here]).astype(bf16)
    head_position = (projection + vectors[1:2, here]).astype(bf16)
    head_segment = projection + vectors[2:3, here]
    keys_t, values_t, rel_t = keys.T, values.T, rel.T
    key_ref[...] = keys_t
    val_ref[...] = values_t
    rel_ref[...] = rel_t
    hs_ref[...] = head_segment.T
    head_content = (head_content.astype(f32) * SCALE).astype(bf16)
    head_position = (head_position.astype(f32) * SCALE).astype(bf16)
    hc_ref[...] = head_content.T
    hp_ref[...] = head_position.T
    same = column_of(se_ref[0:1, :])
    differ = column_of(se_ref[1:2, :] - se_ref[0:1, :])
    same = jnp.concatenate([same, same], axis=1)
    differ = jnp.concatenate([differ, differ], axis=1)
    row_head = lax.broadcasted_iota(jnp.int32, (QUAD, QUAD), 0) // HEAD_DIM
    at = lanes((QUAD, QUAD)) - ((row_head // 2) * PAIR + (1 - row_head % 2) * HEAD_DIM)
    embed = jnp.where(
        (at >= 0) & (at < 2), same, jnp.where((at >= 2) & (at < 6), differ, 0.0)
    )
    embed_high = embed.astype(bf16)
    embed_low = (embed - embed_high.astype(f32)).astype(bf16)
    segment_high = head_segment.astype(bf16)
    segment_low = (head_segment - segment_high.astype(f32)).astype(bf16)
    terms = (
        mm(segment_high, embed_high) + mm(segment_high, embed_low) + mm(segment_low, embed_high)
    )
    marks = jnp.concatenate([scol[...], scol[...]], axis=0)
    marks = jnp.concatenate([marks, marks], axis=1)
    lane6 = lanes((2 * half, QUAD)) % HEAD_DIM
    factor = jnp.where(lane6 < 2, 1.0, jnp.where(lane6 < 4, marks, 1.0 - 2.0 * marks))
    terms = SCALE * (terms * factor)
    high = terms.astype(bf16)
    low = (terms - high.astype(f32)).astype(bf16)
    qaug = jnp.where(lane6 % 2 == 0, high, low)
    units = [(pair, head, part) for pair in range(2) for head in range(2) for part in range(2)]
    key_x = []
    for which in range(4):
        own = keys_t[which * HEAD_DIM : (which + 1) * HEAD_DIM]
        sides = [own, kaug_t[...]] if which % 2 == 0 else [kaug_t[...], own]
        key_x.append(jnp.concatenate(sides, axis=0))
    peaks, totals, outs = {}, {}, {}

    def products(index):
        pair, head, part = units[index]
        cols, rows = slice(pair * PAIR, (pair + 1) * PAIR), slice(part * half, (part + 1) * half)
        slot, which = index % 2, pair * 2 + head
        row_mine = (lanes((half, PAIR)) < HEAD_DIM) == (head == 0)
        query_x = jnp.where(row_mine, head_content[rows, cols], qaug[rows, cols])
        place_x = jnp.where(row_mine, head_position[rows, cols], jnp.zeros((), bf16))

        def score(n, stop):
            scores[slot, :, n:stop] = mm(query_x, key_x[which][:, n:stop])

        def placed(r, n, stop):
            at = half - r - PART
            places[slot, r : r + PART, n:stop] = mm(
                place_x[r : r + PART], rel_t[cols, at + n : at + stop]
            )

        return [
            functools.partial(placed, r, n, min(n + WIDE, reach))
            for r in range(0, half, PART)
            for n in range(0, reach, WIDE)
        ] + [
            functools.partial(score, n, min(n + WIDE, KEYS)) for n in range(0, KEYS, WIDE)
        ]

    def softmax(index):
        pair, head, part = units[index]
        slot, which = index % 2, pair * 2 + head
        tops, pieces = [], []

        def join(b):
            block = slice(b, b + BLOCK)
            shifted = pltpu.roll(
                places[slot, block, :], (reach - PART + b % PART) % reach, 1, stride=1, stride_axis=0
            )[:, :KEYS]
            score = (
                scores[slot, block, :]
                + shifted
                + bias[part * half + b : part * half + b + BLOCK, :]
            )
            scores[slot, block, :] = score
            tops.append(lane_tiles(score, jnp.maximum))

        def peak():
            peaks[index] = jnp.max(jnp.concatenate(tops, axis=0), axis=1, keepdims=True)

        def power(b):
            block = slice(b, b + BLOCK)
            prob = jnp.exp(scores[slot, block, :] - peaks[index][block])
            pieces.append(lane_tiles(prob, jnp.add))
            prob_ref[which, part * half + b : part * half + b + BLOCK, :] = prob.astype(bf16)

        def finish():
            totals[index] = 1.0 / jnp.sum(
                jnp.concatenate(pieces, axis=0), axis=1, keepdims=True
            )

        blocks = range(0, half, BLOCK)
        return (
            [functools.partial(join, b) for b in blocks]
            + [peak]
            + [functools.partial(power, b) for b in blocks]
            + [finish]
        )

    def mixture(index):
        pair, head, part = units[index]
        rows = slice(part * half, (part + 1) * half)
        which = pair * 2 + head
        outs[index] = mm_nt(
            values_t[which * HEAD_DIM : (which + 1) * HEAD_DIM], prob_ref[which, rows, :]
        )

    interleave([], products(0))
    for index in range(len(units)):
        tasks = products(index + 1) if index + 1 < len(units) else []
        if index:
            tasks.append(functools.partial(mixture, index - 1))
        interleave(softmax(index), tasks)
    mixture(len(units) - 1)
    sums = [
        jnp.concatenate([totals[2 * which], totals[2 * which + 1]], axis=0) for which in range(4)
    ]
    mixed = jnp.concatenate(
        [
            jnp.concatenate([outs[2 * which], outs[2 * which + 1]], axis=1) for which in range(4)
        ],
        axis=0,
    ).T
    mine = lanes((2 * half, PAIR)) < HEAD_DIM
    for pair in range(2):
        cols = slice(pair * PAIR, (pair + 1) * PAIR)
        att_ref[:, cols] = mixed[:, cols] * jnp.where(mine, sums[2 * pair], sums[2 * pair + 1])
    lane = lanes((2 * half, TILE))
    linv_ref[...] = jnp.where(
        lane == 0, sums[0], jnp.where(lane == 1, sums[1], jnp.where(lane == 2, sums[2], sums[3]))
    )


def norm_forward(summed, gain, shift):
    center = summed - jnp.mean(summed, axis=1, keepdims=True)
    inv = lax.rsqrt(jnp.mean(center * center, axis=1, keepdims=True) + 1e-06)
    unit = center * inv
    return unit, inv, unit * gain + shift


def norm_backward(grad, unit, inv, gain):
    scaled = grad * gain
    return inv * (
        scaled
        - jnp.mean(scaled, axis=1, keepdims=True)
        - unit * jnp.mean(scaled * unit, axis=1, keepdims=True)
    )


def row_sum(value):
    return jnp.sum(value, axis=0, keepdims=True)


def gelu_parts(x):
    square = x * x
    tanh = jnp.tanh((0.7978845608028654 * x) * (1.0 + 0.044715 * square))
    rise = 0.5 * (1.0 + tanh)
    grad = rise + (0.5 * x) * (1.0 - tanh * tanh) * (
        0.7978845608028654 * (1.0 + 0.134145 * square)
    )
    return x * rise, grad


def fold_rows(value):
    return functools.reduce(jnp.add, [value[r : r + 8] for r in range(0, value.shape[0], 8)])


def middle_kernel(
    half,
    size,
    groups,
    chunk,
    att_ref,
    content_ref,
    query_ref,
    ccot_ref,
    qcot_ref,
    wo_ref,
    up_own_hbm,
    up_oth_hbm,
    down_own_hbm,
    down_oth_hbm,
    ubias_ref,
    dbias_ref,
    again_ref,
    ashift_ref,
    fgain_ref,
    fshift_ref,
    cout_ref,
    qout_ref,
    ffn_hbm,
    hid_hbm,
    pre_hbm,
    low_t_ref,
    down_t_ref,
    sgrad_ref,
    agrad_ref,
    out_own_ref,
    out_oth_ref,
    small_ref,
    ubg_ref,
    hidden,
    slope,
    ffn,
    pre,
    work,
    unit,
    low,
    down_grad,
    vectors,
    up,
    down,
    turn_low,
    turn_work,
    sems,
    out_sems,
):
    count = 2 * half
    member = lax.axis_index("tensor")
    first = pl.multiple_of(member * half, half)
    fetches = [
        pltpu.make_async_copy(source, target.at[side], sems.at[kind, side])
        for kind, side, source, target in (
            (0, 0, up_own_hbm, up),
            (1, 0, down_own_hbm, down),
            (0, 1, up_oth_hbm, up),
            (1, 1, down_oth_hbm, down),
        )
    ]
    for fetch in fetches:
        fetch.start()
    ups, downs = (up.at[0], up.at[1]), (down.at[0], down.at[1])
    part_cols = up.shape[2]
    chunks = part_cols // chunk
    vectors[0:1, :] = ubias_ref[...][None, :]
    attended = att_ref[...].astype(bf16)
    work[...] = mm(attended, wo_ref[...])
    attn_gain, attn_shift = again_ref[...][None, :], ashift_ref[...][None, :]
    ffn_gain, ffn_shift = fgain_ref[...][None, :], fshift_ref[...][None, :]
    down_bias = dbias_ref[...][None, :]
    inverse = []
    for b in range(0, count, BLOCK):
        block = slice(b, b + BLOCK)
        if b < half:
            rows_in = content_ref[pl.ds(pl.multiple_of(first + b, BLOCK), BLOCK), :]
        else:
            rows_in = query_ref[b - half : b - half + BLOCK, :]
        found, inv, normed = norm_forward(
            work[block, :] + rows_in.astype(f32), attn_gain, attn_shift
        )
        unit[block, :] = found
        inverse.append(inv)
        low[block, :] = normed.astype(bf16)
        work[block, :] = normed + down_bias
    for fetch in fetches:
        fetch.wait()
    pieces = [(side, at) for side in range(2) for at in range(chunks)]

    def rise(index):
        side, at = pieces[index]

        def task(n):
            pre[index % 2, :, n : n + WIDE] = mm(
                low[...], ups[side][:, at * chunk + n : at * chunk + n + WIDE]
            )

        return [functools.partial(task, n) for n in range(0, chunk, WIDE)]

    def bend(index):
        side, at = pieces[index]
        cols = slice(at * chunk, (at + 1) * chunk)
        start = lax.rem(member + side, 2) * part_cols + at * chunk
        bias = vectors[0:1, pl.ds(pl.multiple_of(start, TILE), chunk)]

        def step(b):
            block = slice(b, b + BLOCK)
            act, grad = gelu_parts(pre[index % 2, block, :] + bias)
            hidden[side, block, cols] = act.astype(bf16)
            slope[side, block, cols] = grad.astype(bf16)

        return [functools.partial(step, b) for b in range(0, count, BLOCK)]

    def fall(index):
        side, at = pieces[index]
        cols = slice(at * chunk, (at + 1) * chunk)

        def task(n):
            work[:, n : n + WIDE] += mm(hidden[side, :, cols], downs[side][cols, n : n + WIDE])

        return [functools.partial(task, n) for n in range(0, D, WIDE)]

    interleave([], rise(0))
    for index in range(len(pieces)):
        tasks = rise(index + 1) if index + 1 < len(pieces) else []
        if index:
            tasks += fall(index - 1)
        interleave(bend(index), tasks)
    interleave([], fall(len(pieces) - 1))
    stores = [
        pltpu.make_async_copy(source, target, out_sems.at[index])
        for index, (source, target) in enumerate(
            (
                (hidden.at[0], hid_hbm),
                (slope.at[0], pre_hbm),
                (ffn.at[:, :part_cols], ffn_hbm.at[:, :part_cols]),
                (ffn.at[:, part_cols:], ffn_hbm.at[:, part_cols:]),
            )
        )
    ]
    stores[0].start()
    sums = [jnp.zeros((8, D), f32) for _ in range(5)]
    for b in range(0, count, BLOCK):
        block = slice(b, b + BLOCK)
        found, inv, out = norm_forward(work[block, :], ffn_gain, ffn_shift)
        if b < half:
            cout_ref[block, :] = out.astype(bf16)
            cot = ccot_ref[block, :].astype(f32)
        else:
            block_q = slice(b - half, b - half + BLOCK)
            qout_ref[block_q, :] = out.astype(bf16)
            cot = qcot_ref[block_q, :].astype(f32)
        residual_grad = norm_backward(cot, found, inv, ffn_gain)
        rounded = residual_grad.astype(bf16)
        down_grad[block, :] = rounded
        work[block, :] = residual_grad
        for index, value in enumerate((cot * found, cot, rounded.astype(f32))):
            sums[index] = sums[index] + fold_rows(value)
    transpose_by_dp(low_t_ref, low[...], turn_low, size)
    transpose_by_dp(down_t_ref, down_grad[...], turn_low, size)
    for side in range(2):
        for at in range(chunks):
            cols = slice(at * chunk, (at + 1) * chunk)
            hidden_grad = mm_nt(down_grad[...], downs[side][cols, :])
            pre_grad = (hidden_grad * slope[side, :, cols].astype(f32)).astype(bf16)
            slope[side, :, cols] = pre_grad
            ubg_ref[side : side + 1, cols] = row_sum(pre_grad.astype(f32))
            work[...] += mm_nt(pre_grad, ups[side][:, cols])

    def settle(b):
        block = slice(b, b + BLOCK)
        grad, found = work[block, :], unit[block, :]
        summed_grad = norm_backward(grad, found, inverse[b // BLOCK], attn_gain)
        sgrad_ref[block, :] = summed_grad
        down_grad[block, :] = summed_grad.astype(bf16)
        sums[3] = sums[3] + fold_rows(grad * found)
        sums[4] = sums[4] + fold_rows(grad)

    quarter = D // 4

    def weigh(kind, n):
        left, right = ((low_t_ref, slope), (down_t_ref, hidden))[kind]
        value = mm(left[...], right[1, :, n : n + WIDE]).astype(bf16)
        cols = slice(kind * part_cols + n, kind * part_cols + n + WIDE)
        places = (0, 2, 1, 3) if size > 2 else (0, 1, 2, 3)
        for q, place in enumerate(places):
            ffn[place * quarter : (place + 1) * quarter, cols] = value[
                q * quarter : (q + 1) * quarter
            ]

    stores[1].start()
    tasks = [
        functools.partial(weigh, kind, n)
        for kind in range(2)
        for n in range(0, part_cols, WIDE)
    ]
    tasks.insert(len(tasks) // 2, stores[2].start)
    interleave([functools.partial(settle, b) for b in range(0, count, BLOCK)], tasks)
    stores[3].start()
    for index, value in enumerate(sums):
        small_ref[index : index + 1, :] = row_sum(value)
    small_ref[5:8, :] = jnp.zeros((3, D), f32)
    agrad_ref[...] = mm_nt(down_grad[...], wo_ref[...]).astype(bf16)
    transpose_by_owner(turn_low, attended, turn_work, size, groups)
    out_part = mm(turn_low[...], down_grad[...]).astype(bf16)
    share = D // groups
    out_own_ref[...] = out_part[:share]
    out_oth_ref[...] = out_part[share : 2 * share]
    for store in stores:
        store.wait()


def weights_kernel(steps, low_t_ref, down_t_ref, pre_ref, hid_ref, out_ref):
    @pl.when(pl.program_id(0) < steps)
    def _():
        out_ref[...] = mm(low_t_ref[...], pre_ref[...]).astype(bf16)

    @pl.when(pl.program_id(0) >= steps)
    def _():
        out_ref[...] = mm(down_t_ref[...], hid_ref[...]).astype(bf16)


def unshift(value, shift, window):
    whole, rest = shift // TILE, shift % TILE
    row = lax.broadcasted_iota(jnp.int32, (BLOCK, TILE), 0)
    lane = lanes((BLOCK, TILE))
    index = (lane + row - rest) & (TILE - 1)
    tiles = [
        jnp.take_along_axis(
            value[:, n : n + TILE], index, axis=1, mode="promise_in_bounds"
        )
        for n in range(0, value.shape[1], TILE)
    ]
    zero = jnp.zeros((BLOCK, TILE), f32)

    def tile(n):
        return tiles[n] if 0 <= n < len(tiles) else zero

    if rest:
        here = lane >= rest - row
        found = [
            jnp.where(here, tile(n - whole), tile(n - whole - 1)) for n in range(window // TILE)
        ]
    else:
        here = lane + row < TILE
        found = [
            jnp.where(here, tile(n - whole), tile(n - whole + 1)) for n in range(window // TILE)
        ]
    return jnp.concatenate(found, axis=1)


def backward_kernel(
    half,
    groups,
    at,
    mode,
    prob_hbm,
    key_ref,
    val_ref,
    rel_ref,
    hc_ref,
    hp_ref,
    hs_ref,
    linv_ref,
    kaug_ref,
    srow_ref,
    att_ref,
    agrad_ref,
    se_ref,
    both_t_hbm,
    stack_t_hbm,
    pos_t_hbm,
    *rest,
):
    more = rest[: {"first": 2, "middle": 0, "last": 4}[mode]]
    own_ref, oth_ref, proj_ref, tok_key_ref, tok_val_ref, small_ref = rest[len(more) :][:6]
    prob, both_t, stack_t, pos_t, spread, grads, turned, sems = rest[-8:]
    count, window = 2 * half, KEYS + half
    heads = 4
    prob_copies = [
        pltpu.make_async_copy(prob_hbm.at[at * heads + h], prob.at[h], sems.at[h])
        for h in range(heads)
    ]
    fetches = [
        pltpu.make_async_copy(source, target, sems.at[heads + index])
        for index, (source, target) in enumerate(
            ((both_t_hbm, both_t), (stack_t_hbm, stack_t), (pos_t_hbm, pos_t))
        )
    ]
    for copy in prob_copies + fetches:
        copy.start()
    share = D // groups
    if mode == "first":
        own_ref[:, 4 * QUAD :] = more[0][...]
        oth_ref[:, 4 * QUAD :] = more[1][...]
    kaug_t = kaug_ref[...]
    filler = jnp.zeros((HEAD_DIM - kaug_t.shape[0], KEYS), bf16)
    marks = jnp.concatenate([srow_ref[0:1, :], srow_ref[0:1, :]], axis=1)
    swing = 1.0 - 2.0 * marks
    key_t, val_t, rel_t = [], [], []
    proj_grads = []
    lane = lanes((count, PAIR))
    agrads, grad_x, agrad_t = [], [], []
    for pair in range(2):
        cols = slice(pair * PAIR, (pair + 1) * PAIR)
        linv = jnp.where(
            lane < HEAD_DIM,
            linv_ref[:, 2 * pair : 2 * pair + 1],
            linv_ref[:, 2 * pair + 1 : 2 * pair + 2],
        )
        agrad = (agrad_ref[:, cols].astype(f32) * linv).astype(bf16).astype(f32)
        products = agrad * att_ref[:, cols]
        agrad_t.append(agrad.astype(bf16).T)
        for head in range(2):
            base = (1 - head) * HEAD_DIM
            mine = (lane < HEAD_DIM) == (head == 0)
            weight = jnp.sum(jnp.where(mine, products, 0.0), axis=1, keepdims=True)
            high = weight.astype(bf16).astype(f32)
            grad_x.append(
                jnp.where(
                    mine,
                    agrad,
                    jnp.where(
                        lane == base, -high, jnp.where(lane == base + 1, high - weight, 0.0)
                    ),
                ).astype(bf16)
            )
    found = {}

    def head_of(ref, which):
        return ref[which * HEAD_DIM : (which + 1) * HEAD_DIM, :]

    def spreads(which):
        own = head_of(val_ref, which)
        sides = [own, kaug_t, filler] if which % 2 == 0 else [kaug_t, filler, own]
        val_x = jnp.concatenate(sides, axis=0)
        prob_copies[which].wait()

        def task(n, stop):
            spread[which % 2, :, n:stop] = mm(grad_x[which], val_x[:, n:stop])

        return [functools.partial(task, n, min(n + WIDE, KEYS)) for n in range(0, KEYS, WIDE)]

    def score_grads(which):
        buffer = which % 2

        def step(part, b):
            at_row = part * half + b
            block = slice(at_row, at_row + BLOCK)
            score_grad = prob[which, block, :].astype(f32) * spread[buffer, block, :]
            grads[buffer, block, :] = score_grad.astype(bf16)
            turned[buffer, block, :] = unshift(score_grad, half - b, window).astype(bf16)

        return [
            functools.partial(step, part, b) for part in range(2) for b in range(0, half, BLOCK)
        ]

    def gathers(which):
        buffer = which % 2
        side = slice(which % 2 * HEAD_DIM, (which % 2 + 1) * HEAD_DIM)
        key_x = jnp.concatenate([head_of(key_ref, which), kaug_t], axis=0)
        found[which] = {"value": [], "key": [], "rel": [], "content": [], "place": []}

        def down_rows(name, left, ref, n, stop):
            found[which][name].append(mm(left, ref[:, n:stop]))

        tasks = []
        for name, left, ref, end in (
            ("value", agrad_t[which // 2][side], prob.at[which], KEYS),
            ("key", head_of(hc_ref, which), grads.at[buffer], KEYS),
            ("rel", head_of(hp_ref, which), turned.at[buffer], window),
        ):
            tasks += [
                functools.partial(down_rows, name, left, ref, n, min(n + WIDE, end))
                for n in range(0, end, WIDE)
            ]

        def content(n):
            found[which]["content"].append(mm_nt(key_x, grads[buffer, n : n + half, :]))

        def placed(n):
            found[which]["place"].append(
                mm_nt(head_of(rel_ref, which), turned[buffer, n : n + half, :])
            )

        for n in (0, half):
            tasks += [functools.partial(content, n), functools.partial(placed, n)]
        return tasks

    interleave([], spreads(0))
    for which in range(heads):
        tasks = spreads(which + 1) if which + 1 < heads else []
        if which:
            tasks += gathers(which - 1)
        interleave(score_grads(which), tasks)
    interleave([], gathers(heads - 1))
    for which in range(heads):
        val_t.append(jnp.concatenate(found[which]["value"], axis=1))
        key_t.append(jnp.concatenate(found[which]["key"], axis=1))
        rel_t.append(jnp.concatenate(found[which]["rel"], axis=1))
    wide = count // TILE
    same_embed = jnp.concatenate([column_of(se_ref[0:1, :])] * wide, axis=1)
    other_embed = jnp.concatenate([column_of(se_ref[1:2, :])] * wide, axis=1)
    sums = [[] for _ in range(5)]
    for which in range(heads):
        content_head = jnp.concatenate(found[which]["content"], axis=1)
        total = content_head[HEAD_DIM : HEAD_DIM + 1]
        marked = content_head[HEAD_DIM + 4 : HEAD_DIM + 5]
        other = SCALE * (marks * total + swing * marked)
        same = SCALE * total - other
        content_grad = (SCALE * content_head[:HEAD_DIM]).astype(bf16).astype(f32)
        place_grad = (SCALE * jnp.concatenate(found[which]["place"], axis=1)).astype(bf16)
        place_grad = place_grad.astype(f32)
        segment_grad = same * head_of(same_embed, which) + other * head_of(other_embed, which)
        proj_grads.append((content_grad + place_grad + segment_grad).astype(bf16))
        head_segment = head_of(hs_ref, which)
        for index, value in enumerate(
            (content_grad, place_grad, segment_grad, same * head_segment, other * head_segment)
        ):
            sums[index].append(lane_tiles(value, jnp.add))
    lane = lanes((QUAD, TILE))
    table = jnp.zeros((QUAD, TILE), f32)
    for index, values in enumerate(sums):
        column = jnp.sum(jnp.concatenate(values, axis=0), axis=1, keepdims=True)
        table = jnp.where(lane == index, column, table)
    small_ref[...] = table.T[:8]
    proj_t = jnp.concatenate(proj_grads, axis=0)
    key_t = jnp.concatenate(key_t, axis=0).astype(bf16)
    val_t = jnp.concatenate(val_t, axis=0).astype(bf16)
    rel_t = jnp.concatenate(rel_t, axis=0).astype(bf16)
    proj_ref[...] = proj_t.T
    tok_key_ref[...] = key_t[:, MEM:].T
    tok_val_ref[...] = val_t[:, MEM:].T
    for fetch in fetches:
        fetch.wait()
    parts = (
        mm_nt(both_t[...], proj_t),
        mm_nt(stack_t[...], key_t),
        mm_nt(stack_t[...], val_t),
        mm_nt(pos_t[...], rel_t),
    )
    for index, value in enumerate(parts):
        cols = slice(index * QUAD, (index + 1) * QUAD)
        own_ref[:, cols] = value[:share].astype(bf16)
        oth_ref[:, cols] = value[share : 2 * share].astype(bf16)
    if mode == "last":
        vec_ref = rest[len(more) + 6]
        early, ubias, before, between = more
        core = lax.axis_index("tensor")
        rows = [early[0:5, :]]
        mine = [ubias[0:1, n : n + D] for n in range(0, ubias.shape[1], D)]
        theirs = [ubias[1:2, n : n + D] for n in range(0, ubias.shape[1], D)]
        for left, right in ((mine, theirs), (theirs, mine)):
            rows += [jnp.where(core == 0, a, b) for a, b in zip(left, right)]
        rows.append(
            jnp.concatenate([before[0:5, :], between[0:5, :], small_ref[0:5, :]], axis=1)
        )
        rows = jnp.concatenate(rows, axis=0)
        spare = jnp.zeros((VECTORS - rows.shape[0], D), f32)
        rows = jnp.concatenate([rows, spare], axis=0)
        packed = jnp.concatenate([rows[:, n : n + TILE] for n in range(0, D, TILE)], axis=0)
        vec_ref[...] = packed
        oth_ref[:VECTOR_ROWS, 4 * QUAD :] = packed.astype(bf16)
        oth_ref[VECTOR_ROWS:, 4 * QUAD :] = jnp.zeros((share - VECTOR_ROWS, TILE), bf16)


def rows_kernel(half, groups, sgrad_ref, *rest):
    proj, keys, vals = rest[:QUADS], rest[QUADS : 2 * QUADS], rest[2 * QUADS : 3 * QUADS]
    wq_ref, wk_ref, wv_ref, own_ref, query_ref, send_ref, both = rest[3 * QUADS :]
    member = lax.axis_index("tensor")
    wide = [jnp.concatenate([ref[...] for ref in refs], axis=1) for refs in (proj, keys, vals)]
    both[...] = mm_nt(wide[1], wk_ref[...]) + mm_nt(wide[2], wv_ref[...])
    rows = sgrad_ref[...] + mm_nt(wide[0], wq_ref[...])
    own = pl.multiple_of(member * half, half)
    other = pl.multiple_of(lax.rem(member + 1, groups) * half, half)
    send_ref[...] = both[pl.ds(other, half), :].astype(bf16)
    own_ref[...] = rows[:half] + both[pl.ds(own, half), :]
    query_ref[...] = rows[half:]


def summed(operands, terms, first, rows, width):
    values = []
    for index, at in terms:
        if rows % 16 == 0:
            value = operands[index][first : first + rows, at : at + width].astype(f32)
        else:
            value = operands[index][:, at : at + width].astype(f32)[first : first + rows]
        values.append(value)
    return functools.reduce(jnp.add, values)


def vector_width(rows):
    return TILE * max(1, VECTOR_ROWS // rows)


def fold_vectors(packed, rows):
    if rows > VECTOR_ROWS:
        return jnp.concatenate([packed, jnp.zeros((rows - VECTOR_ROWS, TILE), f32)], axis=0)
    return jnp.concatenate(
        [packed[n : n + rows] for n in range(0, VECTOR_ROWS, rows)], axis=1
    )


def unfold_vectors(block, rows):
    if rows >= VECTOR_ROWS:
        return block[:VECTOR_ROWS]
    return jnp.concatenate(
        [block[:, n : n + TILE] for n in range(0, vector_width(rows), TILE)], axis=0
    )


def summed_vectors(values, terms):
    return functools.reduce(
        jnp.add,
        [
            unfold_vectors(
                values(index)[:rows, at : at + vector_width(rows)].astype(f32), rows
            )
            for index, at, rows in terms
        ],
    )


def combine_kernel(plans, *refs):
    count = sum(pieces + (1 if vectors else 0) for _, pieces, _, vectors in plans)
    operands, outs = refs[:-count], list(refs[-count:])
    for rows, pieces, parts, vectors in plans:
        if vectors:
            packed = summed_vectors(lambda index: operands[index][...].astype(f32), vectors)
            outs.pop(0)[...] = packed
        for piece in range(pieces):
            out_ref = outs.pop(0)
            column = 0
            for width, terms in parts:
                value = summed(operands, terms, piece * rows, rows, width)
                out_ref[:, column : column + width] = value.astype(out_ref.dtype)
                column += width
            if piece and vectors:
                out_ref[:, column:] = fold_vectors(packed, rows).astype(out_ref.dtype)


def unpack_vectors(packed):
    return jnp.concatenate(
        [packed[n : n + VECTORS] for n in range(0, VECTOR_ROWS, VECTORS)], axis=1
    )


def finish_kernel(size, groups, count, plan, up_rows, *refs):
    operands, outs = refs[:count], refs[count:]
    weights, vec_outs, embed_out, up_out = outs[:5], outs[5:-2], outs[-2], outs[-1]
    place = lax.axis_index("dp") * groups + lax.axis_index("tensor")
    share = D // (size * groups)
    for target, at, width, terms in plan[0]:
        weights[target][:, at : at + width] = summed(operands, terms, 0, share, width)
    value = unpack_vectors(
        summed_vectors(lambda index: operands[index][...].astype(f32), plan[1])
    )
    mine = pltpu.roll(value, lax.rem(D - place * share, D), 1)[:, :TILE]
    rows = [row for row in range(5 + up_rows + 3) if not 5 <= row < 5 + up_rows]
    for row, out_ref in zip(rows, vec_outs):
        out_ref[...] = mine[row, :share]
    embed = jnp.concatenate([mine[5 + up_rows + 3 : 5 + up_rows + 5], jnp.zeros((6, TILE), f32)], axis=0)
    embed_out[...] = embed.T[:share, :2]
    wide = up_rows * share
    each = D // wide
    line = lax.div(place, each)
    chosen = functools.reduce(
        jnp.add,
        [jnp.where(line == r, value[5 + r : 6 + r], 0.0) for r in range(up_rows)],
    )
    chosen = jnp.broadcast_to(chosen, (8, D))
    turned = pltpu.roll(chosen, lax.rem(D - lax.rem(place, each) * wide, D), 1)[:, :TILE]
    up_out[...] = turned[0, :wide]


def whole(shape):
    return pl.BlockSpec(shape, lambda i: (0,) * len(shape))


def columns(rows, width, at=None):
    if at is None:
        return pl.BlockSpec((rows, width), lambda i: (0, i))
    return pl.BlockSpec((rows, width), lambda i: (0, at))


def row_block(rows, width, at=None):
    if at is None:
        return pl.BlockSpec((rows, width), lambda i: (i, 0))
    return pl.BlockSpec((rows, width), lambda i: (at, 0))


def scalars():
    return pl.BlockSpec(memory_space=pltpu.SMEM)


def params(size=VMEM_BYTES):
    return pltpu.CompilerParams(vmem_limit_bytes=size)


def cost(flops, bytes_accessed):
    return pl.CostEstimate(flops=flops, bytes_accessed=bytes_accessed, transcendentals=0)


def in_hbm():
    return pl.BlockSpec(memory_space=pl.ANY)


def attention_forward(
    half, size, groups, ints, memory, content, query, weights, biases, segment_rows
):
    count, window = 2 * half, KEYS + half
    coarse_rows = -(-(window // 32) // 8) * 8
    outs = (
        ((count, D), f32, columns(count, QUAD)),
        ((HEADS, count, KEYS), bf16, pl.BlockSpec((4, count, KEYS), lambda i: (i, 0, 0))),
        ((D, KEYS), bf16, row_block(QUAD, KEYS)),
        ((D, KEYS), bf16, row_block(QUAD, KEYS)),
        ((D, window), bf16, row_block(QUAD, window)),
        ((D, count), bf16, row_block(QUAD, count)),
        ((D, count), bf16, row_block(QUAD, count)),
        ((D, count), f32, row_block(QUAD, count)),
        ((count, QUADS * TILE), f32, columns(count, TILE)),
        ((16, KEYS), bf16, whole((16, KEYS))),
        ((8, half), f32, whole((8, half))),
        ((D, count), bf16, whole((D, count))),
        ((D, KEYS), bf16, whole((D, KEYS))),
        ((D, window), bf16, whole((D, window))),
    )
    return pl.pallas_call(
        functools.partial(forward_kernel, half, size, groups),
        grid=(QUADS,),
        out_shape=[jax.ShapeDtypeStruct(shape, kind) for shape, kind, _ in outs],
        in_specs=[
            scalars(),
            scalars(),
            whole((1, LEN)),
            whole((1, LEN)),
            whole((1, LEN)),
            whole((MEM, D)),
            whole((LEN, D)),
            whole((half, D)),
        ]
        + [columns(D, QUAD)] * 4
        + [whole((D,))] * 3
        + [columns(2, QUAD)],
        out_specs=[spec for _, _, spec in outs],
        scratch_shapes=[
            pltpu.VMEM((KEYS, D), bf16),
            pltpu.VMEM((count, D), bf16),
            pltpu.VMEM((window, D), bf16),
            pltpu.VMEM((count, KEYS), f32),
            pltpu.VMEM((2, 32, D // 2), f32),
            pltpu.VMEM((2, coarse_rows, D // 2), f32),
            pltpu.VMEM((8, D), f32),
            pltpu.VMEM((2, half, KEYS), f32),
            pltpu.VMEM((2, half, KEYS + PART), f32),
            pltpu.VMEM((HEAD_DIM, KEYS), bf16),
            pltpu.VMEM((half, PAIR), f32),
            pltpu.VMEM((8, LEN), f32),
            pltpu.VMEM((D, window), f32),
            pltpu.VMEM((KEYS, PAIR), bf16),
        ],
        compiler_params=params(),
        cost_estimate=cost(30_000_000_000, 40_000_000),
        name="attention_forward",
    )(*ints, memory, content, query, *weights, *biases, segment_rows)


def middle(half, size, groups, arrays, hidden_cols):
    count, share = 2 * half, D // groups
    chunk = min(hidden_cols, 768)
    outs = (
        ((half, D), bf16),
        ((half, D), bf16),
        ((D, 2 * hidden_cols), bf16),
        ((count, hidden_cols), bf16),
        ((count, hidden_cols), bf16),
        ((D, count), bf16),
        ((D, count), bf16),
        ((count, D), f32),
        ((count, D), bf16),
        ((share, D), bf16),
        ((share, D), bf16),
        ((8, D), f32),
        ((2, hidden_cols), f32),
    )
    weights = (6, 7, 8, 9)
    return pl.pallas_call(
        functools.partial(middle_kernel, half, size, groups, chunk),
        grid=(1,),
        out_shape=[jax.ShapeDtypeStruct(shape, kind) for shape, kind in outs],
        in_specs=[
            in_hbm() if i in weights else whole(array.shape) for i, array in enumerate(arrays)
        ],
        out_specs=[in_hbm() if i in (2, 3, 4) else whole(shape) for i, (shape, _) in enumerate(outs)],
        scratch_shapes=[
            pltpu.VMEM((2, count, hidden_cols), bf16),
            pltpu.VMEM((2, count, hidden_cols), bf16),
            pltpu.VMEM((D, 2 * hidden_cols), bf16),
            pltpu.VMEM((2, count, chunk), f32),
            pltpu.VMEM((count, D), f32),
            pltpu.VMEM((count, D), f32),
            pltpu.VMEM((count, D), bf16),
            pltpu.VMEM((count, D), bf16),
            pltpu.VMEM((8, FF), f32),
            pltpu.VMEM((2, D, hidden_cols), bf16),
            pltpu.VMEM((2, hidden_cols, D), bf16),
            pltpu.VMEM((D, count), bf16),
            pltpu.VMEM((D, count), f32),
            pltpu.SemaphoreType.DMA((2, 2)),
            pltpu.SemaphoreType.DMA((4,)),
        ],
        compiler_params=params(),
        cost_estimate=cost(30_000_000_000, 30_000_000),
        name="feed_forward",
    )(*arrays)


def own_weights(low_t, down_t, pre, hid):
    count, hidden_cols = pre.shape
    width = 512
    steps = hidden_cols // width
    return pl.pallas_call(
        functools.partial(weights_kernel, steps),
        grid=(2 * steps,),
        out_shape=jax.ShapeDtypeStruct((D, 2 * hidden_cols), bf16),
        in_specs=[
            whole((D, count)),
            whole((D, count)),
            pl.BlockSpec((count, width), lambda i: (0, jnp.minimum(i, steps - 1))),
            pl.BlockSpec((count, width), lambda i: (0, jnp.maximum(i - steps, 0))),
        ],
        out_specs=columns(D, width),
        compiler_params=params(COMBINE_BYTES),
        cost_estimate=cost(5_000_000_000, 10_000_000),
        name="own_weights",
    )(low_t, down_t, pre, hid)


def attention_backward(half, groups, at, mode, saved, agrad, segment_rows, extra):
    count, window, share = 2 * half, KEYS + half, D // groups
    att, prob, keys, values, rel, hc, hp, hs, linv, kaug, srow, both_t, stack_t, pos_t = saved
    width = 4 * QUAD + (D if mode == "first" else 0)
    operands = (
        (prob, in_hbm()),
        (keys, row_block(QUAD, KEYS, at)),
        (values, row_block(QUAD, KEYS, at)),
        (rel, row_block(QUAD, window, at)),
        (hc, row_block(QUAD, count, at)),
        (hp, row_block(QUAD, count, at)),
        (hs, row_block(QUAD, count, at)),
        (linv, columns(count, TILE, at)),
        (kaug, whole((16, KEYS))),
        (srow, whole((8, half))),
        (att, columns(count, QUAD, at)),
        (agrad, columns(count, QUAD, at)),
        (segment_rows, columns(2, QUAD, at)),
        (both_t, in_hbm()),
        (stack_t, in_hbm()),
        (pos_t, in_hbm()),
    ) + tuple((array, whole(array.shape)) for array in extra)
    outs = (
        ((share, width), bf16),
        ((share, width + (TILE if mode == "last" else 0)), bf16),
        ((count, QUAD), bf16),
        ((LEN, QUAD), bf16),
        ((LEN, QUAD), bf16),
        ((8, QUAD), f32),
    )
    if mode == "last":
        outs += (((VECTOR_ROWS, TILE), f32),)
    return pl.pallas_call(
        functools.partial(backward_kernel, half, groups, at, mode),
        grid=(1,),
        out_shape=[jax.ShapeDtypeStruct(shape, kind) for shape, kind in outs],
        in_specs=[spec for _, spec in operands],
        out_specs=[whole(shape) for shape, _ in outs],
        scratch_shapes=[
            pltpu.VMEM((4, count, KEYS), bf16),
            pltpu.VMEM((D, count), bf16),
            pltpu.VMEM((D, KEYS), bf16),
            pltpu.VMEM((D, window), bf16),
            pltpu.VMEM((2, count, KEYS), f32),
            pltpu.VMEM((2, count, KEYS), bf16),
            pltpu.VMEM((2, count, window), bf16),
            pltpu.SemaphoreType.DMA((7,)),
        ],
        compiler_params=params(),
        cost_estimate=cost(16_000_000_000, 16_000_000),
        name="attention_backward",
    )(*[array for array, _ in operands])


def row_gradients(half, groups, summed_grad, proj, keys, vals, weights):
    count = 2 * half
    arrays = (summed_grad, *proj, *keys, *vals, *weights)
    outs = (((half, D), f32), ((half, D), f32), ((half, D), bf16))
    return pl.pallas_call(
        functools.partial(rows_kernel, half, groups),
        grid=(1,),
        out_shape=[jax.ShapeDtypeStruct(shape, kind) for shape, kind in outs],
        in_specs=[whole(array.shape) for array in arrays],
        out_specs=[whole(shape) for shape, _ in outs],
        scratch_shapes=[pltpu.VMEM((LEN, D), f32)],
        compiler_params=params(),
        cost_estimate=cost(4_000_000_000, 10_000_000),
        name="row_gradients",
    )(*arrays)


def swap(array):
    groups = lax.axis_size("tensor")
    return lax.ppermute(array, "tensor", [(i, (i + 1) % groups) for i in range(groups)])


def across(array, masks):
    size, groups = lax.axis_size("dp"), lax.axis_size("tensor")
    pairs = [
        (place * groups + core, (place ^ masks[core]) * groups + core)
        for place in range(size)
        for core in range(groups)
    ]
    return lax.ppermute(array, ("dp", "tensor"), pairs)


def total(terms):
    return functools.reduce(jnp.add, [term.astype(f32) for term in terms])


class Chain:
    def __init__(self, parts, rows, vectors=()):
        self.parts, self.rows = parts, rows
        self.vectors = list(vectors)
        self.messages = None
        self.done = 0

    def masks(self, part, bits):
        size, groups = lax.axis_size("dp"), lax.axis_size("tensor")
        found = []
        for core in range(groups):
            order = order_of(core, size.bit_length() - 1)[self.done : self.done + bits]
            found.append(
                sum(((part >> (bits - 1 - j)) & 1) << bit for j, bit in enumerate(order))
            )
        return found

    def send(self):
        if not self.bits:
            gots = [swap(self.messages[0])]
        else:
            gots = [
                across(message, self.masks(part + 1, self.bits))
                for part, message in enumerate(self.messages)
            ]
        for got in gots:
            column = 0
            for width, terms in self.parts:
                terms.append((got, column))
                column += width
            if self.vectors:
                self.vectors.append((got, column, self.rows))
        self.pending = gots
        self.done += self.bits
        self.messages = None

    def take(self, results):
        if self.vectors:
            self.vectors = [(results.pop(0), 0, VECTOR_ROWS)]
        kept, column, parts = results.pop(0), 0, []
        for width, _ in self.parts:
            parts.append((width, [(kept, column)]))
            column += width
        self.parts = parts
        self.messages = [results.pop(0) for _ in range((1 << self.bits) - 1)]

    def replace(self, old, new):
        for index, (width, terms) in enumerate(self.parts):
            self.parts[index] = (
                width,
                [(new if array is old else array, at) for array, at in terms],
            )
        self.vectors = [(new if a is old else a, at, rows) for a, at, rows in self.vectors]


def merged(chains):
    chain = Chain(
        [part for chain in chains for part in chain.parts],
        chains[0].rows,
        [term for chain in chains for term in chain.vectors],
    )
    chain.done = chains[0].done
    chain.pending = []
    return chain


class Operands:
    def __init__(self):
        self.arrays = []

    def of(self, array):
        for index, held in enumerate(self.arrays):
            if held is array:
                return index
        self.arrays.append(array)
        return len(self.arrays) - 1

    def in_specs(self):
        return [whole(array.shape) for array in self.arrays]


def prepare(requests):
    operands, plans, outs = Operands(), [], []
    plain = any(chain.rows % (8 << bits) for chain, bits in requests)
    for chain, bits in requests:
        chain.bits = bits
        chain.rows >>= bits
        rows, pieces = chain.rows, 1 << bits
        width = sum(width for width, _ in chain.parts)
        if plain:
            results = [
                jnp.concatenate(
                    [
                        total(
                            [
                                array[piece * rows : (piece + 1) * rows, at : at + width]
                                for array, at in terms
                            ]
                        )
                        for width, terms in chain.parts
                    ],
                    axis=1,
                )
                for piece in range(pieces)
            ]
            if chain.vectors:
                packed = summed_vectors(lambda array: array, chain.vectors)
                folded = fold_vectors(packed, rows)
                results = [packed, results[0]] + [
                    jnp.concatenate([result, folded], axis=1) for result in results[1:]
                ]
            chain.take([result.astype(bf16) for result in results])
            continue
        parts = [
            (width, [(operands.of(array), at) for array, at in terms])
            for width, terms in chain.parts
        ]
        vectors = [(operands.of(array), at, held) for array, at, held in chain.vectors]
        plans.append((rows, pieces, parts, vectors))
        if vectors:
            outs.append(((VECTOR_ROWS, TILE), f32))
        outs.append(((rows, width), bf16))
        wide = width + (vector_width(rows) if vectors else 0)
        outs += [((rows, wide), bf16)] * (pieces - 1)
    if plain:
        return
    results = pl.pallas_call(
        functools.partial(combine_kernel, plans),
        grid=(1,),
        out_shape=[jax.ShapeDtypeStruct(shape, kind) for shape, kind in outs],
        in_specs=operands.in_specs(),
        out_specs=[whole(shape) for shape, _ in outs],
        compiler_params=params(COMBINE_BYTES),
        cost_estimate=cost(1_000_000_000, 8_000_000),
        name="combine",
    )(*operands.arrays)
    results = list(results)
    for chain, bits in requests:
        chain.take(results)


def launch(requests, value, waits=()):
    chains = [chain for chain, bits in requests if bits is not None] + list(waits)
    olds = [got for chain in chains for got in chain.pending]
    if olds:
        value, news = lax.optimization_barrier((value, olds))
        for chain in chains + [chain for chain, _ in requests]:
            for old, new in zip(olds, news):
                chain.replace(old, new)
        for chain in chains:
            chain.pending = []
    sums = [(chain, bits) for chain, bits in requests if bits is not None]
    if sums:
        prepare(sums)
    messages = [chain.messages for chain, _ in requests]
    value, messages = lax.optimization_barrier((value, messages))
    for (chain, bits), message in zip(requests, messages):
        chain.messages = message
        if bits is None:
            chain.bits = 0
        chain.send()
    return value


def finish(size, groups, chain):
    share = D // (size * groups)
    up_rows = FF // D
    pieces = []
    for quad, (width, terms) in enumerate(chain.parts):
        for index in range(4):
            pieces.append((index, quad * QUAD, QUAD, [(a, at + index * QUAD) for a, at in terms]))
        if width > 4 * QUAD:
            pieces.append((4, 0, D, [(a, at + 4 * QUAD) for a, at in terms]))
    if share % 8:
        blocks = {}
        for target, at, width, terms in pieces:
            blocks.setdefault(target, []).append(
                total([array[:share, c : c + width] for array, c in terms])
            )
        weights = [jnp.concatenate(blocks[target], axis=1) for target in range(5)]
        vectors = unpack_vectors(summed_vectors(lambda array: array, chain.vectors))
        place = lax.axis_index("dp") * groups + lax.axis_index("tensor")
        mine = lax.dynamic_slice_in_dim(vectors, place * share, share, 1)
        ups = lax.dynamic_slice_in_dim(
            vectors[5 : 5 + up_rows].reshape(-1), place * up_rows * share, up_rows * share, 0
        )
        late = 5 + up_rows
        return weights, [mine[r] for r in (0, 1, 2, 3, 4, late, late + 1, late + 2)], mine[
            late + 3 : late + 5
        ].T, ups
    operands = Operands()
    plan = [
        (target, at, width, [(operands.of(array), c) for array, c in terms])
        for target, at, width, terms in pieces
    ]
    vectors = [(operands.of(array), at, held) for array, at, held in chain.vectors]
    outs = [(share, D)] * 5 + [(share,)] * 8 + [(share, 2), (up_rows * share,)]
    found = pl.pallas_call(
        functools.partial(
            finish_kernel, size, groups, len(operands.arrays), (plan, vectors), up_rows
        ),
        grid=(1,),
        out_shape=[jax.ShapeDtypeStruct(shape, f32) for shape in outs],
        in_specs=operands.in_specs(),
        out_specs=[whole(shape) for shape in outs],
        compiler_params=params(COMBINE_BYTES),
        name="finish",
    )(*operands.arrays)
    return found[:5], found[5:13], found[13], found[14]


def body(
    content_in,
    query_in,
    memory,
    content_cot,
    query_cot,
    query_weight,
    key_weight,
    value_weight,
    out_weight,
    rel_weight,
    content_bias,
    position_bias,
    segment_bias,
    segment_embed,
    attn_gain,
    attn_shift,
    up_weight,
    up_bias,
    down_weight,
    down_bias,
    ffn_gain,
    ffn_shift,
    lengths,
    memory_lengths,
    segment_ids,
    orders,
    targets,
):
    groups = lax.axis_size("tensor")
    size = lax.axis_size("dp")
    steps = size.bit_length() - 1
    half = LEN // groups
    hidden_cols = up_weight.shape[1]
    up_other, down_other = swap(up_weight), swap(down_weight)
    content, query = content_in[0], query_in[0]
    segment_rows = segment_embed.T
    saved = attention_forward(
        half,
        size,
        groups,
        (lengths, memory_lengths, segment_ids, orders, targets),
        memory[0],
        content,
        query,
        (query_weight, key_weight, value_weight, rel_weight),
        (content_bias, position_bias, segment_bias),
        segment_rows,
    )
    (
        content_out,
        query_out,
        ffn_other,
        hidden,
        pre_grad,
        low_t,
        down_t,
        summed_grad,
        attended_grad,
        out_own,
        out_other,
        early_small,
        up_bias_part,
    ) = middle(
        half,
        size,
        groups,
        (
            saved[0],
            content,
            query,
            content_cot[0],
            query_cot[0],
            out_weight,
            up_weight,
            up_other,
            down_weight,
            down_other,
            up_bias,
            down_bias,
            attn_gain,
            attn_shift,
            ffn_gain,
            ffn_shift,
        ),
        hidden_cols,
    )
    ffn = Chain([(2 * hidden_cols, [])], D)
    ffn.messages = [ffn_other]
    launch([(ffn, None)], summed_grad[:1, :1])
    ffn_own = own_weights(low_t, down_t, pre_grad, hidden)
    ffn.parts[0][1].append((ffn_own, 0))
    proj, tok_keys, tok_vals, small, late = [], [], [], [], []

    def backward(at, mode, grad, extra):
        own, other, proj_part, key_part, val_part, small_part, *vectors = attention_backward(
            half, groups, at, mode, saved, grad, segment_rows, extra
        )
        proj.append(proj_part)
        tok_keys.append(key_part)
        tok_vals.append(val_part)
        small.append(small_part)
        chain = Chain(
            [(own.shape[1], [(own, 0)])],
            own.shape[0],
            [(array, 0, VECTOR_ROWS) for array in vectors],
        )
        chain.messages = [other]
        late.append(chain)

    held = launch([(ffn, 1)], attended_grad)
    backward(0, "first", held, (out_own, out_other))
    held, proj[0] = launch([(late[0], None)], (attended_grad, proj[0]))
    backward(1, "middle", held, ())
    held, proj[1] = launch(
        [(ffn, 1), (late[0], 1), (late[1], None)], (attended_grad, proj[1])
    )
    backward(2, "last", held, (early_small, up_bias_part, *small))
    xy = min(2, steps)
    proj[2] = launch(
        [(late[2], None), (ffn, 1), (late[0], 1), (late[1], 1)], proj[2]
    )
    own_rows, query_grad, row_send = row_gradients(
        half, groups, summed_grad, proj, tok_keys, tok_vals, (query_weight, key_weight, value_weight)
    )
    own_rows, row_send = launch(
        [(late[2], xy), (late[1], 1), (ffn, 1)], (own_rows, row_send)
    )
    final = merged(late)
    own_rows, row_send = launch(
        [(final, min(2, steps - final.done))], (own_rows, row_send), late
    )
    row_got = swap(row_send)
    while final.done < steps:
        own_rows = launch([(final, min(2, steps - final.done))], own_rows)
    while ffn.done < steps:
        own_rows = launch([(ffn, min(2, steps - ffn.done))], own_rows)
    content_grad = own_rows + row_got.astype(f32)
    ffn_sum = total([array[: ffn.rows] for array, _ in ffn.parts[0][1]])
    up_grad, down_grad_own = ffn_sum[:, :hidden_cols], ffn_sum[:, hidden_cols:].T
    weights, vectors, segment_grad, up_bias_grad = finish(size, groups, final)
    return (
        content_out[None],
        query_out[None],
        content_grad[None],
        query_grad[None],
        weights[0],
        weights[1],
        weights[2],
        weights[4],
        weights[3],
        vectors[5],
        vectors[6],
        vectors[7],
        segment_grad,
        vectors[3],
        vectors[4],
        up_grad,
        up_bias_grad,
        down_grad_own,
        vectors[2],
        vectors[0],
        vectors[1],
    )


def solution(mesh):
    in_specs = (
        P("dp", None, None),
        P("dp", "tensor", None),
        P("dp", None, None),
        P("dp", "tensor", None),
        P("dp", "tensor", None),
        P(),
        P(),
        P(),
        P(),
        P(),
        P(),
        P(),
        P(),
        P(),
        P(),
        P(),
        P(None, "tensor"),
        P(),
        P("tensor", None),
        P(),
        P(),
        P(),
        P("dp"),
        P("dp"),
        P("dp", None),
        P("dp", None),
        P("dp", None),
    )
    out_specs = (
        P("dp", "tensor", None),
        P("dp", "tensor", None),
        P("dp", "tensor", None),
        P("dp", "tensor", None),
        P(("dp", "tensor"), None),
        P(("dp", "tensor"), None),
        P(("dp", "tensor"), None),
        P(("dp", "tensor"), None),
        P(("dp", "tensor"), None),
        P(("dp", "tensor")),
        P(("dp", "tensor")),
        P(("dp", "tensor")),
        P(("dp", "tensor"), None),
        P(("dp", "tensor")),
        P(("dp", "tensor")),
        P("dp", "tensor"),
        P(("dp", "tensor")),
        P("tensor", "dp"),
        P(("dp", "tensor")),
        P(("dp", "tensor")),
        P(("dp", "tensor")),
    )
    return jax.shard_map(body, mesh=mesh, in_specs=in_specs, out_specs=out_specs, check_vma=False)
```

```python
import functools

import jax
import jax.numpy as jnp
from jax import lax
from jax.experimental import pallas as pl
from jax.experimental.pallas import tpu as pltpu
from jax.sharding import PartitionSpec as P

D = 768
HEADS = 12
HEAD_DIM = 64
FF = 3072
LEN = 512
MEM = 384
KEYS = MEM + LEN
QUAD = 4 * HEAD_DIM
QUADS = D // QUAD
PAIR = 2 * HEAD_DIM
SCALE = HEAD_DIM ** (-0.5)
VMEM_BYTES = 61 * 1024 * 1024
COMBINE_BYTES = 28 * 1024 * 1024
BLOCK = 32
TILE = 128
WIDE = 256
PART = 128
VECTORS = 16

VECTOR_ROWS = VECTORS * D // TILE

f32 = jnp.float32
bf16 = jnp.bfloat16
precise = lax.Precision.HIGHEST


def mm(left, right):
    return lax.dot_general(left, right, (((1,), (0,)), ((), ())), preferred_element_type=f32)


def mm_nt(left, right):
    return lax.dot_general(left, right, (((1,), (1,)), ((), ())), preferred_element_type=f32)


def mm_tn(left, right):
    return lax.dot_general(left, right, (((0,), (0,)), ((), ())), preferred_element_type=f32)


def unit_matrix(size):
    row = lax.broadcasted_iota(jnp.int32, (size, size), 0)
    return jnp.where(row == lanes((size, size)), 1.0, 0.0).astype(bf16)


def turn(value):
    width = min(value.shape[1], WIDE)
    unit = unit_matrix(width)
    blocks = [mm_nt(unit, value[:, n : n + width]) for n in range(0, value.shape[1], width)]
    return blocks[0] if len(blocks) == 1 else jnp.concatenate(blocks, axis=0)


def split(value):
    high = value.astype(bf16)
    return high, (value - high.astype(f32)).astype(bf16)


def lanes(shape):
    return lax.broadcasted_iota(jnp.int32, shape, 1)


def column_of(row):
    row = row.astype(f32)
    even = 2.0 * jnp.floor(0.5 * row)
    parts = jnp.concatenate([even, row - even, jnp.zeros((14, row.shape[1]), f32)], axis=0)
    return mm_tn(parts.astype(bf16), jnp.ones((16, TILE), bf16))


def lane_tiles(value, combine):
    tiles = [value[:, at : at + TILE] for at in range(0, value.shape[1], TILE)]
    return functools.reduce(combine, tiles)


def interleave(steps, tasks):
    done = 0
    for index, step in enumerate(steps):
        step()
        while done * len(steps) < (index + 1) * len(tasks) and done < len(tasks):
            tasks[done]()
            done += 1
    for task in tasks[done:]:
        task()


def order_of(core, bits):
    plain = list(range(bits))
    return plain[1:2] + plain[:1] + plain[2:] if core == 1 and bits > 1 else plain


def block_owner(place, core, bits):
    owner = jnp.zeros_like(place)
    for step in range(bits):
        owner = owner | (((place >> (bits - 1 - step)) & 1) << step)
    if bits > 1:
        swapped = (owner & ~3) | ((owner & 1) << 1) | ((owner >> 1) & 1)
        owner = jnp.where(core == 1, swapped, owner)
    return owner ^ lax.axis_index("dp")


def one_hot(source):
    return jnp.where(lanes((source.shape[0], D)) == source, 1.0, 0.0).astype(bf16)


def owner_rows(size, groups):
    share = D // (size * groups)
    row = lax.broadcasted_iota(jnp.int32, (D, 1), 0)
    side, rest = lax.div(row, size * share), lax.rem(row, size * share)
    core = lax.rem(lax.axis_index("tensor") + side, groups)
    owner = block_owner(lax.div(rest, share), core, size.bit_length() - 1)
    return one_hot((owner * groups + core) * share + lax.rem(rest, share))


def shared_rows(size, core):
    share = D // size
    row = lax.broadcasted_iota(jnp.int32, (D, 1), 0)
    owner = block_owner(lax.div(row, share), core, size.bit_length() - 1)
    return one_hot(owner * share + lax.rem(row, share))


def transpose_by_owner(out_ref, value, work, size, groups):
    share = D // (size * groups)
    if share % 8 or (2 * share) % 16:
        out_ref[...] = mm_nt(owner_rows(size, groups), value).astype(bf16)
        return
    width = value.shape[0]
    for n in range(0, D, WIDE):
        work[n : n + WIDE, :width] = turn(value[:, n : n + WIDE])
    bits = size.bit_length() - 1
    blocks = []
    for block in range(size * groups):
        core = lax.rem(lax.axis_index("tensor") + block // size, groups)
        owner = block_owner(jnp.int32(block % size), core, bits)
        at = pl.multiple_of((owner * groups + core) * share, 8)
        blocks.append(work[pl.ds(at, share), :width])
        if block % 2:
            out_ref[(block - 1) * share : (block + 1) * share, :] = jnp.concatenate(
                blocks, axis=0
            ).astype(bf16)
            blocks = []


def transpose_by_dp(out_ref, value, work, size):
    share = D // size
    core = lax.axis_index("tensor")
    if share % 16:
        out_ref[...] = mm_nt(shared_rows(size, core), value).astype(bf16)
        return
    for n in range(0, D, WIDE):
        work[n : n + WIDE, :] = turn(value[:, n : n + WIDE]).astype(bf16)
    for block in range(size):
        owner = block_owner(jnp.int32(block), core, size.bit_length() - 1)
        at = pl.multiple_of(owner * share, 16)
        out_ref[block * share : (block + 1) * share, :] = work[pl.ds(at, share), :]


def forward_kernel(
    half,
    length_ref,
    mem_length_ref,
    seg_ref,
    ord_ref,
    tgt_ref,
    memory_ref,
    content_ref,
    query_ref,
    wq_ref,
    wk_ref,
    wv_ref,
    wr_ref,
    cb_ref,
    pb_ref,
    sb_ref,
    se_ref,
    att_ref,
    prob_ref,
    key_ref,
    val_ref,
    rel_ref,
    hc_ref,
    hp_ref,
    hs_ref,
    linv_ref,
    kaug_ref,
    srow_ref,
    pos_ref,
    stack,
    both,
    pos,
    bias,
    fine,
    coarse,
    vectors,
    scores,
    places,
    kaug_t,
    scol,
    seg_row,
    kaug_work,
    order_work,
    seg_work,
):
    window, reach = KEYS + half, KEYS + PART
    first = pl.multiple_of(lax.axis_index("tensor") * half, half)
    step_id = pl.program_id(0)

    @pl.when(step_id == 0)
    def _():
        stack[:MEM, :] = memory_ref[...]
        stack[MEM:, :] = content_ref[...]
        both[:half, :] = content_ref[pl.ds(first, half), :]
        both[half:, :] = query_ref[...]
        vectors[0:1, :] = cb_ref[...][None, :]
        vectors[1:2, :] = pb_ref[...][None, :]
        vectors[2:3, :] = sb_ref[...][None, :]
        step = lax.broadcasted_iota(jnp.int32, (1, D // 2), 1).astype(f32) * (2.0 / D)
        inverse = 1.0 / jnp.power(jnp.full((1, D // 2), 10000.0, f32), step)
        coarse_rows = coarse.shape[1]
        top = (MEM + half + first).astype(f32)
        angle = (
            top - 32.0 * lax.broadcasted_iota(jnp.int32, (coarse_rows, 1), 0).astype(f32)
        ) * inverse
        coarse[0] = jnp.sin(angle)
        coarse[1] = jnp.cos(angle)
        small = lax.broadcasted_iota(jnp.int32, (32, 1), 0).astype(f32) * inverse
        fine[0] = jnp.sin(small)
        fine[1] = jnp.cos(small)
        for a in range(window // 32):
            sa, ca = coarse[0, a : a + 1, :], coarse[1, a : a + 1, :]
            sb, cb = fine[0], fine[1]
            pos[a * 32 : (a + 1) * 32, : D // 2] = (sa * cb - ca * sb).astype(bf16)
            pos[a * 32 : (a + 1) * 32, D // 2 :] = (ca * cb + sa * sb).astype(bf16)
        never = float(LEN + 1)
        mem_at = lax.broadcasted_iota(jnp.int32, (1, MEM), 1)
        tok_at = lax.broadcasted_iota(jnp.int32, (1, LEN), 1)
        open_from = jnp.concatenate(
            [
                jnp.where(mem_at >= MEM - mem_length_ref[0], -1.0, never),
                jnp.where(
                    tok_at < length_ref[0],
                    jnp.where(tgt_ref[...] == 0, -1.0, ord_ref[...].astype(f32)),
                    never,
                ),
            ],
            axis=1,
        )
        order_col = column_of(ord_ref[...])
        seg_col = column_of(seg_ref[...])
        kaug_lane = lanes((LEN, PAIR)) % HEAD_DIM
        kaug_work[:MEM, :] = (lanes((MEM, PAIR)) % HEAD_DIM < 4).astype(f32).astype(bf16)
        kaug_work[MEM:, :] = jnp.where(
            kaug_lane < 4, 1.0, jnp.where(kaug_lane < 6, seg_col, 0.0)
        ).astype(bf16)
        kaug_t[...] = kaug_work[...].T[:HEAD_DIM]
        kaug_ref[...] = kaug_t[:16, :]
        order_work[...] = order_col
        own_order = order_work[pl.ds(first, half), :][:, :1]
        seg_work[...] = seg_col
        scol[...] = seg_work[pl.ds(first, half), :]
        seen = open_from <= own_order
        bias[:half, :] = jnp.where(seen, 0.0, -1e30)
        key_at = lax.broadcasted_iota(jnp.int32, (half, KEYS), 1)
        row_at = lax.broadcasted_iota(jnp.int32, (half, KEYS), 0)
        seen_q = seen & (key_at - MEM != row_at + first)
        bias[half:, :] = jnp.where(seen_q, 0.0, -1e30)
        seg_row[0:1, :] = seg_ref[...].astype(f32)
        srow_ref[...] = jnp.broadcast_to(seg_row[0:1, pl.ds(first, half)], srow_ref.shape)
        pos_ref[...] = pos[...]

    here = pl.ds(pl.multiple_of(step_id * QUAD, QUAD), QUAD)
    keys = mm(stack[...], wk_ref[...]).astype(bf16)
    values = mm(stack[...], wv_ref[...]).astype(bf16)
    rel = mm(pos[...], wr_ref[...]).astype(bf16)
    projection = mm(both[...], wq_ref[...])
    head_content = (projection + vectors[0:1, here]).astype(bf16)
    head_position = (projection + vectors[1:2, here]).astype(bf16)
    head_segment = projection + vectors[2:3, here]
    keys_t, values_t, rel_t = [turn(value).astype(bf16) for value in (keys, values, rel)]
    key_ref[...] = keys_t
    val_ref[...] = values_t
    rel_ref[...] = rel_t
    hs_ref[...] = head_segment
    head_content = (head_content.astype(f32) * SCALE).astype(bf16)
    head_position = (head_position.astype(f32) * SCALE).astype(bf16)
    hc_ref[...] = turn(head_content).astype(bf16)
    hp_ref[...] = turn(head_position).astype(bf16)
    row_head = lax.broadcasted_iota(jnp.int32, (QUAD, QUAD), 0) // HEAD_DIM
    at = lanes((QUAD, QUAD)) - ((row_head // 2) * PAIR + (1 - row_head % 2) * HEAD_DIM)
    place_same = jnp.where((at >= 0) & (at < 2), 1.0, 0.0).astype(bf16)
    place_step = jnp.where((at >= 2) & (at < 6), 1.0, 0.0).astype(bf16)
    same, other = se_ref[0:1, :], se_ref[1:2, :]
    terms = functools.reduce(
        jnp.add,
        [mm(part, place_same) for part in split(head_segment * same)]
        + [mm(part, place_step) for part in split(head_segment * (other - same))],
    )
    marks = jnp.concatenate([scol[...], scol[...]], axis=0)
    marks = jnp.concatenate([marks, marks], axis=1)
    lane6 = lanes((2 * half, QUAD)) % HEAD_DIM
    factor = jnp.where(lane6 < 2, 1.0, jnp.where(lane6 < 4, marks, 1.0 - 2.0 * marks))
    terms = SCALE * (terms * factor)
    high = terms.astype(bf16)
    low = (terms - high.astype(f32)).astype(bf16)
    qaug = jnp.where(lane6 % 2 == 0, high, low)
    units = [(pair, head, part) for pair in range(2) for head in range(2) for part in range(2)]
    key_x = []
    for which in range(4):
        own = keys_t[which * HEAD_DIM : (which + 1) * HEAD_DIM]
        sides = [own, kaug_t[...]] if which % 2 == 0 else [kaug_t[...], own]
        key_x.append(jnp.concatenate(sides, axis=0))
    peaks, totals, outs = {}, {}, {}

    def products(index):
        pair, head, part = units[index]
        cols, rows = slice(pair * PAIR, (pair + 1) * PAIR), slice(part * half, (part + 1) * half)
        slot, which = index % 2, pair * 2 + head
        row_mine = (lanes((half, PAIR)) < HEAD_DIM) == (head == 0)
        query_x = jnp.where(row_mine, head_content[rows, cols], qaug[rows, cols])
        place_x = jnp.where(row_mine, head_position[rows, cols], jnp.zeros((), bf16))

        def score(n, stop):
            scores[slot, :, n:stop] = mm(query_x, key_x[which][:, n:stop])

        def placed(r, n, stop):
            at = half - r - PART
            places[slot, r : r + PART, n:stop] = mm(
                place_x[r : r + PART], rel_t[cols, at + n : at + stop]
            )

        return [
            functools.partial(placed, r, n, min(n + WIDE, reach))
            for r in range(0, half, PART)
            for n in range(0, reach, WIDE)
        ] + [
            functools.partial(score, n, min(n + WIDE, KEYS)) for n in range(0, KEYS, WIDE)
        ]

    def softmax(index):
        pair, head, part = units[index]
        slot, which = index % 2, pair * 2 + head
        tops, pieces = [], []

        def join(b):
            block = slice(b, b + BLOCK)
            shifted = pltpu.roll(
                places[slot, block, :], (reach - PART + b % PART) % reach, 1, stride=1, stride_axis=0
            )[:, :KEYS]
            score = (
                scores[slot, block, :]
                + shifted
                + bias[part * half + b : part * half + b + BLOCK, :]
            )
            scores[slot, block, :] = score
            tops.append(lane_tiles(score, jnp.maximum))

        def peak():
            peaks[index] = jnp.max(jnp.concatenate(tops, axis=0), axis=1, keepdims=True)

        def power(b):
            block = slice(b, b + BLOCK)
            prob = jnp.exp(scores[slot, block, :] - peaks[index][block])
            pieces.append(lane_tiles(prob, jnp.add))
            prob_ref[which, part * half + b : part * half + b + BLOCK, :] = prob.astype(bf16)

        def finish():
            totals[index] = 1.0 / jnp.sum(
                jnp.concatenate(pieces, axis=0), axis=1, keepdims=True
            )

        blocks = range(0, half, BLOCK)
        return (
            [functools.partial(join, b) for b in blocks]
            + [peak]
            + [functools.partial(power, b) for b in blocks]
            + [finish]
        )

    def mixture(index):
        pair, head, part = units[index]
        rows = slice(part * half, (part + 1) * half)
        which = pair * 2 + head
        outs[index] = mm_nt(
            values_t[which * HEAD_DIM : (which + 1) * HEAD_DIM], prob_ref[which, rows, :]
        )

    interleave([], products(0))
    for index in range(len(units)):
        tasks = products(index + 1) if index + 1 < len(units) else []
        if index:
            tasks.append(functools.partial(mixture, index - 1))
        interleave(softmax(index), tasks)
    mixture(len(units) - 1)
    sums = [
        jnp.concatenate([totals[2 * which], totals[2 * which + 1]], axis=0) for which in range(4)
    ]
    mixed = jnp.concatenate(
        [
            jnp.concatenate([outs[2 * which], outs[2 * which + 1]], axis=1) for which in range(4)
        ],
        axis=0,
    )
    mixed = functools.reduce(jnp.add, [turn(part) for part in split(mixed)])
    mine = lanes((2 * half, PAIR)) < HEAD_DIM
    for pair in range(2):
        cols = slice(pair * PAIR, (pair + 1) * PAIR)
        att_ref[:, cols] = mixed[:, cols] * jnp.where(mine, sums[2 * pair], sums[2 * pair + 1])
    lane = lanes((2 * half, TILE))
    linv_ref[...] = jnp.where(
        lane == 0, sums[0], jnp.where(lane == 1, sums[1], jnp.where(lane == 2, sums[2], sums[3]))
    )


def norm_forward(summed, gain, shift):
    center = summed - jnp.mean(summed, axis=1, keepdims=True)
    inv = lax.rsqrt(jnp.mean(center * center, axis=1, keepdims=True) + 1e-06)
    unit = center * inv
    return unit, inv, unit * gain + shift


def norm_backward(grad, unit, inv, gain):
    scaled = grad * gain
    return inv * (
        scaled
        - jnp.mean(scaled, axis=1, keepdims=True)
        - unit * jnp.mean(scaled * unit, axis=1, keepdims=True)
    )


def row_sum(value):
    return jnp.sum(value, axis=0, keepdims=True)


def gelu_parts(x):
    square = x * x
    tanh = jnp.tanh((0.7978845608028654 * x) * (1.0 + 0.044715 * square))
    rise = 0.5 * (1.0 + tanh)
    grad = rise + (0.5 * x) * (1.0 - tanh * tanh) * (
        0.7978845608028654 * (1.0 + 0.134145 * square)
    )
    return x * rise, grad


def fold_rows(value):
    return functools.reduce(jnp.add, [value[r : r + 8] for r in range(0, value.shape[0], 8)])


def middle_kernel(
    half,
    size,
    groups,
    chunk,
    att_ref,
    content_ref,
    query_ref,
    ccot_ref,
    qcot_ref,
    wo_ref,
    up_own_hbm,
    up_oth_hbm,
    down_own_hbm,
    down_oth_hbm,
    ubias_ref,
    dbias_ref,
    again_ref,
    ashift_ref,
    fgain_ref,
    fshift_ref,
    cout_ref,
    qout_ref,
    ffn_own_ref,
    ffn_oth_ref,
    sgrad_ref,
    agrad_ref,
    out_own_ref,
    out_oth_ref,
    small_ref,
    ubg_ref,
    hidden,
    slope,
    pre,
    work,
    unit,
    low,
    down_grad,
    vectors,
    up,
    down,
    low_t,
    down_t,
    turn_low,
    turn_down,
    attended_t,
    turn_work,
    sems,
):
    count = 2 * half
    member = lax.axis_index("tensor")
    first = pl.multiple_of(member * half, half)
    fetches = [
        pltpu.make_async_copy(source, target.at[side], sems.at[kind, side])
        for kind, side, source, target in (
            (0, 0, up_own_hbm, up),
            (1, 0, down_own_hbm, down),
            (0, 1, up_oth_hbm, up),
            (1, 1, down_oth_hbm, down),
        )
    ]
    for fetch in fetches:
        fetch.start()
    ups, downs = (up.at[0], up.at[1]), (down.at[0], down.at[1])
    part_cols = up.shape[2]
    chunks = part_cols // chunk
    vectors[0:1, :] = ubias_ref[...][None, :]
    attended = att_ref[...].astype(bf16)
    work[...] = mm(attended, wo_ref[...])
    attn_gain, attn_shift = again_ref[...][None, :], ashift_ref[...][None, :]
    ffn_gain, ffn_shift = fgain_ref[...][None, :], fshift_ref[...][None, :]
    down_bias = dbias_ref[...][None, :]
    inverse = []
    for b in range(0, count, BLOCK):
        block = slice(b, b + BLOCK)
        if b < half:
            rows_in = content_ref[pl.ds(pl.multiple_of(first + b, BLOCK), BLOCK), :]
        else:
            rows_in = query_ref[b - half : b - half + BLOCK, :]
        found, inv, normed = norm_forward(
            work[block, :] + rows_in.astype(f32), attn_gain, attn_shift
        )
        unit[block, :] = found
        inverse.append(inv)
        low[block, :] = normed.astype(bf16)
        work[block, :] = normed + down_bias
    for fetch in fetches:
        fetch.wait()
    pieces = [(side, at) for side in range(2) for at in range(chunks)]

    def rise(index):
        side, at = pieces[index]

        def task(n):
            pre[index % 2, :, n : n + WIDE] = mm(
                low[...], ups[side][:, at * chunk + n : at * chunk + n + WIDE]
            )

        return [functools.partial(task, n) for n in range(0, chunk, WIDE)]

    def bend(index):
        side, at = pieces[index]
        cols = slice(at * chunk, (at + 1) * chunk)
        start = lax.rem(member + side, 2) * part_cols + at * chunk
        bias = vectors[0:1, pl.ds(pl.multiple_of(start, TILE), chunk)]

        def step(b):
            block = slice(b, b + BLOCK)
            act, grad = gelu_parts(pre[index % 2, block, :] + bias)
            hidden[side, block, cols] = act.astype(bf16)
            slope[side, block, cols] = grad.astype(bf16)

        return [functools.partial(step, b) for b in range(0, count, BLOCK)]

    def fall(index):
        side, at = pieces[index]
        cols = slice(at * chunk, (at + 1) * chunk)

        def task(n):
            work[:, n : n + WIDE] += mm(hidden[side, :, cols], downs[side][cols, n : n + WIDE])

        return [functools.partial(task, n) for n in range(0, D, WIDE)]

    interleave([], rise(0))
    for index in range(len(pieces)):
        tasks = rise(index + 1) if index + 1 < len(pieces) else []
        if index:
            tasks += fall(index - 1)
        interleave(bend(index), tasks)
    interleave([], fall(len(pieces) - 1))
    sums = [jnp.zeros((8, D), f32) for _ in range(5)]
    for b in range(0, count, BLOCK):
        block = slice(b, b + BLOCK)
        found, inv, out = norm_forward(work[block, :], ffn_gain, ffn_shift)
        if b < half:
            cout_ref[block, :] = out.astype(bf16)
            cot = ccot_ref[block, :].astype(f32)
        else:
            block_q = slice(b - half, b - half + BLOCK)
            qout_ref[block_q, :] = out.astype(bf16)
            cot = qcot_ref[block_q, :].astype(f32)
        residual_grad = norm_backward(cot, found, inv, ffn_gain)
        rounded = residual_grad.astype(bf16)
        down_grad[block, :] = rounded
        work[block, :] = residual_grad
        for index, value in enumerate((cot * found, cot, rounded.astype(f32))):
            sums[index] = sums[index] + fold_rows(value)
    transpose_by_dp(low_t, low[...], turn_low, size)
    transpose_by_dp(down_t, down_grad[...], turn_down, size)
    for side in range(2):
        for at in range(chunks):
            cols = slice(at * chunk, (at + 1) * chunk)
            hidden_grad = mm_nt(down_grad[...], downs[side][cols, :])
            pre_grad = (hidden_grad * slope[side, :, cols].astype(f32)).astype(bf16)
            slope[side, :, cols] = pre_grad
            ubg_ref[side : side + 1, cols] = row_sum(pre_grad.astype(f32))
            work[...] += mm_nt(pre_grad, ups[side][:, cols])

    def settle(b):
        block = slice(b, b + BLOCK)
        grad, found = work[block, :], unit[block, :]
        summed_grad = norm_backward(grad, found, inverse[b // BLOCK], attn_gain)
        sgrad_ref[block, :] = summed_grad
        down_grad[block, :] = summed_grad.astype(bf16)
        sums[3] = sums[3] + fold_rows(grad * found)
        sums[4] = sums[4] + fold_rows(grad)

    quarter = D // 4

    def weigh(side, kind, n):
        left, right = ((low_t, slope), (down_t, hidden))[kind]
        value = mm(left[...], right[side, :, n : n + WIDE]).astype(bf16)
        target = (ffn_own_ref, ffn_oth_ref)[side]
        cols = slice(kind * part_cols + n, kind * part_cols + n + WIDE)
        places = (0, 2, 1, 3) if side == 1 and size > 2 else (0, 1, 2, 3)
        for q, place in enumerate(places):
            target[place * quarter : (place + 1) * quarter, cols] = value[
                q * quarter : (q + 1) * quarter
            ]

    tasks = [
        functools.partial(weigh, side, kind, n)
        for side in (1, 0)
        for kind in range(2)
        for n in range(0, part_cols, WIDE)
    ]
    interleave([functools.partial(settle, b) for b in range(0, count, BLOCK)], tasks)
    for index, value in enumerate(sums):
        small_ref[index : index + 1, :] = row_sum(value)
    small_ref[5:8, :] = jnp.zeros((3, D), f32)
    agrad_ref[...] = mm_nt(down_grad[...], wo_ref[...]).astype(bf16)
    transpose_by_owner(attended_t, attended, turn_work, size, groups)
    out_part = mm(attended_t[...], down_grad[...]).astype(bf16)
    share = D // groups
    out_own_ref[...] = out_part[:share]
    out_oth_ref[...] = out_part[share : 2 * share]


def unshift(value, shift, window):
    whole, rest = shift // TILE, shift % TILE
    row = lax.broadcasted_iota(jnp.int32, (BLOCK, TILE), 0)
    lane = lanes((BLOCK, TILE))
    index = (lane + row - rest) & (TILE - 1)
    tiles = [
        jnp.take_along_axis(
            value[:, n : n + TILE], index, axis=1, mode="promise_in_bounds"
        )
        for n in range(0, value.shape[1], TILE)
    ]
    zero = jnp.zeros((BLOCK, TILE), f32)

    def tile(n):
        return tiles[n] if 0 <= n < len(tiles) else zero

    if rest:
        here = lane >= rest - row
        found = [
            jnp.where(here, tile(n - whole), tile(n - whole - 1)) for n in range(window // TILE)
        ]
    else:
        here = lane + row < TILE
        found = [
            jnp.where(here, tile(n - whole), tile(n - whole + 1)) for n in range(window // TILE)
        ]
    return jnp.concatenate(found, axis=1)


def backward_kernel(
    half,
    groups,
    at,
    mode,
    prob_hbm,
    key_ref,
    val_ref,
    rel_ref,
    hc_ref,
    hp_ref,
    hs_ref,
    linv_ref,
    kaug_ref,
    srow_ref,
    att_ref,
    agrad_ref,
    se_ref,
    both_t_hbm,
    stack_t_hbm,
    pos_t_hbm,
    *rest,
):
    more = rest[: {"first": 2, "middle": 0, "last": 4}[mode]]
    own_ref, oth_ref, proj_ref, tok_key_ref, tok_val_ref, small_ref = rest[len(more) :][:6]
    prob, both_t, stack_t, pos_t, spread, grads, turned, sems = rest[-8:]
    count, window = 2 * half, KEYS + half
    heads = 4
    prob_copies = [
        pltpu.make_async_copy(prob_hbm.at[at * heads + h], prob.at[h], sems.at[h])
        for h in range(heads)
    ]
    fetches = [
        pltpu.make_async_copy(source, target, sems.at[heads + index])
        for index, (source, target) in enumerate(
            ((both_t_hbm, both_t), (stack_t_hbm, stack_t), (pos_t_hbm, pos_t))
        )
    ]
    for copy in prob_copies + fetches:
        copy.start()
    share = D // groups
    if mode == "first":
        own_ref[:, 4 * QUAD :] = more[0][...]
        oth_ref[:, 4 * QUAD :] = more[1][...]
    kaug_t = kaug_ref[...]
    filler = jnp.zeros((HEAD_DIM - kaug_t.shape[0], KEYS), bf16)
    marks = jnp.concatenate([srow_ref[0:1, :], srow_ref[0:1, :]], axis=1)
    swing = 1.0 - 2.0 * marks
    key_t, val_t, rel_t = [], [], []
    lane = lanes((count, PAIR))
    agrads, grad_x, agrad_t = [], [], []
    for pair in range(2):
        cols = slice(pair * PAIR, (pair + 1) * PAIR)
        linv = jnp.where(
            lane < HEAD_DIM,
            linv_ref[:, 2 * pair : 2 * pair + 1],
            linv_ref[:, 2 * pair + 1 : 2 * pair + 2],
        )
        agrad = (agrad_ref[:, cols].astype(f32) * linv).astype(bf16).astype(f32)
        products = agrad * att_ref[:, cols]
        agrad_t.append(turn(agrad.astype(bf16)).astype(bf16))
        for head in range(2):
            base = (1 - head) * HEAD_DIM
            mine = (lane < HEAD_DIM) == (head == 0)
            weight = jnp.sum(jnp.where(mine, products, 0.0), axis=1, keepdims=True)
            high = weight.astype(bf16).astype(f32)
            grad_x.append(
                jnp.where(
                    mine,
                    agrad,
                    jnp.where(
                        lane == base, -high, jnp.where(lane == base + 1, high - weight, 0.0)
                    ),
                ).astype(bf16)
            )
    found = {}

    def head_of(ref, which):
        return ref[which * HEAD_DIM : (which + 1) * HEAD_DIM, :]

    def spreads(which):
        own = head_of(val_ref, which)
        sides = [own, kaug_t, filler] if which % 2 == 0 else [kaug_t, filler, own]
        val_x = jnp.concatenate(sides, axis=0)
        prob_copies[which].wait()

        def task(n, stop):
            spread[which % 2, :, n:stop] = mm(grad_x[which], val_x[:, n:stop])

        return [functools.partial(task, n, min(n + WIDE, KEYS)) for n in range(0, KEYS, WIDE)]

    def score_grads(which):
        buffer = which % 2

        def step(part, b):
            at_row = part * half + b
            block = slice(at_row, at_row + BLOCK)
            score_grad = prob[which, block, :].astype(f32) * spread[buffer, block, :]
            grads[buffer, block, :] = score_grad.astype(bf16)
            turned[buffer, block, :] = unshift(score_grad, half - b, window).astype(bf16)

        return [
            functools.partial(step, part, b) for part in range(2) for b in range(0, half, BLOCK)
        ]

    def gathers(which):
        buffer = which % 2
        side = slice(which % 2 * HEAD_DIM, (which % 2 + 1) * HEAD_DIM)
        key_x = jnp.concatenate([head_of(key_ref, which), kaug_t], axis=0)
        found[which] = {"value": [], "key": [], "rel": [], "content": [], "place": []}

        def down_rows(name, left, ref, n, stop):
            found[which][name].append(mm(left, ref[:, n:stop]))

        tasks = []
        for name, left, ref, end in (
            ("value", agrad_t[which // 2][side], prob.at[which], KEYS),
            ("key", head_of(hc_ref, which), grads.at[buffer], KEYS),
            ("rel", head_of(hp_ref, which), turned.at[buffer], window),
        ):
            tasks += [
                functools.partial(down_rows, name, left, ref, n, min(n + WIDE, end))
                for n in range(0, end, WIDE)
            ]

        def content(n):
            found[which]["content"].append(mm_nt(key_x, grads[buffer, n : n + half, :]))

        def placed(n):
            found[which]["place"].append(
                mm_nt(head_of(rel_ref, which), turned[buffer, n : n + half, :])
            )

        for n in (0, half):
            tasks += [functools.partial(content, n), functools.partial(placed, n)]
        return tasks

    interleave([], spreads(0))
    for which in range(heads):
        tasks = spreads(which + 1) if which + 1 < heads else []
        if which:
            tasks += gathers(which - 1)
        interleave(score_grads(which), tasks)
    interleave([], gathers(heads - 1))
    for which in range(heads):
        val_t.append(jnp.concatenate(found[which]["value"], axis=1))
        key_t.append(jnp.concatenate(found[which]["key"], axis=1))
        rel_t.append(jnp.concatenate(found[which]["rel"], axis=1))
    same, other, contents, places = [], [], [], []
    for which in range(heads):
        content_head = jnp.concatenate(found[which]["content"], axis=1)
        total = content_head[HEAD_DIM : HEAD_DIM + 1]
        marked = content_head[HEAD_DIM + 4 : HEAD_DIM + 5]
        other.append(SCALE * (marks * total + swing * marked))
        same.append(SCALE * total - other[-1])
        contents.append((SCALE * content_head[:HEAD_DIM]).astype(bf16))
        places.append((SCALE * jnp.concatenate(found[which]["place"], axis=1)).astype(bf16))
    contents, places = jnp.concatenate(contents, axis=0), jnp.concatenate(places, axis=0)
    term_high, term_low = split(jnp.concatenate(same + other, axis=0))
    line = lax.broadcasted_iota(jnp.int32, (2 * heads, QUAD), 0)
    mine = line % heads == lanes((2 * heads, QUAD)) // HEAD_DIM
    embed = jnp.where(line < heads, se_ref[0:1, :], se_ref[1:2, :])
    embed_high, embed_low = split(jnp.where(mine, embed, 0.0))
    segment_grad = mm_tn(
        jnp.concatenate([embed_high, embed_high, embed_low, embed_low], axis=0),
        jnp.concatenate([term_high, term_low, term_high, term_low], axis=0),
    )
    proj_t = (contents.astype(f32) + places.astype(f32) + segment_grad).astype(bf16)
    ones = jnp.ones((16, count), bf16)
    small_ref[0:1, :] = mm_nt(ones, contents)[0:1]
    small_ref[1:2, :] = mm_nt(ones, places)[0:1]
    small_ref[2:3, :] = functools.reduce(
        jnp.add, [mm_nt(ones, part)[0:1] for part in split(segment_grad)]
    )
    terms = jnp.concatenate([term_high, term_low], axis=0)
    embed_grad = functools.reduce(jnp.add, [mm(terms, part) for part in split(hs_ref[...])])
    embed_grad = jnp.where(mine, embed_grad[: 2 * heads] + embed_grad[2 * heads :], 0.0)
    small_ref[3:4, :] = row_sum(embed_grad[:heads])
    small_ref[4:5, :] = row_sum(embed_grad[heads:])
    small_ref[5:8, :] = jnp.zeros((3, QUAD), f32)
    key_t = jnp.concatenate(key_t, axis=0).astype(bf16)
    val_t = jnp.concatenate(val_t, axis=0).astype(bf16)
    rel_t = jnp.concatenate(rel_t, axis=0).astype(bf16)
    proj_ref[...] = turn(proj_t).astype(bf16)
    tok_key_ref[...] = turn(key_t[:, MEM:]).astype(bf16)
    tok_val_ref[...] = turn(val_t[:, MEM:]).astype(bf16)
    for fetch in fetches:
        fetch.wait()
    parts = (
        mm_nt(both_t[...], proj_t),
        mm_nt(stack_t[...], key_t),
        mm_nt(stack_t[...], val_t),
        mm_nt(pos_t[...], rel_t),
    )
    for index, value in enumerate(parts):
        cols = slice(index * QUAD, (index + 1) * QUAD)
        own_ref[:, cols] = value[:share].astype(bf16)
        oth_ref[:, cols] = value[share : 2 * share].astype(bf16)
    if mode == "last":
        vec_ref = rest[len(more) + 6]
        early, ubias, before, between = more
        core = lax.axis_index("tensor")
        rows = [early[0:5, :]]
        mine = [ubias[0:1, n : n + D] for n in range(0, ubias.shape[1], D)]
        theirs = [ubias[1:2, n : n + D] for n in range(0, ubias.shape[1], D)]
        for left, right in ((mine, theirs), (theirs, mine)):
            rows += [jnp.where(core == 0, a, b) for a, b in zip(left, right)]
        rows.append(
            jnp.concatenate([before[0:5, :], between[0:5, :], small_ref[0:5, :]], axis=1)
        )
        rows = jnp.concatenate(rows, axis=0)
        spare = jnp.zeros((VECTORS - rows.shape[0], D), f32)
        rows = jnp.concatenate([rows, spare], axis=0)
        packed = jnp.concatenate([rows[:, n : n + TILE] for n in range(0, D, TILE)], axis=0)
        vec_ref[...] = packed
        oth_ref[:VECTOR_ROWS, 4 * QUAD :] = packed.astype(bf16)
        oth_ref[VECTOR_ROWS:, 4 * QUAD :] = jnp.zeros((share - VECTOR_ROWS, TILE), bf16)


def rows_kernel(half, groups, sgrad_ref, *rest):
    proj, keys, vals = rest[:QUADS], rest[QUADS : 2 * QUADS], rest[2 * QUADS : 3 * QUADS]
    wq_ref, wk_ref, wv_ref, own_ref, query_ref, send_ref, both = rest[3 * QUADS :]
    member = lax.axis_index("tensor")
    wide = [jnp.concatenate([ref[...] for ref in refs], axis=1) for refs in (proj, keys, vals)]
    both[...] = mm_nt(wide[1], wk_ref[...]) + mm_nt(wide[2], wv_ref[...])
    rows = sgrad_ref[...] + mm_nt(wide[0], wq_ref[...])
    own = pl.multiple_of(member * half, half)
    other = pl.multiple_of(lax.rem(member + 1, groups) * half, half)
    send_ref[...] = both[pl.ds(other, half), :].astype(bf16)
    own_ref[...] = rows[:half] + both[pl.ds(own, half), :]
    query_ref[...] = rows[half:]


def summed(operands, terms, first, rows, width):
    values = []
    for index, at in terms:
        if rows % 16 == 0:
            value = operands[index][first : first + rows, at : at + width].astype(f32)
        else:
            value = operands[index][:, at : at + width].astype(f32)[first : first + rows]
        values.append(value)
    return functools.reduce(jnp.add, values)


def vector_width(rows):
    return TILE * max(1, VECTOR_ROWS // rows)


def fold_vectors(packed, rows):
    if rows > VECTOR_ROWS:
        return jnp.concatenate([packed, jnp.zeros((rows - VECTOR_ROWS, TILE), f32)], axis=0)
    return jnp.concatenate(
        [packed[n : n + rows] for n in range(0, VECTOR_ROWS, rows)], axis=1
    )


def unfold_vectors(block, rows):
    if rows >= VECTOR_ROWS:
        return block[:VECTOR_ROWS]
    return jnp.concatenate(
        [block[:, n : n + TILE] for n in range(0, vector_width(rows), TILE)], axis=0
    )


def summed_vectors(values, terms):
    return functools.reduce(
        jnp.add,
        [
            unfold_vectors(
                values(index)[:rows, at : at + vector_width(rows)].astype(f32), rows
            )
            for index, at, rows in terms
        ],
    )


def combine_kernel(plans, *refs):
    count = sum(pieces + (1 if vectors else 0) for _, pieces, _, vectors in plans)
    operands, outs = refs[:-count], list(refs[-count:])
    for rows, pieces, parts, vectors in plans:
        if vectors:
            packed = summed_vectors(lambda index: operands[index][...].astype(f32), vectors)
            outs.pop(0)[...] = packed
        for piece in range(pieces):
            out_ref = outs.pop(0)
            column = 0
            for width, terms in parts:
                value = summed(operands, terms, piece * rows, rows, width)
                out_ref[:, column : column + width] = value.astype(out_ref.dtype)
                column += width
            if piece and vectors:
                out_ref[:, column:] = fold_vectors(packed, rows).astype(out_ref.dtype)


def unpack_vectors(packed):
    return jnp.concatenate(
        [packed[n : n + VECTORS] for n in range(0, VECTOR_ROWS, VECTORS)], axis=1
    )


def finish_kernel(size, groups, count, plan, up_rows, *refs):
    operands, outs = refs[:count], refs[count:]
    weights, vec_outs, embed_out, up_out = outs[:5], outs[5:-2], outs[-2], outs[-1]
    place = lax.axis_index("dp") * groups + lax.axis_index("tensor")
    share = D // (size * groups)
    for target, at, width, terms in plan[0]:
        weights[target][:, at : at + width] = summed(operands, terms, 0, share, width)
    value = unpack_vectors(
        summed_vectors(lambda index: operands[index][...].astype(f32), plan[1])
    )
    mine = pltpu.roll(value, lax.rem(D - place * share, D), 1)[:, :TILE]
    rows = [row for row in range(5 + up_rows + 3) if not 5 <= row < 5 + up_rows]
    for row, out_ref in zip(rows, vec_outs):
        out_ref[...] = mine[row, :share]
    embed = jnp.concatenate([mine[5 + up_rows + 3 : 5 + up_rows + 5], jnp.zeros((6, TILE), f32)], axis=0)
    embed_out[...] = embed.T[:share, :2]
    wide = up_rows * share
    each = D // wide
    line = lax.div(place, each)
    chosen = functools.reduce(
        jnp.add,
        [jnp.where(line == r, value[5 + r : 6 + r], 0.0) for r in range(up_rows)],
    )
    chosen = jnp.broadcast_to(chosen, (8, D))
    turned = pltpu.roll(chosen, lax.rem(D - lax.rem(place, each) * wide, D), 1)[:, :TILE]
    up_out[...] = turned[0, :wide]


def whole(shape):
    return pl.BlockSpec(shape, lambda i: (0,) * len(shape))


def columns(rows, width, at=None):
    if at is None:
        return pl.BlockSpec((rows, width), lambda i: (0, i))
    return pl.BlockSpec((rows, width), lambda i: (0, at))


def row_block(rows, width, at=None):
    if at is None:
        return pl.BlockSpec((rows, width), lambda i: (i, 0))
    return pl.BlockSpec((rows, width), lambda i: (at, 0))


def scalars():
    return pl.BlockSpec(memory_space=pltpu.SMEM)


def params(size=VMEM_BYTES):
    return pltpu.CompilerParams(vmem_limit_bytes=size)


def cost(flops, bytes_accessed):
    return pl.CostEstimate(flops=flops, bytes_accessed=bytes_accessed, transcendentals=0)


def in_hbm():
    return pl.BlockSpec(memory_space=pl.ANY)


def attention_forward(
    half, ints, memory, content, query, weights, biases, segment_rows
):
    count, window = 2 * half, KEYS + half
    coarse_rows = -(-(window // 32) // 8) * 8
    outs = (
        ((count, D), f32, columns(count, QUAD)),
        ((HEADS, count, KEYS), bf16, pl.BlockSpec((4, count, KEYS), lambda i: (i, 0, 0))),
        ((D, KEYS), bf16, row_block(QUAD, KEYS)),
        ((D, KEYS), bf16, row_block(QUAD, KEYS)),
        ((D, window), bf16, row_block(QUAD, window)),
        ((D, count), bf16, row_block(QUAD, count)),
        ((D, count), bf16, row_block(QUAD, count)),
        ((count, D), f32, columns(count, QUAD)),
        ((count, QUADS * TILE), f32, columns(count, TILE)),
        ((16, KEYS), bf16, whole((16, KEYS))),
        ((8, half), f32, whole((8, half))),
        ((window, D), bf16, whole((window, D))),
    )
    return pl.pallas_call(
        functools.partial(forward_kernel, half),
        grid=(QUADS,),
        out_shape=[jax.ShapeDtypeStruct(shape, kind) for shape, kind, _ in outs],
        in_specs=[
            scalars(),
            scalars(),
            whole((1, LEN)),
            whole((1, LEN)),
            whole((1, LEN)),
            whole((MEM, D)),
            whole((LEN, D)),
            whole((half, D)),
        ]
        + [columns(D, QUAD)] * 4
        + [whole((D,))] * 3
        + [columns(2, QUAD)],
        out_specs=[spec for _, _, spec in outs],
        scratch_shapes=[
            pltpu.VMEM((KEYS, D), bf16),
            pltpu.VMEM((count, D), bf16),
            pltpu.VMEM((window, D), bf16),
            pltpu.VMEM((count, KEYS), f32),
            pltpu.VMEM((2, 32, D // 2), f32),
            pltpu.VMEM((2, coarse_rows, D // 2), f32),
            pltpu.VMEM((8, D), f32),
            pltpu.VMEM((2, half, KEYS), f32),
            pltpu.VMEM((2, half, KEYS + PART), f32),
            pltpu.VMEM((HEAD_DIM, KEYS), bf16),
            pltpu.VMEM((half, PAIR), f32),
            pltpu.VMEM((8, LEN), f32),
            pltpu.VMEM((KEYS, PAIR), bf16),
            pltpu.VMEM((LEN, TILE), f32),
            pltpu.VMEM((LEN, TILE), f32),
        ],
        compiler_params=params(),
        cost_estimate=cost(30_000_000_000, 40_000_000),
        name="attention_forward",
    )(*ints, memory, content, query, *weights, *biases, segment_rows)


def middle(half, size, groups, arrays, hidden_cols):
    count, share = 2 * half, D // groups
    chunk = min(hidden_cols, 768)
    outs = (
        ((half, D), bf16),
        ((half, D), bf16),
        ((D, 2 * hidden_cols), bf16),
        ((D, 2 * hidden_cols), bf16),
        ((count, D), f32),
        ((count, D), bf16),
        ((share, D), bf16),
        ((share, D), bf16),
        ((8, D), f32),
        ((2, hidden_cols), f32),
    )
    weights = (6, 7, 8, 9)
    return pl.pallas_call(
        functools.partial(middle_kernel, half, size, groups, chunk),
        grid=(1,),
        out_shape=[jax.ShapeDtypeStruct(shape, kind) for shape, kind in outs],
        in_specs=[
            in_hbm() if i in weights else whole(array.shape) for i, array in enumerate(arrays)
        ],
        out_specs=[whole(shape) for shape, _ in outs],
        scratch_shapes=[
            pltpu.VMEM((2, count, hidden_cols), bf16),
            pltpu.VMEM((2, count, hidden_cols), bf16),
            pltpu.VMEM((2, count, chunk), f32),
            pltpu.VMEM((count, D), f32),
            pltpu.VMEM((count, D), f32),
            pltpu.VMEM((count, D), bf16),
            pltpu.VMEM((count, D), bf16),
            pltpu.VMEM((8, FF), f32),
            pltpu.VMEM((2, D, hidden_cols), bf16),
            pltpu.VMEM((2, hidden_cols, D), bf16),
            pltpu.VMEM((D, count), bf16),
            pltpu.VMEM((D, count), bf16),
            pltpu.VMEM((D, count), bf16),
            pltpu.VMEM((D, count), bf16),
            pltpu.VMEM((D, count), bf16),
            pltpu.VMEM((D, count), f32),
            pltpu.SemaphoreType.DMA((2, 2)),
        ],
        compiler_params=params(),
        cost_estimate=cost(30_000_000_000, 30_000_000),
        name="feed_forward",
    )(*arrays)


def prepare_kernel(
    half,
    size,
    groups,
    memory_ref,
    content_ref,
    query_ref,
    pos_ref,
    both_t_ref,
    stack_t_ref,
    pos_t_ref,
    both_work,
    stack_work,
    pos_work,
):
    first = pl.multiple_of(lax.axis_index("tensor") * half, half)
    both = jnp.concatenate([content_ref[pl.ds(first, half), :], query_ref[...]], axis=0)
    stack = jnp.concatenate([memory_ref[...], content_ref[...]], axis=0)
    transpose_by_owner(both_t_ref, both, both_work, size, groups)
    transpose_by_owner(stack_t_ref, stack, stack_work, size, groups)
    transpose_by_owner(pos_t_ref, pos_ref[...], pos_work, size, groups)


def transposed_rows(half, size, groups, memory, content, query, pos):
    count, window = 2 * half, KEYS + half
    arrays = (memory, content, query, pos)
    outs = ((D, count), (D, KEYS), (D, window))
    return pl.pallas_call(
        functools.partial(prepare_kernel, half, size, groups),
        grid=(1,),
        out_shape=[jax.ShapeDtypeStruct(shape, bf16) for shape in outs],
        in_specs=[whole(array.shape) for array in arrays],
        out_specs=[whole(shape) for shape in outs],
        scratch_shapes=[pltpu.VMEM(shape, f32) for shape in outs],
        compiler_params=params(),
        cost_estimate=cost(6_000_000_000, 8_000_000),
        name="transposed_rows",
    )(*arrays)


def attention_backward(half, groups, at, mode, saved, agrad, segment_rows, extra):
    count, window, share = 2 * half, KEYS + half, D // groups
    att, prob, keys, values, rel, hc, hp, hs, linv, kaug, srow, _ = saved[:12]
    both_t, stack_t, pos_t = saved[12:]
    width = 4 * QUAD + (D if mode == "first" else 0)
    operands = (
        (prob, in_hbm()),
        (keys, row_block(QUAD, KEYS, at)),
        (values, row_block(QUAD, KEYS, at)),
        (rel, row_block(QUAD, window, at)),
        (hc, row_block(QUAD, count, at)),
        (hp, row_block(QUAD, count, at)),
        (hs, columns(count, QUAD, at)),
        (linv, columns(count, TILE, at)),
        (kaug, whole((16, KEYS))),
        (srow, whole((8, half))),
        (att, columns(count, QUAD, at)),
        (agrad, columns(count, QUAD, at)),
        (segment_rows, columns(2, QUAD, at)),
        (both_t, in_hbm()),
        (stack_t, in_hbm()),
        (pos_t, in_hbm()),
    ) + tuple((array, whole(array.shape)) for array in extra)
    outs = (
        ((share, width), bf16),
        ((share, width + (TILE if mode == "last" else 0)), bf16),
        ((count, QUAD), bf16),
        ((LEN, QUAD), bf16),
        ((LEN, QUAD), bf16),
        ((8, QUAD), f32),
    )
    if mode == "last":
        outs += (((VECTOR_ROWS, TILE), f32),)
    return pl.pallas_call(
        functools.partial(backward_kernel, half, groups, at, mode),
        grid=(1,),
        out_shape=[jax.ShapeDtypeStruct(shape, kind) for shape, kind in outs],
        in_specs=[spec for _, spec in operands],
        out_specs=[whole(shape) for shape, _ in outs],
        scratch_shapes=[
            pltpu.VMEM((4, count, KEYS), bf16),
            pltpu.VMEM((D, count), bf16),
            pltpu.VMEM((D, KEYS), bf16),
            pltpu.VMEM((D, window), bf16),
            pltpu.VMEM((2, count, KEYS), f32),
            pltpu.VMEM((2, count, KEYS), bf16),
            pltpu.VMEM((2, count, window), bf16),
            pltpu.SemaphoreType.DMA((7,)),
        ],
        compiler_params=params(),
        cost_estimate=cost(16_000_000_000, 16_000_000),
        name="attention_backward",
    )(*[array for array, _ in operands])


def row_gradients(half, groups, summed_grad, proj, keys, vals, weights):
    count = 2 * half
    arrays = (summed_grad, *proj, *keys, *vals, *weights)
    outs = (((half, D), f32), ((half, D), f32), ((half, D), bf16))
    return pl.pallas_call(
        functools.partial(rows_kernel, half, groups),
        grid=(1,),
        out_shape=[jax.ShapeDtypeStruct(shape, kind) for shape, kind in outs],
        in_specs=[whole(array.shape) for array in arrays],
        out_specs=[whole(shape) for shape, _ in outs],
        scratch_shapes=[pltpu.VMEM((LEN, D), f32)],
        compiler_params=params(),
        cost_estimate=cost(4_000_000_000, 10_000_000),
        name="row_gradients",
    )(*arrays)


def swap(array):
    groups = lax.axis_size("tensor")
    return lax.ppermute(array, "tensor", [(i, (i + 1) % groups) for i in range(groups)])


def across(array, masks):
    size, groups = lax.axis_size("dp"), lax.axis_size("tensor")
    pairs = [
        (place * groups + core, (place ^ masks[core]) * groups + core)
        for place in range(size)
        for core in range(groups)
    ]
    return lax.ppermute(array, ("dp", "tensor"), pairs)


def total(terms):
    return functools.reduce(jnp.add, [term.astype(f32) for term in terms])


class Chain:
    def __init__(self, parts, rows, vectors=()):
        self.parts, self.rows = parts, rows
        self.vectors = list(vectors)
        self.messages = None
        self.done = 0

    def masks(self, part, bits):
        size, groups = lax.axis_size("dp"), lax.axis_size("tensor")
        found = []
        for core in range(groups):
            order = order_of(core, size.bit_length() - 1)[self.done : self.done + bits]
            found.append(
                sum(((part >> (bits - 1 - j)) & 1) << bit for j, bit in enumerate(order))
            )
        return found

    def send(self):
        if not self.bits:
            gots = [swap(self.messages[0])]
        else:
            gots = [
                across(message, self.masks(part + 1, self.bits))
                for part, message in enumerate(self.messages)
            ]
        for got in gots:
            column = 0
            for width, terms in self.parts:
                terms.append((got, column))
                column += width
            if self.vectors:
                self.vectors.append((got, column, self.rows))
        self.pending = gots
        self.done += self.bits
        self.messages = None

    def take(self, results):
        if self.vectors:
            self.vectors = [(results.pop(0), 0, VECTOR_ROWS)]
        kept, column, parts = results.pop(0), 0, []
        for width, _ in self.parts:
            parts.append((width, [(kept, column)]))
            column += width
        self.parts = parts
        self.messages = [results.pop(0) for _ in range((1 << self.bits) - 1)]

    def replace(self, old, new):
        for index, (width, terms) in enumerate(self.parts):
            self.parts[index] = (
                width,
                [(new if array is old else array, at) for array, at in terms],
            )
        self.vectors = [(new if a is old else a, at, rows) for a, at, rows in self.vectors]


def merged(chains):
    chain = Chain(
        [part for chain in chains for part in chain.parts],
        chains[0].rows,
        [term for chain in chains for term in chain.vectors],
    )
    chain.done = chains[0].done
    chain.pending = []
    return chain


class Operands:
    def __init__(self):
        self.arrays = []

    def of(self, array):
        for index, held in enumerate(self.arrays):
            if held is array:
                return index
        self.arrays.append(array)
        return len(self.arrays) - 1

    def in_specs(self):
        return [whole(array.shape) for array in self.arrays]


def prepare(requests):
    operands, plans, outs = Operands(), [], []
    plain = any(chain.rows % (8 << bits) for chain, bits in requests)
    for chain, bits in requests:
        chain.bits = bits
        chain.rows >>= bits
        rows, pieces = chain.rows, 1 << bits
        width = sum(width for width, _ in chain.parts)
        if plain:
            results = [
                jnp.concatenate(
                    [
                        total(
                            [
                                array[piece * rows : (piece + 1) * rows, at : at + width]
                                for array, at in terms
                            ]
                        )
                        for width, terms in chain.parts
                    ],
                    axis=1,
                )
                for piece in range(pieces)
            ]
            if chain.vectors:
                packed = summed_vectors(lambda array: array, chain.vectors)
                folded = fold_vectors(packed, rows)
                results = [packed, results[0]] + [
                    jnp.concatenate([result, folded], axis=1) for result in results[1:]
                ]
            chain.take([result.astype(bf16) for result in results])
            continue
        parts = [
            (width, [(operands.of(array), at) for array, at in terms])
            for width, terms in chain.parts
        ]
        vectors = [(operands.of(array), at, held) for array, at, held in chain.vectors]
        plans.append((rows, pieces, parts, vectors))
        if vectors:
            outs.append(((VECTOR_ROWS, TILE), f32))
        outs.append(((rows, width), bf16))
        wide = width + (vector_width(rows) if vectors else 0)
        outs += [((rows, wide), bf16)] * (pieces - 1)
    if plain:
        return
    results = pl.pallas_call(
        functools.partial(combine_kernel, plans),
        grid=(1,),
        out_shape=[jax.ShapeDtypeStruct(shape, kind) for shape, kind in outs],
        in_specs=operands.in_specs(),
        out_specs=[whole(shape) for shape, _ in outs],
        compiler_params=params(COMBINE_BYTES),
        cost_estimate=cost(1_000_000_000, 8_000_000),
        name="combine",
    )(*operands.arrays)
    results = list(results)
    for chain, bits in requests:
        chain.take(results)


def launch(requests, value, waits=()):
    chains = [chain for chain, bits in requests if bits is not None] + list(waits)
    olds = [got for chain in chains for got in chain.pending]
    if olds:
        value, news = lax.optimization_barrier((value, olds))
        for chain in chains + [chain for chain, _ in requests]:
            for old, new in zip(olds, news):
                chain.replace(old, new)
        for chain in chains:
            chain.pending = []
    sums = [(chain, bits) for chain, bits in requests if bits is not None]
    if sums:
        prepare(sums)
    messages = [chain.messages for chain, _ in requests]
    value, messages = lax.optimization_barrier((value, messages))
    for (chain, bits), message in zip(requests, messages):
        chain.messages = message
        if bits is None:
            chain.bits = 0
        chain.send()
    return value


def finish(size, groups, chain):
    share = D // (size * groups)
    up_rows = FF // D
    pieces = []
    for quad, (width, terms) in enumerate(chain.parts):
        for index in range(4):
            pieces.append((index, quad * QUAD, QUAD, [(a, at + index * QUAD) for a, at in terms]))
        if width > 4 * QUAD:
            pieces.append((4, 0, D, [(a, at + 4 * QUAD) for a, at in terms]))
    if share % 8:
        blocks = {}
        for target, at, width, terms in pieces:
            blocks.setdefault(target, []).append(
                total([array[:share, c : c + width] for array, c in terms])
            )
        weights = [jnp.concatenate(blocks[target], axis=1) for target in range(5)]
        vectors = unpack_vectors(summed_vectors(lambda array: array, chain.vectors))
        place = lax.axis_index("dp") * groups + lax.axis_index("tensor")
        mine = lax.dynamic_slice_in_dim(vectors, place * share, share, 1)
        ups = lax.dynamic_slice_in_dim(
            vectors[5 : 5 + up_rows].reshape(-1), place * up_rows * share, up_rows * share, 0
        )
        late = 5 + up_rows
        return weights, [mine[r] for r in (0, 1, 2, 3, 4, late, late + 1, late + 2)], mine[
            late + 3 : late + 5
        ].T, ups
    operands = Operands()
    plan = [
        (target, at, width, [(operands.of(array), c) for array, c in terms])
        for target, at, width, terms in pieces
    ]
    vectors = [(operands.of(array), at, held) for array, at, held in chain.vectors]
    outs = [(share, D)] * 5 + [(share,)] * 8 + [(share, 2), (up_rows * share,)]
    found = pl.pallas_call(
        functools.partial(
            finish_kernel, size, groups, len(operands.arrays), (plan, vectors), up_rows
        ),
        grid=(1,),
        out_shape=[jax.ShapeDtypeStruct(shape, f32) for shape in outs],
        in_specs=operands.in_specs(),
        out_specs=[whole(shape) for shape in outs],
        compiler_params=params(COMBINE_BYTES),
        name="finish",
    )(*operands.arrays)
    return found[:5], found[5:13], found[13], found[14]


def body(
    content_in,
    query_in,
    memory,
    content_cot,
    query_cot,
    query_weight,
    key_weight,
    value_weight,
    out_weight,
    rel_weight,
    content_bias,
    position_bias,
    segment_bias,
    segment_embed,
    attn_gain,
    attn_shift,
    up_weight,
    up_bias,
    down_weight,
    down_bias,
    ffn_gain,
    ffn_shift,
    lengths,
    memory_lengths,
    segment_ids,
    orders,
    targets,
):
    groups = lax.axis_size("tensor")
    size = lax.axis_size("dp")
    steps = size.bit_length() - 1
    half = LEN // groups
    hidden_cols = up_weight.shape[1]
    up_other, down_other = swap(up_weight), swap(down_weight)
    content, query = content_in[0], query_in[0]
    segment_rows = segment_embed.T
    saved = attention_forward(
        half,
        (lengths, memory_lengths, segment_ids, orders, targets),
        memory[0],
        content,
        query,
        (query_weight, key_weight, value_weight, rel_weight),
        (content_bias, position_bias, segment_bias),
        segment_rows,
    )
    (
        content_out,
        query_out,
        ffn_own,
        ffn_other,
        summed_grad,
        attended_grad,
        out_own,
        out_other,
        early_small,
        up_bias_part,
    ) = middle(
        half,
        size,
        groups,
        (
            saved[0],
            content,
            query,
            content_cot[0],
            query_cot[0],
            out_weight,
            up_weight,
            up_other,
            down_weight,
            down_other,
            up_bias,
            down_bias,
            attn_gain,
            attn_shift,
            ffn_gain,
            ffn_shift,
        ),
        hidden_cols,
    )
    ffn = Chain([(2 * hidden_cols, [(ffn_own, 0)])], D)
    ffn.messages = [ffn_other]
    held = launch([(ffn, None)], attended_grad)
    content_late, held = lax.optimization_barrier((content, held))
    turned = transposed_rows(half, size, groups, memory[0], content_late, query, saved[11])
    turned, held = lax.optimization_barrier((turned, held))
    saved = (*saved, *turned)
    proj, tok_keys, tok_vals, small, late = [], [], [], [], []

    def backward(at, mode, grad, extra):
        own, other, proj_part, key_part, val_part, small_part, *vectors = attention_backward(
            half, groups, at, mode, saved, grad, segment_rows, extra
        )
        proj.append(proj_part)
        tok_keys.append(key_part)
        tok_vals.append(val_part)
        small.append(small_part)
        chain = Chain(
            [(own.shape[1], [(own, 0)])],
            own.shape[0],
            [(array, 0, VECTOR_ROWS) for array in vectors],
        )
        chain.messages = [other]
        late.append(chain)

    held = launch([(ffn, 1)], held)
    backward(0, "first", held, (out_own, out_other))
    held, proj[0] = launch([(late[0], None)], (attended_grad, proj[0]))
    backward(1, "middle", held, ())
    held, proj[1] = launch(
        [(ffn, 1), (late[0], 1), (late[1], None)], (attended_grad, proj[1])
    )
    backward(2, "last", held, (early_small, up_bias_part, *small))
    xy = min(2, steps)
    proj[2] = launch(
        [(late[2], None), (ffn, 1), (late[0], 1), (late[1], 1)], proj[2]
    )
    own_rows, query_grad, row_send = row_gradients(
        half, groups, summed_grad, proj, tok_keys, tok_vals, (query_weight, key_weight, value_weight)
    )
    own_rows, row_send = launch(
        [(late[2], xy), (late[1], 1), (ffn, 1)], (own_rows, row_send)
    )
    final = merged(late)
    own_rows, row_send = launch(
        [(final, min(2, steps - final.done))], (own_rows, row_send), late
    )
    row_got = swap(row_send)
    while final.done < steps:
        own_rows = launch([(final, min(2, steps - final.done))], own_rows)
    while ffn.done < steps:
        own_rows = launch([(ffn, min(2, steps - ffn.done))], own_rows)
    content_grad = own_rows + row_got.astype(f32)
    ffn_sum = total([array[: ffn.rows] for array, _ in ffn.parts[0][1]])
    up_grad, down_grad_own = ffn_sum[:, :hidden_cols], ffn_sum[:, hidden_cols:].T
    weights, vectors, segment_grad, up_bias_grad = finish(size, groups, final)
    return (
        content_out[None],
        query_out[None],
        content_grad[None],
        query_grad[None],
        weights[0],
        weights[1],
        weights[2],
        weights[4],
        weights[3],
        vectors[5],
        vectors[6],
        vectors[7],
        segment_grad,
        vectors[3],
        vectors[4],
        up_grad,
        up_bias_grad,
        down_grad_own,
        vectors[2],
        vectors[0],
        vectors[1],
    )


def solution(mesh):
    in_specs = (
        P("dp", None, None),
        P("dp", "tensor", None),
        P("dp", None, None),
        P("dp", "tensor", None),
        P("dp", "tensor", None),
        P(),
        P(),
        P(),
        P(),
        P(),
        P(),
        P(),
        P(),
        P(),
        P(),
        P(),
        P(None, "tensor"),
        P(),
        P("tensor", None),
        P(),
        P(),
        P(),
        P("dp"),
        P("dp"),
        P("dp", None),
        P("dp", None),
        P("dp", None),
    )
    out_specs = (
        P("dp", "tensor", None),
        P("dp", "tensor", None),
        P("dp", "tensor", None),
        P("dp", "tensor", None),
        P(("dp", "tensor"), None),
        P(("dp", "tensor"), None),
        P(("dp", "tensor"), None),
        P(("dp", "tensor"), None),
        P(("dp", "tensor"), None),
        P(("dp", "tensor")),
        P(("dp", "tensor")),
        P(("dp", "tensor")),
        P(("dp", "tensor"), None),
        P(("dp", "tensor")),
        P(("dp", "tensor")),
        P("dp", "tensor"),
        P(("dp", "tensor")),
        P("tensor", "dp"),
        P(("dp", "tensor")),
        P(("dp", "tensor")),
        P(("dp", "tensor")),
    )
    return jax.shard_map(body, mesh=mesh, in_specs=in_specs, out_specs=out_specs, check_vma=False)
```

```python
import functools

import jax
import jax.numpy as jnp
from jax import lax
from jax.experimental import pallas as pl
from jax.experimental.pallas import tpu as pltpu
from jax.sharding import PartitionSpec as P

D = 768
HEADS = 12
HEAD_DIM = 64
FF = 3072
LEN = 512
MEM = 384
KEYS = MEM + LEN
QUAD = 4 * HEAD_DIM
QUADS = D // QUAD
PAIR = 2 * HEAD_DIM
SCALE = HEAD_DIM ** (-0.5)
VMEM_BYTES = 61 * 1024 * 1024
COMBINE_BYTES = 28 * 1024 * 1024
BACKWARD_BYTES = 54 * 1024 * 1024
BLOCK = 32
TILE = 128
WIDE = 256
VECTORS = 16

VECTOR_ROWS = VECTORS * D // TILE

f32 = jnp.float32
bf16 = jnp.bfloat16
precise = lax.Precision.HIGHEST


def mm(left, right):
    return lax.dot_general(left, right, (((1,), (0,)), ((), ())), preferred_element_type=f32)


def mm_nt(left, right):
    return lax.dot_general(left, right, (((1,), (1,)), ((), ())), preferred_element_type=f32)


def mm_tn(left, right):
    return lax.dot_general(left, right, (((0,), (0,)), ((), ())), preferred_element_type=f32)


def unit_matrix(size):
    row = lax.broadcasted_iota(jnp.int32, (size, size), 0)
    return jnp.where(row == lanes((size, size)), 1.0, 0.0).astype(bf16)


def turn(value):
    width = min(value.shape[1], WIDE)
    unit = unit_matrix(width)
    blocks = [mm_nt(unit, value[:, n : n + width]) for n in range(0, value.shape[1], width)]
    return blocks[0] if len(blocks) == 1 else jnp.concatenate(blocks, axis=0)


def split(value):
    high = value.astype(bf16)
    return high, (value - high.astype(f32)).astype(bf16)


def lanes(shape):
    return lax.broadcasted_iota(jnp.int32, shape, 1)


def column_of(row):
    row = row.astype(f32)
    even = 2.0 * jnp.floor(0.5 * row)
    parts = jnp.concatenate([even, row - even, jnp.zeros((14, row.shape[1]), f32)], axis=0)
    return mm_tn(parts.astype(bf16), jnp.ones((16, TILE), bf16))


def lane_tiles(value, combine):
    tiles = [value[:, at : at + TILE] for at in range(0, value.shape[1], TILE)]
    return functools.reduce(combine, tiles)


def interleave(steps, tasks):
    done = 0
    for index, step in enumerate(steps):
        step()
        while done * len(steps) < (index + 1) * len(tasks) and done < len(tasks):
            tasks[done]()
            done += 1
    for task in tasks[done:]:
        task()


def order_of(core, bits):
    order = list(range(bits))
    if core == 1:
        for at in range(0, bits - 1, 2):
            order[at], order[at + 1] = order[at + 1], order[at]
    return order


def block_owner(place, core, bits):
    owners = []
    for each in range(2):
        owner = place * 0
        for step, bit in enumerate(order_of(each, bits)):
            owner = owner | (((place >> (bits - 1 - step)) & 1) << bit)
        owners.append(owner)
    return jnp.where(core == 1, owners[1], owners[0]) ^ lax.axis_index("dp")


def one_hot(source):
    return jnp.where(lanes((source.shape[0], D)) == source, 1.0, 0.0).astype(bf16)


def owner_rows(size, groups):
    share = D // (size * groups)
    row = lax.broadcasted_iota(jnp.int32, (D, 1), 0)
    side, rest = lax.div(row, size * share), lax.rem(row, size * share)
    core = lax.rem(lax.axis_index("tensor") + side, groups)
    owner = block_owner(lax.div(rest, share), core, size.bit_length() - 1)
    return one_hot((owner * groups + core) * share + lax.rem(rest, share))


def shared_rows(size, core):
    share = D // size
    row = lax.broadcasted_iota(jnp.int32, (D, 1), 0)
    owner = block_owner(lax.div(row, share), core, size.bit_length() - 1)
    return one_hot(owner * share + lax.rem(row, share))


def transpose_by_owner(out_ref, value, work, size, groups):
    share = D // (size * groups)
    if share % 8 or (2 * share) % 16:
        out_ref[...] = mm_nt(owner_rows(size, groups), value).astype(bf16)
        return
    width = value.shape[0]
    for n in range(0, D, WIDE):
        work[n : n + WIDE, :width] = turn(value[:, n : n + WIDE])
    bits = size.bit_length() - 1
    blocks = []
    for block in range(size * groups):
        core = lax.rem(lax.axis_index("tensor") + block // size, groups)
        owner = block_owner(jnp.int32(block % size), core, bits)
        at = pl.multiple_of((owner * groups + core) * share, 8)
        blocks.append(work[pl.ds(at, share), :width])
        if block % 2:
            out_ref[(block - 1) * share : (block + 1) * share, :] = jnp.concatenate(
                blocks, axis=0
            ).astype(bf16)
            blocks = []


def transpose_by_dp(out_ref, value, work, size):
    share = D // size
    core = lax.axis_index("tensor")
    if share % 16:
        out_ref[...] = mm_nt(shared_rows(size, core), value).astype(bf16)
        return
    for n in range(0, D, WIDE):
        work[n : n + WIDE, :] = turn(value[:, n : n + WIDE]).astype(bf16)
    for block in range(size):
        owner = block_owner(jnp.int32(block), core, size.bit_length() - 1)
        at = pl.multiple_of(owner * share, 16)
        out_ref[block * share : (block + 1) * share, :] = work[pl.ds(at, share), :]


def forward_kernel(
    half,
    length_ref,
    mem_length_ref,
    seg_ref,
    ord_ref,
    tgt_ref,
    memory_ref,
    content_ref,
    query_ref,
    wq_ref,
    wk_ref,
    wv_ref,
    wr_ref,
    cb_ref,
    pb_ref,
    sb_ref,
    se_ref,
    att_ref,
    prob_ref,
    key_ref,
    val_ref,
    rel_ref,
    hc_ref,
    hp_ref,
    hs_ref,
    linv_ref,
    kaug_ref,
    srow_ref,
    pos_ref,
    stack,
    both,
    pos,
    bias,
    fine,
    coarse,
    vectors,
    scores,
    places,
    kaug_t,
    scol,
    seg_row,
    kaug_work,
    order_work,
    seg_work,
):
    window = KEYS + half
    first = pl.multiple_of(lax.axis_index("tensor") * half, half)
    step_id = pl.program_id(0)

    @pl.when(step_id == 0)
    def _():
        stack[:MEM, :] = memory_ref[...]
        stack[MEM:, :] = content_ref[...]
        both[:half, :] = content_ref[pl.ds(first, half), :]
        both[half:, :] = query_ref[...]
        vectors[0:1, :] = cb_ref[...][None, :]
        vectors[1:2, :] = pb_ref[...][None, :]
        vectors[2:3, :] = sb_ref[...][None, :]
        step = lax.broadcasted_iota(jnp.int32, (1, D // 2), 1).astype(f32) * (2.0 / D)
        inverse = 1.0 / jnp.power(jnp.full((1, D // 2), 10000.0, f32), step)
        coarse_rows = coarse.shape[1]
        top = (MEM + half + first).astype(f32)
        angle = (
            top - 32.0 * lax.broadcasted_iota(jnp.int32, (coarse_rows, 1), 0).astype(f32)
        ) * inverse
        coarse[0] = jnp.sin(angle)
        coarse[1] = jnp.cos(angle)
        small = lax.broadcasted_iota(jnp.int32, (32, 1), 0).astype(f32) * inverse
        fine[0] = jnp.sin(small)
        fine[1] = jnp.cos(small)
        for a in range(window // 32):
            sa, ca = coarse[0, a : a + 1, :], coarse[1, a : a + 1, :]
            sb, cb = fine[0], fine[1]
            pos[a * 32 : (a + 1) * 32, : D // 2] = (sa * cb - ca * sb).astype(bf16)
            pos[a * 32 : (a + 1) * 32, D // 2 :] = (ca * cb + sa * sb).astype(bf16)
        never = float(LEN + 1)
        mem_at = lax.broadcasted_iota(jnp.int32, (1, MEM), 1)
        tok_at = lax.broadcasted_iota(jnp.int32, (1, LEN), 1)
        open_from = jnp.concatenate(
            [
                jnp.where(mem_at >= MEM - mem_length_ref[0], -1.0, never),
                jnp.where(
                    tok_at < length_ref[0],
                    jnp.where(tgt_ref[...] == 0, -1.0, ord_ref[...].astype(f32)),
                    never,
                ),
            ],
            axis=1,
        )
        order_col = column_of(ord_ref[...])
        seg_col = column_of(seg_ref[...])
        kaug_lane = lanes((LEN, PAIR)) % HEAD_DIM
        kaug_work[:MEM, :] = (lanes((MEM, PAIR)) % HEAD_DIM < 4).astype(f32).astype(bf16)
        kaug_work[MEM:, :] = jnp.where(
            kaug_lane < 4, 1.0, jnp.where(kaug_lane < 6, seg_col, 0.0)
        ).astype(bf16)
        kaug_t[...] = kaug_work[...].T[:HEAD_DIM]
        kaug_ref[...] = kaug_t[:16, :]
        order_work[...] = order_col
        own_order = order_work[pl.ds(first, half), :][:, :1]
        seg_work[...] = seg_col
        scol[...] = seg_work[pl.ds(first, half), :]
        seen = open_from <= own_order
        bias[:half, :] = jnp.where(seen, 0.0, -1e30)
        key_at = lax.broadcasted_iota(jnp.int32, (half, KEYS), 1)
        row_at = lax.broadcasted_iota(jnp.int32, (half, KEYS), 0)
        seen_q = seen & (key_at - MEM != row_at + first)
        bias[half:, :] = jnp.where(seen_q, 0.0, -1e30)
        seg_row[0:1, :] = seg_ref[...].astype(f32)
        srow_ref[...] = jnp.broadcast_to(seg_row[0:1, pl.ds(first, half)], srow_ref.shape)
        pos_ref[...] = pos[...]

    here = pl.ds(pl.multiple_of(step_id * QUAD, QUAD), QUAD)
    keys = mm(stack[...], wk_ref[...]).astype(bf16)
    values = mm(stack[...], wv_ref[...]).astype(bf16)
    rel = mm(pos[...], wr_ref[...]).astype(bf16)
    projection = mm(both[...], wq_ref[...])
    head_content = (projection + vectors[0:1, here]).astype(bf16)
    head_position = (projection + vectors[1:2, here]).astype(bf16)
    head_segment = projection + vectors[2:3, here]
    keys_t, values_t, rel_t = [turn(value).astype(bf16) for value in (keys, values, rel)]
    key_ref[...] = keys_t
    val_ref[...] = values_t
    rel_ref[...] = rel_t
    hs_ref[...] = head_segment
    head_content = (head_content.astype(f32) * SCALE).astype(bf16)
    head_position = (head_position.astype(f32) * SCALE).astype(bf16)
    hc_ref[...] = turn(head_content).astype(bf16)
    hp_ref[...] = turn(head_position).astype(bf16)
    row_head = lax.broadcasted_iota(jnp.int32, (QUAD, QUAD), 0) // HEAD_DIM
    at = lanes((QUAD, QUAD)) - ((row_head // 2) * PAIR + (1 - row_head % 2) * HEAD_DIM)
    place_same = jnp.where((at >= 0) & (at < 2), 1.0, 0.0).astype(bf16)
    place_step = jnp.where((at >= 2) & (at < 6), 1.0, 0.0).astype(bf16)
    same, other = se_ref[0:1, :], se_ref[1:2, :]
    terms = functools.reduce(
        jnp.add,
        [mm(part, place_same) for part in split(head_segment * same)]
        + [mm(part, place_step) for part in split(head_segment * (other - same))],
    )
    marks = jnp.concatenate([scol[...], scol[...]], axis=0)
    marks = jnp.concatenate([marks, marks], axis=1)
    lane6 = lanes((2 * half, QUAD)) % HEAD_DIM
    factor = jnp.where(lane6 < 2, 1.0, jnp.where(lane6 < 4, marks, 1.0 - 2.0 * marks))
    terms = SCALE * (terms * factor)
    high = terms.astype(bf16)
    low = (terms - high.astype(f32)).astype(bf16)
    qaug = jnp.where(lane6 % 2 == 0, high, low)
    key_x = []
    for which in range(4):
        own = keys_t[which * HEAD_DIM : (which + 1) * HEAD_DIM]
        sides = [own, kaug_t[...]] if which % 2 == 0 else [kaug_t[...], own]
        key_x.append(jnp.concatenate(sides, axis=0))
    peaks, totals, outs = {}, {}, {}
    row_first = lanes((2 * half, PAIR)) < HEAD_DIM

    def products(which):
        cols = slice(which // 2 * PAIR, (which // 2 + 1) * PAIR)
        slot = which % 2
        row_mine = row_first == (which % 2 == 0)
        query_x = jnp.where(row_mine, head_content[:, cols], qaug[:, cols])
        place_x = jnp.where(row_mine, head_position[:, cols], jnp.zeros((), bf16))

        def score(n, stop):
            scores[slot, :, n:stop] = mm(query_x, key_x[which][:, n:stop])

        def placed(n, stop):
            places[slot, :, n:stop] = mm(place_x, rel_t[cols, n:stop])

        return [functools.partial(placed, n, min(n + WIDE, window)) for n in range(0, window, WIDE)] + [
            functools.partial(score, n, min(n + WIDE, KEYS)) for n in range(0, KEYS, WIDE)
        ]

    def softmax(which):
        slot = which % 2
        tops, pieces = [], []

        def join(b):
            block = slice(b, b + BLOCK)
            shifted = pltpu.roll(
                places[slot, block, :], (KEYS + b % half) % window, 1, stride=1, stride_axis=0
            )[:, :KEYS]
            score = scores[slot, block, :] + shifted + bias[block, :]
            scores[slot, block, :] = score
            tops.append(lane_tiles(score, jnp.maximum))

        def peak():
            peaks[which] = jnp.max(jnp.concatenate(tops, axis=0), axis=1, keepdims=True)

        def power(b):
            block = slice(b, b + BLOCK)
            prob = jnp.exp(scores[slot, block, :] - peaks[which][block])
            pieces.append(lane_tiles(prob, jnp.add))
            prob_ref[which, block, :] = prob.astype(bf16)

        def finish():
            totals[which] = 1.0 / jnp.sum(
                jnp.concatenate(pieces, axis=0), axis=1, keepdims=True
            )

        blocks = range(0, 2 * half, BLOCK)
        return (
            [functools.partial(join, b) for b in blocks]
            + [peak]
            + [functools.partial(power, b) for b in blocks]
            + [finish]
        )

    def mixture(which, part):
        outs[which, part] = mm_nt(
            values_t[which * HEAD_DIM : (which + 1) * HEAD_DIM],
            prob_ref[which, part * half : (part + 1) * half, :],
        )

    interleave([], products(0))
    for which in range(4):
        tasks = products(which + 1) if which < 3 else []
        if which:
            tasks += [functools.partial(mixture, which - 1, part) for part in range(2)]
        interleave(softmax(which), tasks)
    for part in range(2):
        mixture(3, part)
    sums = [totals[which] for which in range(4)]
    mixed = jnp.concatenate(
        [jnp.concatenate([outs[which, 0], outs[which, 1]], axis=1) for which in range(4)], axis=0
    )
    mixed = functools.reduce(jnp.add, [turn(part) for part in split(mixed)])
    mine = lanes((2 * half, PAIR)) < HEAD_DIM
    for pair in range(2):
        cols = slice(pair * PAIR, (pair + 1) * PAIR)
        att_ref[:, cols] = mixed[:, cols] * jnp.where(mine, sums[2 * pair], sums[2 * pair + 1])
    lane = lanes((2 * half, TILE))
    linv_ref[...] = jnp.where(
        lane == 0, sums[0], jnp.where(lane == 1, sums[1], jnp.where(lane == 2, sums[2], sums[3]))
    )


def norm_forward(summed, gain, shift):
    center = summed - jnp.mean(summed, axis=1, keepdims=True)
    inv = lax.rsqrt(jnp.mean(center * center, axis=1, keepdims=True) + 1e-06)
    unit = center * inv
    return unit, inv, unit * gain + shift


def norm_backward(grad, unit, inv, gain):
    scaled = grad * gain
    return inv * (
        scaled
        - jnp.mean(scaled, axis=1, keepdims=True)
        - unit * jnp.mean(scaled * unit, axis=1, keepdims=True)
    )


def row_sum(value):
    return jnp.sum(value, axis=0, keepdims=True)


def gelu_parts(x):
    square = x * x
    tanh = jnp.tanh((0.7978845608028654 * x) * (1.0 + 0.044715 * square))
    rise = 0.5 * (1.0 + tanh)
    grad = rise + (0.5 * x) * (1.0 - tanh * tanh) * (
        0.7978845608028654 * (1.0 + 0.134145 * square)
    )
    return x * rise, grad


def fold_rows(value):
    return functools.reduce(jnp.add, [value[r : r + 8] for r in range(0, value.shape[0], 8)])


def middle_kernel(
    half,
    size,
    groups,
    chunk,
    att_ref,
    content_ref,
    query_ref,
    ccot_ref,
    qcot_ref,
    wo_ref,
    up_own_hbm,
    up_oth_hbm,
    down_own_hbm,
    down_oth_hbm,
    ubias_ref,
    dbias_ref,
    again_ref,
    ashift_ref,
    fgain_ref,
    fshift_ref,
    cout_ref,
    qout_ref,
    ffn_own_ref,
    ffn_oth_ref,
    sgrad_ref,
    agrad_ref,
    out_own_ref,
    out_oth_ref,
    small_ref,
    ubg_ref,
    hidden,
    slope,
    pre,
    work,
    unit,
    low,
    down_grad,
    vectors,
    up,
    down,
    low_t,
    down_t,
    turn_low,
    turn_down,
    attended_t,
    turn_work,
    sems,
):
    count = 2 * half
    member = lax.axis_index("tensor")
    first = pl.multiple_of(member * half, half)
    fetches = [
        pltpu.make_async_copy(source, target.at[side], sems.at[kind, side])
        for kind, side, source, target in (
            (0, 0, up_own_hbm, up),
            (1, 0, down_own_hbm, down),
            (0, 1, up_oth_hbm, up),
            (1, 1, down_oth_hbm, down),
        )
    ]
    for fetch in fetches:
        fetch.start()
    ups, downs = (up.at[0], up.at[1]), (down.at[0], down.at[1])
    part_cols = up.shape[2]
    chunks = part_cols // chunk
    vectors[0:1, :] = ubias_ref[...][None, :]
    attended = att_ref[...].astype(bf16)
    work[...] = mm(attended, wo_ref[...])
    attn_gain, attn_shift = again_ref[...][None, :], ashift_ref[...][None, :]
    ffn_gain, ffn_shift = fgain_ref[...][None, :], fshift_ref[...][None, :]
    down_bias = dbias_ref[...][None, :]
    inverse = []
    for b in range(0, count, BLOCK):
        block = slice(b, b + BLOCK)
        if b < half:
            rows_in = content_ref[pl.ds(pl.multiple_of(first + b, BLOCK), BLOCK), :]
        else:
            rows_in = query_ref[b - half : b - half + BLOCK, :]
        found, inv, normed = norm_forward(
            work[block, :] + rows_in.astype(f32), attn_gain, attn_shift
        )
        unit[block, :] = found
        inverse.append(inv)
        low[block, :] = normed.astype(bf16)
        work[block, :] = normed + down_bias
    for fetch in fetches:
        fetch.wait()
    pieces = [(side, at) for side in range(2) for at in range(chunks)]

    def rise(index):
        side, at = pieces[index]

        def task(n):
            pre[index % 2, :, n : n + WIDE] = mm(
                low[...], ups[side][:, at * chunk + n : at * chunk + n + WIDE]
            )

        return [functools.partial(task, n) for n in range(0, chunk, WIDE)]

    def bend(index):
        side, at = pieces[index]
        cols = slice(at * chunk, (at + 1) * chunk)
        start = lax.rem(member + side, 2) * part_cols + at * chunk
        bias = vectors[0:1, pl.ds(pl.multiple_of(start, TILE), chunk)]

        def step(b):
            block = slice(b, b + BLOCK)
            act, grad = gelu_parts(pre[index % 2, block, :] + bias)
            hidden[side, block, cols] = act.astype(bf16)
            slope[side, block, cols] = grad.astype(bf16)

        return [functools.partial(step, b) for b in range(0, count, BLOCK)]

    def fall(index):
        side, at = pieces[index]
        cols = slice(at * chunk, (at + 1) * chunk)

        def task(n):
            work[:, n : n + WIDE] += mm(hidden[side, :, cols], downs[side][cols, n : n + WIDE])

        return [functools.partial(task, n) for n in range(0, D, WIDE)]

    interleave([], rise(0))
    for index in range(len(pieces)):
        tasks = rise(index + 1) if index + 1 < len(pieces) else []
        if index:
            tasks += fall(index - 1)
        interleave(bend(index), tasks)
    interleave([], fall(len(pieces) - 1))
    sums = [jnp.zeros((8, D), f32) for _ in range(5)]
    for b in range(0, count, BLOCK):
        block = slice(b, b + BLOCK)
        found, inv, out = norm_forward(work[block, :], ffn_gain, ffn_shift)
        if b < half:
            cout_ref[block, :] = out.astype(bf16)
            cot = ccot_ref[block, :].astype(f32)
        else:
            block_q = slice(b - half, b - half + BLOCK)
            qout_ref[block_q, :] = out.astype(bf16)
            cot = qcot_ref[block_q, :].astype(f32)
        residual_grad = norm_backward(cot, found, inv, ffn_gain)
        rounded = residual_grad.astype(bf16)
        down_grad[block, :] = rounded
        work[block, :] = residual_grad
        for index, value in enumerate((cot * found, cot, rounded.astype(f32))):
            sums[index] = sums[index] + fold_rows(value)
    transpose_by_dp(low_t, low[...], turn_low, size)
    transpose_by_dp(down_t, down_grad[...], turn_down, size)
    for side in range(2):
        for at in range(chunks):
            cols = slice(at * chunk, (at + 1) * chunk)
            hidden_grad = mm_nt(down_grad[...], downs[side][cols, :])
            pre_grad = (hidden_grad * slope[side, :, cols].astype(f32)).astype(bf16)
            slope[side, :, cols] = pre_grad
            ubg_ref[side : side + 1, cols] = row_sum(pre_grad.astype(f32))
            work[...] += mm_nt(pre_grad, ups[side][:, cols])

    def settle(b):
        block = slice(b, b + BLOCK)
        grad, found = work[block, :], unit[block, :]
        summed_grad = norm_backward(grad, found, inverse[b // BLOCK], attn_gain)
        sgrad_ref[block, :] = summed_grad
        down_grad[block, :] = summed_grad.astype(bf16)
        sums[3] = sums[3] + fold_rows(grad * found)
        sums[4] = sums[4] + fold_rows(grad)

    share = D // size
    bits = size.bit_length() - 1

    def other_place(place):
        found = 0
        for step in range(bits):
            there = order_of(1, bits)[step]
            found |= ((place >> (bits - 1 - there)) & 1) << (bits - 1 - step)
        return found

    def weigh(side, kind, n):
        left, right = ((low_t, slope), (down_t, hidden))[kind]
        value = mm(left[...], right[side, :, n : n + WIDE]).astype(bf16)
        target = (ffn_own_ref, ffn_oth_ref)[side]
        cols = slice(kind * part_cols + n, kind * part_cols + n + WIDE)
        if side == 0:
            target[:, cols] = value
            return
        for place in range(size):
            to = other_place(place)
            target[to * share : (to + 1) * share, cols] = value[
                place * share : (place + 1) * share
            ]

    tasks = [
        functools.partial(weigh, side, kind, n)
        for side in (1, 0)
        for kind in range(2)
        for n in range(0, part_cols, WIDE)
    ]
    interleave([functools.partial(settle, b) for b in range(0, count, BLOCK)], tasks)
    for index, value in enumerate(sums):
        small_ref[index : index + 1, :] = row_sum(value)
    small_ref[5:8, :] = jnp.zeros((3, D), f32)
    agrad_ref[...] = mm_nt(down_grad[...], wo_ref[...]).astype(bf16)
    transpose_by_owner(attended_t, attended, turn_work, size, groups)
    out_part = mm(attended_t[...], down_grad[...]).astype(bf16)
    half_rows = D // groups
    out_own_ref[...] = out_part[:half_rows]
    out_oth_ref[...] = out_part[half_rows : 2 * half_rows]


def unshift(value, shift, window):
    whole, rest = shift // TILE, shift % TILE
    row = lax.broadcasted_iota(jnp.int32, (BLOCK, TILE), 0)
    lane = lanes((BLOCK, TILE))
    index = (lane + row - rest) & (TILE - 1)
    tiles = [
        jnp.take_along_axis(
            value[:, n : n + TILE], index, axis=1, mode="promise_in_bounds"
        )
        for n in range(0, value.shape[1], TILE)
    ]
    zero = jnp.zeros((BLOCK, TILE), f32)

    def tile(n):
        return tiles[n] if 0 <= n < len(tiles) else zero

    if rest:
        here = lane >= rest - row
        found = [
            jnp.where(here, tile(n - whole), tile(n - whole - 1)) for n in range(window // TILE)
        ]
    else:
        here = lane + row < TILE
        found = [
            jnp.where(here, tile(n - whole), tile(n - whole + 1)) for n in range(window // TILE)
        ]
    return jnp.concatenate(found, axis=1)


def backward_kernel(
    half,
    groups,
    at,
    mode,
    prob_hbm,
    key_ref,
    val_ref,
    rel_ref,
    hc_ref,
    hp_ref,
    hs_ref,
    linv_ref,
    kaug_ref,
    srow_ref,
    att_ref,
    agrad_ref,
    se_ref,
    both_t_hbm,
    stack_t_hbm,
    pos_t_hbm,
    *rest,
):
    more = rest[: {"first": 2, "middle": 0, "last": 4}[mode]]
    own_ref, oth_ref, proj_ref, tok_key_ref, tok_val_ref, small_ref = rest[len(more) :][:6]
    prob, both_t, stack_t, pos_t, spread, grads, turned, sems = rest[-8:]
    count, window = 2 * half, KEYS + half
    heads = 4
    prob_copies = [
        pltpu.make_async_copy(prob_hbm.at[at * heads + h], prob.at[h], sems.at[h])
        for h in range(heads)
    ]
    fetches = [
        pltpu.make_async_copy(source, target, sems.at[heads + index])
        for index, (source, target) in enumerate(
            ((both_t_hbm, both_t), (stack_t_hbm, stack_t), (pos_t_hbm, pos_t))
        )
    ]
    for copy in prob_copies + fetches:
        copy.start()
    share = D // groups
    if mode == "first":
        own_ref[:, 4 * QUAD :] = more[0][...]
        oth_ref[:, 4 * QUAD :] = more[1][...]
    kaug_t = kaug_ref[...]
    filler = jnp.zeros((HEAD_DIM - kaug_t.shape[0], KEYS), bf16)
    marks = jnp.concatenate([srow_ref[0:1, :], srow_ref[0:1, :]], axis=1)
    swing = 1.0 - 2.0 * marks
    key_t, val_t, rel_t = [], [], []
    lane = lanes((count, PAIR))
    agrads, grad_x, agrad_t = [], [], []
    for pair in range(2):
        cols = slice(pair * PAIR, (pair + 1) * PAIR)
        linv = jnp.where(
            lane < HEAD_DIM,
            linv_ref[:, 2 * pair : 2 * pair + 1],
            linv_ref[:, 2 * pair + 1 : 2 * pair + 2],
        )
        agrad = (agrad_ref[:, cols].astype(f32) * linv).astype(bf16).astype(f32)
        products = agrad * att_ref[:, cols]
        agrad_t.append(turn(agrad.astype(bf16)).astype(bf16))
        for head in range(2):
            base = (1 - head) * HEAD_DIM
            mine = (lane < HEAD_DIM) == (head == 0)
            weight = jnp.sum(jnp.where(mine, products, 0.0), axis=1, keepdims=True)
            high = weight.astype(bf16).astype(f32)
            grad_x.append(
                jnp.where(
                    mine,
                    agrad,
                    jnp.where(
                        lane == base, -high, jnp.where(lane == base + 1, high - weight, 0.0)
                    ),
                ).astype(bf16)
            )
    found = {}

    def head_of(ref, which):
        return ref[which * HEAD_DIM : (which + 1) * HEAD_DIM, :]

    def spreads(which):
        own = head_of(val_ref, which)
        sides = [own, kaug_t, filler] if which % 2 == 0 else [kaug_t, filler, own]
        val_x = jnp.concatenate(sides, axis=0)
        prob_copies[which].wait()

        def task(n, stop):
            spread[which % 2, :, n:stop] = mm(grad_x[which], val_x[:, n:stop])

        return [functools.partial(task, n, min(n + WIDE, KEYS)) for n in range(0, KEYS, WIDE)]

    def score_grads(which):
        buffer = which % 2

        def step(part, b):
            at_row = part * half + b
            block = slice(at_row, at_row + BLOCK)
            score_grad = prob[which, block, :].astype(f32) * spread[buffer, block, :]
            grads[buffer, block, :] = score_grad.astype(bf16)
            turned[buffer, block, :] = unshift(score_grad, half - b, window).astype(bf16)

        return [
            functools.partial(step, part, b) for part in range(2) for b in range(0, half, BLOCK)
        ]

    def gathers(which):
        buffer = which % 2
        side = slice(which % 2 * HEAD_DIM, (which % 2 + 1) * HEAD_DIM)
        key_x = jnp.concatenate([head_of(key_ref, which), kaug_t], axis=0)
        found[which] = {"value": [], "key": [], "rel": [], "content": [], "place": []}

        def down_rows(name, left, ref, n, stop):
            found[which][name].append(mm(left, ref[:, n:stop]))

        tasks = []
        for name, left, ref, end in (
            ("value", agrad_t[which // 2][side], prob.at[which], KEYS),
            ("key", head_of(hc_ref, which), grads.at[buffer], KEYS),
            ("rel", head_of(hp_ref, which), turned.at[buffer], window),
        ):
            tasks += [
                functools.partial(down_rows, name, left, ref, n, min(n + WIDE, end))
                for n in range(0, end, WIDE)
            ]

        def content(n):
            found[which]["content"].append(mm_nt(key_x, grads[buffer, n : n + half, :]))

        def placed(n):
            found[which]["place"].append(
                mm_nt(head_of(rel_ref, which), turned[buffer, n : n + half, :])
            )

        for n in (0, half):
            tasks += [functools.partial(content, n), functools.partial(placed, n)]
        return tasks

    interleave([], spreads(0))
    for which in range(heads):
        tasks = spreads(which + 1) if which + 1 < heads else []
        if which:
            tasks += gathers(which - 1)
        interleave(score_grads(which), tasks)
    interleave([], gathers(heads - 1))
    for which in range(heads):
        val_t.append(jnp.concatenate(found[which]["value"], axis=1))
        key_t.append(jnp.concatenate(found[which]["key"], axis=1))
        rel_t.append(jnp.concatenate(found[which]["rel"], axis=1))
    same, other, contents, places = [], [], [], []
    for which in range(heads):
        content_head = jnp.concatenate(found[which]["content"], axis=1)
        total = content_head[HEAD_DIM : HEAD_DIM + 1]
        marked = content_head[HEAD_DIM + 4 : HEAD_DIM + 5]
        other.append(SCALE * (marks * total + swing * marked))
        same.append(SCALE * total - other[-1])
        contents.append((SCALE * content_head[:HEAD_DIM]).astype(bf16))
        places.append((SCALE * jnp.concatenate(found[which]["place"], axis=1)).astype(bf16))
    contents, places = jnp.concatenate(contents, axis=0), jnp.concatenate(places, axis=0)
    term_high, term_low = split(jnp.concatenate(same + other, axis=0))
    line = lax.broadcasted_iota(jnp.int32, (2 * heads, QUAD), 0)
    mine = line % heads == lanes((2 * heads, QUAD)) // HEAD_DIM
    embed = jnp.where(line < heads, se_ref[0:1, :], se_ref[1:2, :])
    embed_high, embed_low = split(jnp.where(mine, embed, 0.0))
    segment_grad = mm_tn(
        jnp.concatenate([embed_high, embed_high, embed_low, embed_low], axis=0),
        jnp.concatenate([term_high, term_low, term_high, term_low], axis=0),
    )
    proj_t = (contents.astype(f32) + places.astype(f32) + segment_grad).astype(bf16)
    ones = jnp.ones((16, count), bf16)
    small_ref[0:1, :] = mm_nt(ones, contents)[0:1]
    small_ref[1:2, :] = mm_nt(ones, places)[0:1]
    small_ref[2:3, :] = functools.reduce(
        jnp.add, [mm_nt(ones, part)[0:1] for part in split(segment_grad)]
    )
    terms = jnp.concatenate([term_high, term_low], axis=0)
    embed_grad = functools.reduce(jnp.add, [mm(terms, part) for part in split(hs_ref[...])])
    embed_grad = jnp.where(mine, embed_grad[: 2 * heads] + embed_grad[2 * heads :], 0.0)
    small_ref[3:4, :] = row_sum(embed_grad[:heads])
    small_ref[4:5, :] = row_sum(embed_grad[heads:])
    small_ref[5:8, :] = jnp.zeros((3, QUAD), f32)
    key_t = jnp.concatenate(key_t, axis=0).astype(bf16)
    val_t = jnp.concatenate(val_t, axis=0).astype(bf16)
    rel_t = jnp.concatenate(rel_t, axis=0).astype(bf16)
    proj_ref[...] = turn(proj_t).astype(bf16)
    tok_key_ref[...] = turn(key_t[:, MEM:]).astype(bf16)
    tok_val_ref[...] = turn(val_t[:, MEM:]).astype(bf16)
    for fetch in fetches:
        fetch.wait()
    parts = (
        mm_nt(both_t[...], proj_t),
        mm_nt(stack_t[...], key_t),
        mm_nt(stack_t[...], val_t),
        mm_nt(pos_t[...], rel_t),
    )
    for index, value in enumerate(parts):
        cols = slice(index * QUAD, (index + 1) * QUAD)
        own_ref[:, cols] = value[:share].astype(bf16)
        oth_ref[:, cols] = value[share : 2 * share].astype(bf16)
    if mode == "last":
        vec_ref = rest[len(more) + 6]
        early, ubias, before, between = more
        core = lax.axis_index("tensor")
        rows = [early[0:5, :]]
        mine = [ubias[0:1, n : n + D] for n in range(0, ubias.shape[1], D)]
        theirs = [ubias[1:2, n : n + D] for n in range(0, ubias.shape[1], D)]
        for left, right in ((mine, theirs), (theirs, mine)):
            rows += [jnp.where(core == 0, a, b) for a, b in zip(left, right)]
        rows.append(
            jnp.concatenate([before[0:5, :], between[0:5, :], small_ref[0:5, :]], axis=1)
        )
        rows = jnp.concatenate(rows, axis=0)
        spare = jnp.zeros((VECTORS - rows.shape[0], D), f32)
        rows = jnp.concatenate([rows, spare], axis=0)
        packed = jnp.concatenate([rows[:, n : n + TILE] for n in range(0, D, TILE)], axis=0)
        vec_ref[...] = packed
        oth_ref[:VECTOR_ROWS, 4 * QUAD :] = packed.astype(bf16)
        oth_ref[VECTOR_ROWS:, 4 * QUAD :] = jnp.zeros((share - VECTOR_ROWS, TILE), bf16)


def rows_kernel(half, groups, sgrad_ref, *rest):
    proj, keys, vals = rest[:QUADS], rest[QUADS : 2 * QUADS], rest[2 * QUADS : 3 * QUADS]
    wq_ref, wk_ref, wv_ref, own_ref, query_ref, send_ref, both = rest[3 * QUADS :]
    member = lax.axis_index("tensor")
    wide = [jnp.concatenate([ref[...] for ref in refs], axis=1) for refs in (proj, keys, vals)]
    both[...] = mm_nt(wide[1], wk_ref[...]) + mm_nt(wide[2], wv_ref[...])
    rows = sgrad_ref[...] + mm_nt(wide[0], wq_ref[...])
    own = pl.multiple_of(member * half, half)
    other = pl.multiple_of(lax.rem(member + 1, groups) * half, half)
    send_ref[...] = both[pl.ds(other, half), :].astype(bf16)
    own_ref[...] = rows[:half] + both[pl.ds(own, half), :]
    query_ref[...] = rows[half:]


def summed(operands, terms, first, rows, width):
    values = []
    for index, at in terms:
        if rows % 16 == 0:
            value = operands[index][first : first + rows, at : at + width].astype(f32)
        else:
            value = operands[index][:, at : at + width].astype(f32)[first : first + rows]
        values.append(value)
    return functools.reduce(jnp.add, values)


def vector_width(rows):
    return TILE * max(1, VECTOR_ROWS // rows)


def fold_vectors(packed, rows):
    if rows > VECTOR_ROWS:
        return jnp.concatenate([packed, jnp.zeros((rows - VECTOR_ROWS, TILE), f32)], axis=0)
    return jnp.concatenate(
        [packed[n : n + rows] for n in range(0, VECTOR_ROWS, rows)], axis=1
    )


def unfold_vectors(block, rows):
    if rows >= VECTOR_ROWS:
        return block[:VECTOR_ROWS]
    return jnp.concatenate(
        [block[:, n : n + TILE] for n in range(0, vector_width(rows), TILE)], axis=0
    )


def summed_vectors(values, terms):
    return functools.reduce(
        jnp.add,
        [
            unfold_vectors(
                values(index)[:rows, at : at + vector_width(rows)].astype(f32), rows
            )
            for index, at, rows in terms
        ],
    )


def combine_kernel(plans, *refs):
    count = sum(pieces + (1 if vectors else 0) for _, pieces, _, vectors in plans)
    operands, outs = refs[:-count], list(refs[-count:])
    for rows, pieces, parts, vectors in plans:
        if vectors:
            packed = summed_vectors(lambda index: operands[index][...].astype(f32), vectors)
            outs.pop(0)[...] = packed
        for piece in range(pieces):
            out_ref = outs.pop(0)
            column = 0
            for width, terms in parts:
                value = summed(operands, terms, piece * rows, rows, width)
                out_ref[:, column : column + width] = value.astype(out_ref.dtype)
                column += width
            if piece and vectors:
                out_ref[:, column:] = fold_vectors(packed, rows).astype(out_ref.dtype)


def unpack_vectors(packed):
    return jnp.concatenate(
        [packed[n : n + VECTORS] for n in range(0, VECTOR_ROWS, VECTORS)], axis=1
    )


def finish_kernel(size, groups, count, plan, up_rows, *refs):
    operands, outs = refs[:count], refs[count:]
    weights, vec_outs, embed_out, up_out = outs[:5], outs[5:-2], outs[-2], outs[-1]
    place = lax.axis_index("dp") * groups + lax.axis_index("tensor")
    share = D // (size * groups)
    for target, at, width, terms in plan[0]:
        weights[target][:, at : at + width] = summed(operands, terms, 0, share, width)
    value = unpack_vectors(
        summed_vectors(lambda index: operands[index][...].astype(f32), plan[1])
    )
    mine = pltpu.roll(value, lax.rem(D - place * share, D), 1)[:, :TILE]
    rows = [row for row in range(5 + up_rows + 3) if not 5 <= row < 5 + up_rows]
    for row, out_ref in zip(rows, vec_outs):
        out_ref[...] = mine[row, :share]
    embed = jnp.concatenate([mine[5 + up_rows + 3 : 5 + up_rows + 5], jnp.zeros((6, TILE), f32)], axis=0)
    embed_out[...] = embed.T[:share, :2]
    wide = up_rows * share
    each = D // wide
    line = lax.div(place, each)
    chosen = functools.reduce(
        jnp.add,
        [jnp.where(line == r, value[5 + r : 6 + r], 0.0) for r in range(up_rows)],
    )
    chosen = jnp.broadcast_to(chosen, (8, D))
    turned = pltpu.roll(chosen, lax.rem(D - lax.rem(place, each) * wide, D), 1)[:, :TILE]
    up_out[...] = turned[0, :wide]


def whole(shape):
    return pl.BlockSpec(shape, lambda i: (0,) * len(shape))


def columns(rows, width, at=None):
    if at is None:
        return pl.BlockSpec((rows, width), lambda i: (0, i))
    return pl.BlockSpec((rows, width), lambda i: (0, at))


def row_block(rows, width, at=None):
    if at is None:
        return pl.BlockSpec((rows, width), lambda i: (i, 0))
    return pl.BlockSpec((rows, width), lambda i: (at, 0))


def scalars():
    return pl.BlockSpec(memory_space=pltpu.SMEM)


def params(size=VMEM_BYTES):
    return pltpu.CompilerParams(vmem_limit_bytes=size)


def cost(flops, bytes_accessed):
    return pl.CostEstimate(flops=flops, bytes_accessed=bytes_accessed, transcendentals=0)


def in_hbm():
    return pl.BlockSpec(memory_space=pl.ANY)


def attention_forward(
    half, ints, memory, content, query, weights, biases, segment_rows
):
    count, window = 2 * half, KEYS + half
    coarse_rows = -(-(window // 32) // 8) * 8
    outs = (
        ((count, D), f32, columns(count, QUAD)),
        ((HEADS, count, KEYS), bf16, pl.BlockSpec((4, count, KEYS), lambda i: (i, 0, 0))),
        ((D, KEYS), bf16, row_block(QUAD, KEYS)),
        ((D, KEYS), bf16, row_block(QUAD, KEYS)),
        ((D, window), bf16, row_block(QUAD, window)),
        ((D, count), bf16, row_block(QUAD, count)),
        ((D, count), bf16, row_block(QUAD, count)),
        ((count, D), f32, columns(count, QUAD)),
        ((count, QUADS * TILE), f32, columns(count, TILE)),
        ((16, KEYS), bf16, whole((16, KEYS))),
        ((8, half), f32, whole((8, half))),
        ((window, D), bf16, whole((window, D))),
    )
    return pl.pallas_call(
        functools.partial(forward_kernel, half),
        grid=(QUADS,),
        out_shape=[jax.ShapeDtypeStruct(shape, kind) for shape, kind, _ in outs],
        in_specs=[
            scalars(),
            scalars(),
            whole((1, LEN)),
            whole((1, LEN)),
            whole((1, LEN)),
            whole((MEM, D)),
            whole((LEN, D)),
            whole((half, D)),
        ]
        + [columns(D, QUAD)] * 4
        + [whole((D,))] * 3
        + [columns(2, QUAD)],
        out_specs=[spec for _, _, spec in outs],
        scratch_shapes=[
            pltpu.VMEM((KEYS, D), bf16),
            pltpu.VMEM((count, D), bf16),
            pltpu.VMEM((window, D), bf16),
            pltpu.VMEM((count, KEYS), f32),
            pltpu.VMEM((2, 32, D // 2), f32),
            pltpu.VMEM((2, coarse_rows, D // 2), f32),
            pltpu.VMEM((8, D), f32),
            pltpu.VMEM((2, count, KEYS), f32),
            pltpu.VMEM((2, count, window), f32),
            pltpu.VMEM((HEAD_DIM, KEYS), bf16),
            pltpu.VMEM((half, PAIR), f32),
            pltpu.VMEM((8, LEN), f32),
            pltpu.VMEM((KEYS, PAIR), bf16),
            pltpu.VMEM((LEN, TILE), f32),
            pltpu.VMEM((LEN, TILE), f32),
        ],
        compiler_params=params(),
        cost_estimate=cost(30_000_000_000, 40_000_000),
        name="attention_forward",
    )(*ints, memory, content, query, *weights, *biases, segment_rows)


def middle(half, size, groups, arrays, hidden_cols):
    count, share = 2 * half, D // groups
    chunk = min(hidden_cols, 768)
    outs = (
        ((half, D), bf16),
        ((half, D), bf16),
        ((D, 2 * hidden_cols), bf16),
        ((D, 2 * hidden_cols), bf16),
        ((count, D), f32),
        ((count, D), bf16),
        ((share, D), bf16),
        ((share, D), bf16),
        ((8, D), f32),
        ((2, hidden_cols), f32),
    )
    weights = (6, 7, 8, 9)
    return pl.pallas_call(
        functools.partial(middle_kernel, half, size, groups, chunk),
        grid=(1,),
        out_shape=[jax.ShapeDtypeStruct(shape, kind) for shape, kind in outs],
        in_specs=[
            in_hbm() if i in weights else whole(array.shape) for i, array in enumerate(arrays)
        ],
        out_specs=[whole(shape) for shape, _ in outs],
        scratch_shapes=[
            pltpu.VMEM((2, count, hidden_cols), bf16),
            pltpu.VMEM((2, count, hidden_cols), bf16),
            pltpu.VMEM((2, count, chunk), f32),
            pltpu.VMEM((count, D), f32),
            pltpu.VMEM((count, D), f32),
            pltpu.VMEM((count, D), bf16),
            pltpu.VMEM((count, D), bf16),
            pltpu.VMEM((8, FF), f32),
            pltpu.VMEM((2, D, hidden_cols), bf16),
            pltpu.VMEM((2, hidden_cols, D), bf16),
            pltpu.VMEM((D, count), bf16),
            pltpu.VMEM((D, count), bf16),
            pltpu.VMEM((D, count), bf16),
            pltpu.VMEM((D, count), bf16),
            pltpu.VMEM((D, count), bf16),
            pltpu.VMEM((D, count), f32),
            pltpu.SemaphoreType.DMA((2, 2)),
        ],
        compiler_params=params(),
        cost_estimate=cost(30_000_000_000, 30_000_000),
        name="feed_forward",
    )(*arrays)


def prepare_kernel(
    half,
    size,
    groups,
    memory_ref,
    content_ref,
    query_ref,
    pos_ref,
    both_t_ref,
    stack_t_ref,
    pos_t_ref,
    both_work,
    stack_work,
    pos_work,
):
    first = pl.multiple_of(lax.axis_index("tensor") * half, half)
    both = jnp.concatenate([content_ref[pl.ds(first, half), :], query_ref[...]], axis=0)
    stack = jnp.concatenate([memory_ref[...], content_ref[...]], axis=0)
    transpose_by_owner(both_t_ref, both, both_work, size, groups)
    transpose_by_owner(stack_t_ref, stack, stack_work, size, groups)
    transpose_by_owner(pos_t_ref, pos_ref[...], pos_work, size, groups)


def transposed_rows(half, size, groups, memory, content, query, pos):
    count, window = 2 * half, KEYS + half
    arrays = (memory, content, query, pos)
    outs = ((D, count), (D, KEYS), (D, window))
    return pl.pallas_call(
        functools.partial(prepare_kernel, half, size, groups),
        grid=(1,),
        out_shape=[jax.ShapeDtypeStruct(shape, bf16) for shape in outs],
        in_specs=[whole(array.shape) for array in arrays],
        out_specs=[whole(shape) for shape in outs],
        scratch_shapes=[pltpu.VMEM(shape, f32) for shape in outs],
        compiler_params=params(BACKWARD_BYTES),
        cost_estimate=cost(6_000_000_000, 8_000_000),
        name="transposed_rows",
    )(*arrays)


def attention_backward(half, groups, at, mode, saved, agrad, segment_rows, extra):
    count, window, share = 2 * half, KEYS + half, D // groups
    att, prob, keys, values, rel, hc, hp, hs, linv, kaug, srow, _ = saved[:12]
    both_t, stack_t, pos_t = saved[12:]
    width = 4 * QUAD + (D if mode == "first" else 0)
    operands = (
        (prob, in_hbm()),
        (keys, row_block(QUAD, KEYS, at)),
        (values, row_block(QUAD, KEYS, at)),
        (rel, row_block(QUAD, window, at)),
        (hc, row_block(QUAD, count, at)),
        (hp, row_block(QUAD, count, at)),
        (hs, columns(count, QUAD, at)),
        (linv, columns(count, TILE, at)),
        (kaug, whole((16, KEYS))),
        (srow, whole((8, half))),
        (att, columns(count, QUAD, at)),
        (agrad, columns(count, QUAD, at)),
        (segment_rows, columns(2, QUAD, at)),
        (both_t, in_hbm()),
        (stack_t, in_hbm()),
        (pos_t, in_hbm()),
    ) + tuple((array, whole(array.shape)) for array in extra)
    outs = (
        ((share, width), bf16),
        ((share, width + (TILE if mode == "last" else 0)), bf16),
        ((count, QUAD), bf16),
        ((LEN, QUAD), bf16),
        ((LEN, QUAD), bf16),
        ((8, QUAD), f32),
    )
    if mode == "last":
        outs += (((VECTOR_ROWS, TILE), f32),)
    return pl.pallas_call(
        functools.partial(backward_kernel, half, groups, at, mode),
        grid=(1,),
        out_shape=[jax.ShapeDtypeStruct(shape, kind) for shape, kind in outs],
        in_specs=[spec for _, spec in operands],
        out_specs=[whole(shape) for shape, _ in outs],
        scratch_shapes=[
            pltpu.VMEM((4, count, KEYS), bf16),
            pltpu.VMEM((D, count), bf16),
            pltpu.VMEM((D, KEYS), bf16),
            pltpu.VMEM((D, window), bf16),
            pltpu.VMEM((2, count, KEYS), f32),
            pltpu.VMEM((2, count, KEYS), bf16),
            pltpu.VMEM((2, count, window), bf16),
            pltpu.SemaphoreType.DMA((7,)),
        ],
        compiler_params=params(BACKWARD_BYTES),
        cost_estimate=cost(16_000_000_000, 16_000_000),
        name="attention_backward",
    )(*[array for array, _ in operands])


def row_gradients(half, groups, summed_grad, proj, keys, vals, weights):
    count = 2 * half
    arrays = (summed_grad, *proj, *keys, *vals, *weights)
    outs = (((half, D), f32), ((half, D), f32), ((half, D), bf16))
    return pl.pallas_call(
        functools.partial(rows_kernel, half, groups),
        grid=(1,),
        out_shape=[jax.ShapeDtypeStruct(shape, kind) for shape, kind in outs],
        in_specs=[whole(array.shape) for array in arrays],
        out_specs=[whole(shape) for shape, _ in outs],
        scratch_shapes=[pltpu.VMEM((LEN, D), f32)],
        compiler_params=params(COMBINE_BYTES),
        cost_estimate=cost(4_000_000_000, 10_000_000),
        name="row_gradients",
    )(*arrays)


def swap(array):
    groups = lax.axis_size("tensor")
    return lax.ppermute(array, "tensor", [(i, (i + 1) % groups) for i in range(groups)])


def across(array, masks):
    size, groups = lax.axis_size("dp"), lax.axis_size("tensor")
    pairs = [
        (place * groups + core, (place ^ masks[core]) * groups + core)
        for place in range(size)
        for core in range(groups)
    ]
    return lax.ppermute(array, ("dp", "tensor"), pairs)


def total(terms):
    return functools.reduce(jnp.add, [term.astype(f32) for term in terms])


class Chain:
    def __init__(self, parts, rows, vectors=()):
        self.parts, self.rows = parts, rows
        self.vectors = list(vectors)
        self.messages = None
        self.done = 0

    def masks(self, part, bits):
        size, groups = lax.axis_size("dp"), lax.axis_size("tensor")
        found = []
        for core in range(groups):
            order = order_of(core, size.bit_length() - 1)[self.done : self.done + bits]
            found.append(
                sum(((part >> (bits - 1 - j)) & 1) << bit for j, bit in enumerate(order))
            )
        return found

    def send(self):
        if not self.bits:
            gots = [swap(self.messages[0])]
        else:
            gots = [
                across(message, self.masks(part + 1, self.bits))
                for part, message in enumerate(self.messages)
            ]
        for got in gots:
            column = 0
            for width, terms in self.parts:
                terms.append((got, column))
                column += width
            if self.vectors:
                self.vectors.append((got, column, self.rows))
        self.pending = gots
        self.done += self.bits
        self.messages = None

    def take(self, results):
        if self.vectors:
            self.vectors = [(results.pop(0), 0, VECTOR_ROWS)]
        kept, column, parts = results.pop(0), 0, []
        for width, _ in self.parts:
            parts.append((width, [(kept, column)]))
            column += width
        self.parts = parts
        self.messages = [results.pop(0) for _ in range((1 << self.bits) - 1)]

    def replace(self, old, new):
        for index, (width, terms) in enumerate(self.parts):
            self.parts[index] = (
                width,
                [(new if array is old else array, at) for array, at in terms],
            )
        self.vectors = [(new if a is old else a, at, rows) for a, at, rows in self.vectors]


def merged(chains):
    chain = Chain(
        [part for chain in chains for part in chain.parts],
        chains[0].rows,
        [term for chain in chains for term in chain.vectors],
    )
    chain.done = chains[0].done
    chain.pending = []
    return chain


class Operands:
    def __init__(self):
        self.arrays = []

    def of(self, array):
        for index, held in enumerate(self.arrays):
            if held is array:
                return index
        self.arrays.append(array)
        return len(self.arrays) - 1

    def in_specs(self):
        return [whole(array.shape) for array in self.arrays]


def prepare(requests):
    operands, plans, outs = Operands(), [], []
    plain = any(chain.rows % (8 << bits) for chain, bits in requests)
    for chain, bits in requests:
        chain.bits = bits
        chain.rows >>= bits
        rows, pieces = chain.rows, 1 << bits
        width = sum(width for width, _ in chain.parts)
        if plain:
            results = [
                jnp.concatenate(
                    [
                        total(
                            [
                                array[piece * rows : (piece + 1) * rows, at : at + width]
                                for array, at in terms
                            ]
                        )
                        for width, terms in chain.parts
                    ],
                    axis=1,
                )
                for piece in range(pieces)
            ]
            if chain.vectors:
                packed = summed_vectors(lambda array: array, chain.vectors)
                folded = fold_vectors(packed, rows)
                results = [packed, results[0]] + [
                    jnp.concatenate([result, folded], axis=1) for result in results[1:]
                ]
            chain.take([result.astype(bf16) for result in results])
            continue
        parts = [
            (width, [(operands.of(array), at) for array, at in terms])
            for width, terms in chain.parts
        ]
        vectors = [(operands.of(array), at, held) for array, at, held in chain.vectors]
        plans.append((rows, pieces, parts, vectors))
        if vectors:
            outs.append(((VECTOR_ROWS, TILE), f32))
        outs.append(((rows, width), bf16))
        wide = width + (vector_width(rows) if vectors else 0)
        outs += [((rows, wide), bf16)] * (pieces - 1)
    if plain:
        return
    results = pl.pallas_call(
        functools.partial(combine_kernel, plans),
        grid=(1,),
        out_shape=[jax.ShapeDtypeStruct(shape, kind) for shape, kind in outs],
        in_specs=operands.in_specs(),
        out_specs=[whole(shape) for shape, _ in outs],
        compiler_params=params(COMBINE_BYTES),
        cost_estimate=cost(1_000_000_000, 8_000_000),
        name="combine",
    )(*operands.arrays)
    results = list(results)
    for chain, bits in requests:
        chain.take(results)


def launch(requests, value, waits=()):
    chains = [chain for chain, bits in requests if bits is not None] + list(waits)
    olds = [got for chain in chains for got in chain.pending]
    if olds:
        value, news = lax.optimization_barrier((value, olds))
        for chain in chains + [chain for chain, _ in requests]:
            for old, new in zip(olds, news):
                chain.replace(old, new)
        for chain in chains:
            chain.pending = []
    sums = [(chain, bits) for chain, bits in requests if bits is not None]
    if sums:
        prepare(sums)
    messages = [chain.messages for chain, _ in requests]
    value, messages = lax.optimization_barrier((value, messages))
    for (chain, bits), message in zip(requests, messages):
        chain.messages = message
        if bits is None:
            chain.bits = 0
        chain.send()
    return value


def finish(size, groups, chain):
    share = D // (size * groups)
    up_rows = FF // D
    pieces = []
    for quad, (width, terms) in enumerate(chain.parts):
        for index in range(4):
            pieces.append((index, quad * QUAD, QUAD, [(a, at + index * QUAD) for a, at in terms]))
        if width > 4 * QUAD:
            pieces.append((4, 0, D, [(a, at + 4 * QUAD) for a, at in terms]))
    if share % 8:
        blocks = {}
        for target, at, width, terms in pieces:
            blocks.setdefault(target, []).append(
                total([array[:share, c : c + width] for array, c in terms])
            )
        weights = [jnp.concatenate(blocks[target], axis=1) for target in range(5)]
        vectors = unpack_vectors(summed_vectors(lambda array: array, chain.vectors))
        place = lax.axis_index("dp") * groups + lax.axis_index("tensor")
        mine = lax.dynamic_slice_in_dim(vectors, place * share, share, 1)
        ups = lax.dynamic_slice_in_dim(
            vectors[5 : 5 + up_rows].reshape(-1), place * up_rows * share, up_rows * share, 0
        )
        late = 5 + up_rows
        return weights, [mine[r] for r in (0, 1, 2, 3, 4, late, late + 1, late + 2)], mine[
            late + 3 : late + 5
        ].T, ups
    operands = Operands()
    plan = [
        (target, at, width, [(operands.of(array), c) for array, c in terms])
        for target, at, width, terms in pieces
    ]
    vectors = [(operands.of(array), at, held) for array, at, held in chain.vectors]
    outs = [(share, D)] * 5 + [(share,)] * 8 + [(share, 2), (up_rows * share,)]
    found = pl.pallas_call(
        functools.partial(
            finish_kernel, size, groups, len(operands.arrays), (plan, vectors), up_rows
        ),
        grid=(1,),
        out_shape=[jax.ShapeDtypeStruct(shape, f32) for shape in outs],
        in_specs=operands.in_specs(),
        out_specs=[whole(shape) for shape in outs],
        compiler_params=params(COMBINE_BYTES),
        name="finish",
    )(*operands.arrays)
    return found[:5], found[5:13], found[13], found[14]


def body(
    content_in,
    query_in,
    memory,
    content_cot,
    query_cot,
    query_weight,
    key_weight,
    value_weight,
    out_weight,
    rel_weight,
    content_bias,
    position_bias,
    segment_bias,
    segment_embed,
    attn_gain,
    attn_shift,
    up_weight,
    up_bias,
    down_weight,
    down_bias,
    ffn_gain,
    ffn_shift,
    lengths,
    memory_lengths,
    segment_ids,
    orders,
    targets,
):
    groups = lax.axis_size("tensor")
    size = lax.axis_size("dp")
    steps = size.bit_length() - 1
    half = LEN // groups
    hidden_cols = up_weight.shape[1]
    up_other, down_other = swap(up_weight), swap(down_weight)
    content, query = content_in[0], query_in[0]
    segment_rows = segment_embed.T
    saved = attention_forward(
        half,
        (lengths, memory_lengths, segment_ids, orders, targets),
        memory[0],
        content,
        query,
        (query_weight, key_weight, value_weight, rel_weight),
        (content_bias, position_bias, segment_bias),
        segment_rows,
    )
    (
        content_out,
        query_out,
        ffn_own,
        ffn_other,
        summed_grad,
        attended_grad,
        out_own,
        out_other,
        early_small,
        up_bias_part,
    ) = middle(
        half,
        size,
        groups,
        (
            saved[0],
            content,
            query,
            content_cot[0],
            query_cot[0],
            out_weight,
            up_weight,
            up_other,
            down_weight,
            down_other,
            up_bias,
            down_bias,
            attn_gain,
            attn_shift,
            ffn_gain,
            ffn_shift,
        ),
        hidden_cols,
    )
    ffn = Chain([(2 * hidden_cols, [(ffn_own, 0)])], D)
    ffn.messages = [ffn_other]
    held = launch([(ffn, None)], attended_grad)
    content_late, held = lax.optimization_barrier((content, held))
    turned = transposed_rows(half, size, groups, memory[0], content_late, query, saved[11])
    turned, held = lax.optimization_barrier((turned, held))
    saved = (*saved, *turned)
    proj, tok_keys, tok_vals, small, late = [], [], [], [], []

    def backward(at, mode, grad, extra):
        own, other, proj_part, key_part, val_part, small_part, *vectors = attention_backward(
            half, groups, at, mode, saved, grad, segment_rows, extra
        )
        proj.append(proj_part)
        tok_keys.append(key_part)
        tok_vals.append(val_part)
        small.append(small_part)
        chain = Chain(
            [(own.shape[1], [(own, 0)])],
            own.shape[0],
            [(array, 0, VECTOR_ROWS) for array in vectors],
        )
        chain.messages = [other]
        late.append(chain)

    held = launch([(ffn, 1)], held)
    backward(0, "first", held, (out_own, out_other))
    held, proj[0] = launch([(late[0], None)], (attended_grad, proj[0]))
    backward(1, "middle", held, ())
    held, proj[1] = launch(
        [(ffn, 1), (late[0], 1), (late[1], None)], (attended_grad, proj[1])
    )
    backward(2, "last", held, (early_small, up_bias_part, *small))
    xy = min(2, steps)
    proj[2] = launch(
        [(late[2], None), (ffn, 1), (late[0], 1), (late[1], 1)], proj[2]
    )
    own_rows, query_grad, row_send = row_gradients(
        half, groups, summed_grad, proj, tok_keys, tok_vals, (query_weight, key_weight, value_weight)
    )
    own_rows, row_send = launch(
        [(late[2], xy), (late[1], 1), (ffn, 1)], (own_rows, row_send)
    )
    final = merged(late)
    own_rows, row_send = launch(
        [(final, min(2, steps - final.done))], (own_rows, row_send), late
    )
    row_got = swap(row_send)
    while final.done < steps:
        own_rows = launch([(final, min(2, steps - final.done))], own_rows)
    while ffn.done < steps:
        own_rows = launch([(ffn, min(2, steps - ffn.done))], own_rows)
    content_grad = own_rows + row_got.astype(f32)
    ffn_sum = total([array[: ffn.rows] for array, _ in ffn.parts[0][1]])
    up_grad, down_grad_own = ffn_sum[:, :hidden_cols], ffn_sum[:, hidden_cols:].T
    weights, vectors, segment_grad, up_bias_grad = finish(size, groups, final)
    return (
        content_out[None],
        query_out[None],
        content_grad[None],
        query_grad[None],
        weights[0],
        weights[1],
        weights[2],
        weights[4],
        weights[3],
        vectors[5],
        vectors[6],
        vectors[7],
        segment_grad,
        vectors[3],
        vectors[4],
        up_grad,
        up_bias_grad,
        down_grad_own,
        vectors[2],
        vectors[0],
        vectors[1],
    )


def solution(mesh):
    in_specs = (
        P("dp", None, None),
        P("dp", "tensor", None),
        P("dp", None, None),
        P("dp", "tensor", None),
        P("dp", "tensor", None),
        P(),
        P(),
        P(),
        P(),
        P(),
        P(),
        P(),
        P(),
        P(),
        P(),
        P(),
        P(None, "tensor"),
        P(),
        P("tensor", None),
        P(),
        P(),
        P(),
        P("dp"),
        P("dp"),
        P("dp", None),
        P("dp", None),
        P("dp", None),
    )
    out_specs = (
        P("dp", "tensor", None),
        P("dp", "tensor", None),
        P("dp", "tensor", None),
        P("dp", "tensor", None),
        P(("dp", "tensor"), None),
        P(("dp", "tensor"), None),
        P(("dp", "tensor"), None),
        P(("dp", "tensor"), None),
        P(("dp", "tensor"), None),
        P(("dp", "tensor")),
        P(("dp", "tensor")),
        P(("dp", "tensor")),
        P(("dp", "tensor"), None),
        P(("dp", "tensor")),
        P(("dp", "tensor")),
        P("dp", "tensor"),
        P(("dp", "tensor")),
        P("tensor", "dp"),
        P(("dp", "tensor")),
        P(("dp", "tensor")),
        P(("dp", "tensor")),
    )
    return jax.shard_map(body, mesh=mesh, in_specs=in_specs, out_specs=out_specs, check_vma=False)
```

```python
import functools

import jax
import jax.numpy as jnp
from jax import lax
from jax.experimental import pallas as pl
from jax.experimental.pallas import tpu as pltpu
from jax.sharding import PartitionSpec as P

D = 768
HEADS = 12
HEAD_DIM = 64
FF = 3072
LEN = 512
MEM = 384
KEYS = MEM + LEN
QUAD = 4 * HEAD_DIM
QUADS = D // QUAD
PAIR = 2 * HEAD_DIM
SCALE = HEAD_DIM ** (-0.5)
VMEM_BYTES = 61 * 1024 * 1024
COMBINE_BYTES = 28 * 1024 * 1024
BACKWARD_BYTES = 54 * 1024 * 1024
MIDDLE_BYTES = 61 * 1024 * 1024
BLOCK = 32
TILE = 128
WIDE = 256
VECTORS = 16

VECTOR_ROWS = VECTORS * D // TILE

f32 = jnp.float32
bf16 = jnp.bfloat16
precise = lax.Precision.HIGHEST


def mm(left, right):
    return lax.dot_general(left, right, (((1,), (0,)), ((), ())), preferred_element_type=f32)


def mm_nt(left, right):
    return lax.dot_general(left, right, (((1,), (1,)), ((), ())), preferred_element_type=f32)


def mm_tn(left, right):
    return lax.dot_general(left, right, (((0,), (0,)), ((), ())), preferred_element_type=f32)


def unit_matrix(size):
    row = lax.broadcasted_iota(jnp.int32, (size, size), 0)
    return jnp.where(row == lanes((size, size)), 1.0, 0.0).astype(bf16)


def turn(value):
    width = min(value.shape[1], WIDE)
    unit = unit_matrix(width)
    blocks = [mm_nt(unit, value[:, n : n + width]) for n in range(0, value.shape[1], width)]
    return blocks[0] if len(blocks) == 1 else jnp.concatenate(blocks, axis=0)


def split(value):
    high = value.astype(bf16)
    return high, (value - high.astype(f32)).astype(bf16)


def lanes(shape):
    return lax.broadcasted_iota(jnp.int32, shape, 1)


def column_of(row):
    row = row.astype(f32)
    even = 2.0 * jnp.floor(0.5 * row)
    parts = jnp.concatenate([even, row - even, jnp.zeros((14, row.shape[1]), f32)], axis=0)
    return mm_tn(parts.astype(bf16), jnp.ones((16, TILE), bf16))


def lane_tiles(value, combine):
    tiles = [value[:, at : at + TILE] for at in range(0, value.shape[1], TILE)]
    return functools.reduce(combine, tiles)


def interleave(steps, tasks):
    done = 0
    for index, step in enumerate(steps):
        step()
        while done * len(steps) < (index + 1) * len(tasks) and done < len(tasks):
            tasks[done]()
            done += 1
    for task in tasks[done:]:
        task()


def order_of(core, bits):
    order = list(range(bits))
    if core == 1:
        for at in range(0, bits - 1, 2):
            order[at], order[at + 1] = order[at + 1], order[at]
    return order


def block_owner(place, core, bits):
    owners = []
    for each in range(2):
        owner = place * 0
        for step, bit in enumerate(order_of(each, bits)):
            owner = owner | (((place >> (bits - 1 - step)) & 1) << bit)
        owners.append(owner)
    return jnp.where(core == 1, owners[1], owners[0]) ^ lax.axis_index("dp")


def one_hot(source):
    return jnp.where(lanes((source.shape[0], D)) == source, 1.0, 0.0).astype(bf16)


def owner_rows(size, groups):
    share = D // (size * groups)
    row = lax.broadcasted_iota(jnp.int32, (D, 1), 0)
    side, rest = lax.div(row, size * share), lax.rem(row, size * share)
    core = lax.rem(lax.axis_index("tensor") + side, groups)
    owner = block_owner(lax.div(rest, share), core, size.bit_length() - 1)
    return one_hot((owner * groups + core) * share + lax.rem(rest, share))


def shared_rows(size, core):
    share = D // size
    row = lax.broadcasted_iota(jnp.int32, (D, 1), 0)
    owner = block_owner(lax.div(row, share), core, size.bit_length() - 1)
    return one_hot(owner * share + lax.rem(row, share))


def transpose_by_owner(out_ref, value, work, size, groups):
    share = D // (size * groups)
    if share % 8 or (2 * share) % 16:
        out_ref[...] = mm_nt(owner_rows(size, groups), value).astype(bf16)
        return
    width = value.shape[0]
    for n in range(0, D, WIDE):
        work[n : n + WIDE, :width] = turn(value[:, n : n + WIDE])
    bits = size.bit_length() - 1
    blocks = []
    for block in range(size * groups):
        core = lax.rem(lax.axis_index("tensor") + block // size, groups)
        owner = block_owner(jnp.int32(block % size), core, bits)
        at = pl.multiple_of((owner * groups + core) * share, 8)
        blocks.append(work[pl.ds(at, share), :width])
        if block % 2:
            out_ref[(block - 1) * share : (block + 1) * share, :] = jnp.concatenate(
                blocks, axis=0
            ).astype(bf16)
            blocks = []


def transpose_by_dp(out_ref, value, work, size):
    share = D // size
    core = lax.axis_index("tensor")
    if share % 16:
        out_ref[...] = mm_nt(shared_rows(size, core), value).astype(bf16)
        return
    for n in range(0, D, WIDE):
        work[n : n + WIDE, :] = turn(value[:, n : n + WIDE]).astype(bf16)
    for block in range(size):
        owner = block_owner(jnp.int32(block), core, size.bit_length() - 1)
        at = pl.multiple_of(owner * share, 16)
        out_ref[block * share : (block + 1) * share, :] = work[pl.ds(at, share), :]


def forward_kernel(
    half,
    length_ref,
    mem_length_ref,
    seg_ref,
    ord_ref,
    tgt_ref,
    memory_ref,
    content_ref,
    query_ref,
    wq_ref,
    wk_ref,
    wv_ref,
    wr_ref,
    cb_ref,
    pb_ref,
    sb_ref,
    se_ref,
    att_ref,
    prob_ref,
    key_ref,
    val_ref,
    rel_ref,
    hc_ref,
    hp_ref,
    hs_ref,
    linv_ref,
    kaug_ref,
    srow_ref,
    pos_ref,
    stack,
    both,
    pos,
    bias,
    fine,
    coarse,
    vectors,
    scores,
    places,
    kaug_t,
    scol,
    seg_row,
    kaug_work,
    order_work,
    seg_work,
):
    window = KEYS + half
    first = pl.multiple_of(lax.axis_index("tensor") * half, half)
    step_id = pl.program_id(0)

    @pl.when(step_id == 0)
    def _():
        stack[:MEM, :] = memory_ref[...]
        stack[MEM:, :] = content_ref[...]
        both[:half, :] = content_ref[pl.ds(first, half), :]
        both[half:, :] = query_ref[...]
        vectors[0:1, :] = cb_ref[...][None, :]
        vectors[1:2, :] = pb_ref[...][None, :]
        vectors[2:3, :] = sb_ref[...][None, :]
        step = lax.broadcasted_iota(jnp.int32, (1, D // 2), 1).astype(f32) * (2.0 / D)
        inverse = 1.0 / jnp.power(jnp.full((1, D // 2), 10000.0, f32), step)
        coarse_rows = coarse.shape[1]
        top = (MEM + half + first).astype(f32)
        angle = (
            top - 32.0 * lax.broadcasted_iota(jnp.int32, (coarse_rows, 1), 0).astype(f32)
        ) * inverse
        coarse[0] = jnp.sin(angle)
        coarse[1] = jnp.cos(angle)
        small = lax.broadcasted_iota(jnp.int32, (32, 1), 0).astype(f32) * inverse
        fine[0] = jnp.sin(small)
        fine[1] = jnp.cos(small)
        for a in range(window // 32):
            sa, ca = coarse[0, a : a + 1, :], coarse[1, a : a + 1, :]
            sb, cb = fine[0], fine[1]
            pos[a * 32 : (a + 1) * 32, : D // 2] = (sa * cb - ca * sb).astype(bf16)
            pos[a * 32 : (a + 1) * 32, D // 2 :] = (ca * cb + sa * sb).astype(bf16)
        never = float(LEN + 1)
        mem_at = lax.broadcasted_iota(jnp.int32, (1, MEM), 1)
        tok_at = lax.broadcasted_iota(jnp.int32, (1, LEN), 1)
        open_from = jnp.concatenate(
            [
                jnp.where(mem_at >= MEM - mem_length_ref[0], -1.0, never),
                jnp.where(
                    tok_at < length_ref[0],
                    jnp.where(tgt_ref[...] == 0, -1.0, ord_ref[...].astype(f32)),
                    never,
                ),
            ],
            axis=1,
        )
        order_col = column_of(ord_ref[...])
        seg_col = column_of(seg_ref[...])
        kaug_lane = lanes((LEN, PAIR)) % HEAD_DIM
        kaug_work[:MEM, :] = (lanes((MEM, PAIR)) % HEAD_DIM < 4).astype(f32).astype(bf16)
        kaug_work[MEM:, :] = jnp.where(
            kaug_lane < 4, 1.0, jnp.where(kaug_lane < 6, seg_col, 0.0)
        ).astype(bf16)
        kaug_t[...] = kaug_work[...].T[:HEAD_DIM]
        kaug_ref[...] = kaug_t[:16, :]
        order_work[...] = order_col
        own_order = order_work[pl.ds(first, half), :][:, :1]
        seg_work[...] = seg_col
        scol[...] = seg_work[pl.ds(first, half), :]
        seen = open_from <= own_order
        bias[:half, :] = jnp.where(seen, 0.0, -1e30)
        key_at = lax.broadcasted_iota(jnp.int32, (half, KEYS), 1)
        row_at = lax.broadcasted_iota(jnp.int32, (half, KEYS), 0)
        seen_q = seen & (key_at - MEM != row_at + first)
        bias[half:, :] = jnp.where(seen_q, 0.0, -1e30)
        seg_row[0:1, :] = seg_ref[...].astype(f32)
        srow_ref[...] = jnp.broadcast_to(seg_row[0:1, pl.ds(first, half)], srow_ref.shape)
        pos_ref[...] = pos[...]

    here = pl.ds(pl.multiple_of(step_id * QUAD, QUAD), QUAD)
    keys = mm(stack[...], wk_ref[...]).astype(bf16)
    values = mm(stack[...], wv_ref[...]).astype(bf16)
    rel = mm(pos[...], wr_ref[...]).astype(bf16)
    projection = mm(both[...], wq_ref[...])
    head_content = (projection + vectors[0:1, here]).astype(bf16)
    head_position = (projection + vectors[1:2, here]).astype(bf16)
    head_segment = projection + vectors[2:3, here]
    keys_t, values_t, rel_t = [turn(value).astype(bf16) for value in (keys, values, rel)]
    key_ref[...] = keys_t
    val_ref[...] = values_t
    rel_ref[...] = rel_t
    hs_ref[...] = head_segment
    head_content = (head_content.astype(f32) * SCALE).astype(bf16)
    head_position = (head_position.astype(f32) * SCALE).astype(bf16)
    hc_ref[...] = turn(head_content).astype(bf16)
    hp_ref[...] = turn(head_position).astype(bf16)
    row_head = lax.broadcasted_iota(jnp.int32, (QUAD, QUAD), 0) // HEAD_DIM
    at = lanes((QUAD, QUAD)) - ((row_head // 2) * PAIR + (1 - row_head % 2) * HEAD_DIM)
    place_same = jnp.where((at >= 0) & (at < 2), 1.0, 0.0).astype(bf16)
    place_step = jnp.where((at >= 2) & (at < 6), 1.0, 0.0).astype(bf16)
    same, other = se_ref[0:1, :], se_ref[1:2, :]
    terms = functools.reduce(
        jnp.add,
        [mm(part, place_same) for part in split(head_segment * same)]
        + [mm(part, place_step) for part in split(head_segment * (other - same))],
    )
    marks = jnp.concatenate([scol[...], scol[...]], axis=0)
    marks = jnp.concatenate([marks, marks], axis=1)
    lane6 = lanes((2 * half, QUAD)) % HEAD_DIM
    factor = jnp.where(lane6 < 2, 1.0, jnp.where(lane6 < 4, marks, 1.0 - 2.0 * marks))
    terms = SCALE * (terms * factor)
    high = terms.astype(bf16)
    low = (terms - high.astype(f32)).astype(bf16)
    qaug = jnp.where(lane6 % 2 == 0, high, low)
    key_x = []
    for which in range(4):
        own = keys_t[which * HEAD_DIM : (which + 1) * HEAD_DIM]
        sides = [own, kaug_t[...]] if which % 2 == 0 else [kaug_t[...], own]
        key_x.append(jnp.concatenate(sides, axis=0))
    peaks, totals, outs = {}, {}, {}
    row_first = lanes((2 * half, PAIR)) < HEAD_DIM

    def products(which):
        cols = slice(which // 2 * PAIR, (which // 2 + 1) * PAIR)
        slot = which % 2
        row_mine = row_first == (which % 2 == 0)
        query_x = jnp.where(row_mine, head_content[:, cols], qaug[:, cols])
        place_x = jnp.where(row_mine, head_position[:, cols], jnp.zeros((), bf16))

        def score(n, stop):
            scores[slot, :, n:stop] = mm(query_x, key_x[which][:, n:stop])

        def placed(n, stop):
            places[slot, :, n:stop] = mm(place_x, rel_t[cols, n:stop])

        return [functools.partial(placed, n, min(n + WIDE, window)) for n in range(0, window, WIDE)] + [
            functools.partial(score, n, min(n + WIDE, KEYS)) for n in range(0, KEYS, WIDE)
        ]

    def softmax(which):
        slot = which % 2
        tops, pieces = [], []

        def join(b):
            block = slice(b, b + BLOCK)
            shifted = pltpu.roll(
                places[slot, block, :], (KEYS + b % half) % window, 1, stride=1, stride_axis=0
            )[:, :KEYS]
            score = scores[slot, block, :] + shifted + bias[block, :]
            scores[slot, block, :] = score
            tops.append(lane_tiles(score, jnp.maximum))

        def peak():
            peaks[which] = jnp.max(jnp.concatenate(tops, axis=0), axis=1, keepdims=True)

        def power(b):
            block = slice(b, b + BLOCK)
            prob = jnp.exp(scores[slot, block, :] - peaks[which][block])
            pieces.append(lane_tiles(prob, jnp.add))
            prob_ref[which, block, :] = prob.astype(bf16)

        def finish():
            totals[which] = 1.0 / jnp.sum(
                jnp.concatenate(pieces, axis=0), axis=1, keepdims=True
            )

        blocks = range(0, 2 * half, BLOCK)
        return (
            [functools.partial(join, b) for b in blocks]
            + [peak]
            + [functools.partial(power, b) for b in blocks]
            + [finish]
        )

    def mixture(which, part):
        outs[which, part] = mm_nt(
            values_t[which * HEAD_DIM : (which + 1) * HEAD_DIM],
            prob_ref[which, part * half : (part + 1) * half, :],
        )

    interleave([], products(0))
    for which in range(4):
        tasks = products(which + 1) if which < 3 else []
        if which:
            tasks += [functools.partial(mixture, which - 1, part) for part in range(2)]
        interleave(softmax(which), tasks)
    for part in range(2):
        mixture(3, part)
    sums = [totals[which] for which in range(4)]
    mixed = jnp.concatenate(
        [jnp.concatenate([outs[which, 0], outs[which, 1]], axis=1) for which in range(4)], axis=0
    )
    mixed = functools.reduce(jnp.add, [turn(part) for part in split(mixed)])
    mine = lanes((2 * half, PAIR)) < HEAD_DIM
    for pair in range(2):
        cols = slice(pair * PAIR, (pair + 1) * PAIR)
        att_ref[:, cols] = mixed[:, cols] * jnp.where(mine, sums[2 * pair], sums[2 * pair + 1])
    lane = lanes((2 * half, TILE))
    linv_ref[...] = jnp.where(
        lane == 0, sums[0], jnp.where(lane == 1, sums[1], jnp.where(lane == 2, sums[2], sums[3]))
    )


def norm_forward(summed, gain, shift):
    center = summed - jnp.mean(summed, axis=1, keepdims=True)
    inv = lax.rsqrt(jnp.mean(center * center, axis=1, keepdims=True) + 1e-06)
    unit = center * inv
    return unit, inv, unit * gain + shift


def norm_backward(grad, unit, inv, gain):
    scaled = grad * gain
    return inv * (
        scaled
        - jnp.mean(scaled, axis=1, keepdims=True)
        - unit * jnp.mean(scaled * unit, axis=1, keepdims=True)
    )


def row_sum(value):
    return jnp.sum(value, axis=0, keepdims=True)


def gelu_parts(x):
    square = x * x
    tanh = jnp.tanh((0.7978845608028654 * x) * (1.0 + 0.044715 * square))
    rise = 0.5 * (1.0 + tanh)
    grad = rise + (0.5 * x) * (1.0 - tanh * tanh) * (
        0.7978845608028654 * (1.0 + 0.134145 * square)
    )
    return x * rise, grad


def fold_rows(value):
    return functools.reduce(jnp.add, [value[r : r + 8] for r in range(0, value.shape[0], 8)])


def middle_kernel(
    half,
    size,
    groups,
    chunk,
    att_ref,
    content_ref,
    query_ref,
    ccot_ref,
    qcot_ref,
    wo_ref,
    up_own_hbm,
    up_oth_hbm,
    down_own_hbm,
    down_oth_hbm,
    ubias_ref,
    dbias_ref,
    again_ref,
    ashift_ref,
    fgain_ref,
    fshift_ref,
    cout_ref,
    qout_ref,
    ffn_own_ref,
    ffn_oth_ref,
    sgrad_ref,
    agrad_ref,
    out_own_ref,
    out_oth_ref,
    small_ref,
    ubg_ref,
    hidden,
    slope,
    pre,
    work,
    unit,
    low,
    down_grad,
    vectors,
    up,
    down,
    low_t,
    down_t,
    turn_low,
    turn_down,
    attended_t,
    turn_work,
    sems,
):
    count = 2 * half
    member = lax.axis_index("tensor")
    first = pl.multiple_of(member * half, half)
    fetches = [
        pltpu.make_async_copy(source, target.at[side], sems.at[kind, side])
        for kind, side, source, target in (
            (0, 0, up_own_hbm, up),
            (1, 0, down_own_hbm, down),
            (0, 1, up_oth_hbm, up),
            (1, 1, down_oth_hbm, down),
        )
    ]
    for fetch in fetches:
        fetch.start()
    ups, downs = (up.at[0], up.at[1]), (down.at[0], down.at[1])
    part_cols = up.shape[2]
    chunks = part_cols // chunk
    vectors[0:1, :] = ubias_ref[...][None, :]
    attended = att_ref[...].astype(bf16)
    work[...] = mm(attended, wo_ref[...])
    attn_gain, attn_shift = again_ref[...][None, :], ashift_ref[...][None, :]
    ffn_gain, ffn_shift = fgain_ref[...][None, :], fshift_ref[...][None, :]
    down_bias = dbias_ref[...][None, :]
    inverse = []
    for b in range(0, count, BLOCK):
        block = slice(b, b + BLOCK)
        if b < half:
            rows_in = content_ref[pl.ds(pl.multiple_of(first + b, BLOCK), BLOCK), :]
        else:
            rows_in = query_ref[b - half : b - half + BLOCK, :]
        found, inv, normed = norm_forward(
            work[block, :] + rows_in.astype(f32), attn_gain, attn_shift
        )
        unit[block, :] = found
        inverse.append(inv)
        low[block, :] = normed.astype(bf16)
        work[block, :] = normed + down_bias
    for fetch in fetches:
        fetch.wait()
    pieces = [(side, at) for side in range(2) for at in range(chunks)]

    def rise(index):
        side, at = pieces[index]

        def task(n):
            pre[index % 2, :, n : n + WIDE] = mm(
                low[...], ups[side][:, at * chunk + n : at * chunk + n + WIDE]
            )

        return [functools.partial(task, n) for n in range(0, chunk, WIDE)]

    def bend(index):
        side, at = pieces[index]
        cols = slice(at * chunk, (at + 1) * chunk)
        start = lax.rem(member + side, 2) * part_cols + at * chunk
        bias = vectors[0:1, pl.ds(pl.multiple_of(start, TILE), chunk)]

        def step(b):
            block = slice(b, b + BLOCK)
            act, grad = gelu_parts(pre[index % 2, block, :] + bias)
            hidden[side, block, cols] = act.astype(bf16)
            slope[side, block, cols] = grad.astype(bf16)

        return [functools.partial(step, b) for b in range(0, count, BLOCK)]

    def fall(index):
        side, at = pieces[index]
        cols = slice(at * chunk, (at + 1) * chunk)

        def task(n):
            work[:, n : n + WIDE] += mm(hidden[side, :, cols], downs[side][cols, n : n + WIDE])

        return [functools.partial(task, n) for n in range(0, D, WIDE)]

    interleave([], rise(0))
    for index in range(len(pieces)):
        tasks = rise(index + 1) if index + 1 < len(pieces) else []
        if index:
            tasks += fall(index - 1)
        interleave(bend(index), tasks)
    interleave([], fall(len(pieces) - 1))
    sums = [jnp.zeros((8, D), f32) for _ in range(5)]
    for b in range(0, count, BLOCK):
        block = slice(b, b + BLOCK)
        found, inv, out = norm_forward(work[block, :], ffn_gain, ffn_shift)
        if b < half:
            cout_ref[block, :] = out.astype(bf16)
            cot = ccot_ref[block, :].astype(f32)
        else:
            block_q = slice(b - half, b - half + BLOCK)
            qout_ref[block_q, :] = out.astype(bf16)
            cot = qcot_ref[block_q, :].astype(f32)
        residual_grad = norm_backward(cot, found, inv, ffn_gain)
        rounded = residual_grad.astype(bf16)
        down_grad[block, :] = rounded
        work[block, :] = residual_grad
        for index, value in enumerate((cot * found, cot, rounded.astype(f32))):
            sums[index] = sums[index] + fold_rows(value)
    transpose_by_dp(low_t, low[...], turn_low, size)
    transpose_by_dp(down_t, down_grad[...], turn_down, size)
    for side in range(2):
        for at in range(chunks):
            cols = slice(at * chunk, (at + 1) * chunk)
            hidden_grad = mm_nt(down_grad[...], downs[side][cols, :])
            pre_grad = (hidden_grad * slope[side, :, cols].astype(f32)).astype(bf16)
            slope[side, :, cols] = pre_grad
            ubg_ref[side : side + 1, cols] = row_sum(pre_grad.astype(f32))
            work[...] += mm_nt(pre_grad, ups[side][:, cols])

    def settle(b):
        block = slice(b, b + BLOCK)
        grad, found = work[block, :], unit[block, :]
        summed_grad = norm_backward(grad, found, inverse[b // BLOCK], attn_gain)
        sgrad_ref[block, :] = summed_grad
        down_grad[block, :] = summed_grad.astype(bf16)
        sums[3] = sums[3] + fold_rows(grad * found)
        sums[4] = sums[4] + fold_rows(grad)

    share = D // size
    bits = size.bit_length() - 1

    def other_place(place):
        found = 0
        for step in range(bits):
            there = order_of(1, bits)[step]
            found |= ((place >> (bits - 1 - there)) & 1) << (bits - 1 - step)
        return found

    def weigh(side, kind, n):
        left, right = ((low_t, slope), (down_t, hidden))[kind]
        value = mm(left[...], right[side, :, n : n + WIDE]).astype(bf16)
        target = (ffn_own_ref, ffn_oth_ref)[side]
        cols = slice(kind * part_cols + n, kind * part_cols + n + WIDE)
        if side == 0:
            target[:, cols] = value
            return
        for place in range(size):
            to = other_place(place)
            target[to * share : (to + 1) * share, cols] = value[
                place * share : (place + 1) * share
            ]

    tasks = [
        functools.partial(weigh, side, kind, n)
        for side in (1, 0)
        for kind in range(2)
        for n in range(0, part_cols, WIDE)
    ]
    interleave([functools.partial(settle, b) for b in range(0, count, BLOCK)], tasks)
    for index, value in enumerate(sums):
        small_ref[index : index + 1, :] = row_sum(value)
    small_ref[5:8, :] = jnp.zeros((3, D), f32)
    agrad_ref[...] = mm_nt(down_grad[...], wo_ref[...]).astype(bf16)
    transpose_by_owner(attended_t, attended, turn_work, size, groups)
    out_part = mm(attended_t[...], down_grad[...]).astype(bf16)
    half_rows = D // groups
    out_own_ref[...] = out_part[:half_rows]
    out_oth_ref[...] = out_part[half_rows : 2 * half_rows]


def unshift(value, shift, window):
    whole, rest = shift // TILE, shift % TILE
    row = lax.broadcasted_iota(jnp.int32, (BLOCK, TILE), 0)
    lane = lanes((BLOCK, TILE))
    index = (lane + row - rest) & (TILE - 1)
    tiles = [
        jnp.take_along_axis(
            value[:, n : n + TILE], index, axis=1, mode="promise_in_bounds"
        )
        for n in range(0, value.shape[1], TILE)
    ]
    zero = jnp.zeros((BLOCK, TILE), f32)

    def tile(n):
        return tiles[n] if 0 <= n < len(tiles) else zero

    if rest:
        here = lane >= rest - row
        found = [
            jnp.where(here, tile(n - whole), tile(n - whole - 1)) for n in range(window // TILE)
        ]
    else:
        here = lane + row < TILE
        found = [
            jnp.where(here, tile(n - whole), tile(n - whole + 1)) for n in range(window // TILE)
        ]
    return jnp.concatenate(found, axis=1)


def backward_kernel(
    half,
    groups,
    at,
    mode,
    prob_hbm,
    key_ref,
    val_ref,
    rel_ref,
    hc_ref,
    hp_ref,
    hs_ref,
    linv_ref,
    kaug_ref,
    srow_ref,
    att_ref,
    agrad_ref,
    se_ref,
    both_t_hbm,
    stack_t_hbm,
    pos_t_hbm,
    *rest,
):
    more = rest[: {"first": 2, "middle": 0, "last": 4}[mode]]
    own_ref, oth_ref, proj_ref, tok_key_ref, tok_val_ref, small_ref = rest[len(more) :][:6]
    prob, both_t, stack_t, pos_t, spread, grads, turned, sems = rest[-8:]
    count, window = 2 * half, KEYS + half
    heads = 4
    prob_copies = [
        pltpu.make_async_copy(prob_hbm.at[at * heads + h], prob.at[h], sems.at[h])
        for h in range(heads)
    ]
    fetches = [
        pltpu.make_async_copy(source, target, sems.at[heads + index])
        for index, (source, target) in enumerate(
            ((both_t_hbm, both_t), (stack_t_hbm, stack_t), (pos_t_hbm, pos_t))
        )
    ]
    for copy in prob_copies + fetches:
        copy.start()
    share = D // groups
    if mode == "first":
        own_ref[:, 4 * QUAD :] = more[0][...]
        oth_ref[:, 4 * QUAD :] = more[1][...]
    kaug_t = kaug_ref[...]
    filler = jnp.zeros((HEAD_DIM - kaug_t.shape[0], KEYS), bf16)
    marks = jnp.concatenate([srow_ref[0:1, :], srow_ref[0:1, :]], axis=1)
    swing = 1.0 - 2.0 * marks
    key_t, val_t, rel_t = [], [], []
    lane = lanes((count, PAIR))
    agrads, grad_x, agrad_t = [], [], []
    for pair in range(2):
        cols = slice(pair * PAIR, (pair + 1) * PAIR)
        linv = jnp.where(
            lane < HEAD_DIM,
            linv_ref[:, 2 * pair : 2 * pair + 1],
            linv_ref[:, 2 * pair + 1 : 2 * pair + 2],
        )
        agrad = (agrad_ref[:, cols].astype(f32) * linv).astype(bf16).astype(f32)
        products = agrad * att_ref[:, cols]
        agrad_t.append(turn(agrad.astype(bf16)).astype(bf16))
        for head in range(2):
            base = (1 - head) * HEAD_DIM
            mine = (lane < HEAD_DIM) == (head == 0)
            weight = jnp.sum(jnp.where(mine, products, 0.0), axis=1, keepdims=True)
            high = weight.astype(bf16).astype(f32)
            grad_x.append(
                jnp.where(
                    mine,
                    agrad,
                    jnp.where(
                        lane == base, -high, jnp.where(lane == base + 1, high - weight, 0.0)
                    ),
                ).astype(bf16)
            )
    found = {}

    def head_of(ref, which):
        return ref[which * HEAD_DIM : (which + 1) * HEAD_DIM, :]

    def spreads(which):
        own = head_of(val_ref, which)
        sides = [own, kaug_t, filler] if which % 2 == 0 else [kaug_t, filler, own]
        val_x = jnp.concatenate(sides, axis=0)
        prob_copies[which].wait()

        def task(n, stop):
            spread[which % 2, :, n:stop] = mm(grad_x[which], val_x[:, n:stop])

        return [functools.partial(task, n, min(n + WIDE, KEYS)) for n in range(0, KEYS, WIDE)]

    def score_grads(which):
        buffer = which % 2

        def step(part, b):
            at_row = part * half + b
            block = slice(at_row, at_row + BLOCK)
            score_grad = prob[which, block, :].astype(f32) * spread[buffer, block, :]
            grads[buffer, block, :] = score_grad.astype(bf16)
            turned[buffer, block, :] = unshift(score_grad, half - b, window).astype(bf16)

        return [
            functools.partial(step, part, b) for part in range(2) for b in range(0, half, BLOCK)
        ]

    def gathers(which):
        buffer = which % 2
        side = slice(which % 2 * HEAD_DIM, (which % 2 + 1) * HEAD_DIM)
        key_x = jnp.concatenate([head_of(key_ref, which), kaug_t], axis=0)
        found[which] = {"value": [], "key": [], "rel": [], "content": [], "place": []}

        def down_rows(name, left, ref, n, stop):
            found[which][name].append(mm(left, ref[:, n:stop]))

        tasks = []
        for name, left, ref, end in (
            ("value", agrad_t[which // 2][side], prob.at[which], KEYS),
            ("key", head_of(hc_ref, which), grads.at[buffer], KEYS),
            ("rel", head_of(hp_ref, which), turned.at[buffer], window),
        ):
            tasks += [
                functools.partial(down_rows, name, left, ref, n, min(n + WIDE, end))
                for n in range(0, end, WIDE)
            ]

        def content(n):
            found[which]["content"].append(mm_nt(key_x, grads[buffer, n : n + half, :]))

        def placed(n):
            found[which]["place"].append(
                mm_nt(head_of(rel_ref, which), turned[buffer, n : n + half, :])
            )

        for n in (0, half):
            tasks += [functools.partial(content, n), functools.partial(placed, n)]
        return tasks

    interleave([], spreads(0))
    for which in range(heads):
        tasks = spreads(which + 1) if which + 1 < heads else []
        if which:
            tasks += gathers(which - 1)
        interleave(score_grads(which), tasks)
    interleave([], gathers(heads - 1))
    for which in range(heads):
        val_t.append(jnp.concatenate(found[which]["value"], axis=1))
        key_t.append(jnp.concatenate(found[which]["key"], axis=1))
        rel_t.append(jnp.concatenate(found[which]["rel"], axis=1))
    same, other, contents, places = [], [], [], []
    for which in range(heads):
        content_head = jnp.concatenate(found[which]["content"], axis=1)
        total = content_head[HEAD_DIM : HEAD_DIM + 1]
        marked = content_head[HEAD_DIM + 4 : HEAD_DIM + 5]
        other.append(SCALE * (marks * total + swing * marked))
        same.append(SCALE * total - other[-1])
        contents.append((SCALE * content_head[:HEAD_DIM]).astype(bf16))
        places.append((SCALE * jnp.concatenate(found[which]["place"], axis=1)).astype(bf16))
    contents, places = jnp.concatenate(contents, axis=0), jnp.concatenate(places, axis=0)
    term_high, term_low = split(jnp.concatenate(same + other, axis=0))
    line = lax.broadcasted_iota(jnp.int32, (2 * heads, QUAD), 0)
    mine = line % heads == lanes((2 * heads, QUAD)) // HEAD_DIM
    embed = jnp.where(line < heads, se_ref[0:1, :], se_ref[1:2, :])
    embed_high, embed_low = split(jnp.where(mine, embed, 0.0))
    segment_grad = mm_tn(
        jnp.concatenate([embed_high, embed_high, embed_low, embed_low], axis=0),
        jnp.concatenate([term_high, term_low, term_high, term_low], axis=0),
    )
    proj_t = (contents.astype(f32) + places.astype(f32) + segment_grad).astype(bf16)
    ones = jnp.ones((16, count), bf16)
    small_ref[0:1, :] = mm_nt(ones, contents)[0:1]
    small_ref[1:2, :] = mm_nt(ones, places)[0:1]
    small_ref[2:3, :] = functools.reduce(
        jnp.add, [mm_nt(ones, part)[0:1] for part in split(segment_grad)]
    )
    terms = jnp.concatenate([term_high, term_low], axis=0)
    embed_grad = functools.reduce(jnp.add, [mm(terms, part) for part in split(hs_ref[...])])
    embed_grad = jnp.where(mine, embed_grad[: 2 * heads] + embed_grad[2 * heads :], 0.0)
    small_ref[3:4, :] = row_sum(embed_grad[:heads])
    small_ref[4:5, :] = row_sum(embed_grad[heads:])
    small_ref[5:8, :] = jnp.zeros((3, QUAD), f32)
    key_t = jnp.concatenate(key_t, axis=0).astype(bf16)
    val_t = jnp.concatenate(val_t, axis=0).astype(bf16)
    rel_t = jnp.concatenate(rel_t, axis=0).astype(bf16)
    proj_ref[...] = turn(proj_t).astype(bf16)
    tok_key_ref[...] = turn(key_t[:, MEM:]).astype(bf16)
    tok_val_ref[...] = turn(val_t[:, MEM:]).astype(bf16)
    for fetch in fetches:
        fetch.wait()
    parts = (
        mm_nt(both_t[...], proj_t),
        mm_nt(stack_t[...], key_t),
        mm_nt(stack_t[...], val_t),
        mm_nt(pos_t[...], rel_t),
    )
    for index, value in enumerate(parts):
        cols = slice(index * QUAD, (index + 1) * QUAD)
        own_ref[:, cols] = value[:share].astype(bf16)
        oth_ref[:, cols] = value[share : 2 * share].astype(bf16)
    if mode == "last":
        vec_ref = rest[len(more) + 6]
        early, ubias, before, between = more
        core = lax.axis_index("tensor")
        rows = [early[0:5, :]]
        mine = [ubias[0:1, n : n + D] for n in range(0, ubias.shape[1], D)]
        theirs = [ubias[1:2, n : n + D] for n in range(0, ubias.shape[1], D)]
        for left, right in ((mine, theirs), (theirs, mine)):
            rows += [jnp.where(core == 0, a, b) for a, b in zip(left, right)]
        rows.append(
            jnp.concatenate([before[0:5, :], between[0:5, :], small_ref[0:5, :]], axis=1)
        )
        rows = jnp.concatenate(rows, axis=0)
        spare = jnp.zeros((VECTORS - rows.shape[0], D), f32)
        rows = jnp.concatenate([rows, spare], axis=0)
        packed = jnp.concatenate([rows[:, n : n + TILE] for n in range(0, D, TILE)], axis=0)
        vec_ref[...] = packed
        oth_ref[:VECTOR_ROWS, 4 * QUAD :] = packed.astype(bf16)
        oth_ref[VECTOR_ROWS:, 4 * QUAD :] = jnp.zeros((share - VECTOR_ROWS, TILE), bf16)


def rows_kernel(half, groups, sgrad_ref, *rest):
    proj, keys, vals = rest[:QUADS], rest[QUADS : 2 * QUADS], rest[2 * QUADS : 3 * QUADS]
    wq_ref, wk_ref, wv_ref, own_ref, query_ref, send_ref, both = rest[3 * QUADS :]
    member = lax.axis_index("tensor")
    wide = [jnp.concatenate([ref[...] for ref in refs], axis=1) for refs in (proj, keys, vals)]
    both[...] = mm_nt(wide[1], wk_ref[...]) + mm_nt(wide[2], wv_ref[...])
    rows = sgrad_ref[...] + mm_nt(wide[0], wq_ref[...])
    own = pl.multiple_of(member * half, half)
    other = pl.multiple_of(lax.rem(member + 1, groups) * half, half)
    send_ref[...] = both[pl.ds(other, half), :].astype(bf16)
    own_ref[...] = rows[:half] + both[pl.ds(own, half), :]
    query_ref[...] = rows[half:]


def summed(operands, terms, first, rows, width):
    values = []
    for index, at in terms:
        if rows % 16 == 0:
            value = operands[index][first : first + rows, at : at + width].astype(f32)
        else:
            value = operands[index][:, at : at + width].astype(f32)[first : first + rows]
        values.append(value)
    return functools.reduce(jnp.add, values)


def vector_width(rows):
    return TILE * max(1, VECTOR_ROWS // rows)


def fold_vectors(packed, rows):
    if rows > VECTOR_ROWS:
        return jnp.concatenate([packed, jnp.zeros((rows - VECTOR_ROWS, TILE), f32)], axis=0)
    return jnp.concatenate(
        [packed[n : n + rows] for n in range(0, VECTOR_ROWS, rows)], axis=1
    )


def unfold_vectors(block, rows):
    if rows >= VECTOR_ROWS:
        return block[:VECTOR_ROWS]
    return jnp.concatenate(
        [block[:, n : n + TILE] for n in range(0, vector_width(rows), TILE)], axis=0
    )


def summed_vectors(values, terms):
    return functools.reduce(
        jnp.add,
        [
            unfold_vectors(
                values(index)[:rows, at : at + vector_width(rows)].astype(f32), rows
            )
            for index, at, rows in terms
        ],
    )


def combine_kernel(plans, *refs):
    count = sum(pieces + (1 if vectors else 0) for _, pieces, _, vectors in plans)
    operands, outs = refs[:-count], list(refs[-count:])
    for rows, pieces, parts, vectors in plans:
        if vectors:
            packed = summed_vectors(lambda index: operands[index][...].astype(f32), vectors)
            outs.pop(0)[...] = packed
        for piece in range(pieces):
            out_ref = outs.pop(0)
            column = 0
            for width, terms in parts:
                value = summed(operands, terms, piece * rows, rows, width)
                out_ref[:, column : column + width] = value.astype(out_ref.dtype)
                column += width
            if piece and vectors:
                out_ref[:, column:] = fold_vectors(packed, rows).astype(out_ref.dtype)


def unpack_vectors(packed):
    return jnp.concatenate(
        [packed[n : n + VECTORS] for n in range(0, VECTOR_ROWS, VECTORS)], axis=1
    )


def finish_kernel(size, groups, count, plan, up_rows, *refs):
    operands, outs = refs[:count], refs[count:]
    weights, vec_outs, embed_out, up_out = outs[:5], outs[5:-2], outs[-2], outs[-1]
    place = lax.axis_index("dp") * groups + lax.axis_index("tensor")
    share = D // (size * groups)
    for target, at, width, terms in plan[0]:
        weights[target][:, at : at + width] = summed(operands, terms, 0, share, width)
    value = unpack_vectors(
        summed_vectors(lambda index: operands[index][...].astype(f32), plan[1])
    )
    mine = pltpu.roll(value, lax.rem(D - place * share, D), 1)[:, :TILE]
    rows = [row for row in range(5 + up_rows + 3) if not 5 <= row < 5 + up_rows]
    for row, out_ref in zip(rows, vec_outs):
        out_ref[...] = mine[row, :share]
    embed = jnp.concatenate([mine[5 + up_rows + 3 : 5 + up_rows + 5], jnp.zeros((6, TILE), f32)], axis=0)
    embed_out[...] = embed[:2, :share]
    wide = up_rows * share
    each = D // wide
    line = lax.div(place, each)
    chosen = functools.reduce(
        jnp.add,
        [jnp.where(line == r, value[5 + r : 6 + r], 0.0) for r in range(up_rows)],
    )
    chosen = jnp.broadcast_to(chosen, (8, D))
    turned = pltpu.roll(chosen, lax.rem(D - lax.rem(place, each) * wide, D), 1)[:, :TILE]
    up_out[...] = turned[0, :wide]


def whole(shape):
    return pl.BlockSpec(shape, lambda i: (0,) * len(shape))


def columns(rows, width, at=None):
    if at is None:
        return pl.BlockSpec((rows, width), lambda i: (0, i))
    return pl.BlockSpec((rows, width), lambda i: (0, at))


def row_block(rows, width, at=None):
    if at is None:
        return pl.BlockSpec((rows, width), lambda i: (i, 0))
    return pl.BlockSpec((rows, width), lambda i: (at, 0))


def scalars():
    return pl.BlockSpec(memory_space=pltpu.SMEM)


def params(size=VMEM_BYTES):
    return pltpu.CompilerParams(vmem_limit_bytes=size)


def cost(flops, bytes_accessed):
    return pl.CostEstimate(flops=flops, bytes_accessed=bytes_accessed, transcendentals=0)


def in_hbm():
    return pl.BlockSpec(memory_space=pl.ANY)


def attention_forward(
    half, ints, memory, content, query, weights, biases, segment_rows
):
    count, window = 2 * half, KEYS + half
    coarse_rows = -(-(window // 32) // 8) * 8
    outs = (
        ((count, D), f32, columns(count, QUAD)),
        ((HEADS, count, KEYS), bf16, pl.BlockSpec((4, count, KEYS), lambda i: (i, 0, 0))),
        ((D, KEYS), bf16, row_block(QUAD, KEYS)),
        ((D, KEYS), bf16, row_block(QUAD, KEYS)),
        ((D, window), bf16, row_block(QUAD, window)),
        ((D, count), bf16, row_block(QUAD, count)),
        ((D, count), bf16, row_block(QUAD, count)),
        ((count, D), f32, columns(count, QUAD)),
        ((count, QUADS * TILE), f32, columns(count, TILE)),
        ((16, KEYS), bf16, whole((16, KEYS))),
        ((8, half), f32, whole((8, half))),
        ((window, D), bf16, whole((window, D))),
    )
    return pl.pallas_call(
        functools.partial(forward_kernel, half),
        grid=(QUADS,),
        out_shape=[jax.ShapeDtypeStruct(shape, kind) for shape, kind, _ in outs],
        in_specs=[
            scalars(),
            scalars(),
            whole((1, LEN)),
            whole((1, LEN)),
            whole((1, LEN)),
            whole((MEM, D)),
            whole((LEN, D)),
            whole((half, D)),
        ]
        + [columns(D, QUAD)] * 4
        + [whole((D,))] * 3
        + [columns(2, QUAD)],
        out_specs=[spec for _, _, spec in outs],
        scratch_shapes=[
            pltpu.VMEM((KEYS, D), bf16),
            pltpu.VMEM((count, D), bf16),
            pltpu.VMEM((window, D), bf16),
            pltpu.VMEM((count, KEYS), f32),
            pltpu.VMEM((2, 32, D // 2), f32),
            pltpu.VMEM((2, coarse_rows, D // 2), f32),
            pltpu.VMEM((8, D), f32),
            pltpu.VMEM((2, count, KEYS), f32),
            pltpu.VMEM((2, count, window), f32),
            pltpu.VMEM((HEAD_DIM, KEYS), bf16),
            pltpu.VMEM((half, PAIR), f32),
            pltpu.VMEM((8, LEN), f32),
            pltpu.VMEM((KEYS, PAIR), bf16),
            pltpu.VMEM((LEN, TILE), f32),
            pltpu.VMEM((LEN, TILE), f32),
        ],
        compiler_params=params(),
        cost_estimate=cost(30_000_000_000, 40_000_000),
        name="attention_forward",
    )(*ints, memory, content, query, *weights, *biases, segment_rows)


def middle(half, size, groups, arrays, hidden_cols):
    count, share = 2 * half, D // groups
    chunk = min(hidden_cols, 768)
    outs = (
        ((half, D), bf16),
        ((half, D), bf16),
        ((D, 2 * hidden_cols), bf16),
        ((D, 2 * hidden_cols), bf16),
        ((count, D), f32),
        ((count, D), bf16),
        ((share, D), bf16),
        ((share, D), bf16),
        ((8, D), f32),
        ((2, hidden_cols), f32),
    )
    weights = (6, 7, 8, 9)
    return pl.pallas_call(
        functools.partial(middle_kernel, half, size, groups, chunk),
        grid=(1,),
        out_shape=[jax.ShapeDtypeStruct(shape, kind) for shape, kind in outs],
        in_specs=[
            in_hbm() if i in weights else whole(array.shape) for i, array in enumerate(arrays)
        ],
        out_specs=[whole(shape) for shape, _ in outs],
        scratch_shapes=[
            pltpu.VMEM((2, count, hidden_cols), bf16),
            pltpu.VMEM((2, count, hidden_cols), bf16),
            pltpu.VMEM((2, count, chunk), f32),
            pltpu.VMEM((count, D), f32),
            pltpu.VMEM((count, D), f32),
            pltpu.VMEM((count, D), bf16),
            pltpu.VMEM((count, D), bf16),
            pltpu.VMEM((8, FF), f32),
            pltpu.VMEM((2, D, hidden_cols), bf16),
            pltpu.VMEM((2, hidden_cols, D), bf16),
            pltpu.VMEM((D, count), bf16),
            pltpu.VMEM((D, count), bf16),
            pltpu.VMEM((D, count), bf16),
            pltpu.VMEM((D, count), bf16),
            pltpu.VMEM((D, count), bf16),
            pltpu.VMEM((D, count), f32),
            pltpu.SemaphoreType.DMA((2, 2)),
        ],
        compiler_params=params(MIDDLE_BYTES),
        cost_estimate=cost(30_000_000_000, 30_000_000),
        name="feed_forward",
    )(*arrays)


def prepare_kernel(
    half,
    size,
    groups,
    memory_ref,
    content_ref,
    query_ref,
    pos_ref,
    both_t_ref,
    stack_t_ref,
    pos_t_ref,
    both_work,
    stack_work,
    pos_work,
):
    first = pl.multiple_of(lax.axis_index("tensor") * half, half)
    both = jnp.concatenate([content_ref[pl.ds(first, half), :], query_ref[...]], axis=0)
    stack = jnp.concatenate([memory_ref[...], content_ref[...]], axis=0)
    transpose_by_owner(both_t_ref, both, both_work, size, groups)
    transpose_by_owner(stack_t_ref, stack, stack_work, size, groups)
    transpose_by_owner(pos_t_ref, pos_ref[...], pos_work, size, groups)


def transposed_rows(half, size, groups, memory, content, query, pos):
    count, window = 2 * half, KEYS + half
    arrays = (memory, content, query, pos)
    outs = ((D, count), (D, KEYS), (D, window))
    return pl.pallas_call(
        functools.partial(prepare_kernel, half, size, groups),
        grid=(1,),
        out_shape=[jax.ShapeDtypeStruct(shape, bf16) for shape in outs],
        in_specs=[whole(array.shape) for array in arrays],
        out_specs=[whole(shape) for shape in outs],
        scratch_shapes=[pltpu.VMEM(shape, f32) for shape in outs],
        compiler_params=params(BACKWARD_BYTES),
        cost_estimate=cost(6_000_000_000, 8_000_000),
        name="transposed_rows",
    )(*arrays)


def attention_backward(half, groups, at, mode, saved, agrad, segment_rows, extra):
    count, window, share = 2 * half, KEYS + half, D // groups
    att, prob, keys, values, rel, hc, hp, hs, linv, kaug, srow, _ = saved[:12]
    both_t, stack_t, pos_t = saved[12:]
    width = 4 * QUAD + (D if mode == "first" else 0)
    operands = (
        (prob, in_hbm()),
        (keys, row_block(QUAD, KEYS, at)),
        (values, row_block(QUAD, KEYS, at)),
        (rel, row_block(QUAD, window, at)),
        (hc, row_block(QUAD, count, at)),
        (hp, row_block(QUAD, count, at)),
        (hs, columns(count, QUAD, at)),
        (linv, columns(count, TILE, at)),
        (kaug, whole((16, KEYS))),
        (srow, whole((8, half))),
        (att, columns(count, QUAD, at)),
        (agrad, columns(count, QUAD, at)),
        (segment_rows, columns(2, QUAD, at)),
        (both_t, in_hbm()),
        (stack_t, in_hbm()),
        (pos_t, in_hbm()),
    ) + tuple((array, whole(array.shape)) for array in extra)
    outs = (
        ((share, width), bf16),
        ((share, width + (TILE if mode == "last" else 0)), bf16),
        ((count, QUAD), bf16),
        ((LEN, QUAD), bf16),
        ((LEN, QUAD), bf16),
        ((8, QUAD), f32),
    )
    if mode == "last":
        outs += (((VECTOR_ROWS, TILE), f32),)
    return pl.pallas_call(
        functools.partial(backward_kernel, half, groups, at, mode),
        grid=(1,),
        out_shape=[jax.ShapeDtypeStruct(shape, kind) for shape, kind in outs],
        in_specs=[spec for _, spec in operands],
        out_specs=[whole(shape) for shape, _ in outs],
        scratch_shapes=[
            pltpu.VMEM((4, count, KEYS), bf16),
            pltpu.VMEM((D, count), bf16),
            pltpu.VMEM((D, KEYS), bf16),
            pltpu.VMEM((D, window), bf16),
            pltpu.VMEM((2, count, KEYS), f32),
            pltpu.VMEM((2, count, KEYS), bf16),
            pltpu.VMEM((2, count, window), bf16),
            pltpu.SemaphoreType.DMA((7,)),
        ],
        compiler_params=params(BACKWARD_BYTES),
        cost_estimate=cost(16_000_000_000, 16_000_000),
        name="attention_backward",
    )(*[array for array, _ in operands])


def row_gradients(half, groups, summed_grad, proj, keys, vals, weights):
    count = 2 * half
    arrays = (summed_grad, *proj, *keys, *vals, *weights)
    outs = (((half, D), f32), ((half, D), f32), ((half, D), bf16))
    return pl.pallas_call(
        functools.partial(rows_kernel, half, groups),
        grid=(1,),
        out_shape=[jax.ShapeDtypeStruct(shape, kind) for shape, kind in outs],
        in_specs=[whole(array.shape) for array in arrays],
        out_specs=[whole(shape) for shape, _ in outs],
        scratch_shapes=[pltpu.VMEM((LEN, D), f32)],
        compiler_params=params(),
        cost_estimate=cost(4_000_000_000, 10_000_000),
        name="row_gradients",
    )(*arrays)


def swap(array):
    groups = lax.axis_size("tensor")
    return lax.ppermute(array, "tensor", [(i, (i + 1) % groups) for i in range(groups)])


def across(array, masks):
    size, groups = lax.axis_size("dp"), lax.axis_size("tensor")
    pairs = [
        (place * groups + core, (place ^ masks[core]) * groups + core)
        for place in range(size)
        for core in range(groups)
    ]
    return lax.ppermute(array, ("dp", "tensor"), pairs)


def total(terms):
    return functools.reduce(jnp.add, [term.astype(f32) for term in terms])


class Chain:
    def __init__(self, parts, rows, vectors=()):
        self.parts, self.rows = parts, rows
        self.vectors = list(vectors)
        self.messages = None
        self.done = 0

    def masks(self, part, bits):
        size, groups = lax.axis_size("dp"), lax.axis_size("tensor")
        found = []
        for core in range(groups):
            order = order_of(core, size.bit_length() - 1)[self.done : self.done + bits]
            found.append(
                sum(((part >> (bits - 1 - j)) & 1) << bit for j, bit in enumerate(order))
            )
        return found

    def send(self):
        if not self.bits:
            gots = [swap(self.messages[0])]
        else:
            gots = [
                across(message, self.masks(part + 1, self.bits))
                for part, message in enumerate(self.messages)
            ]
        for got in gots:
            column = 0
            for width, terms in self.parts:
                terms.append((got, column))
                column += width
            if self.vectors:
                self.vectors.append((got, column, self.rows))
        self.pending = gots
        self.done += self.bits
        self.messages = None

    def take(self, results):
        if self.vectors:
            self.vectors = [(results.pop(0), 0, VECTOR_ROWS)]
        kept, column, parts = results.pop(0), 0, []
        for width, _ in self.parts:
            parts.append((width, [(kept, column)]))
            column += width
        self.parts = parts
        self.messages = [results.pop(0) for _ in range((1 << self.bits) - 1)]

    def replace(self, old, new):
        for index, (width, terms) in enumerate(self.parts):
            self.parts[index] = (
                width,
                [(new if array is old else array, at) for array, at in terms],
            )
        self.vectors = [(new if a is old else a, at, rows) for a, at, rows in self.vectors]


def merged(chains):
    chain = Chain(
        [part for chain in chains for part in chain.parts],
        chains[0].rows,
        [term for chain in chains for term in chain.vectors],
    )
    chain.done = chains[0].done
    chain.pending = []
    return chain


class Operands:
    def __init__(self):
        self.arrays = []

    def of(self, array):
        for index, held in enumerate(self.arrays):
            if held is array:
                return index
        self.arrays.append(array)
        return len(self.arrays) - 1

    def in_specs(self):
        return [whole(array.shape) for array in self.arrays]


def prepare(requests):
    operands, plans, outs = Operands(), [], []
    plain = any(chain.rows % (8 << bits) for chain, bits in requests)
    for chain, bits in requests:
        chain.bits = bits
        chain.rows >>= bits
        rows, pieces = chain.rows, 1 << bits
        width = sum(width for width, _ in chain.parts)
        if plain:
            results = [
                jnp.concatenate(
                    [
                        total(
                            [
                                array[piece * rows : (piece + 1) * rows, at : at + width]
                                for array, at in terms
                            ]
                        )
                        for width, terms in chain.parts
                    ],
                    axis=1,
                )
                for piece in range(pieces)
            ]
            if chain.vectors:
                packed = summed_vectors(lambda array: array, chain.vectors)
                folded = fold_vectors(packed, rows)
                results = [packed, results[0]] + [
                    jnp.concatenate([result, folded], axis=1) for result in results[1:]
                ]
            chain.take([result.astype(bf16) for result in results])
            continue
        parts = [
            (width, [(operands.of(array), at) for array, at in terms])
            for width, terms in chain.parts
        ]
        vectors = [(operands.of(array), at, held) for array, at, held in chain.vectors]
        plans.append((rows, pieces, parts, vectors))
        if vectors:
            outs.append(((VECTOR_ROWS, TILE), f32))
        outs.append(((rows, width), bf16))
        wide = width + (vector_width(rows) if vectors else 0)
        outs += [((rows, wide), bf16)] * (pieces - 1)
    if plain:
        return
    results = pl.pallas_call(
        functools.partial(combine_kernel, plans),
        grid=(1,),
        out_shape=[jax.ShapeDtypeStruct(shape, kind) for shape, kind in outs],
        in_specs=operands.in_specs(),
        out_specs=[whole(shape) for shape, _ in outs],
        compiler_params=params(COMBINE_BYTES),
        cost_estimate=cost(1_000_000_000, 8_000_000),
        name="combine",
    )(*operands.arrays)
    results = list(results)
    for chain, bits in requests:
        chain.take(results)


def launch(requests, value, waits=()):
    chains = [chain for chain, bits in requests if bits is not None] + list(waits)
    olds = [got for chain in chains for got in chain.pending]
    if olds:
        value, news = lax.optimization_barrier((value, olds))
        for chain in chains + [chain for chain, _ in requests]:
            for old, new in zip(olds, news):
                chain.replace(old, new)
        for chain in chains:
            chain.pending = []
    sums = [(chain, bits) for chain, bits in requests if bits is not None]
    if sums:
        prepare(sums)
    messages = [chain.messages for chain, _ in requests]
    value, messages = lax.optimization_barrier((value, messages))
    for (chain, bits), message in zip(requests, messages):
        chain.messages = message
        if bits is None:
            chain.bits = 0
        chain.send()
    return value


def finish(size, groups, chain):
    share = D // (size * groups)
    up_rows = FF // D
    pieces = []
    for quad, (width, terms) in enumerate(chain.parts):
        for index in range(4):
            pieces.append((index, quad * QUAD, QUAD, [(a, at + index * QUAD) for a, at in terms]))
        if width > 4 * QUAD:
            pieces.append((4, 0, D, [(a, at + 4 * QUAD) for a, at in terms]))
    if share % 8:
        blocks = {}
        for target, at, width, terms in pieces:
            blocks.setdefault(target, []).append(
                total([array[:share, c : c + width] for array, c in terms])
            )
        weights = [jnp.concatenate(blocks[target], axis=1) for target in range(5)]
        vectors = unpack_vectors(summed_vectors(lambda array: array, chain.vectors))
        place = lax.axis_index("dp") * groups + lax.axis_index("tensor")
        mine = lax.dynamic_slice_in_dim(vectors, place * share, share, 1)
        ups = lax.dynamic_slice_in_dim(
            vectors[5 : 5 + up_rows].reshape(-1), place * up_rows * share, up_rows * share, 0
        )
        late = 5 + up_rows
        return weights, [mine[r] for r in (0, 1, 2, 3, 4, late, late + 1, late + 2)], mine[
            late + 3 : late + 5
        ].T, ups
    operands = Operands()
    plan = [
        (target, at, width, [(operands.of(array), c) for array, c in terms])
        for target, at, width, terms in pieces
    ]
    vectors = [(operands.of(array), at, held) for array, at, held in chain.vectors]
    outs = [(share, D)] * 5 + [(share,)] * 8 + [(2, share), (up_rows * share,)]
    found = pl.pallas_call(
        functools.partial(
            finish_kernel, size, groups, len(operands.arrays), (plan, vectors), up_rows
        ),
        grid=(1,),
        out_shape=[jax.ShapeDtypeStruct(shape, f32) for shape in outs],
        in_specs=operands.in_specs(),
        out_specs=[whole(shape) for shape in outs],
        compiler_params=params(COMBINE_BYTES),
        name="finish",
    )(*operands.arrays)
    return found[:5], found[5:13], found[13].T, found[14]


def body(
    content_in,
    query_in,
    memory,
    content_cot,
    query_cot,
    query_weight,
    key_weight,
    value_weight,
    out_weight,
    rel_weight,
    content_bias,
    position_bias,
    segment_bias,
    segment_embed,
    attn_gain,
    attn_shift,
    up_weight,
    up_bias,
    down_weight,
    down_bias,
    ffn_gain,
    ffn_shift,
    lengths,
    memory_lengths,
    segment_ids,
    orders,
    targets,
):
    groups = lax.axis_size("tensor")
    size = lax.axis_size("dp")
    steps = size.bit_length() - 1
    half = LEN // groups
    hidden_cols = up_weight.shape[1]
    up_other, down_other = swap(up_weight), swap(down_weight)
    content, query = content_in[0], query_in[0]
    segment_rows = segment_embed.T
    saved = attention_forward(
        half,
        (lengths, memory_lengths, segment_ids, orders, targets),
        memory[0],
        content,
        query,
        (query_weight, key_weight, value_weight, rel_weight),
        (content_bias, position_bias, segment_bias),
        segment_rows,
    )
    (
        content_out,
        query_out,
        ffn_own,
        ffn_other,
        summed_grad,
        attended_grad,
        out_own,
        out_other,
        early_small,
        up_bias_part,
    ) = middle(
        half,
        size,
        groups,
        (
            saved[0],
            content,
            query,
            content_cot[0],
            query_cot[0],
            out_weight,
            up_weight,
            up_other,
            down_weight,
            down_other,
            up_bias,
            down_bias,
            attn_gain,
            attn_shift,
            ffn_gain,
            ffn_shift,
        ),
        hidden_cols,
    )
    ffn = Chain([(2 * hidden_cols, [(ffn_own, 0)])], D)
    ffn.messages = [ffn_other]
    held = launch([(ffn, None)], attended_grad)
    content_late, held = lax.optimization_barrier((content, held))
    turned = transposed_rows(half, size, groups, memory[0], content_late, query, saved[11])
    turned, held = lax.optimization_barrier((turned, held))
    saved = (*saved, *turned)
    proj, tok_keys, tok_vals, small, late = [], [], [], [], []

    def backward(at, mode, grad, extra):
        own, other, proj_part, key_part, val_part, small_part, *vectors = attention_backward(
            half, groups, at, mode, saved, grad, segment_rows, extra
        )
        proj.append(proj_part)
        tok_keys.append(key_part)
        tok_vals.append(val_part)
        small.append(small_part)
        chain = Chain(
            [(own.shape[1], [(own, 0)])],
            own.shape[0],
            [(array, 0, VECTOR_ROWS) for array in vectors],
        )
        chain.messages = [other]
        late.append(chain)

    held = launch([(ffn, 1)], held)
    backward(0, "first", held, (out_own, out_other))
    held, proj[0] = launch([(late[0], None)], (attended_grad, proj[0]))
    backward(1, "middle", held, ())
    held, proj[1] = launch(
        [(ffn, 1), (late[0], 1), (late[1], None)], (attended_grad, proj[1])
    )
    backward(2, "last", held, (early_small, up_bias_part, *small))
    xy = min(2, steps)
    tok_vals[2] = launch(
        [(late[2], None), (ffn, 1), (late[0], 1), (late[1], 1)], tok_vals[2]
    )
    tok_vals[2] = launch([(late[2], xy), (late[1], 1)], tok_vals[2])
    own_rows, query_grad, row_send = row_gradients(
        half, groups, summed_grad, proj, tok_keys, tok_vals, (query_weight, key_weight, value_weight)
    )
    own_rows, row_send = launch([(ffn, 1)], (own_rows, row_send))
    final = merged(late)
    own_rows, row_send = launch(
        [(final, min(2, steps - final.done))], (own_rows, row_send), late
    )
    row_got = swap(row_send)
    while final.done < steps:
        own_rows = launch([(final, min(2, steps - final.done))], own_rows)
    while ffn.done < steps:
        own_rows = launch([(ffn, min(2, steps - ffn.done))], own_rows)
    content_grad = own_rows + row_got.astype(f32)
    ffn_sum = total([array[: ffn.rows] for array, _ in ffn.parts[0][1]])
    up_grad, down_grad_own = ffn_sum[:, :hidden_cols], ffn_sum[:, hidden_cols:].T
    (content_grad, up_grad, down_grad_own), olds = lax.optimization_barrier(
        ((content_grad, up_grad, down_grad_own), final.pending)
    )
    for old, new in zip(final.pending, olds):
        final.replace(old, new)
    weights, vectors, segment_grad, up_bias_grad = finish(size, groups, final)
    return (
        content_out[None],
        query_out[None],
        content_grad[None],
        query_grad[None],
        weights[0],
        weights[1],
        weights[2],
        weights[4],
        weights[3],
        vectors[5],
        vectors[6],
        vectors[7],
        segment_grad,
        vectors[3],
        vectors[4],
        up_grad,
        up_bias_grad,
        down_grad_own,
        vectors[2],
        vectors[0],
        vectors[1],
    )


def solution(mesh):
    in_specs = (
        P("dp", None, None),
        P("dp", "tensor", None),
        P("dp", None, None),
        P("dp", "tensor", None),
        P("dp", "tensor", None),
        P(),
        P(),
        P(),
        P(),
        P(),
        P(),
        P(),
        P(),
        P(),
        P(),
        P(),
        P(None, "tensor"),
        P(),
        P("tensor", None),
        P(),
        P(),
        P(),
        P("dp"),
        P("dp"),
        P("dp", None),
        P("dp", None),
        P("dp", None),
    )
    out_specs = (
        P("dp", "tensor", None),
        P("dp", "tensor", None),
        P("dp", "tensor", None),
        P("dp", "tensor", None),
        P(("dp", "tensor"), None),
        P(("dp", "tensor"), None),
        P(("dp", "tensor"), None),
        P(("dp", "tensor"), None),
        P(("dp", "tensor"), None),
        P(("dp", "tensor")),
        P(("dp", "tensor")),
        P(("dp", "tensor")),
        P(("dp", "tensor"), None),
        P(("dp", "tensor")),
        P(("dp", "tensor")),
        P("dp", "tensor"),
        P(("dp", "tensor")),
        P("tensor", "dp"),
        P(("dp", "tensor")),
        P(("dp", "tensor")),
        P(("dp", "tensor")),
    )
    return jax.shard_map(body, mesh=mesh, in_specs=in_specs, out_specs=out_specs, check_vma=False)
```

```python
import functools

import jax
import jax.numpy as jnp
from jax import lax
from jax.experimental import pallas as pl
from jax.experimental.pallas import tpu as pltpu
from jax.sharding import PartitionSpec as P

D = 768
HEADS = 12
HEAD_DIM = 64
FF = 3072
LEN = 512
MEM = 384
KEYS = MEM + LEN
QUAD = 4 * HEAD_DIM
QUADS = D // QUAD
PAIR = 2 * HEAD_DIM
SCALE = HEAD_DIM ** (-0.5)
VMEM_BYTES = 61 * 1024 * 1024
COMBINE_BYTES = 28 * 1024 * 1024
BACKWARD_BYTES = 54 * 1024 * 1024
MIDDLE_BYTES = 61 * 1024 * 1024
BLOCK = 16
TILE = 128
WIDE = 256
VECTORS = 16

VECTOR_ROWS = VECTORS * D // TILE

f32 = jnp.float32
bf16 = jnp.bfloat16
precise = lax.Precision.HIGHEST


def mm(left, right):
    return lax.dot_general(left, right, (((1,), (0,)), ((), ())), preferred_element_type=f32)


def mm_nt(left, right):
    return lax.dot_general(left, right, (((1,), (1,)), ((), ())), preferred_element_type=f32)


def mm_tn(left, right):
    return lax.dot_general(left, right, (((0,), (0,)), ((), ())), preferred_element_type=f32)


def unit_matrix(size):
    row = lax.broadcasted_iota(jnp.int32, (size, size), 0)
    return jnp.where(row == lanes((size, size)), 1.0, 0.0).astype(bf16)


def turn(value):
    width = min(value.shape[1], WIDE)
    unit = unit_matrix(width)
    blocks = [mm_nt(unit, value[:, n : n + width]) for n in range(0, value.shape[1], width)]
    return blocks[0] if len(blocks) == 1 else jnp.concatenate(blocks, axis=0)


def split(value):
    high = value.astype(bf16)
    return high, (value - high.astype(f32)).astype(bf16)


def lanes(shape):
    return lax.broadcasted_iota(jnp.int32, shape, 1)


def column_of(row):
    row = row.astype(f32)
    even = 2.0 * jnp.floor(0.5 * row)
    parts = jnp.concatenate([even, row - even, jnp.zeros((14, row.shape[1]), f32)], axis=0)
    return mm_tn(parts.astype(bf16), jnp.ones((16, TILE), bf16))


def lane_tiles(value, combine):
    tiles = [value[:, at : at + TILE] for at in range(0, value.shape[1], TILE)]
    return functools.reduce(combine, tiles)


def interleave(steps, tasks):
    done = 0
    for index, step in enumerate(steps):
        step()
        while done * len(steps) < (index + 1) * len(tasks) and done < len(tasks):
            tasks[done]()
            done += 1
    for task in tasks[done:]:
        task()


def order_of(core, bits):
    order = list(range(bits))
    if core == 1:
        for at in range(0, bits - 1, 2):
            order[at], order[at + 1] = order[at + 1], order[at]
    return order


def block_owner(place, core, bits):
    owners = []
    for each in range(2):
        owner = place * 0
        for step, bit in enumerate(order_of(each, bits)):
            owner = owner | (((place >> (bits - 1 - step)) & 1) << bit)
        owners.append(owner)
    return jnp.where(core == 1, owners[1], owners[0]) ^ lax.axis_index("dp")


def one_hot(source):
    return jnp.where(lanes((source.shape[0], D)) == source, 1.0, 0.0).astype(bf16)


def owner_rows(size, groups):
    share = D // (size * groups)
    row = lax.broadcasted_iota(jnp.int32, (D, 1), 0)
    side, rest = lax.div(row, size * share), lax.rem(row, size * share)
    core = lax.rem(lax.axis_index("tensor") + side, groups)
    owner = block_owner(lax.div(rest, share), core, size.bit_length() - 1)
    return one_hot((owner * groups + core) * share + lax.rem(rest, share))


def shared_rows(size, core):
    share = D // size
    row = lax.broadcasted_iota(jnp.int32, (D, 1), 0)
    owner = block_owner(lax.div(row, share), core, size.bit_length() - 1)
    return one_hot(owner * share + lax.rem(row, share))


def transpose_by_owner(out_ref, value, work, size, groups):
    share = D // (size * groups)
    if share % 8 or (2 * share) % 16:
        out_ref[...] = mm_nt(owner_rows(size, groups), value).astype(bf16)
        return
    width = value.shape[0]
    for n in range(0, D, WIDE):
        work[n : n + WIDE, :width] = turn(value[:, n : n + WIDE])
    bits = size.bit_length() - 1
    blocks = []
    for block in range(size * groups):
        core = lax.rem(lax.axis_index("tensor") + block // size, groups)
        owner = block_owner(jnp.int32(block % size), core, bits)
        at = pl.multiple_of((owner * groups + core) * share, 8)
        blocks.append(work[pl.ds(at, share), :width])
        if block % 2:
            out_ref[(block - 1) * share : (block + 1) * share, :] = jnp.concatenate(
                blocks, axis=0
            ).astype(bf16)
            blocks = []


def transpose_by_dp(out_ref, value, work, size):
    share = D // size
    core = lax.axis_index("tensor")
    if share % 16:
        out_ref[...] = mm_nt(shared_rows(size, core), value).astype(bf16)
        return
    for n in range(0, D, WIDE):
        work[n : n + WIDE, :] = turn(value[:, n : n + WIDE]).astype(bf16)
    for block in range(size):
        owner = block_owner(jnp.int32(block), core, size.bit_length() - 1)
        at = pl.multiple_of(owner * share, 16)
        out_ref[block * share : (block + 1) * share, :] = work[pl.ds(at, share), :]


def forward_kernel(
    half,
    length_ref,
    mem_length_ref,
    seg_ref,
    ord_ref,
    tgt_ref,
    memory_ref,
    content_ref,
    query_ref,
    wq_ref,
    wk_ref,
    wv_ref,
    wr_ref,
    cb_ref,
    pb_ref,
    sb_ref,
    se_ref,
    att_ref,
    prob_ref,
    key_ref,
    val_ref,
    rel_ref,
    hc_ref,
    hp_ref,
    hs_ref,
    linv_ref,
    kaug_ref,
    srow_ref,
    pos_ref,
    stack,
    both,
    pos,
    bias,
    fine,
    coarse,
    vectors,
    scores,
    places,
    kaug_t,
    scol,
    seg_row,
    kaug_work,
    order_work,
    seg_work,
):
    window = KEYS + half
    first = pl.multiple_of(lax.axis_index("tensor") * half, half)
    step_id = pl.program_id(0)

    @pl.when(step_id == 0)
    def _():
        stack[:MEM, :] = memory_ref[...]
        stack[MEM:, :] = content_ref[...]
        both[:half, :] = content_ref[pl.ds(first, half), :]
        both[half:, :] = query_ref[...]
        vectors[0:1, :] = cb_ref[...][None, :]
        vectors[1:2, :] = pb_ref[...][None, :]
        vectors[2:3, :] = sb_ref[...][None, :]
        step = lax.broadcasted_iota(jnp.int32, (1, D // 2), 1).astype(f32) * (2.0 / D)
        inverse = 1.0 / jnp.power(jnp.full((1, D // 2), 10000.0, f32), step)
        coarse_rows = coarse.shape[1]
        top = (MEM + half + first).astype(f32)
        angle = (
            top - 32.0 * lax.broadcasted_iota(jnp.int32, (coarse_rows, 1), 0).astype(f32)
        ) * inverse
        coarse[0] = jnp.sin(angle)
        coarse[1] = jnp.cos(angle)
        small = lax.broadcasted_iota(jnp.int32, (32, 1), 0).astype(f32) * inverse
        fine[0] = jnp.sin(small)
        fine[1] = jnp.cos(small)
        for a in range(window // 32):
            sa, ca = coarse[0, a : a + 1, :], coarse[1, a : a + 1, :]
            sb, cb = fine[0], fine[1]
            pos[a * 32 : (a + 1) * 32, : D // 2] = (sa * cb - ca * sb).astype(bf16)
            pos[a * 32 : (a + 1) * 32, D // 2 :] = (ca * cb + sa * sb).astype(bf16)
        never = float(LEN + 1)
        mem_at = lax.broadcasted_iota(jnp.int32, (1, MEM), 1)
        tok_at = lax.broadcasted_iota(jnp.int32, (1, LEN), 1)
        open_from = jnp.concatenate(
            [
                jnp.where(mem_at >= MEM - mem_length_ref[0], -1.0, never),
                jnp.where(
                    tok_at < length_ref[0],
                    jnp.where(tgt_ref[...] == 0, -1.0, ord_ref[...].astype(f32)),
                    never,
                ),
            ],
            axis=1,
        )
        order_col = column_of(ord_ref[...])
        seg_col = column_of(seg_ref[...])
        kaug_lane = lanes((LEN, PAIR)) % HEAD_DIM
        kaug_work[:MEM, :] = (lanes((MEM, PAIR)) % HEAD_DIM < 4).astype(f32).astype(bf16)
        kaug_work[MEM:, :] = jnp.where(
            kaug_lane < 4, 1.0, jnp.where(kaug_lane < 6, seg_col, 0.0)
        ).astype(bf16)
        kaug_t[...] = kaug_work[...].T[:HEAD_DIM]
        kaug_ref[...] = kaug_t[:16, :]
        order_work[...] = order_col
        own_order = order_work[pl.ds(first, half), :][:, :1]
        seg_work[...] = seg_col
        scol[...] = seg_work[pl.ds(first, half), :]
        seen = open_from <= own_order
        bias[:half, :] = jnp.where(seen, 0.0, -1e30)
        key_at = lax.broadcasted_iota(jnp.int32, (half, KEYS), 1)
        row_at = lax.broadcasted_iota(jnp.int32, (half, KEYS), 0)
        seen_q = seen & (key_at - MEM != row_at + first)
        bias[half:, :] = jnp.where(seen_q, 0.0, -1e30)
        seg_row[0:1, :] = seg_ref[...].astype(f32)
        srow_ref[...] = jnp.broadcast_to(seg_row[0:1, pl.ds(first, half)], srow_ref.shape)
        pos_ref[...] = pos[...]

    here = pl.ds(pl.multiple_of(step_id * QUAD, QUAD), QUAD)
    keys = mm(stack[...], wk_ref[...]).astype(bf16)
    values = mm(stack[...], wv_ref[...]).astype(bf16)
    rel = mm(pos[...], wr_ref[...]).astype(bf16)
    projection = mm(both[...], wq_ref[...])
    head_content = (projection + vectors[0:1, here]).astype(bf16)
    head_position = (projection + vectors[1:2, here]).astype(bf16)
    head_segment = projection + vectors[2:3, here]
    keys_t, values_t, rel_t = [turn(value).astype(bf16) for value in (keys, values, rel)]
    key_ref[...] = keys_t
    val_ref[...] = values_t
    rel_ref[...] = rel_t
    hs_ref[...] = head_segment
    head_content = (head_content.astype(f32) * SCALE).astype(bf16)
    head_position = (head_position.astype(f32) * SCALE).astype(bf16)
    hc_ref[...] = turn(head_content).astype(bf16)
    hp_ref[...] = turn(head_position).astype(bf16)
    row_head = lax.broadcasted_iota(jnp.int32, (QUAD, QUAD), 0) // HEAD_DIM
    at = lanes((QUAD, QUAD)) - ((row_head // 2) * PAIR + (1 - row_head % 2) * HEAD_DIM)
    place_same = jnp.where((at >= 0) & (at < 2), 1.0, 0.0).astype(bf16)
    place_step = jnp.where((at >= 2) & (at < 6), 1.0, 0.0).astype(bf16)
    same, other = se_ref[0:1, :], se_ref[1:2, :]
    terms = functools.reduce(
        jnp.add,
        [mm(part, place_same) for part in split(head_segment * same)]
        + [mm(part, place_step) for part in split(head_segment * (other - same))],
    )
    marks = jnp.concatenate([scol[...], scol[...]], axis=0)
    marks = jnp.concatenate([marks, marks], axis=1)
    lane6 = lanes((2 * half, QUAD)) % HEAD_DIM
    factor = jnp.where(lane6 < 2, 1.0, jnp.where(lane6 < 4, marks, 1.0 - 2.0 * marks))
    terms = SCALE * (terms * factor)
    high = terms.astype(bf16)
    low = (terms - high.astype(f32)).astype(bf16)
    qaug = jnp.where(lane6 % 2 == 0, high, low)
    key_x = []
    for which in range(4):
        own = keys_t[which * HEAD_DIM : (which + 1) * HEAD_DIM]
        sides = [own, kaug_t[...]] if which % 2 == 0 else [kaug_t[...], own]
        key_x.append(jnp.concatenate(sides, axis=0))
    peaks, totals, outs = {}, {}, {}
    row_first = lanes((2 * half, PAIR)) < HEAD_DIM

    def products(which):
        cols = slice(which // 2 * PAIR, (which // 2 + 1) * PAIR)
        slot = which % 2
        row_mine = row_first == (which % 2 == 0)
        query_x = jnp.where(row_mine, head_content[:, cols], qaug[:, cols])
        place_x = jnp.where(row_mine, head_position[:, cols], jnp.zeros((), bf16))

        def score(n, stop):
            scores[slot, :, n:stop] = mm(query_x, key_x[which][:, n:stop])

        def placed(n, stop):
            places[slot, :, n:stop] = mm(place_x, rel_t[cols, n:stop])

        return [functools.partial(placed, n, min(n + WIDE, window)) for n in range(0, window, WIDE)] + [
            functools.partial(score, n, min(n + WIDE, KEYS)) for n in range(0, KEYS, WIDE)
        ]

    def softmax(which):
        slot = which % 2
        tops, pieces = [], []

        def join(b):
            block = slice(b, b + BLOCK)
            shifted = pltpu.roll(
                places[slot, block, :], (KEYS + b % half) % window, 1, stride=1, stride_axis=0
            )[:, :KEYS]
            score = scores[slot, block, :] + shifted + bias[block, :]
            scores[slot, block, :] = score
            tops.append(lane_tiles(score, jnp.maximum))

        def peak():
            peaks[which] = jnp.max(jnp.concatenate(tops, axis=0), axis=1, keepdims=True)

        def power(b):
            block = slice(b, b + BLOCK)
            prob = jnp.exp(scores[slot, block, :] - peaks[which][block])
            pieces.append(lane_tiles(prob, jnp.add))
            prob_ref[which, block, :] = prob.astype(bf16)

        def finish():
            totals[which] = 1.0 / jnp.sum(
                jnp.concatenate(pieces, axis=0), axis=1, keepdims=True
            )

        blocks = range(0, 2 * half, BLOCK)
        return (
            [functools.partial(join, b) for b in blocks]
            + [peak]
            + [functools.partial(power, b) for b in blocks]
            + [finish]
        )

    def mixture(which, part):
        outs[which, part] = mm_nt(
            values_t[which * HEAD_DIM : (which + 1) * HEAD_DIM],
            prob_ref[which, part * half : (part + 1) * half, :],
        )

    interleave([], products(0))
    for which in range(4):
        tasks = products(which + 1) if which < 3 else []
        if which:
            tasks += [functools.partial(mixture, which - 1, part) for part in range(2)]
        interleave(softmax(which), tasks)
    for part in range(2):
        mixture(3, part)
    sums = [totals[which] for which in range(4)]
    mixed = jnp.concatenate(
        [jnp.concatenate([outs[which, 0], outs[which, 1]], axis=1) for which in range(4)], axis=0
    )
    mixed = functools.reduce(jnp.add, [turn(part) for part in split(mixed)])
    mine = lanes((2 * half, PAIR)) < HEAD_DIM
    for pair in range(2):
        cols = slice(pair * PAIR, (pair + 1) * PAIR)
        att_ref[:, cols] = mixed[:, cols] * jnp.where(mine, sums[2 * pair], sums[2 * pair + 1])
    lane = lanes((2 * half, TILE))
    linv_ref[...] = jnp.where(
        lane == 0, sums[0], jnp.where(lane == 1, sums[1], jnp.where(lane == 2, sums[2], sums[3]))
    )


def norm_forward(summed, gain, shift):
    center = summed - jnp.mean(summed, axis=1, keepdims=True)
    inv = lax.rsqrt(jnp.mean(center * center, axis=1, keepdims=True) + 1e-06)
    unit = center * inv
    return unit, inv, unit * gain + shift


def norm_backward(grad, unit, inv, gain):
    scaled = grad * gain
    return inv * (
        scaled
        - jnp.mean(scaled, axis=1, keepdims=True)
        - unit * jnp.mean(scaled * unit, axis=1, keepdims=True)
    )


def row_sum(value):
    return jnp.sum(value, axis=0, keepdims=True)


def gelu_parts(x):
    square = x * x
    tanh = jnp.tanh((0.7978845608028654 * x) * (1.0 + 0.044715 * square))
    rise = 0.5 * (1.0 + tanh)
    grad = rise + (0.5 * x) * (1.0 - tanh * tanh) * (
        0.7978845608028654 * (1.0 + 0.134145 * square)
    )
    return x * rise, grad


def fold_rows(value):
    return functools.reduce(jnp.add, [value[r : r + 8] for r in range(0, value.shape[0], 8)])


def middle_kernel(
    half,
    size,
    groups,
    chunk,
    att_ref,
    content_ref,
    query_ref,
    ccot_ref,
    qcot_ref,
    wo_ref,
    up_own_hbm,
    up_oth_hbm,
    down_own_hbm,
    down_oth_hbm,
    ubias_ref,
    dbias_ref,
    again_ref,
    ashift_ref,
    fgain_ref,
    fshift_ref,
    cout_ref,
    qout_ref,
    ffn_own_ref,
    ffn_oth_ref,
    sgrad_ref,
    agrad_ref,
    out_own_ref,
    out_oth_ref,
    small_ref,
    ubg_ref,
    hidden,
    slope,
    pre,
    work,
    unit,
    low,
    down_grad,
    vectors,
    up,
    down,
    low_t,
    down_t,
    turn_low,
    turn_down,
    attended_t,
    turn_work,
    sems,
):
    count = 2 * half
    member = lax.axis_index("tensor")
    first = pl.multiple_of(member * half, half)
    fetches = [
        pltpu.make_async_copy(source, target.at[side], sems.at[kind, side])
        for kind, side, source, target in (
            (0, 0, up_own_hbm, up),
            (1, 0, down_own_hbm, down),
            (0, 1, up_oth_hbm, up),
            (1, 1, down_oth_hbm, down),
        )
    ]
    for fetch in fetches:
        fetch.start()
    ups, downs = (up.at[0], up.at[1]), (down.at[0], down.at[1])
    part_cols = up.shape[2]
    chunks = part_cols // chunk
    vectors[0:1, :] = ubias_ref[...][None, :]
    attended = att_ref[...].astype(bf16)
    work[...] = mm(attended, wo_ref[...])
    attn_gain, attn_shift = again_ref[...][None, :], ashift_ref[...][None, :]
    ffn_gain, ffn_shift = fgain_ref[...][None, :], fshift_ref[...][None, :]
    down_bias = dbias_ref[...][None, :]
    inverse = []
    for b in range(0, count, BLOCK):
        block = slice(b, b + BLOCK)
        if b < half:
            rows_in = content_ref[pl.ds(pl.multiple_of(first + b, BLOCK), BLOCK), :]
        else:
            rows_in = query_ref[b - half : b - half + BLOCK, :]
        found, inv, normed = norm_forward(
            work[block, :] + rows_in.astype(f32), attn_gain, attn_shift
        )
        unit[block, :] = found
        inverse.append(inv)
        low[block, :] = normed.astype(bf16)
        work[block, :] = normed + down_bias
    for fetch in fetches:
        fetch.wait()
    pieces = [(side, at) for side in range(2) for at in range(chunks)]

    def rise(index):
        side, at = pieces[index]

        def task(n):
            pre[index % 2, :, n : n + WIDE] = mm(
                low[...], ups[side][:, at * chunk + n : at * chunk + n + WIDE]
            )

        return [functools.partial(task, n) for n in range(0, chunk, WIDE)]

    def bend(index):
        side, at = pieces[index]
        cols = slice(at * chunk, (at + 1) * chunk)
        start = lax.rem(member + side, 2) * part_cols + at * chunk
        bias = vectors[0:1, pl.ds(pl.multiple_of(start, TILE), chunk)]

        def step(b):
            block = slice(b, b + BLOCK)
            act, grad = gelu_parts(pre[index % 2, block, :] + bias)
            hidden[side, block, cols] = act.astype(bf16)
            slope[side, block, cols] = grad.astype(bf16)

        return [functools.partial(step, b) for b in range(0, count, BLOCK)]

    def fall(index):
        side, at = pieces[index]
        cols = slice(at * chunk, (at + 1) * chunk)

        def task(n):
            work[:, n : n + WIDE] += mm(hidden[side, :, cols], downs[side][cols, n : n + WIDE])

        return [functools.partial(task, n) for n in range(0, D, WIDE)]

    interleave([], rise(0))
    for index in range(len(pieces)):
        tasks = rise(index + 1) if index + 1 < len(pieces) else []
        if index:
            tasks += fall(index - 1)
        interleave(bend(index), tasks)
    interleave([], fall(len(pieces) - 1))
    sums = [jnp.zeros((8, D), f32) for _ in range(5)]
    for b in range(0, count, BLOCK):
        block = slice(b, b + BLOCK)
        found, inv, out = norm_forward(work[block, :], ffn_gain, ffn_shift)
        if b < half:
            cout_ref[block, :] = out.astype(bf16)
            cot = ccot_ref[block, :].astype(f32)
        else:
            block_q = slice(b - half, b - half + BLOCK)
            qout_ref[block_q, :] = out.astype(bf16)
            cot = qcot_ref[block_q, :].astype(f32)
        residual_grad = norm_backward(cot, found, inv, ffn_gain)
        rounded = residual_grad.astype(bf16)
        down_grad[block, :] = rounded
        work[block, :] = residual_grad
        for index, value in enumerate((cot * found, cot, rounded.astype(f32))):
            sums[index] = sums[index] + fold_rows(value)
    transpose_by_dp(low_t, low[...], turn_low, size)
    transpose_by_dp(down_t, down_grad[...], turn_down, size)
    for side in range(2):
        for at in range(chunks):
            cols = slice(at * chunk, (at + 1) * chunk)
            hidden_grad = mm_nt(down_grad[...], downs[side][cols, :])
            pre_grad = (hidden_grad * slope[side, :, cols].astype(f32)).astype(bf16)
            slope[side, :, cols] = pre_grad
            ubg_ref[side : side + 1, cols] = row_sum(pre_grad.astype(f32))
            work[...] += mm_nt(pre_grad, ups[side][:, cols])

    def settle(b):
        block = slice(b, b + BLOCK)
        grad, found = work[block, :], unit[block, :]
        summed_grad = norm_backward(grad, found, inverse[b // BLOCK], attn_gain)
        sgrad_ref[block, :] = summed_grad
        down_grad[block, :] = summed_grad.astype(bf16)
        sums[3] = sums[3] + fold_rows(grad * found)
        sums[4] = sums[4] + fold_rows(grad)

    share = D // size
    bits = size.bit_length() - 1

    def other_place(place):
        found = 0
        for step in range(bits):
            there = order_of(1, bits)[step]
            found |= ((place >> (bits - 1 - there)) & 1) << (bits - 1 - step)
        return found

    def weigh(side, kind, n):
        left, right = ((low_t, slope), (down_t, hidden))[kind]
        value = mm(left[...], right[side, :, n : n + WIDE]).astype(bf16)
        target = (ffn_own_ref, ffn_oth_ref)[side]
        cols = slice(kind * part_cols + n, kind * part_cols + n + WIDE)
        if side == 0:
            target[:, cols] = value
            return
        for place in range(size):
            to = other_place(place)
            target[to * share : (to + 1) * share, cols] = value[
                place * share : (place + 1) * share
            ]

    tasks = [
        functools.partial(weigh, side, kind, n)
        for side in (1, 0)
        for kind in range(2)
        for n in range(0, part_cols, WIDE)
    ]
    interleave([functools.partial(settle, b) for b in range(0, count, BLOCK)], tasks)
    for index, value in enumerate(sums):
        small_ref[index : index + 1, :] = row_sum(value)
    small_ref[5:8, :] = jnp.zeros((3, D), f32)
    agrad_ref[...] = mm_nt(down_grad[...], wo_ref[...]).astype(bf16)
    transpose_by_owner(attended_t, attended, turn_work, size, groups)
    out_part = mm(attended_t[...], down_grad[...]).astype(bf16)
    half_rows = D // groups
    out_own_ref[...] = out_part[:half_rows]
    out_oth_ref[...] = out_part[half_rows : 2 * half_rows]


def unshift(value, shift, window):
    whole, rest = shift // TILE, shift % TILE
    row = lax.broadcasted_iota(jnp.int32, (BLOCK, TILE), 0)
    lane = lanes((BLOCK, TILE))
    index = (lane + row - rest) & (TILE - 1)
    tiles = [
        jnp.take_along_axis(
            value[:, n : n + TILE], index, axis=1, mode="promise_in_bounds"
        )
        for n in range(0, value.shape[1], TILE)
    ]
    zero = jnp.zeros((BLOCK, TILE), f32)

    def tile(n):
        return tiles[n] if 0 <= n < len(tiles) else zero

    if rest:
        here = lane >= rest - row
        found = [
            jnp.where(here, tile(n - whole), tile(n - whole - 1)) for n in range(window // TILE)
        ]
    else:
        here = lane + row < TILE
        found = [
            jnp.where(here, tile(n - whole), tile(n - whole + 1)) for n in range(window // TILE)
        ]
    return jnp.concatenate(found, axis=1)


def backward_kernel(
    half,
    groups,
    at,
    mode,
    prob_hbm,
    key_ref,
    val_ref,
    rel_ref,
    hc_ref,
    hp_ref,
    hs_ref,
    linv_ref,
    kaug_ref,
    srow_ref,
    att_ref,
    agrad_ref,
    se_ref,
    both_t_hbm,
    stack_t_hbm,
    pos_t_hbm,
    *rest,
):
    more = rest[: {"first": 2, "middle": 0, "last": 4}[mode]]
    own_ref, oth_ref, proj_ref, tok_key_ref, tok_val_ref, small_ref = rest[len(more) :][:6]
    prob, both_t, stack_t, pos_t, spread, grads, turned, sems = rest[-8:]
    count, window = 2 * half, KEYS + half
    heads = 4
    prob_copies = [
        pltpu.make_async_copy(prob_hbm.at[at * heads + h], prob.at[h], sems.at[h])
        for h in range(heads)
    ]
    fetches = [
        pltpu.make_async_copy(source, target, sems.at[heads + index])
        for index, (source, target) in enumerate(
            ((both_t_hbm, both_t), (stack_t_hbm, stack_t), (pos_t_hbm, pos_t))
        )
    ]
    for copy in prob_copies + fetches:
        copy.start()
    share = D // groups
    if mode == "first":
        own_ref[:, 4 * QUAD :] = more[0][...]
        oth_ref[:, 4 * QUAD :] = more[1][...]
    kaug_t = kaug_ref[...]
    filler = jnp.zeros((HEAD_DIM - kaug_t.shape[0], KEYS), bf16)
    marks = jnp.concatenate([srow_ref[0:1, :], srow_ref[0:1, :]], axis=1)
    swing = 1.0 - 2.0 * marks
    key_t, val_t, rel_t = [], [], []
    lane = lanes((count, PAIR))
    agrads, grad_x, agrad_t = [], [], []
    for pair in range(2):
        cols = slice(pair * PAIR, (pair + 1) * PAIR)
        linv = jnp.where(
            lane < HEAD_DIM,
            linv_ref[:, 2 * pair : 2 * pair + 1],
            linv_ref[:, 2 * pair + 1 : 2 * pair + 2],
        )
        agrad = (agrad_ref[:, cols].astype(f32) * linv).astype(bf16).astype(f32)
        products = agrad * att_ref[:, cols]
        agrad_t.append(turn(agrad.astype(bf16)).astype(bf16))
        for head in range(2):
            base = (1 - head) * HEAD_DIM
            mine = (lane < HEAD_DIM) == (head == 0)
            weight = jnp.sum(jnp.where(mine, products, 0.0), axis=1, keepdims=True)
            high = weight.astype(bf16).astype(f32)
            grad_x.append(
                jnp.where(
                    mine,
                    agrad,
                    jnp.where(
                        lane == base, -high, jnp.where(lane == base + 1, high - weight, 0.0)
                    ),
                ).astype(bf16)
            )
    found = {}

    def head_of(ref, which):
        return ref[which * HEAD_DIM : (which + 1) * HEAD_DIM, :]

    def spreads(which):
        own = head_of(val_ref, which)
        sides = [own, kaug_t, filler] if which % 2 == 0 else [kaug_t, filler, own]
        val_x = jnp.concatenate(sides, axis=0)
        prob_copies[which].wait()

        def task(n, stop):
            spread[which % 2, :, n:stop] = mm(grad_x[which], val_x[:, n:stop])

        return [functools.partial(task, n, min(n + WIDE, KEYS)) for n in range(0, KEYS, WIDE)]

    def score_grads(which):
        buffer = which % 2

        def step(part, b):
            at_row = part * half + b
            block = slice(at_row, at_row + BLOCK)
            score_grad = prob[which, block, :].astype(f32) * spread[buffer, block, :]
            grads[buffer, block, :] = score_grad.astype(bf16)
            turned[buffer, block, :] = unshift(score_grad, half - b, window).astype(bf16)

        return [
            functools.partial(step, part, b) for part in range(2) for b in range(0, half, BLOCK)
        ]

    def gathers(which):
        buffer = which % 2
        side = slice(which % 2 * HEAD_DIM, (which % 2 + 1) * HEAD_DIM)
        key_x = jnp.concatenate([head_of(key_ref, which), kaug_t], axis=0)
        found[which] = {"value": [], "key": [], "rel": [], "content": [], "place": []}

        def down_rows(name, left, ref, n, stop):
            found[which][name].append(mm(left, ref[:, n:stop]))

        tasks = []
        for name, left, ref, end in (
            ("value", agrad_t[which // 2][side], prob.at[which], KEYS),
            ("key", head_of(hc_ref, which), grads.at[buffer], KEYS),
            ("rel", head_of(hp_ref, which), turned.at[buffer], window),
        ):
            tasks += [
                functools.partial(down_rows, name, left, ref, n, min(n + WIDE, end))
                for n in range(0, end, WIDE)
            ]

        def content(n):
            found[which]["content"].append(mm_nt(key_x, grads[buffer, n : n + half, :]))

        def placed(n):
            found[which]["place"].append(
                mm_nt(head_of(rel_ref, which), turned[buffer, n : n + half, :])
            )

        for n in (0, half):
            tasks += [functools.partial(content, n), functools.partial(placed, n)]
        return tasks

    interleave([], spreads(0))
    for which in range(heads):
        tasks = spreads(which + 1) if which + 1 < heads else []
        if which:
            tasks += gathers(which - 1)
        interleave(score_grads(which), tasks)
    interleave([], gathers(heads - 1))
    for which in range(heads):
        val_t.append(jnp.concatenate(found[which]["value"], axis=1))
        key_t.append(jnp.concatenate(found[which]["key"], axis=1))
        rel_t.append(jnp.concatenate(found[which]["rel"], axis=1))
    same, other, contents, places = [], [], [], []
    for which in range(heads):
        content_head = jnp.concatenate(found[which]["content"], axis=1)
        total = content_head[HEAD_DIM : HEAD_DIM + 1]
        marked = content_head[HEAD_DIM + 4 : HEAD_DIM + 5]
        other.append(SCALE * (marks * total + swing * marked))
        same.append(SCALE * total - other[-1])
        contents.append((SCALE * content_head[:HEAD_DIM]).astype(bf16))
        places.append((SCALE * jnp.concatenate(found[which]["place"], axis=1)).astype(bf16))
    contents, places = jnp.concatenate(contents, axis=0), jnp.concatenate(places, axis=0)
    term_high, term_low = split(jnp.concatenate(same + other, axis=0))
    line = lax.broadcasted_iota(jnp.int32, (2 * heads, QUAD), 0)
    mine = line % heads == lanes((2 * heads, QUAD)) // HEAD_DIM
    embed = jnp.where(line < heads, se_ref[0:1, :], se_ref[1:2, :])
    embed_high, embed_low = split(jnp.where(mine, embed, 0.0))
    segment_grad = mm_tn(
        jnp.concatenate([embed_high, embed_high, embed_low, embed_low], axis=0),
        jnp.concatenate([term_high, term_low, term_high, term_low], axis=0),
    )
    proj_t = (contents.astype(f32) + places.astype(f32) + segment_grad).astype(bf16)
    ones = jnp.ones((16, count), bf16)
    small_ref[0:1, :] = mm_nt(ones, contents)[0:1]
    small_ref[1:2, :] = mm_nt(ones, places)[0:1]
    small_ref[2:3, :] = functools.reduce(
        jnp.add, [mm_nt(ones, part)[0:1] for part in split(segment_grad)]
    )
    terms = jnp.concatenate([term_high, term_low], axis=0)
    embed_grad = functools.reduce(jnp.add, [mm(terms, part) for part in split(hs_ref[...])])
    embed_grad = jnp.where(mine, embed_grad[: 2 * heads] + embed_grad[2 * heads :], 0.0)
    small_ref[3:4, :] = row_sum(embed_grad[:heads])
    small_ref[4:5, :] = row_sum(embed_grad[heads:])
    small_ref[5:8, :] = jnp.zeros((3, QUAD), f32)
    key_t = jnp.concatenate(key_t, axis=0).astype(bf16)
    val_t = jnp.concatenate(val_t, axis=0).astype(bf16)
    rel_t = jnp.concatenate(rel_t, axis=0).astype(bf16)
    proj_ref[...] = turn(proj_t).astype(bf16)
    tok_key_ref[...] = turn(key_t[:, MEM:]).astype(bf16)
    tok_val_ref[...] = turn(val_t[:, MEM:]).astype(bf16)
    for fetch in fetches:
        fetch.wait()
    parts = (
        mm_nt(both_t[...], proj_t),
        mm_nt(stack_t[...], key_t),
        mm_nt(stack_t[...], val_t),
        mm_nt(pos_t[...], rel_t),
    )
    for index, value in enumerate(parts):
        cols = slice(index * QUAD, (index + 1) * QUAD)
        own_ref[:, cols] = value[:share].astype(bf16)
        oth_ref[:, cols] = value[share : 2 * share].astype(bf16)
    if mode == "last":
        vec_ref = rest[len(more) + 6]
        early, ubias, before, between = more
        core = lax.axis_index("tensor")
        rows = [early[0:5, :]]
        mine = [ubias[0:1, n : n + D] for n in range(0, ubias.shape[1], D)]
        theirs = [ubias[1:2, n : n + D] for n in range(0, ubias.shape[1], D)]
        for left, right in ((mine, theirs), (theirs, mine)):
            rows += [jnp.where(core == 0, a, b) for a, b in zip(left, right)]
        rows.append(
            jnp.concatenate([before[0:5, :], between[0:5, :], small_ref[0:5, :]], axis=1)
        )
        rows = jnp.concatenate(rows, axis=0)
        spare = jnp.zeros((VECTORS - rows.shape[0], D), f32)
        rows = jnp.concatenate([rows, spare], axis=0)
        packed = jnp.concatenate([rows[:, n : n + TILE] for n in range(0, D, TILE)], axis=0)
        vec_ref[...] = packed
        oth_ref[:VECTOR_ROWS, 4 * QUAD :] = packed.astype(bf16)
        oth_ref[VECTOR_ROWS:, 4 * QUAD :] = jnp.zeros((share - VECTOR_ROWS, TILE), bf16)


def rows_kernel(half, groups, sgrad_ref, *rest):
    proj, keys, vals = rest[:QUADS], rest[QUADS : 2 * QUADS], rest[2 * QUADS : 3 * QUADS]
    wq_ref, wk_ref, wv_ref, own_ref, query_ref, send_ref, both = rest[3 * QUADS :]
    member = lax.axis_index("tensor")
    wide = [jnp.concatenate([ref[...] for ref in refs], axis=1) for refs in (proj, keys, vals)]
    both[...] = mm_nt(wide[1], wk_ref[...]) + mm_nt(wide[2], wv_ref[...])
    rows = sgrad_ref[...] + mm_nt(wide[0], wq_ref[...])
    own = pl.multiple_of(member * half, half)
    other = pl.multiple_of(lax.rem(member + 1, groups) * half, half)
    send_ref[...] = both[pl.ds(other, half), :].astype(bf16)
    own_ref[...] = rows[:half] + both[pl.ds(own, half), :]
    query_ref[...] = rows[half:]


def summed(operands, terms, first, rows, width):
    values = []
    for index, at in terms:
        if rows % 16 == 0:
            value = operands[index][first : first + rows, at : at + width].astype(f32)
        else:
            value = operands[index][:, at : at + width].astype(f32)[first : first + rows]
        values.append(value)
    return functools.reduce(jnp.add, values)


def vector_width(rows):
    return TILE * max(1, VECTOR_ROWS // rows)


def fold_vectors(packed, rows):
    if rows > VECTOR_ROWS:
        return jnp.concatenate([packed, jnp.zeros((rows - VECTOR_ROWS, TILE), f32)], axis=0)
    return jnp.concatenate(
        [packed[n : n + rows] for n in range(0, VECTOR_ROWS, rows)], axis=1
    )


def unfold_vectors(block, rows):
    if rows >= VECTOR_ROWS:
        return block[:VECTOR_ROWS]
    return jnp.concatenate(
        [block[:, n : n + TILE] for n in range(0, vector_width(rows), TILE)], axis=0
    )


def summed_vectors(values, terms):
    return functools.reduce(
        jnp.add,
        [
            unfold_vectors(
                values(index)[:rows, at : at + vector_width(rows)].astype(f32), rows
            )
            for index, at, rows in terms
        ],
    )


def combine_kernel(plans, *refs):
    count = sum(pieces + (1 if vectors else 0) for _, pieces, _, vectors in plans)
    operands, outs = refs[:-count], list(refs[-count:])
    for rows, pieces, parts, vectors in plans:
        if vectors:
            packed = summed_vectors(lambda index: operands[index][...].astype(f32), vectors)
            outs.pop(0)[...] = packed
        for piece in range(pieces):
            out_ref = outs.pop(0)
            column = 0
            for width, terms in parts:
                value = summed(operands, terms, piece * rows, rows, width)
                out_ref[:, column : column + width] = value.astype(out_ref.dtype)
                column += width
            if piece and vectors:
                out_ref[:, column:] = fold_vectors(packed, rows).astype(out_ref.dtype)


def unpack_vectors(packed):
    return jnp.concatenate(
        [packed[n : n + VECTORS] for n in range(0, VECTOR_ROWS, VECTORS)], axis=1
    )


def finish_kernel(size, groups, count, plan, up_rows, *refs):
    operands, outs = refs[:count], refs[count:]
    weights, vec_outs, embed_out, up_out = outs[:5], outs[5:-2], outs[-2], outs[-1]
    place = lax.axis_index("dp") * groups + lax.axis_index("tensor")
    share = D // (size * groups)
    for target, at, width, terms in plan[0]:
        weights[target][:, at : at + width] = summed(operands, terms, 0, share, width)
    value = unpack_vectors(
        summed_vectors(lambda index: operands[index][...].astype(f32), plan[1])
    )
    mine = pltpu.roll(value, lax.rem(D - place * share, D), 1)[:, :TILE]
    rows = [row for row in range(5 + up_rows + 3) if not 5 <= row < 5 + up_rows]
    for row, out_ref in zip(rows, vec_outs):
        out_ref[...] = mine[row, :share]
    embed = jnp.concatenate([mine[5 + up_rows + 3 : 5 + up_rows + 5], jnp.zeros((6, TILE), f32)], axis=0)
    embed_out[...] = embed[:2, :share]
    wide = up_rows * share
    each = D // wide
    line = lax.div(place, each)
    chosen = functools.reduce(
        jnp.add,
        [jnp.where(line == r, value[5 + r : 6 + r], 0.0) for r in range(up_rows)],
    )
    chosen = jnp.broadcast_to(chosen, (8, D))
    turned = pltpu.roll(chosen, lax.rem(D - lax.rem(place, each) * wide, D), 1)[:, :TILE]
    up_out[...] = turned[0, :wide]


def whole(shape):
    return pl.BlockSpec(shape, lambda i: (0,) * len(shape))


def columns(rows, width, at=None):
    if at is None:
        return pl.BlockSpec((rows, width), lambda i: (0, i))
    return pl.BlockSpec((rows, width), lambda i: (0, at))


def row_block(rows, width, at=None):
    if at is None:
        return pl.BlockSpec((rows, width), lambda i: (i, 0))
    return pl.BlockSpec((rows, width), lambda i: (at, 0))


def scalars():
    return pl.BlockSpec(memory_space=pltpu.SMEM)


def params(size=VMEM_BYTES):
    return pltpu.CompilerParams(vmem_limit_bytes=size)


def cost(flops, bytes_accessed):
    return pl.CostEstimate(flops=flops, bytes_accessed=bytes_accessed, transcendentals=0)


def in_hbm():
    return pl.BlockSpec(memory_space=pl.ANY)


def attention_forward(
    half, ints, memory, content, query, weights, biases, segment_rows
):
    count, window = 2 * half, KEYS + half
    coarse_rows = -(-(window // 32) // 8) * 8
    outs = (
        ((count, D), f32, columns(count, QUAD)),
        ((HEADS, count, KEYS), bf16, pl.BlockSpec((4, count, KEYS), lambda i: (i, 0, 0))),
        ((D, KEYS), bf16, row_block(QUAD, KEYS)),
        ((D, KEYS), bf16, row_block(QUAD, KEYS)),
        ((D, window), bf16, row_block(QUAD, window)),
        ((D, count), bf16, row_block(QUAD, count)),
        ((D, count), bf16, row_block(QUAD, count)),
        ((count, D), f32, columns(count, QUAD)),
        ((count, QUADS * TILE), f32, columns(count, TILE)),
        ((16, KEYS), bf16, whole((16, KEYS))),
        ((8, half), f32, whole((8, half))),
        ((window, D), bf16, whole((window, D))),
    )
    return pl.pallas_call(
        functools.partial(forward_kernel, half),
        grid=(QUADS,),
        out_shape=[jax.ShapeDtypeStruct(shape, kind) for shape, kind, _ in outs],
        in_specs=[
            scalars(),
            scalars(),
            whole((1, LEN)),
            whole((1, LEN)),
            whole((1, LEN)),
            whole((MEM, D)),
            whole((LEN, D)),
            whole((half, D)),
        ]
        + [columns(D, QUAD)] * 4
        + [whole((D,))] * 3
        + [columns(2, QUAD)],
        out_specs=[spec for _, _, spec in outs],
        scratch_shapes=[
            pltpu.VMEM((KEYS, D), bf16),
            pltpu.VMEM((count, D), bf16),
            pltpu.VMEM((window, D), bf16),
            pltpu.VMEM((count, KEYS), f32),
            pltpu.VMEM((2, 32, D // 2), f32),
            pltpu.VMEM((2, coarse_rows, D // 2), f32),
            pltpu.VMEM((8, D), f32),
            pltpu.VMEM((2, count, KEYS), f32),
            pltpu.VMEM((2, count, window), f32),
            pltpu.VMEM((HEAD_DIM, KEYS), bf16),
            pltpu.VMEM((half, PAIR), f32),
            pltpu.VMEM((8, LEN), f32),
            pltpu.VMEM((KEYS, PAIR), bf16),
            pltpu.VMEM((LEN, TILE), f32),
            pltpu.VMEM((LEN, TILE), f32),
        ],
        compiler_params=params(),
        cost_estimate=cost(30_000_000_000, 40_000_000),
        name="attention_forward",
    )(*ints, memory, content, query, *weights, *biases, segment_rows)


def middle(half, size, groups, arrays, hidden_cols):
    count, share = 2 * half, D // groups
    chunk = min(hidden_cols, 768)
    outs = (
        ((half, D), bf16),
        ((half, D), bf16),
        ((D, 2 * hidden_cols), bf16),
        ((D, 2 * hidden_cols), bf16),
        ((count, D), f32),
        ((count, D), bf16),
        ((share, D), bf16),
        ((share, D), bf16),
        ((8, D), f32),
        ((2, hidden_cols), f32),
    )
    weights = (6, 7, 8, 9)
    return pl.pallas_call(
        functools.partial(middle_kernel, half, size, groups, chunk),
        grid=(1,),
        out_shape=[jax.ShapeDtypeStruct(shape, kind) for shape, kind in outs],
        in_specs=[
            in_hbm() if i in weights else whole(array.shape) for i, array in enumerate(arrays)
        ],
        out_specs=[whole(shape) for shape, _ in outs],
        scratch_shapes=[
            pltpu.VMEM((2, count, hidden_cols), bf16),
            pltpu.VMEM((2, count, hidden_cols), bf16),
            pltpu.VMEM((2, count, chunk), f32),
            pltpu.VMEM((count, D), f32),
            pltpu.VMEM((count, D), f32),
            pltpu.VMEM((count, D), bf16),
            pltpu.VMEM((count, D), bf16),
            pltpu.VMEM((8, FF), f32),
            pltpu.VMEM((2, D, hidden_cols), bf16),
            pltpu.VMEM((2, hidden_cols, D), bf16),
            pltpu.VMEM((D, count), bf16),
            pltpu.VMEM((D, count), bf16),
            pltpu.VMEM((D, count), bf16),
            pltpu.VMEM((D, count), bf16),
            pltpu.VMEM((D, count), bf16),
            pltpu.VMEM((D, count), f32),
            pltpu.SemaphoreType.DMA((2, 2)),
        ],
        compiler_params=params(MIDDLE_BYTES),
        cost_estimate=cost(30_000_000_000, 30_000_000),
        name="feed_forward",
    )(*arrays)


def prepare_kernel(
    half,
    size,
    groups,
    memory_ref,
    content_ref,
    query_ref,
    pos_ref,
    both_t_ref,
    stack_t_ref,
    pos_t_ref,
    both_work,
    stack_work,
    pos_work,
):
    first = pl.multiple_of(lax.axis_index("tensor") * half, half)
    both = jnp.concatenate([content_ref[pl.ds(first, half), :], query_ref[...]], axis=0)
    stack = jnp.concatenate([memory_ref[...], content_ref[...]], axis=0)
    transpose_by_owner(both_t_ref, both, both_work, size, groups)
    transpose_by_owner(stack_t_ref, stack, stack_work, size, groups)
    transpose_by_owner(pos_t_ref, pos_ref[...], pos_work, size, groups)


def transposed_rows(half, size, groups, memory, content, query, pos):
    count, window = 2 * half, KEYS + half
    arrays = (memory, content, query, pos)
    outs = ((D, count), (D, KEYS), (D, window))
    return pl.pallas_call(
        functools.partial(prepare_kernel, half, size, groups),
        grid=(1,),
        out_shape=[jax.ShapeDtypeStruct(shape, bf16) for shape in outs],
        in_specs=[whole(array.shape) for array in arrays],
        out_specs=[whole(shape) for shape in outs],
        scratch_shapes=[pltpu.VMEM(shape, f32) for shape in outs],
        compiler_params=params(BACKWARD_BYTES),
        cost_estimate=cost(6_000_000_000, 8_000_000),
        name="transposed_rows",
    )(*arrays)


def attention_backward(half, groups, at, mode, saved, agrad, segment_rows, extra):
    count, window, share = 2 * half, KEYS + half, D // groups
    att, prob, keys, values, rel, hc, hp, hs, linv, kaug, srow, _ = saved[:12]
    both_t, stack_t, pos_t = saved[12:]
    width = 4 * QUAD + (D if mode == "first" else 0)
    operands = (
        (prob, in_hbm()),
        (keys, row_block(QUAD, KEYS, at)),
        (values, row_block(QUAD, KEYS, at)),
        (rel, row_block(QUAD, window, at)),
        (hc, row_block(QUAD, count, at)),
        (hp, row_block(QUAD, count, at)),
        (hs, columns(count, QUAD, at)),
        (linv, columns(count, TILE, at)),
        (kaug, whole((16, KEYS))),
        (srow, whole((8, half))),
        (att, columns(count, QUAD, at)),
        (agrad, columns(count, QUAD, at)),
        (segment_rows, columns(2, QUAD, at)),
        (both_t, in_hbm()),
        (stack_t, in_hbm()),
        (pos_t, in_hbm()),
    ) + tuple((array, whole(array.shape)) for array in extra)
    outs = (
        ((share, width), bf16),
        ((share, width + (TILE if mode == "last" else 0)), bf16),
        ((count, QUAD), bf16),
        ((LEN, QUAD), bf16),
        ((LEN, QUAD), bf16),
        ((8, QUAD), f32),
    )
    if mode == "last":
        outs += (((VECTOR_ROWS, TILE), f32),)
    return pl.pallas_call(
        functools.partial(backward_kernel, half, groups, at, mode),
        grid=(1,),
        out_shape=[jax.ShapeDtypeStruct(shape, kind) for shape, kind in outs],
        in_specs=[spec for _, spec in operands],
        out_specs=[whole(shape) for shape, _ in outs],
        scratch_shapes=[
            pltpu.VMEM((4, count, KEYS), bf16),
            pltpu.VMEM((D, count), bf16),
            pltpu.VMEM((D, KEYS), bf16),
            pltpu.VMEM((D, window), bf16),
            pltpu.VMEM((2, count, KEYS), f32),
            pltpu.VMEM((2, count, KEYS), bf16),
            pltpu.VMEM((2, count, window), bf16),
            pltpu.SemaphoreType.DMA((7,)),
        ],
        compiler_params=params(BACKWARD_BYTES),
        cost_estimate=cost(16_000_000_000, 16_000_000),
        name="attention_backward",
    )(*[array for array, _ in operands])


def row_gradients(half, groups, summed_grad, proj, keys, vals, weights):
    count = 2 * half
    arrays = (summed_grad, *proj, *keys, *vals, *weights)
    outs = (((half, D), f32), ((half, D), f32), ((half, D), bf16))
    return pl.pallas_call(
        functools.partial(rows_kernel, half, groups),
        grid=(1,),
        out_shape=[jax.ShapeDtypeStruct(shape, kind) for shape, kind in outs],
        in_specs=[whole(array.shape) for array in arrays],
        out_specs=[whole(shape) for shape, _ in outs],
        scratch_shapes=[pltpu.VMEM((LEN, D), f32)],
        compiler_params=params(),
        cost_estimate=cost(4_000_000_000, 10_000_000),
        name="row_gradients",
    )(*arrays)


def swap(array):
    groups = lax.axis_size("tensor")
    return lax.ppermute(array, "tensor", [(i, (i + 1) % groups) for i in range(groups)])


def across(array, masks):
    size, groups = lax.axis_size("dp"), lax.axis_size("tensor")
    pairs = [
        (place * groups + core, (place ^ masks[core]) * groups + core)
        for place in range(size)
        for core in range(groups)
    ]
    return lax.ppermute(array, ("dp", "tensor"), pairs)


def total(terms):
    return functools.reduce(jnp.add, [term.astype(f32) for term in terms])


class Chain:
    def __init__(self, parts, rows, vectors=()):
        self.parts, self.rows = parts, rows
        self.vectors = list(vectors)
        self.messages = None
        self.done = 0

    def masks(self, part, bits):
        size, groups = lax.axis_size("dp"), lax.axis_size("tensor")
        found = []
        for core in range(groups):
            order = order_of(core, size.bit_length() - 1)[self.done : self.done + bits]
            found.append(
                sum(((part >> (bits - 1 - j)) & 1) << bit for j, bit in enumerate(order))
            )
        return found

    def send(self):
        if not self.bits:
            gots = [swap(self.messages[0])]
        else:
            gots = [
                across(message, self.masks(part + 1, self.bits))
                for part, message in enumerate(self.messages)
            ]
        for got in gots:
            column = 0
            for width, terms in self.parts:
                terms.append((got, column))
                column += width
            if self.vectors:
                self.vectors.append((got, column, self.rows))
        self.pending = gots
        self.done += self.bits
        self.messages = None

    def take(self, results):
        if self.vectors:
            self.vectors = [(results.pop(0), 0, VECTOR_ROWS)]
        kept, column, parts = results.pop(0), 0, []
        for width, _ in self.parts:
            parts.append((width, [(kept, column)]))
            column += width
        self.parts = parts
        self.messages = [results.pop(0) for _ in range((1 << self.bits) - 1)]

    def replace(self, old, new):
        for index, (width, terms) in enumerate(self.parts):
            self.parts[index] = (
                width,
                [(new if array is old else array, at) for array, at in terms],
            )
        self.vectors = [(new if a is old else a, at, rows) for a, at, rows in self.vectors]


def merged(chains):
    chain = Chain(
        [part for chain in chains for part in chain.parts],
        chains[0].rows,
        [term for chain in chains for term in chain.vectors],
    )
    chain.done = chains[0].done
    chain.pending = []
    return chain


class Operands:
    def __init__(self):
        self.arrays = []

    def of(self, array):
        for index, held in enumerate(self.arrays):
            if held is array:
                return index
        self.arrays.append(array)
        return len(self.arrays) - 1

    def in_specs(self):
        return [whole(array.shape) for array in self.arrays]


def prepare(requests):
    operands, plans, outs = Operands(), [], []
    plain = any(chain.rows % (8 << bits) for chain, bits in requests)
    for chain, bits in requests:
        chain.bits = bits
        chain.rows >>= bits
        rows, pieces = chain.rows, 1 << bits
        width = sum(width for width, _ in chain.parts)
        if plain:
            results = [
                jnp.concatenate(
                    [
                        total(
                            [
                                array[piece * rows : (piece + 1) * rows, at : at + width]
                                for array, at in terms
                            ]
                        )
                        for width, terms in chain.parts
                    ],
                    axis=1,
                )
                for piece in range(pieces)
            ]
            if chain.vectors:
                packed = summed_vectors(lambda array: array, chain.vectors)
                folded = fold_vectors(packed, rows)
                results = [packed, results[0]] + [
                    jnp.concatenate([result, folded], axis=1) for result in results[1:]
                ]
            chain.take([result.astype(bf16) for result in results])
            continue
        parts = [
            (width, [(operands.of(array), at) for array, at in terms])
            for width, terms in chain.parts
        ]
        vectors = [(operands.of(array), at, held) for array, at, held in chain.vectors]
        plans.append((rows, pieces, parts, vectors))
        if vectors:
            outs.append(((VECTOR_ROWS, TILE), f32))
        outs.append(((rows, width), bf16))
        wide = width + (vector_width(rows) if vectors else 0)
        outs += [((rows, wide), bf16)] * (pieces - 1)
    if plain:
        return
    results = pl.pallas_call(
        functools.partial(combine_kernel, plans),
        grid=(1,),
        out_shape=[jax.ShapeDtypeStruct(shape, kind) for shape, kind in outs],
        in_specs=operands.in_specs(),
        out_specs=[whole(shape) for shape, _ in outs],
        compiler_params=params(COMBINE_BYTES),
        cost_estimate=cost(1_000_000_000, 8_000_000),
        name="combine",
    )(*operands.arrays)
    results = list(results)
    for chain, bits in requests:
        chain.take(results)


def launch(requests, value, waits=()):
    chains = [chain for chain, bits in requests if bits is not None] + list(waits)
    olds = [got for chain in chains for got in chain.pending]
    if olds:
        value, news = lax.optimization_barrier((value, olds))
        for chain in chains + [chain for chain, _ in requests]:
            for old, new in zip(olds, news):
                chain.replace(old, new)
        for chain in chains:
            chain.pending = []
    sums = [(chain, bits) for chain, bits in requests if bits is not None]
    if sums:
        prepare(sums)
    messages = [chain.messages for chain, _ in requests]
    value, messages = lax.optimization_barrier((value, messages))
    for (chain, bits), message in zip(requests, messages):
        chain.messages = message
        if bits is None:
            chain.bits = 0
        chain.send()
    return value


def finish(size, groups, chain):
    share = D // (size * groups)
    up_rows = FF // D
    pieces = []
    for quad, (width, terms) in enumerate(chain.parts):
        for index in range(4):
            pieces.append((index, quad * QUAD, QUAD, [(a, at + index * QUAD) for a, at in terms]))
        if width > 4 * QUAD:
            pieces.append((4, 0, D, [(a, at + 4 * QUAD) for a, at in terms]))
    if share % 8:
        blocks = {}
        for target, at, width, terms in pieces:
            blocks.setdefault(target, []).append(
                total([array[:share, c : c + width] for array, c in terms])
            )
        weights = [jnp.concatenate(blocks[target], axis=1) for target in range(5)]
        vectors = unpack_vectors(summed_vectors(lambda array: array, chain.vectors))
        place = lax.axis_index("dp") * groups + lax.axis_index("tensor")
        mine = lax.dynamic_slice_in_dim(vectors, place * share, share, 1)
        ups = lax.dynamic_slice_in_dim(
            vectors[5 : 5 + up_rows].reshape(-1), place * up_rows * share, up_rows * share, 0
        )
        late = 5 + up_rows
        return weights, [mine[r] for r in (0, 1, 2, 3, 4, late, late + 1, late + 2)], mine[
            late + 3 : late + 5
        ].T, ups
    operands = Operands()
    plan = [
        (target, at, width, [(operands.of(array), c) for array, c in terms])
        for target, at, width, terms in pieces
    ]
    vectors = [(operands.of(array), at, held) for array, at, held in chain.vectors]
    outs = [(share, D)] * 5 + [(share,)] * 8 + [(2, share), (up_rows * share,)]
    found = pl.pallas_call(
        functools.partial(
            finish_kernel, size, groups, len(operands.arrays), (plan, vectors), up_rows
        ),
        grid=(1,),
        out_shape=[jax.ShapeDtypeStruct(shape, f32) for shape in outs],
        in_specs=operands.in_specs(),
        out_specs=[whole(shape) for shape in outs],
        compiler_params=params(COMBINE_BYTES),
        name="finish",
    )(*operands.arrays)
    return found[:5], found[5:13], found[13].T, found[14]


def body(
    content_in,
    query_in,
    memory,
    content_cot,
    query_cot,
    query_weight,
    key_weight,
    value_weight,
    out_weight,
    rel_weight,
    content_bias,
    position_bias,
    segment_bias,
    segment_embed,
    attn_gain,
    attn_shift,
    up_weight,
    up_bias,
    down_weight,
    down_bias,
    ffn_gain,
    ffn_shift,
    lengths,
    memory_lengths,
    segment_ids,
    orders,
    targets,
):
    groups = lax.axis_size("tensor")
    size = lax.axis_size("dp")
    steps = size.bit_length() - 1
    half = LEN // groups
    hidden_cols = up_weight.shape[1]
    up_other, down_other = swap(up_weight), swap(down_weight)
    content, query = content_in[0], query_in[0]
    segment_rows = segment_embed.T
    saved = attention_forward(
        half,
        (lengths, memory_lengths, segment_ids, orders, targets),
        memory[0],
        content,
        query,
        (query_weight, key_weight, value_weight, rel_weight),
        (content_bias, position_bias, segment_bias),
        segment_rows,
    )
    (
        content_out,
        query_out,
        ffn_own,
        ffn_other,
        summed_grad,
        attended_grad,
        out_own,
        out_other,
        early_small,
        up_bias_part,
    ) = middle(
        half,
        size,
        groups,
        (
            saved[0],
            content,
            query,
            content_cot[0],
            query_cot[0],
            out_weight,
            up_weight,
            up_other,
            down_weight,
            down_other,
            up_bias,
            down_bias,
            attn_gain,
            attn_shift,
            ffn_gain,
            ffn_shift,
        ),
        hidden_cols,
    )
    ffn = Chain([(2 * hidden_cols, [(ffn_own, 0)])], D)
    ffn.messages = [ffn_other]
    held = launch([(ffn, None)], attended_grad)
    content_late, held = lax.optimization_barrier((content, held))
    turned = transposed_rows(half, size, groups, memory[0], content_late, query, saved[11])
    turned, held = lax.optimization_barrier((turned, held))
    saved = (*saved, *turned)
    proj, tok_keys, tok_vals, small, late = [], [], [], [], []

    def backward(at, mode, grad, extra):
        own, other, proj_part, key_part, val_part, small_part, *vectors = attention_backward(
            half, groups, at, mode, saved, grad, segment_rows, extra
        )
        proj.append(proj_part)
        tok_keys.append(key_part)
        tok_vals.append(val_part)
        small.append(small_part)
        chain = Chain(
            [(own.shape[1], [(own, 0)])],
            own.shape[0],
            [(array, 0, VECTOR_ROWS) for array in vectors],
        )
        chain.messages = [other]
        late.append(chain)

    held = launch([(ffn, 1)], held)
    backward(0, "first", held, (out_own, out_other))
    held, proj[0] = launch([(late[0], None)], (attended_grad, proj[0]))
    backward(1, "middle", held, ())
    held, proj[1] = launch(
        [(ffn, 1), (late[0], 1), (late[1], None)], (attended_grad, proj[1])
    )
    backward(2, "last", held, (early_small, up_bias_part, *small))
    xy = min(2, steps)
    tok_vals[2] = launch(
        [(late[2], None), (ffn, 1), (late[0], 1), (late[1], 1)], tok_vals[2]
    )
    tok_vals[2] = launch([(late[2], xy), (late[1], 1), (ffn, 1)], tok_vals[2], [late[0]])
    final = merged(late)
    tok_vals[2] = launch([(final, min(2, steps - final.done))], tok_vals[2], late)
    own_rows, query_grad, row_send = row_gradients(
        half, groups, summed_grad, proj, tok_keys, tok_vals, (query_weight, key_weight, value_weight)
    )
    row_got = swap(row_send)
    while final.done < steps:
        own_rows = launch([(final, min(2, steps - final.done))], own_rows)
    while ffn.done < steps:
        own_rows = launch([(ffn, min(2, steps - ffn.done))], own_rows)
    content_grad = own_rows + row_got.astype(f32)
    ffn_sum = total([array[: ffn.rows] for array, _ in ffn.parts[0][1]])
    up_grad, down_grad_own = ffn_sum[:, :hidden_cols], ffn_sum[:, hidden_cols:].T
    (content_grad, up_grad, down_grad_own), olds = lax.optimization_barrier(
        ((content_grad, up_grad, down_grad_own), final.pending)
    )
    for old, new in zip(final.pending, olds):
        final.replace(old, new)
    weights, vectors, segment_grad, up_bias_grad = finish(size, groups, final)
    return (
        content_out[None],
        query_out[None],
        content_grad[None],
        query_grad[None],
        weights[0],
        weights[1],
        weights[2],
        weights[4],
        weights[3],
        vectors[5],
        vectors[6],
        vectors[7],
        segment_grad,
        vectors[3],
        vectors[4],
        up_grad,
        up_bias_grad,
        down_grad_own,
        vectors[2],
        vectors[0],
        vectors[1],
    )


def solution(mesh):
    in_specs = (
        P("dp", None, None),
        P("dp", "tensor", None),
        P("dp", None, None),
        P("dp", "tensor", None),
        P("dp", "tensor", None),
        P(),
        P(),
        P(),
        P(),
        P(),
        P(),
        P(),
        P(),
        P(),
        P(),
        P(),
        P(None, "tensor"),
        P(),
        P("tensor", None),
        P(),
        P(),
        P(),
        P("dp"),
        P("dp"),
        P("dp", None),
        P("dp", None),
        P("dp", None),
    )
    out_specs = (
        P("dp", "tensor", None),
        P("dp", "tensor", None),
        P("dp", "tensor", None),
        P("dp", "tensor", None),
        P(("dp", "tensor"), None),
        P(("dp", "tensor"), None),
        P(("dp", "tensor"), None),
        P(("dp", "tensor"), None),
        P(("dp", "tensor"), None),
        P(("dp", "tensor")),
        P(("dp", "tensor")),
        P(("dp", "tensor")),
        P(("dp", "tensor"), None),
        P(("dp", "tensor")),
        P(("dp", "tensor")),
        P("dp", "tensor"),
        P(("dp", "tensor")),
        P("tensor", "dp"),
        P(("dp", "tensor")),
        P(("dp", "tensor")),
        P(("dp", "tensor")),
    )
    return jax.shard_map(body, mesh=mesh, in_specs=in_specs, out_specs=out_specs, check_vma=False)
```

```python
import functools

import jax
import jax.numpy as jnp
from jax import lax
from jax.experimental import pallas as pl
from jax.experimental.pallas import tpu as pltpu
from jax.sharding import PartitionSpec as P

D = 768
HEADS = 12
HEAD_DIM = 64
FF = 3072
LEN = 512
MEM = 384
KEYS = MEM + LEN
QUAD = 4 * HEAD_DIM
QUADS = D // QUAD
PAIR = 2 * HEAD_DIM
SCALE = HEAD_DIM ** (-0.5)
VMEM_BYTES = 61 * 1024 * 1024
COMBINE_BYTES = 28 * 1024 * 1024
BACKWARD_BYTES = 54 * 1024 * 1024
MIDDLE_BYTES = 61 * 1024 * 1024
FORWARD_BYTES = 62 * 1024 * 1024
BLOCK = 16
TILE = 128
WIDE = 256
VECTORS = 16

VECTOR_ROWS = VECTORS * D // TILE

f32 = jnp.float32
bf16 = jnp.bfloat16
precise = lax.Precision.HIGHEST


def mm(left, right):
    return lax.dot_general(left, right, (((1,), (0,)), ((), ())), preferred_element_type=f32)


def mm_nt(left, right):
    return lax.dot_general(left, right, (((1,), (1,)), ((), ())), preferred_element_type=f32)


def mm_tn(left, right):
    return lax.dot_general(left, right, (((0,), (0,)), ((), ())), preferred_element_type=f32)


def unit_matrix(size):
    row = lax.broadcasted_iota(jnp.int32, (size, size), 0)
    return jnp.where(row == lanes((size, size)), 1.0, 0.0).astype(bf16)


def turn(value):
    width = min(value.shape[1], WIDE)
    unit = unit_matrix(width)
    blocks = [mm_nt(unit, value[:, n : n + width]) for n in range(0, value.shape[1], width)]
    return blocks[0] if len(blocks) == 1 else jnp.concatenate(blocks, axis=0)


def split(value):
    high = value.astype(bf16)
    return high, (value - high.astype(f32)).astype(bf16)


def lanes(shape):
    return lax.broadcasted_iota(jnp.int32, shape, 1)


def column_of(row):
    row = row.astype(f32)
    even = 2.0 * jnp.floor(0.5 * row)
    parts = jnp.concatenate([even, row - even, jnp.zeros((14, row.shape[1]), f32)], axis=0)
    return mm_tn(parts.astype(bf16), jnp.ones((16, TILE), bf16))


def lane_tiles(value, combine):
    tiles = [value[:, at : at + TILE] for at in range(0, value.shape[1], TILE)]
    return functools.reduce(combine, tiles)


def interleave(steps, tasks):
    done = 0
    for index, step in enumerate(steps):
        step()
        while done * len(steps) < (index + 1) * len(tasks) and done < len(tasks):
            tasks[done]()
            done += 1
    for task in tasks[done:]:
        task()


def order_of(core, bits):
    order = list(range(bits))
    if core == 1:
        for at in range(0, bits - 1, 2):
            order[at], order[at + 1] = order[at + 1], order[at]
    return order


def block_owner(place, core, bits):
    owners = []
    for each in range(2):
        owner = place * 0
        for step, bit in enumerate(order_of(each, bits)):
            owner = owner | (((place >> (bits - 1 - step)) & 1) << bit)
        owners.append(owner)
    return jnp.where(core == 1, owners[1], owners[0]) ^ lax.axis_index("dp")


def one_hot(source):
    return jnp.where(lanes((source.shape[0], D)) == source, 1.0, 0.0).astype(bf16)


def owner_rows(size, groups):
    share = D // (size * groups)
    row = lax.broadcasted_iota(jnp.int32, (D, 1), 0)
    side, rest = lax.div(row, size * share), lax.rem(row, size * share)
    core = lax.rem(lax.axis_index("tensor") + side, groups)
    owner = block_owner(lax.div(rest, share), core, size.bit_length() - 1)
    return one_hot((owner * groups + core) * share + lax.rem(rest, share))


def shared_rows(size, core):
    share = D // size
    row = lax.broadcasted_iota(jnp.int32, (D, 1), 0)
    owner = block_owner(lax.div(row, share), core, size.bit_length() - 1)
    return one_hot(owner * share + lax.rem(row, share))


def transpose_by_owner(out_ref, value, work, size, groups):
    share = D // (size * groups)
    if share % 8 or (2 * share) % 16:
        out_ref[...] = mm_nt(owner_rows(size, groups), value).astype(bf16)
        return
    width = value.shape[0]
    for n in range(0, D, WIDE):
        work[n : n + WIDE, :width] = turn(value[:, n : n + WIDE])
    bits = size.bit_length() - 1
    blocks = []
    for block in range(size * groups):
        core = lax.rem(lax.axis_index("tensor") + block // size, groups)
        owner = block_owner(jnp.int32(block % size), core, bits)
        at = pl.multiple_of((owner * groups + core) * share, 8)
        blocks.append(work[pl.ds(at, share), :width])
        if block % 2:
            out_ref[(block - 1) * share : (block + 1) * share, :] = jnp.concatenate(
                blocks, axis=0
            ).astype(bf16)
            blocks = []


def transpose_by_dp(out_ref, value, work, size):
    share = D // size
    core = lax.axis_index("tensor")
    if share % 16:
        out_ref[...] = mm_nt(shared_rows(size, core), value).astype(bf16)
        return
    for n in range(0, D, WIDE):
        work[n : n + WIDE, :] = turn(value[:, n : n + WIDE]).astype(bf16)
    for block in range(size):
        owner = block_owner(jnp.int32(block), core, size.bit_length() - 1)
        at = pl.multiple_of(owner * share, 16)
        out_ref[block * share : (block + 1) * share, :] = work[pl.ds(at, share), :]


def forward_kernel(
    half,
    length_ref,
    mem_length_ref,
    seg_ref,
    ord_ref,
    tgt_ref,
    memory_ref,
    content_ref,
    query_ref,
    wq_ref,
    wk_ref,
    wv_ref,
    wr_ref,
    cb_ref,
    pb_ref,
    sb_ref,
    se_ref,
    att_ref,
    prob_ref,
    key_ref,
    val_ref,
    rel_ref,
    hc_ref,
    hp_ref,
    hs_ref,
    linv_ref,
    kaug_ref,
    srow_ref,
    pos_ref,
    stack,
    both,
    pos,
    bias,
    fine,
    coarse,
    vectors,
    scores,
    places,
    kaug_t,
    scol,
    seg_row,
    kaug_work,
    order_work,
    seg_work,
):
    window = KEYS + half
    first = pl.multiple_of(lax.axis_index("tensor") * half, half)
    step_id = pl.program_id(0)

    @pl.when(step_id == 0)
    def _():
        stack[:MEM, :] = memory_ref[...]
        stack[MEM:, :] = content_ref[...]
        both[:half, :] = content_ref[pl.ds(first, half), :]
        both[half:, :] = query_ref[...]
        vectors[0:1, :] = cb_ref[...][None, :]
        vectors[1:2, :] = pb_ref[...][None, :]
        vectors[2:3, :] = sb_ref[...][None, :]
        step = lax.broadcasted_iota(jnp.int32, (1, D // 2), 1).astype(f32) * (2.0 / D)
        inverse = 1.0 / jnp.power(jnp.full((1, D // 2), 10000.0, f32), step)
        coarse_rows = coarse.shape[1]
        top = (MEM + half + first).astype(f32)
        angle = (
            top - 32.0 * lax.broadcasted_iota(jnp.int32, (coarse_rows, 1), 0).astype(f32)
        ) * inverse
        coarse[0] = jnp.sin(angle)
        coarse[1] = jnp.cos(angle)
        small = lax.broadcasted_iota(jnp.int32, (32, 1), 0).astype(f32) * inverse
        fine[0] = jnp.sin(small)
        fine[1] = jnp.cos(small)
        for a in range(window // 32):
            sa, ca = coarse[0, a : a + 1, :], coarse[1, a : a + 1, :]
            sb, cb = fine[0], fine[1]
            pos[a * 32 : (a + 1) * 32, : D // 2] = (sa * cb - ca * sb).astype(bf16)
            pos[a * 32 : (a + 1) * 32, D // 2 :] = (ca * cb + sa * sb).astype(bf16)
        never = float(LEN + 1)
        mem_at = lax.broadcasted_iota(jnp.int32, (1, MEM), 1)
        tok_at = lax.broadcasted_iota(jnp.int32, (1, LEN), 1)
        open_from = jnp.concatenate(
            [
                jnp.where(mem_at >= MEM - mem_length_ref[0], -1.0, never),
                jnp.where(
                    tok_at < length_ref[0],
                    jnp.where(tgt_ref[...] == 0, -1.0, ord_ref[...].astype(f32)),
                    never,
                ),
            ],
            axis=1,
        )
        order_col = column_of(ord_ref[...])
        seg_col = column_of(seg_ref[...])
        kaug_lane = lanes((LEN, PAIR)) % HEAD_DIM
        kaug_work[:MEM, :] = (lanes((MEM, PAIR)) % HEAD_DIM < 4).astype(f32).astype(bf16)
        kaug_work[MEM:, :] = jnp.where(
            kaug_lane < 4, 1.0, jnp.where(kaug_lane < 6, seg_col, 0.0)
        ).astype(bf16)
        kaug_t[...] = kaug_work[...].T[:HEAD_DIM]
        kaug_ref[...] = kaug_t[:16, :]
        order_work[...] = order_col
        own_order = order_work[pl.ds(first, half), :][:, :1]
        seg_work[...] = seg_col
        scol[...] = seg_work[pl.ds(first, half), :]
        seen = open_from <= own_order
        bias[:half, :] = jnp.where(seen, 0.0, -1e30)
        key_at = lax.broadcasted_iota(jnp.int32, (half, KEYS), 1)
        row_at = lax.broadcasted_iota(jnp.int32, (half, KEYS), 0)
        seen_q = seen & (key_at - MEM != row_at + first)
        bias[half:, :] = jnp.where(seen_q, 0.0, -1e30)
        seg_row[0:1, :] = seg_ref[...].astype(f32)
        srow_ref[...] = jnp.broadcast_to(seg_row[0:1, pl.ds(first, half)], srow_ref.shape)
        pos_ref[...] = pos[...]

    here = pl.ds(pl.multiple_of(step_id * QUAD, QUAD), QUAD)
    keys = mm(stack[...], wk_ref[...]).astype(bf16)
    values = mm(stack[...], wv_ref[...]).astype(bf16)
    rel = mm(pos[...], wr_ref[...]).astype(bf16)
    projection = mm(both[...], wq_ref[...])
    head_content = (projection + vectors[0:1, here]).astype(bf16)
    head_position = (projection + vectors[1:2, here]).astype(bf16)
    head_segment = projection + vectors[2:3, here]
    keys_t, values_t, rel_t = [turn(value).astype(bf16) for value in (keys, values, rel)]
    key_ref[...] = keys_t
    val_ref[...] = values_t
    rel_ref[...] = rel_t
    hs_ref[...] = head_segment
    head_content = (head_content.astype(f32) * SCALE).astype(bf16)
    head_position = (head_position.astype(f32) * SCALE).astype(bf16)
    hc_ref[...] = turn(head_content).astype(bf16)
    hp_ref[...] = turn(head_position).astype(bf16)
    row_head = lax.broadcasted_iota(jnp.int32, (QUAD, QUAD), 0) // HEAD_DIM
    at = lanes((QUAD, QUAD)) - ((row_head // 2) * PAIR + (1 - row_head % 2) * HEAD_DIM)
    place_same = jnp.where((at >= 0) & (at < 2), 1.0, 0.0).astype(bf16)
    place_step = jnp.where((at >= 2) & (at < 6), 1.0, 0.0).astype(bf16)
    same, other = se_ref[0:1, :], se_ref[1:2, :]
    terms = functools.reduce(
        jnp.add,
        [mm(part, place_same) for part in split(head_segment * same)]
        + [mm(part, place_step) for part in split(head_segment * (other - same))],
    )
    marks = jnp.concatenate([scol[...], scol[...]], axis=0)
    marks = jnp.concatenate([marks, marks], axis=1)
    lane6 = lanes((2 * half, QUAD)) % HEAD_DIM
    factor = jnp.where(lane6 < 2, 1.0, jnp.where(lane6 < 4, marks, 1.0 - 2.0 * marks))
    terms = SCALE * (terms * factor)
    high = terms.astype(bf16)
    low = (terms - high.astype(f32)).astype(bf16)
    qaug = jnp.where(lane6 % 2 == 0, high, low)
    key_x = []
    for which in range(4):
        own = keys_t[which * HEAD_DIM : (which + 1) * HEAD_DIM]
        sides = [own, kaug_t[...]] if which % 2 == 0 else [kaug_t[...], own]
        key_x.append(jnp.concatenate(sides, axis=0))
    peaks, totals, outs = {}, {}, {}
    row_first = lanes((2 * half, PAIR)) < HEAD_DIM

    def products(which):
        cols = slice(which // 2 * PAIR, (which // 2 + 1) * PAIR)
        slot = which % 2
        row_mine = row_first == (which % 2 == 0)
        query_x = jnp.where(row_mine, head_content[:, cols], qaug[:, cols])
        place_x = jnp.where(row_mine, head_position[:, cols], jnp.zeros((), bf16))

        def score(n, stop):
            scores[slot, :, n:stop] = mm(query_x, key_x[which][:, n:stop])

        def placed(n, stop):
            places[slot, :, n:stop] = mm(place_x, rel_t[cols, n:stop])

        return [functools.partial(placed, n, min(n + WIDE, window)) for n in range(0, window, WIDE)] + [
            functools.partial(score, n, min(n + WIDE, KEYS)) for n in range(0, KEYS, WIDE)
        ]

    def softmax(which):
        slot = which % 2
        tops, pieces = [], []

        def join(b):
            block = slice(b, b + BLOCK)
            shifted = pltpu.roll(
                places[slot, block, :], (KEYS + b % half) % window, 1, stride=1, stride_axis=0
            )[:, :KEYS]
            score = scores[slot, block, :] + shifted + bias[block, :]
            scores[slot, block, :] = score
            tops.append(lane_tiles(score, jnp.maximum))

        def peak():
            peaks[which] = jnp.max(jnp.concatenate(tops, axis=0), axis=1, keepdims=True)

        def power(b):
            block = slice(b, b + BLOCK)
            prob = jnp.exp(scores[slot, block, :] - peaks[which][block])
            pieces.append(lane_tiles(prob, jnp.add))
            prob_ref[which, block, :] = prob.astype(bf16)

        def finish():
            totals[which] = 1.0 / jnp.sum(
                jnp.concatenate(pieces, axis=0), axis=1, keepdims=True
            )

        blocks = range(0, 2 * half, BLOCK)
        return (
            [functools.partial(join, b) for b in blocks]
            + [peak]
            + [functools.partial(power, b) for b in blocks]
            + [finish]
        )

    def mixture(which, part):
        outs[which, part] = mm_nt(
            values_t[which * HEAD_DIM : (which + 1) * HEAD_DIM],
            prob_ref[which, part * half : (part + 1) * half, :],
        )

    interleave([], products(0))
    for which in range(4):
        tasks = products(which + 1) if which < 3 else []
        if which:
            tasks += [functools.partial(mixture, which - 1, part) for part in range(2)]
        interleave(softmax(which), tasks)
    for part in range(2):
        mixture(3, part)
    sums = [totals[which] for which in range(4)]
    mixed = jnp.concatenate(
        [jnp.concatenate([outs[which, 0], outs[which, 1]], axis=1) for which in range(4)], axis=0
    )
    mixed = functools.reduce(jnp.add, [turn(part) for part in split(mixed)])
    mine = lanes((2 * half, PAIR)) < HEAD_DIM
    for pair in range(2):
        cols = slice(pair * PAIR, (pair + 1) * PAIR)
        att_ref[:, cols] = mixed[:, cols] * jnp.where(mine, sums[2 * pair], sums[2 * pair + 1])
    lane = lanes((2 * half, TILE))
    linv_ref[...] = jnp.where(
        lane == 0, sums[0], jnp.where(lane == 1, sums[1], jnp.where(lane == 2, sums[2], sums[3]))
    )


def norm_forward(summed, gain, shift):
    center = summed - jnp.mean(summed, axis=1, keepdims=True)
    inv = lax.rsqrt(jnp.mean(center * center, axis=1, keepdims=True) + 1e-06)
    unit = center * inv
    return unit, inv, unit * gain + shift


def norm_backward(grad, unit, inv, gain):
    scaled = grad * gain
    return inv * (
        scaled
        - jnp.mean(scaled, axis=1, keepdims=True)
        - unit * jnp.mean(scaled * unit, axis=1, keepdims=True)
    )


def row_sum(value):
    return jnp.sum(value, axis=0, keepdims=True)


def gelu_parts(x):
    square = x * x
    tanh = jnp.tanh((0.7978845608028654 * x) * (1.0 + 0.044715 * square))
    rise = 0.5 * (1.0 + tanh)
    grad = rise + (0.5 * x) * (1.0 - tanh * tanh) * (
        0.7978845608028654 * (1.0 + 0.134145 * square)
    )
    return x * rise, grad


def fold_rows(value):
    return functools.reduce(jnp.add, [value[r : r + 8] for r in range(0, value.shape[0], 8)])


def middle_kernel(
    half,
    size,
    groups,
    chunk,
    att_ref,
    content_ref,
    query_ref,
    ccot_ref,
    qcot_ref,
    wo_ref,
    up_own_hbm,
    up_oth_hbm,
    down_own_hbm,
    down_oth_hbm,
    ubias_ref,
    dbias_ref,
    again_ref,
    ashift_ref,
    fgain_ref,
    fshift_ref,
    cout_ref,
    qout_ref,
    ffn_own_ref,
    ffn_oth_ref,
    sgrad_ref,
    agrad_ref,
    small_ref,
    ubg_ref,
    hidden,
    slope,
    pre,
    work,
    unit,
    low,
    down_grad,
    vectors,
    up,
    down,
    low_t,
    down_t,
    turn_low,
    turn_down,
    attended_t,
    turn_work,
    sems,
):
    count = 2 * half
    member = lax.axis_index("tensor")
    first = pl.multiple_of(member * half, half)
    fetches = [
        pltpu.make_async_copy(source, target.at[side], sems.at[kind, side])
        for kind, side, source, target in (
            (0, 0, up_own_hbm, up),
            (1, 0, down_own_hbm, down),
            (0, 1, up_oth_hbm, up),
            (1, 1, down_oth_hbm, down),
        )
    ]
    for fetch in fetches:
        fetch.start()
    ups, downs = (up.at[0], up.at[1]), (down.at[0], down.at[1])
    part_cols = up.shape[2]
    chunks = part_cols // chunk
    vectors[0:1, :] = ubias_ref[...][None, :]
    attended = att_ref[...].astype(bf16)
    work[...] = mm(attended, wo_ref[...])
    attn_gain, attn_shift = again_ref[...][None, :], ashift_ref[...][None, :]
    ffn_gain, ffn_shift = fgain_ref[...][None, :], fshift_ref[...][None, :]
    down_bias = dbias_ref[...][None, :]
    inverse = []
    for b in range(0, count, BLOCK):
        block = slice(b, b + BLOCK)
        if b < half:
            rows_in = content_ref[pl.ds(pl.multiple_of(first + b, BLOCK), BLOCK), :]
        else:
            rows_in = query_ref[b - half : b - half + BLOCK, :]
        found, inv, normed = norm_forward(
            work[block, :] + rows_in.astype(f32), attn_gain, attn_shift
        )
        unit[block, :] = found
        inverse.append(inv)
        low[block, :] = normed.astype(bf16)
        work[block, :] = normed + down_bias
    for fetch in fetches:
        fetch.wait()
    pieces = [(side, at) for side in range(2) for at in range(chunks)]

    def rise(index):
        side, at = pieces[index]

        def task(n):
            pre[index % 2, :, n : n + WIDE] = mm(
                low[...], ups[side][:, at * chunk + n : at * chunk + n + WIDE]
            )

        return [functools.partial(task, n) for n in range(0, chunk, WIDE)]

    def bend(index):
        side, at = pieces[index]
        cols = slice(at * chunk, (at + 1) * chunk)
        start = lax.rem(member + side, 2) * part_cols + at * chunk
        bias = vectors[0:1, pl.ds(pl.multiple_of(start, TILE), chunk)]

        def step(b):
            block = slice(b, b + BLOCK)
            act, grad = gelu_parts(pre[index % 2, block, :] + bias)
            hidden[side, block, cols] = act.astype(bf16)
            slope[side, block, cols] = grad.astype(bf16)

        return [functools.partial(step, b) for b in range(0, count, BLOCK)]

    def fall(index):
        side, at = pieces[index]
        cols = slice(at * chunk, (at + 1) * chunk)

        def task(n):
            work[:, n : n + WIDE] += mm(hidden[side, :, cols], downs[side][cols, n : n + WIDE])

        return [functools.partial(task, n) for n in range(0, D, WIDE)]

    interleave([], rise(0))
    for index in range(len(pieces)):
        tasks = rise(index + 1) if index + 1 < len(pieces) else []
        if index:
            tasks += fall(index - 1)
        interleave(bend(index), tasks)
    interleave([], fall(len(pieces) - 1))
    sums = [jnp.zeros((8, D), f32) for _ in range(5)]
    for b in range(0, count, BLOCK):
        block = slice(b, b + BLOCK)
        found, inv, out = norm_forward(work[block, :], ffn_gain, ffn_shift)
        if b < half:
            cout_ref[block, :] = out.astype(bf16)
            cot = ccot_ref[block, :].astype(f32)
        else:
            block_q = slice(b - half, b - half + BLOCK)
            qout_ref[block_q, :] = out.astype(bf16)
            cot = qcot_ref[block_q, :].astype(f32)
        residual_grad = norm_backward(cot, found, inv, ffn_gain)
        rounded = residual_grad.astype(bf16)
        down_grad[block, :] = rounded
        work[block, :] = residual_grad
        for index, value in enumerate((cot * found, cot, rounded.astype(f32))):
            sums[index] = sums[index] + fold_rows(value)
    transpose_by_dp(low_t, low[...], turn_low, size)
    transpose_by_dp(down_t, down_grad[...], turn_down, size)
    for side in range(2):
        for at in range(chunks):
            cols = slice(at * chunk, (at + 1) * chunk)
            hidden_grad = mm_nt(down_grad[...], downs[side][cols, :])
            pre_grad = (hidden_grad * slope[side, :, cols].astype(f32)).astype(bf16)
            slope[side, :, cols] = pre_grad
            ubg_ref[side : side + 1, cols] = row_sum(pre_grad.astype(f32))
            work[...] += mm_nt(pre_grad, ups[side][:, cols])

    def settle(b):
        block = slice(b, b + BLOCK)
        grad, found = work[block, :], unit[block, :]
        summed_grad = norm_backward(grad, found, inverse[b // BLOCK], attn_gain)
        sgrad_ref[block, :] = summed_grad
        down_grad[block, :] = summed_grad.astype(bf16)
        sums[3] = sums[3] + fold_rows(grad * found)
        sums[4] = sums[4] + fold_rows(grad)

    share = D // size
    bits = size.bit_length() - 1

    def other_place(place):
        found = 0
        for step in range(bits):
            there = order_of(1, bits)[step]
            found |= ((place >> (bits - 1 - there)) & 1) << (bits - 1 - step)
        return found

    def weigh(side, kind, n):
        left, right = ((low_t, slope), (down_t, hidden))[kind]
        value = mm(left[...], right[side, :, n : n + WIDE]).astype(bf16)
        target = (ffn_own_ref, ffn_oth_ref)[side]
        cols = slice(kind * part_cols + n, kind * part_cols + n + WIDE)
        if side == 0:
            target[:, cols] = value
            return
        for place in range(size):
            to = other_place(place)
            target[to * share : (to + 1) * share, cols] = value[
                place * share : (place + 1) * share
            ]

    tasks = [
        functools.partial(weigh, side, kind, n)
        for side in (1, 0)
        for kind in range(2)
        for n in range(0, part_cols, WIDE)
    ]
    interleave([functools.partial(settle, b) for b in range(0, count, BLOCK)], tasks)
    for index, value in enumerate(sums):
        small_ref[index : index + 1, :] = row_sum(value)
    small_ref[5:8, :] = jnp.zeros((3, D), f32)
    agrad_ref[...] = mm_nt(down_grad[...], wo_ref[...]).astype(bf16)
    part_rows, part_width = share // groups, D // groups
    cols = slice(2 * part_cols, 2 * part_cols + part_width)
    targets = (ffn_own_ref, ffn_oth_ref)
    if part_rows % 8 == 0:
        transpose_by_owner(attended_t, attended, turn_work, size, groups)
        out_part = mm(attended_t[...], down_grad[...])
        for side in range(2):
            for place in range(size):
                at = side * size * part_rows + place * part_rows
                rows = out_part[at : at + part_rows]
                targets[side][place * share : (place + 1) * share, cols] = jnp.concatenate(
                    [rows[:, n : n + part_width] for n in range(0, D, part_width)], axis=0
                ).astype(bf16)
    else:
        row = lax.broadcasted_iota(jnp.int32, (D, 1), 0)
        inner = lax.rem(row, share)
        for side in range(2):
            core = lax.rem(member + side, groups)
            owner = block_owner(lax.div(row, share), core, bits)
            source = (owner * groups + core) * part_rows + lax.rem(inner, part_rows)
            left = mm_nt(one_hot(source), attended).astype(bf16)
            value = jnp.zeros((D, part_width), f32)
            for part in range(groups):
                columns_at = slice(part * part_width, (part + 1) * part_width)
                product = mm(left, down_grad[:, columns_at])
                value = jnp.where(lax.div(inner, part_rows) == part, product, value)
            targets[side][:, cols] = value.astype(bf16)


def unshift(value, shift, window):
    whole, rest = shift // TILE, shift % TILE
    row = lax.broadcasted_iota(jnp.int32, (BLOCK, TILE), 0)
    lane = lanes((BLOCK, TILE))
    index = (lane + row - rest) & (TILE - 1)
    tiles = [
        jnp.take_along_axis(
            value[:, n : n + TILE], index, axis=1, mode="promise_in_bounds"
        )
        for n in range(0, value.shape[1], TILE)
    ]
    zero = jnp.zeros((BLOCK, TILE), f32)

    def tile(n):
        return tiles[n] if 0 <= n < len(tiles) else zero

    if rest:
        here = lane >= rest - row
        found = [
            jnp.where(here, tile(n - whole), tile(n - whole - 1)) for n in range(window // TILE)
        ]
    else:
        here = lane + row < TILE
        found = [
            jnp.where(here, tile(n - whole), tile(n - whole + 1)) for n in range(window // TILE)
        ]
    return jnp.concatenate(found, axis=1)


def backward_kernel(
    half,
    groups,
    at,
    mode,
    prob_hbm,
    key_ref,
    val_ref,
    rel_ref,
    hc_ref,
    hp_ref,
    hs_ref,
    linv_ref,
    kaug_ref,
    srow_ref,
    att_ref,
    agrad_ref,
    se_ref,
    both_t_hbm,
    stack_t_hbm,
    pos_t_hbm,
    *rest,
):
    more = rest[: 4 if mode == "last" else 0]
    own_ref, oth_ref, proj_ref, tok_key_ref, tok_val_ref, small_ref = rest[len(more) :][:6]
    prob, both_t, stack_t, pos_t, spread, grads, turned, sems = rest[-8:]
    count, window = 2 * half, KEYS + half
    heads = 4
    prob_copies = [
        pltpu.make_async_copy(prob_hbm.at[at * heads + h], prob.at[h], sems.at[h])
        for h in range(heads)
    ]
    fetches = [
        pltpu.make_async_copy(source, target, sems.at[heads + index])
        for index, (source, target) in enumerate(
            ((both_t_hbm, both_t), (stack_t_hbm, stack_t), (pos_t_hbm, pos_t))
        )
    ]
    for copy in prob_copies + fetches:
        copy.start()
    share = D // groups
    kaug_t = kaug_ref[...]
    filler = jnp.zeros((HEAD_DIM - kaug_t.shape[0], KEYS), bf16)
    marks = jnp.concatenate([srow_ref[0:1, :], srow_ref[0:1, :]], axis=1)
    swing = 1.0 - 2.0 * marks
    key_t, val_t, rel_t = [], [], []
    lane = lanes((count, PAIR))
    agrads, grad_x, agrad_t = [], [], []
    for pair in range(2):
        cols = slice(pair * PAIR, (pair + 1) * PAIR)
        linv = jnp.where(
            lane < HEAD_DIM,
            linv_ref[:, 2 * pair : 2 * pair + 1],
            linv_ref[:, 2 * pair + 1 : 2 * pair + 2],
        )
        agrad = (agrad_ref[:, cols].astype(f32) * linv).astype(bf16).astype(f32)
        products = agrad * att_ref[:, cols]
        agrad_t.append(turn(agrad.astype(bf16)).astype(bf16))
        for head in range(2):
            base = (1 - head) * HEAD_DIM
            mine = (lane < HEAD_DIM) == (head == 0)
            weight = jnp.sum(jnp.where(mine, products, 0.0), axis=1, keepdims=True)
            high = weight.astype(bf16).astype(f32)
            grad_x.append(
                jnp.where(
                    mine,
                    agrad,
                    jnp.where(
                        lane == base, -high, jnp.where(lane == base + 1, high - weight, 0.0)
                    ),
                ).astype(bf16)
            )
    found = {}

    def head_of(ref, which):
        return ref[which * HEAD_DIM : (which + 1) * HEAD_DIM, :]

    def spreads(which):
        own = head_of(val_ref, which)
        sides = [own, kaug_t, filler] if which % 2 == 0 else [kaug_t, filler, own]
        val_x = jnp.concatenate(sides, axis=0)
        prob_copies[which].wait()

        def task(n, stop):
            spread[which % 2, :, n:stop] = mm(grad_x[which], val_x[:, n:stop])

        return [functools.partial(task, n, min(n + WIDE, KEYS)) for n in range(0, KEYS, WIDE)]

    def score_grads(which):
        buffer = which % 2

        def step(part, b):
            at_row = part * half + b
            block = slice(at_row, at_row + BLOCK)
            score_grad = prob[which, block, :].astype(f32) * spread[buffer, block, :]
            grads[buffer, block, :] = score_grad.astype(bf16)
            turned[buffer, block, :] = unshift(score_grad, half - b, window).astype(bf16)

        return [
            functools.partial(step, part, b) for part in range(2) for b in range(0, half, BLOCK)
        ]

    def gathers(which):
        buffer = which % 2
        side = slice(which % 2 * HEAD_DIM, (which % 2 + 1) * HEAD_DIM)
        key_x = jnp.concatenate([head_of(key_ref, which), kaug_t], axis=0)
        found[which] = {"value": [], "key": [], "rel": [], "content": [], "place": []}

        def down_rows(name, left, ref, n, stop):
            found[which][name].append(mm(left, ref[:, n:stop]))

        tasks = []
        for name, left, ref, end in (
            ("value", agrad_t[which // 2][side], prob.at[which], KEYS),
            ("key", head_of(hc_ref, which), grads.at[buffer], KEYS),
            ("rel", head_of(hp_ref, which), turned.at[buffer], window),
        ):
            tasks += [
                functools.partial(down_rows, name, left, ref, n, min(n + WIDE, end))
                for n in range(0, end, WIDE)
            ]

        def content(n):
            found[which]["content"].append(mm_nt(key_x, grads[buffer, n : n + half, :]))

        def placed(n):
            found[which]["place"].append(
                mm_nt(head_of(rel_ref, which), turned[buffer, n : n + half, :])
            )

        for n in (0, half):
            tasks += [functools.partial(content, n), functools.partial(placed, n)]
        return tasks

    interleave([], spreads(0))
    for which in range(heads):
        tasks = spreads(which + 1) if which + 1 < heads else []
        if which:
            tasks += gathers(which - 1)
        interleave(score_grads(which), tasks)
    interleave([], gathers(heads - 1))
    for which in range(heads):
        val_t.append(jnp.concatenate(found[which]["value"], axis=1))
        key_t.append(jnp.concatenate(found[which]["key"], axis=1))
        rel_t.append(jnp.concatenate(found[which]["rel"], axis=1))
    same, other, contents, places = [], [], [], []
    for which in range(heads):
        content_head = jnp.concatenate(found[which]["content"], axis=1)
        total = content_head[HEAD_DIM : HEAD_DIM + 1]
        marked = content_head[HEAD_DIM + 4 : HEAD_DIM + 5]
        other.append(SCALE * (marks * total + swing * marked))
        same.append(SCALE * total - other[-1])
        contents.append((SCALE * content_head[:HEAD_DIM]).astype(bf16))
        places.append((SCALE * jnp.concatenate(found[which]["place"], axis=1)).astype(bf16))
    contents, places = jnp.concatenate(contents, axis=0), jnp.concatenate(places, axis=0)
    term_high, term_low = split(jnp.concatenate(same + other, axis=0))
    line = lax.broadcasted_iota(jnp.int32, (2 * heads, QUAD), 0)
    mine = line % heads == lanes((2 * heads, QUAD)) // HEAD_DIM
    embed = jnp.where(line < heads, se_ref[0:1, :], se_ref[1:2, :])
    embed_high, embed_low = split(jnp.where(mine, embed, 0.0))
    segment_grad = mm_tn(
        jnp.concatenate([embed_high, embed_high, embed_low, embed_low], axis=0),
        jnp.concatenate([term_high, term_low, term_high, term_low], axis=0),
    )
    proj_t = (contents.astype(f32) + places.astype(f32) + segment_grad).astype(bf16)
    ones = jnp.ones((16, count), bf16)
    small_ref[0:1, :] = mm_nt(ones, contents)[0:1]
    small_ref[1:2, :] = mm_nt(ones, places)[0:1]
    small_ref[2:3, :] = functools.reduce(
        jnp.add, [mm_nt(ones, part)[0:1] for part in split(segment_grad)]
    )
    terms = jnp.concatenate([term_high, term_low], axis=0)
    embed_grad = functools.reduce(jnp.add, [mm(terms, part) for part in split(hs_ref[...])])
    embed_grad = jnp.where(mine, embed_grad[: 2 * heads] + embed_grad[2 * heads :], 0.0)
    small_ref[3:4, :] = row_sum(embed_grad[:heads])
    small_ref[4:5, :] = row_sum(embed_grad[heads:])
    small_ref[5:8, :] = jnp.zeros((3, QUAD), f32)
    key_t = jnp.concatenate(key_t, axis=0).astype(bf16)
    val_t = jnp.concatenate(val_t, axis=0).astype(bf16)
    rel_t = jnp.concatenate(rel_t, axis=0).astype(bf16)
    proj_ref[...] = turn(proj_t).astype(bf16)
    tok_key_ref[...] = turn(key_t[:, MEM:]).astype(bf16)
    tok_val_ref[...] = turn(val_t[:, MEM:]).astype(bf16)
    for fetch in fetches:
        fetch.wait()
    parts = (
        mm_nt(both_t[...], proj_t),
        mm_nt(stack_t[...], key_t),
        mm_nt(stack_t[...], val_t),
        mm_nt(pos_t[...], rel_t),
    )
    for index, value in enumerate(parts):
        cols = slice(index * QUAD, (index + 1) * QUAD)
        own_ref[:, cols] = value[:share].astype(bf16)
        oth_ref[:, cols] = value[share : 2 * share].astype(bf16)
    if mode == "last":
        vec_ref = rest[len(more) + 6]
        early, ubias, before, between = more
        core = lax.axis_index("tensor")
        rows = [early[0:5, :]]
        mine = [ubias[0:1, n : n + D] for n in range(0, ubias.shape[1], D)]
        theirs = [ubias[1:2, n : n + D] for n in range(0, ubias.shape[1], D)]
        for left, right in ((mine, theirs), (theirs, mine)):
            rows += [jnp.where(core == 0, a, b) for a, b in zip(left, right)]
        rows.append(
            jnp.concatenate([before[0:5, :], between[0:5, :], small_ref[0:5, :]], axis=1)
        )
        rows = jnp.concatenate(rows, axis=0)
        spare = jnp.zeros((VECTORS - rows.shape[0], D), f32)
        rows = jnp.concatenate([rows, spare], axis=0)
        packed = jnp.concatenate([rows[:, n : n + TILE] for n in range(0, D, TILE)], axis=0)
        vec_ref[...] = packed
        oth_ref[:VECTOR_ROWS, 4 * QUAD :] = packed.astype(bf16)
        oth_ref[VECTOR_ROWS:, 4 * QUAD :] = jnp.zeros((share - VECTOR_ROWS, TILE), bf16)


def rows_kernel(half, groups, sgrad_ref, *rest):
    proj, keys, vals = rest[:QUADS], rest[QUADS : 2 * QUADS], rest[2 * QUADS : 3 * QUADS]
    wq_ref, wk_ref, wv_ref, own_ref, query_ref, send_ref, both = rest[3 * QUADS :]
    member = lax.axis_index("tensor")
    wide = [jnp.concatenate([ref[...] for ref in refs], axis=1) for refs in (proj, keys, vals)]
    both[...] = mm_nt(wide[1], wk_ref[...]) + mm_nt(wide[2], wv_ref[...])
    rows = sgrad_ref[...] + mm_nt(wide[0], wq_ref[...])
    own = pl.multiple_of(member * half, half)
    other = pl.multiple_of(lax.rem(member + 1, groups) * half, half)
    send_ref[...] = both[pl.ds(other, half), :].astype(bf16)
    own_ref[...] = rows[:half] + both[pl.ds(own, half), :]
    query_ref[...] = rows[half:]


def summed(operands, terms, first, rows, width):
    values = []
    for index, at in terms:
        if rows % 16 == 0:
            value = operands[index][first : first + rows, at : at + width].astype(f32)
        else:
            value = operands[index][:, at : at + width].astype(f32)[first : first + rows]
        values.append(value)
    return functools.reduce(jnp.add, values)


def vector_width(rows):
    return TILE * max(1, VECTOR_ROWS // rows)


def fold_vectors(packed, rows):
    if rows > VECTOR_ROWS:
        return jnp.concatenate([packed, jnp.zeros((rows - VECTOR_ROWS, TILE), f32)], axis=0)
    return jnp.concatenate(
        [packed[n : n + rows] for n in range(0, VECTOR_ROWS, rows)], axis=1
    )


def unfold_vectors(block, rows):
    if rows >= VECTOR_ROWS:
        return block[:VECTOR_ROWS]
    return jnp.concatenate(
        [block[:, n : n + TILE] for n in range(0, vector_width(rows), TILE)], axis=0
    )


def summed_vectors(values, terms):
    return functools.reduce(
        jnp.add,
        [
            unfold_vectors(
                values(index)[:rows, at : at + vector_width(rows)].astype(f32), rows
            )
            for index, at, rows in terms
        ],
    )


def combine_kernel(plans, *refs):
    count = sum(pieces + (1 if vectors else 0) for _, pieces, _, vectors in plans)
    operands, outs = refs[:-count], list(refs[-count:])
    for rows, pieces, parts, vectors in plans:
        if vectors:
            packed = summed_vectors(lambda index: operands[index][...].astype(f32), vectors)
            outs.pop(0)[...] = packed
        for piece in range(pieces):
            out_ref = outs.pop(0)
            column = 0
            for width, terms in parts:
                value = summed(operands, terms, piece * rows, rows, width)
                out_ref[:, column : column + width] = value.astype(out_ref.dtype)
                column += width
            if piece and vectors:
                out_ref[:, column:] = fold_vectors(packed, rows).astype(out_ref.dtype)


def unpack_vectors(packed):
    return jnp.concatenate(
        [packed[n : n + VECTORS] for n in range(0, VECTOR_ROWS, VECTORS)], axis=1
    )


def finish_kernel(size, groups, count, plan, up_rows, *refs):
    operands, outs = refs[:count], refs[count:]
    weights, vec_outs, embed_out, up_out = outs[:4], outs[4:-2], outs[-2], outs[-1]
    place = lax.axis_index("dp") * groups + lax.axis_index("tensor")
    share = D // (size * groups)
    for target, at, width, terms in plan[0]:
        weights[target][:, at : at + width] = summed(operands, terms, 0, share, width)
    value = unpack_vectors(
        summed_vectors(lambda index: operands[index][...].astype(f32), plan[1])
    )
    mine = pltpu.roll(value, lax.rem(D - place * share, D), 1)[:, :TILE]
    rows = [row for row in range(5 + up_rows + 3) if not 5 <= row < 5 + up_rows]
    for row, out_ref in zip(rows, vec_outs):
        out_ref[...] = mine[row, :share]
    embed = jnp.concatenate([mine[5 + up_rows + 3 : 5 + up_rows + 5], jnp.zeros((6, TILE), f32)], axis=0)
    embed_out[...] = embed[:2, :share]
    wide = up_rows * share
    each = D // wide
    line = lax.div(place, each)
    chosen = functools.reduce(
        jnp.add,
        [jnp.where(line == r, value[5 + r : 6 + r], 0.0) for r in range(up_rows)],
    )
    chosen = jnp.broadcast_to(chosen, (8, D))
    turned = pltpu.roll(chosen, lax.rem(D - lax.rem(place, each) * wide, D), 1)[:, :TILE]
    up_out[...] = turned[0, :wide]


def whole(shape):
    return pl.BlockSpec(shape, lambda i: (0,) * len(shape))


def columns(rows, width, at=None):
    if at is None:
        return pl.BlockSpec((rows, width), lambda i: (0, i))
    return pl.BlockSpec((rows, width), lambda i: (0, at))


def row_block(rows, width, at=None):
    if at is None:
        return pl.BlockSpec((rows, width), lambda i: (i, 0))
    return pl.BlockSpec((rows, width), lambda i: (at, 0))


def scalars():
    return pl.BlockSpec(memory_space=pltpu.SMEM)


def params(size=VMEM_BYTES):
    return pltpu.CompilerParams(vmem_limit_bytes=size)


def cost(flops, bytes_accessed):
    return pl.CostEstimate(flops=flops, bytes_accessed=bytes_accessed, transcendentals=0)


def in_hbm():
    return pl.BlockSpec(memory_space=pl.ANY)


def attention_forward(
    half, ints, memory, content, query, weights, biases, segment_rows
):
    count, window = 2 * half, KEYS + half
    coarse_rows = -(-(window // 32) // 8) * 8
    outs = (
        ((count, D), f32, columns(count, QUAD)),
        ((HEADS, count, KEYS), bf16, pl.BlockSpec((4, count, KEYS), lambda i: (i, 0, 0))),
        ((D, KEYS), bf16, row_block(QUAD, KEYS)),
        ((D, KEYS), bf16, row_block(QUAD, KEYS)),
        ((D, window), bf16, row_block(QUAD, window)),
        ((D, count), bf16, row_block(QUAD, count)),
        ((D, count), bf16, row_block(QUAD, count)),
        ((count, D), f32, columns(count, QUAD)),
        ((count, QUADS * TILE), f32, columns(count, TILE)),
        ((16, KEYS), bf16, whole((16, KEYS))),
        ((8, half), f32, whole((8, half))),
        ((window, D), bf16, whole((window, D))),
    )
    return pl.pallas_call(
        functools.partial(forward_kernel, half),
        grid=(QUADS,),
        out_shape=[jax.ShapeDtypeStruct(shape, kind) for shape, kind, _ in outs],
        in_specs=[
            scalars(),
            scalars(),
            whole((1, LEN)),
            whole((1, LEN)),
            whole((1, LEN)),
            whole((MEM, D)),
            whole((LEN, D)),
            whole((half, D)),
        ]
        + [columns(D, QUAD)] * 4
        + [whole((D,))] * 3
        + [columns(2, QUAD)],
        out_specs=[spec for _, _, spec in outs],
        scratch_shapes=[
            pltpu.VMEM((KEYS, D), bf16),
            pltpu.VMEM((count, D), bf16),
            pltpu.VMEM((window, D), bf16),
            pltpu.VMEM((count, KEYS), f32),
            pltpu.VMEM((2, 32, D // 2), f32),
            pltpu.VMEM((2, coarse_rows, D // 2), f32),
            pltpu.VMEM((8, D), f32),
            pltpu.VMEM((2, count, KEYS), f32),
            pltpu.VMEM((2, count, window), f32),
            pltpu.VMEM((HEAD_DIM, KEYS), bf16),
            pltpu.VMEM((half, PAIR), f32),
            pltpu.VMEM((8, LEN), f32),
            pltpu.VMEM((KEYS, PAIR), bf16),
            pltpu.VMEM((LEN, TILE), f32),
            pltpu.VMEM((LEN, TILE), f32),
        ],
        compiler_params=params(FORWARD_BYTES),
        cost_estimate=cost(30_000_000_000, 40_000_000),
        name="attention_forward",
    )(*ints, memory, content, query, *weights, *biases, segment_rows)


def middle(half, size, groups, arrays, hidden_cols):
    count = 2 * half
    chunk = min(hidden_cols, 768)
    outs = (
        ((half, D), bf16),
        ((half, D), bf16),
        ((D, 2 * hidden_cols + D // groups), bf16),
        ((D, 2 * hidden_cols + D // groups), bf16),
        ((count, D), f32),
        ((count, D), bf16),
        ((8, D), f32),
        ((2, hidden_cols), f32),
    )
    weights = (6, 7, 8, 9)
    return pl.pallas_call(
        functools.partial(middle_kernel, half, size, groups, chunk),
        grid=(1,),
        out_shape=[jax.ShapeDtypeStruct(shape, kind) for shape, kind in outs],
        in_specs=[
            in_hbm() if i in weights else whole(array.shape) for i, array in enumerate(arrays)
        ],
        out_specs=[whole(shape) for shape, _ in outs],
        scratch_shapes=[
            pltpu.VMEM((2, count, hidden_cols), bf16),
            pltpu.VMEM((2, count, hidden_cols), bf16),
            pltpu.VMEM((2, count, chunk), f32),
            pltpu.VMEM((count, D), f32),
            pltpu.VMEM((count, D), f32),
            pltpu.VMEM((count, D), bf16),
            pltpu.VMEM((count, D), bf16),
            pltpu.VMEM((8, FF), f32),
            pltpu.VMEM((2, D, hidden_cols), bf16),
            pltpu.VMEM((2, hidden_cols, D), bf16),
            pltpu.VMEM((D, count), bf16),
            pltpu.VMEM((D, count), bf16),
            pltpu.VMEM((D, count), bf16),
            pltpu.VMEM((D, count), bf16),
            pltpu.VMEM((D, count), bf16),
            pltpu.VMEM((D, count), f32),
            pltpu.SemaphoreType.DMA((2, 2)),
        ],
        compiler_params=params(MIDDLE_BYTES),
        cost_estimate=cost(30_000_000_000, 30_000_000),
        name="feed_forward",
    )(*arrays)


def prepare_kernel(
    half,
    size,
    groups,
    memory_ref,
    content_ref,
    query_ref,
    pos_ref,
    both_t_ref,
    stack_t_ref,
    pos_t_ref,
    both_work,
    stack_work,
    pos_work,
):
    first = pl.multiple_of(lax.axis_index("tensor") * half, half)
    both = jnp.concatenate([content_ref[pl.ds(first, half), :], query_ref[...]], axis=0)
    stack = jnp.concatenate([memory_ref[...], content_ref[...]], axis=0)
    transpose_by_owner(both_t_ref, both, both_work, size, groups)
    transpose_by_owner(stack_t_ref, stack, stack_work, size, groups)
    transpose_by_owner(pos_t_ref, pos_ref[...], pos_work, size, groups)


def transposed_rows(half, size, groups, memory, content, query, pos):
    count, window = 2 * half, KEYS + half
    arrays = (memory, content, query, pos)
    outs = ((D, count), (D, KEYS), (D, window))
    return pl.pallas_call(
        functools.partial(prepare_kernel, half, size, groups),
        grid=(1,),
        out_shape=[jax.ShapeDtypeStruct(shape, bf16) for shape in outs],
        in_specs=[whole(array.shape) for array in arrays],
        out_specs=[whole(shape) for shape in outs],
        scratch_shapes=[pltpu.VMEM(shape, f32) for shape in outs],
        compiler_params=params(BACKWARD_BYTES),
        cost_estimate=cost(6_000_000_000, 8_000_000),
        name="transposed_rows",
    )(*arrays)


def attention_backward(half, groups, at, mode, saved, agrad, segment_rows, extra):
    count, window, share = 2 * half, KEYS + half, D // groups
    att, prob, keys, values, rel, hc, hp, hs, linv, kaug, srow, _ = saved[:12]
    both_t, stack_t, pos_t = saved[12:]
    width = 4 * QUAD
    operands = (
        (prob, in_hbm()),
        (keys, row_block(QUAD, KEYS, at)),
        (values, row_block(QUAD, KEYS, at)),
        (rel, row_block(QUAD, window, at)),
        (hc, row_block(QUAD, count, at)),
        (hp, row_block(QUAD, count, at)),
        (hs, columns(count, QUAD, at)),
        (linv, columns(count, TILE, at)),
        (kaug, whole((16, KEYS))),
        (srow, whole((8, half))),
        (att, columns(count, QUAD, at)),
        (agrad, columns(count, QUAD, at)),
        (segment_rows, columns(2, QUAD, at)),
        (both_t, in_hbm()),
        (stack_t, in_hbm()),
        (pos_t, in_hbm()),
    ) + tuple((array, whole(array.shape)) for array in extra)
    outs = (
        ((share, width), bf16),
        ((share, width + (TILE if mode == "last" else 0)), bf16),
        ((count, QUAD), bf16),
        ((LEN, QUAD), bf16),
        ((LEN, QUAD), bf16),
        ((8, QUAD), f32),
    )
    if mode == "last":
        outs += (((VECTOR_ROWS, TILE), f32),)
    return pl.pallas_call(
        functools.partial(backward_kernel, half, groups, at, mode),
        grid=(1,),
        out_shape=[jax.ShapeDtypeStruct(shape, kind) for shape, kind in outs],
        in_specs=[spec for _, spec in operands],
        out_specs=[whole(shape) for shape, _ in outs],
        scratch_shapes=[
            pltpu.VMEM((4, count, KEYS), bf16),
            pltpu.VMEM((D, count), bf16),
            pltpu.VMEM((D, KEYS), bf16),
            pltpu.VMEM((D, window), bf16),
            pltpu.VMEM((2, count, KEYS), f32),
            pltpu.VMEM((2, count, KEYS), bf16),
            pltpu.VMEM((2, count, window), bf16),
            pltpu.SemaphoreType.DMA((7,)),
        ],
        compiler_params=params(BACKWARD_BYTES),
        cost_estimate=cost(16_000_000_000, 16_000_000),
        name="attention_backward",
    )(*[array for array, _ in operands])


def row_gradients(half, groups, summed_grad, proj, keys, vals, weights):
    count = 2 * half
    arrays = (summed_grad, *proj, *keys, *vals, *weights)
    outs = (((half, D), f32), ((half, D), f32), ((half, D), bf16))
    return pl.pallas_call(
        functools.partial(rows_kernel, half, groups),
        grid=(1,),
        out_shape=[jax.ShapeDtypeStruct(shape, kind) for shape, kind in outs],
        in_specs=[whole(array.shape) for array in arrays],
        out_specs=[whole(shape) for shape, _ in outs],
        scratch_shapes=[pltpu.VMEM((LEN, D), f32)],
        compiler_params=params(),
        cost_estimate=cost(4_000_000_000, 10_000_000),
        name="row_gradients",
    )(*arrays)


def swap(array):
    groups = lax.axis_size("tensor")
    return lax.ppermute(array, "tensor", [(i, (i + 1) % groups) for i in range(groups)])


def across(array, masks):
    size, groups = lax.axis_size("dp"), lax.axis_size("tensor")
    pairs = [
        (place * groups + core, (place ^ masks[core]) * groups + core)
        for place in range(size)
        for core in range(groups)
    ]
    return lax.ppermute(array, ("dp", "tensor"), pairs)


def total(terms):
    return functools.reduce(jnp.add, [term.astype(f32) for term in terms])


class Chain:
    def __init__(self, parts, rows, vectors=()):
        self.parts, self.rows = parts, rows
        self.vectors = list(vectors)
        self.messages = None
        self.done = 0

    def masks(self, part, bits):
        size, groups = lax.axis_size("dp"), lax.axis_size("tensor")
        found = []
        for core in range(groups):
            order = order_of(core, size.bit_length() - 1)[self.done : self.done + bits]
            found.append(
                sum(((part >> (bits - 1 - j)) & 1) << bit for j, bit in enumerate(order))
            )
        return found

    def send(self):
        if not self.bits:
            gots = [swap(self.messages[0])]
        else:
            gots = [
                across(message, self.masks(part + 1, self.bits))
                for part, message in enumerate(self.messages)
            ]
        for got in gots:
            column = 0
            for width, terms in self.parts:
                terms.append((got, column))
                column += width
            if self.vectors:
                self.vectors.append((got, column, self.rows))
        self.pending = gots
        self.done += self.bits
        self.messages = None

    def take(self, results):
        if self.vectors:
            self.vectors = [(results.pop(0), 0, VECTOR_ROWS)]
        kept, column, parts = results.pop(0), 0, []
        for width, _ in self.parts:
            parts.append((width, [(kept, column)]))
            column += width
        self.parts = parts
        self.messages = [results.pop(0) for _ in range((1 << self.bits) - 1)]

    def replace(self, old, new):
        for index, (width, terms) in enumerate(self.parts):
            self.parts[index] = (
                width,
                [(new if array is old else array, at) for array, at in terms],
            )
        self.vectors = [(new if a is old else a, at, rows) for a, at, rows in self.vectors]


def merged(chains):
    chain = Chain(
        [part for chain in chains for part in chain.parts],
        chains[0].rows,
        [term for chain in chains for term in chain.vectors],
    )
    chain.done = chains[0].done
    chain.pending = []
    return chain


class Operands:
    def __init__(self):
        self.arrays = []

    def of(self, array):
        for index, held in enumerate(self.arrays):
            if held is array:
                return index
        self.arrays.append(array)
        return len(self.arrays) - 1

    def in_specs(self):
        return [whole(array.shape) for array in self.arrays]


def prepare(requests):
    operands, plans, outs = Operands(), [], []
    plain = any(chain.rows % (8 << bits) for chain, bits in requests)
    for chain, bits in requests:
        chain.bits = bits
        chain.rows >>= bits
        rows, pieces = chain.rows, 1 << bits
        width = sum(width for width, _ in chain.parts)
        if plain:
            results = [
                jnp.concatenate(
                    [
                        total(
                            [
                                array[piece * rows : (piece + 1) * rows, at : at + width]
                                for array, at in terms
                            ]
                        )
                        for width, terms in chain.parts
                    ],
                    axis=1,
                )
                for piece in range(pieces)
            ]
            if chain.vectors:
                packed = summed_vectors(lambda array: array, chain.vectors)
                folded = fold_vectors(packed, rows)
                results = [packed, results[0]] + [
                    jnp.concatenate([result, folded], axis=1) for result in results[1:]
                ]
            chain.take([result.astype(bf16) for result in results])
            continue
        parts = [
            (width, [(operands.of(array), at) for array, at in terms])
            for width, terms in chain.parts
        ]
        vectors = [(operands.of(array), at, held) for array, at, held in chain.vectors]
        plans.append((rows, pieces, parts, vectors))
        if vectors:
            outs.append(((VECTOR_ROWS, TILE), f32))
        outs.append(((rows, width), bf16))
        wide = width + (vector_width(rows) if vectors else 0)
        outs += [((rows, wide), bf16)] * (pieces - 1)
    if plain:
        return
    results = pl.pallas_call(
        functools.partial(combine_kernel, plans),
        grid=(1,),
        out_shape=[jax.ShapeDtypeStruct(shape, kind) for shape, kind in outs],
        in_specs=operands.in_specs(),
        out_specs=[whole(shape) for shape, _ in outs],
        compiler_params=params(COMBINE_BYTES),
        cost_estimate=cost(1_000_000_000, 8_000_000),
        name="combine",
    )(*operands.arrays)
    results = list(results)
    for chain, bits in requests:
        chain.take(results)


def launch(requests, value, waits=()):
    chains = [chain for chain, bits in requests if bits is not None] + list(waits)
    olds = [got for chain in chains for got in chain.pending]
    if olds:
        value, news = lax.optimization_barrier((value, olds))
        for chain in chains + [chain for chain, _ in requests]:
            for old, new in zip(olds, news):
                chain.replace(old, new)
        for chain in chains:
            chain.pending = []
    sums = [(chain, bits) for chain, bits in requests if bits is not None]
    if sums:
        prepare(sums)
    messages = [chain.messages for chain, _ in requests]
    value, messages = lax.optimization_barrier((value, messages))
    for (chain, bits), message in zip(requests, messages):
        chain.messages = message
        if bits is None:
            chain.bits = 0
        chain.send()
    return value


def finish(size, groups, chain):
    share = D // (size * groups)
    up_rows = FF // D
    pieces = []
    for quad, (width, terms) in enumerate(chain.parts):
        for index in range(4):
            pieces.append((index, quad * QUAD, QUAD, [(a, at + index * QUAD) for a, at in terms]))
    if share % 8:
        blocks = {}
        for target, at, width, terms in pieces:
            blocks.setdefault(target, []).append(
                total([array[:share, c : c + width] for array, c in terms])
            )
        weights = [jnp.concatenate(blocks[target], axis=1) for target in range(4)]
        vectors = unpack_vectors(summed_vectors(lambda array: array, chain.vectors))
        place = lax.axis_index("dp") * groups + lax.axis_index("tensor")
        mine = lax.dynamic_slice_in_dim(vectors, place * share, share, 1)
        ups = lax.dynamic_slice_in_dim(
            vectors[5 : 5 + up_rows].reshape(-1), place * up_rows * share, up_rows * share, 0
        )
        late = 5 + up_rows
        return weights, [mine[r] for r in (0, 1, 2, 3, 4, late, late + 1, late + 2)], mine[
            late + 3 : late + 5
        ].T, ups
    operands = Operands()
    plan = [
        (target, at, width, [(operands.of(array), c) for array, c in terms])
        for target, at, width, terms in pieces
    ]
    vectors = [(operands.of(array), at, held) for array, at, held in chain.vectors]
    outs = [(share, D)] * 4 + [(share,)] * 8 + [(2, share), (up_rows * share,)]
    found = pl.pallas_call(
        functools.partial(
            finish_kernel, size, groups, len(operands.arrays), (plan, vectors), up_rows
        ),
        grid=(1,),
        out_shape=[jax.ShapeDtypeStruct(shape, f32) for shape in outs],
        in_specs=operands.in_specs(),
        out_specs=[whole(shape) for shape in outs],
        compiler_params=params(COMBINE_BYTES),
        name="finish",
    )(*operands.arrays)
    return found[:4], found[4:12], found[12].T, found[13]


def body(
    content_in,
    query_in,
    memory,
    content_cot,
    query_cot,
    query_weight,
    key_weight,
    value_weight,
    out_weight,
    rel_weight,
    content_bias,
    position_bias,
    segment_bias,
    segment_embed,
    attn_gain,
    attn_shift,
    up_weight,
    up_bias,
    down_weight,
    down_bias,
    ffn_gain,
    ffn_shift,
    lengths,
    memory_lengths,
    segment_ids,
    orders,
    targets,
):
    groups = lax.axis_size("tensor")
    size = lax.axis_size("dp")
    steps = size.bit_length() - 1
    half = LEN // groups
    hidden_cols = up_weight.shape[1]
    up_other, down_other = swap(up_weight), swap(down_weight)
    content, query = content_in[0], query_in[0]
    segment_rows = segment_embed.T
    saved = attention_forward(
        half,
        (lengths, memory_lengths, segment_ids, orders, targets),
        memory[0],
        content,
        query,
        (query_weight, key_weight, value_weight, rel_weight),
        (content_bias, position_bias, segment_bias),
        segment_rows,
    )
    (
        content_out,
        query_out,
        ffn_own,
        ffn_other,
        summed_grad,
        attended_grad,
        early_small,
        up_bias_part,
    ) = middle(
        half,
        size,
        groups,
        (
            saved[0],
            content,
            query,
            content_cot[0],
            query_cot[0],
            out_weight,
            up_weight,
            up_other,
            down_weight,
            down_other,
            up_bias,
            down_bias,
            attn_gain,
            attn_shift,
            ffn_gain,
            ffn_shift,
        ),
        hidden_cols,
    )
    ffn = Chain([(ffn_own.shape[1], [(ffn_own, 0)])], D)
    ffn.messages = [ffn_other]
    held = launch([(ffn, None)], attended_grad)
    content_late, held = lax.optimization_barrier((content, held))
    turned = transposed_rows(half, size, groups, memory[0], content_late, query, saved[11])
    turned, held = lax.optimization_barrier((turned, held))
    saved = (*saved, *turned)
    proj, tok_keys, tok_vals, small, late = [], [], [], [], []

    def backward(at, mode, grad, extra):
        own, other, proj_part, key_part, val_part, small_part, *vectors = attention_backward(
            half, groups, at, mode, saved, grad, segment_rows, extra
        )
        proj.append(proj_part)
        tok_keys.append(key_part)
        tok_vals.append(val_part)
        small.append(small_part)
        chain = Chain(
            [(own.shape[1], [(own, 0)])],
            own.shape[0],
            [(array, 0, VECTOR_ROWS) for array in vectors],
        )
        chain.messages = [other]
        late.append(chain)

    held = launch([(ffn, 1)], held)
    backward(0, "middle", held, ())
    held, proj[0] = launch([(late[0], None)], (attended_grad, proj[0]))
    backward(1, "middle", held, ())
    held, proj[1] = launch(
        [(ffn, 1), (late[1], None)], (attended_grad, proj[1])
    )
    backward(2, "last", held, (early_small, up_bias_part, *small))
    xy = min(2, steps)
    early = merged(late[:2])
    tok_vals[2] = launch([(late[2], None), (ffn, 1), (early, 1)], tok_vals[2], late[:2])
    own_rows, query_grad, row_send = row_gradients(
        half, groups, summed_grad, proj, tok_keys, tok_vals, (query_weight, key_weight, value_weight)
    )
    own_rows, row_send = launch(
        [(late[2], xy), (early, 1), (ffn, 1)], (own_rows, row_send)
    )
    final = merged([early, late[2]])
    own_rows, row_send = launch(
        [(final, min(2, steps - final.done))], (own_rows, row_send), [early, late[2]]
    )
    row_got = swap(row_send)
    while final.done < steps:
        own_rows = launch([(final, min(2, steps - final.done))], own_rows)
    while ffn.done < steps:
        own_rows = launch([(ffn, min(2, steps - ffn.done))], own_rows)
    content_grad = own_rows + row_got.astype(f32)
    ffn_sum = total([array[: ffn.rows] for array, _ in ffn.parts[0][1]])
    up_grad, down_grad_own = ffn_sum[:, :hidden_cols], ffn_sum[:, hidden_cols : 2 * hidden_cols].T
    out_rows = ffn.rows // groups
    out_grad = jnp.concatenate(
        [ffn_sum[n : n + out_rows, 2 * hidden_cols :] for n in range(0, ffn.rows, out_rows)], axis=1
    )
    (content_grad, up_grad, down_grad_own, out_grad), olds = lax.optimization_barrier(
        ((content_grad, up_grad, down_grad_own, out_grad), final.pending)
    )
    for old, new in zip(final.pending, olds):
        final.replace(old, new)
    weights, vectors, segment_grad, up_bias_grad = finish(size, groups, final)
    return (
        content_out[None],
        query_out[None],
        content_grad[None],
        query_grad[None],
        weights[0],
        weights[1],
        weights[2],
        out_grad,
        weights[3],
        vectors[5],
        vectors[6],
        vectors[7],
        segment_grad,
        vectors[3],
        vectors[4],
        up_grad,
        up_bias_grad,
        down_grad_own,
        vectors[2],
        vectors[0],
        vectors[1],
    )


def solution(mesh):
    in_specs = (
        P("dp", None, None),
        P("dp", "tensor", None),
        P("dp", None, None),
        P("dp", "tensor", None),
        P("dp", "tensor", None),
        P(),
        P(),
        P(),
        P(),
        P(),
        P(),
        P(),
        P(),
        P(),
        P(),
        P(),
        P(None, "tensor"),
        P(),
        P("tensor", None),
        P(),
        P(),
        P(),
        P("dp"),
        P("dp"),
        P("dp", None),
        P("dp", None),
        P("dp", None),
    )
    out_specs = (
        P("dp", "tensor", None),
        P("dp", "tensor", None),
        P("dp", "tensor", None),
        P("dp", "tensor", None),
        P(("dp", "tensor"), None),
        P(("dp", "tensor"), None),
        P(("dp", "tensor"), None),
        P(("dp", "tensor"), None),
        P(("dp", "tensor"), None),
        P(("dp", "tensor")),
        P(("dp", "tensor")),
        P(("dp", "tensor")),
        P(("dp", "tensor"), None),
        P(("dp", "tensor")),
        P(("dp", "tensor")),
        P("dp", "tensor"),
        P(("dp", "tensor")),
        P("tensor", "dp"),
        P(("dp", "tensor")),
        P(("dp", "tensor")),
        P(("dp", "tensor")),
    )
    return jax.shard_map(body, mesh=mesh, in_specs=in_specs, out_specs=out_specs, check_vma=False)
```

```python
import functools

import jax
import jax.numpy as jnp
from jax import lax
from jax.experimental import pallas as pl
from jax.experimental.pallas import tpu as pltpu
from jax.sharding import PartitionSpec as P

D = 768
HEADS = 12
HEAD_DIM = 64
FF = 3072
LEN = 512
MEM = 384
KEYS = MEM + LEN
QUAD = 4 * HEAD_DIM
QUADS = D // QUAD
PAIR = 2 * HEAD_DIM
SCALE = HEAD_DIM ** (-0.5)
VMEM_BYTES = 61 * 1024 * 1024
COMBINE_BYTES = 28 * 1024 * 1024
BACKWARD_BYTES = 54 * 1024 * 1024
MIDDLE_BYTES = 61 * 1024 * 1024
FORWARD_BYTES = 62 * 1024 * 1024
BLOCK = 16
TILE = 128
WIDE = 256
VECTORS = 16

VECTOR_ROWS = VECTORS * D // TILE

f32 = jnp.float32
bf16 = jnp.bfloat16
precise = lax.Precision.HIGHEST


def mm(left, right):
    return lax.dot_general(left, right, (((1,), (0,)), ((), ())), preferred_element_type=f32)


def mm_nt(left, right):
    return lax.dot_general(left, right, (((1,), (1,)), ((), ())), preferred_element_type=f32)


def mm_tn(left, right):
    return lax.dot_general(left, right, (((0,), (0,)), ((), ())), preferred_element_type=f32)


def unit_matrix(size):
    row = lax.broadcasted_iota(jnp.int32, (size, size), 0)
    return jnp.where(row == lanes((size, size)), 1.0, 0.0).astype(bf16)


def turn(value):
    width = min(value.shape[1], WIDE)
    unit = unit_matrix(width)
    blocks = [mm_nt(unit, value[:, n : n + width]) for n in range(0, value.shape[1], width)]
    return blocks[0] if len(blocks) == 1 else jnp.concatenate(blocks, axis=0)


def split(value):
    high = value.astype(bf16)
    return high, (value - high.astype(f32)).astype(bf16)


def lanes(shape):
    return lax.broadcasted_iota(jnp.int32, shape, 1)


def column_of(row):
    row = row.astype(f32)
    even = 2.0 * jnp.floor(0.5 * row)
    parts = jnp.concatenate([even, row - even, jnp.zeros((14, row.shape[1]), f32)], axis=0)
    return mm_tn(parts.astype(bf16), jnp.ones((16, TILE), bf16))


def lane_tiles(value, combine):
    tiles = [value[:, at : at + TILE] for at in range(0, value.shape[1], TILE)]
    return functools.reduce(combine, tiles)


def interleave(steps, tasks):
    done = 0
    for index, step in enumerate(steps):
        step()
        while done * len(steps) < (index + 1) * len(tasks) and done < len(tasks):
            tasks[done]()
            done += 1
    for task in tasks[done:]:
        task()


def order_of(core, bits):
    order = list(range(bits))
    if core == 1:
        for at in range(0, bits - 1, 2):
            order[at], order[at + 1] = order[at + 1], order[at]
    return order


def block_owner(place, core, bits):
    owners = []
    for each in range(2):
        owner = place * 0
        for step, bit in enumerate(order_of(each, bits)):
            owner = owner | (((place >> (bits - 1 - step)) & 1) << bit)
        owners.append(owner)
    return jnp.where(core == 1, owners[1], owners[0]) ^ lax.axis_index("dp")


def one_hot(source):
    return jnp.where(lanes((source.shape[0], D)) == source, 1.0, 0.0).astype(bf16)


def owner_rows(size, groups):
    share = D // (size * groups)
    row = lax.broadcasted_iota(jnp.int32, (D, 1), 0)
    side, rest = lax.div(row, size * share), lax.rem(row, size * share)
    core = lax.rem(lax.axis_index("tensor") + side, groups)
    owner = block_owner(lax.div(rest, share), core, size.bit_length() - 1)
    return one_hot((owner * groups + core) * share + lax.rem(rest, share))


def shared_rows(size, core):
    share = D // size
    row = lax.broadcasted_iota(jnp.int32, (D, 1), 0)
    owner = block_owner(lax.div(row, share), core, size.bit_length() - 1)
    return one_hot(owner * share + lax.rem(row, share))


def transpose_by_owner(out_ref, value, work, size, groups):
    share = D // (size * groups)
    if share % 8 or (2 * share) % 16:
        out_ref[...] = mm_nt(owner_rows(size, groups), value).astype(bf16)
        return
    width = value.shape[0]
    for n in range(0, D, WIDE):
        work[n : n + WIDE, :width] = turn(value[:, n : n + WIDE])
    bits = size.bit_length() - 1
    blocks = []
    for block in range(size * groups):
        core = lax.rem(lax.axis_index("tensor") + block // size, groups)
        owner = block_owner(jnp.int32(block % size), core, bits)
        at = pl.multiple_of((owner * groups + core) * share, 8)
        blocks.append(work[pl.ds(at, share), :width])
        if block % 2:
            out_ref[(block - 1) * share : (block + 1) * share, :] = jnp.concatenate(
                blocks, axis=0
            ).astype(bf16)
            blocks = []


def transpose_by_dp(out_ref, value, work, size):
    share = D // size
    core = lax.axis_index("tensor")
    if share % 16:
        out_ref[...] = mm_nt(shared_rows(size, core), value).astype(bf16)
        return
    for n in range(0, D, WIDE):
        work[n : n + WIDE, :] = turn(value[:, n : n + WIDE]).astype(bf16)
    for block in range(size):
        owner = block_owner(jnp.int32(block), core, size.bit_length() - 1)
        at = pl.multiple_of(owner * share, 16)
        out_ref[block * share : (block + 1) * share, :] = work[pl.ds(at, share), :]


def forward_kernel(
    half,
    length_ref,
    mem_length_ref,
    seg_ref,
    ord_ref,
    tgt_ref,
    memory_ref,
    content_ref,
    query_ref,
    wq_ref,
    wk_ref,
    wv_ref,
    wr_ref,
    cb_ref,
    pb_ref,
    sb_ref,
    se_ref,
    att_ref,
    prob_ref,
    key_ref,
    val_ref,
    rel_ref,
    hc_ref,
    hp_ref,
    hs_ref,
    linv_ref,
    kaug_ref,
    srow_ref,
    pos_ref,
    stack,
    both,
    pos,
    bias,
    fine,
    coarse,
    vectors,
    scores,
    places,
    kaug_t,
    scol,
    seg_row,
    kaug_work,
    order_work,
    seg_work,
):
    window = KEYS + half
    first = pl.multiple_of(lax.axis_index("tensor") * half, half)
    step_id = pl.program_id(0)

    @pl.when(step_id == 0)
    def _():
        stack[:MEM, :] = memory_ref[...]
        stack[MEM:, :] = content_ref[...]
        both[:half, :] = content_ref[pl.ds(first, half), :]
        both[half:, :] = query_ref[...]
        vectors[0:1, :] = cb_ref[...][None, :]
        vectors[1:2, :] = pb_ref[...][None, :]
        vectors[2:3, :] = sb_ref[...][None, :]
        step = lax.broadcasted_iota(jnp.int32, (1, D // 2), 1).astype(f32) * (2.0 / D)
        inverse = 1.0 / jnp.power(jnp.full((1, D // 2), 10000.0, f32), step)
        coarse_rows = coarse.shape[1]
        top = (MEM + half + first).astype(f32)
        angle = (
            top - 32.0 * lax.broadcasted_iota(jnp.int32, (coarse_rows, 1), 0).astype(f32)
        ) * inverse
        coarse[0] = jnp.sin(angle)
        coarse[1] = jnp.cos(angle)
        small = lax.broadcasted_iota(jnp.int32, (32, 1), 0).astype(f32) * inverse
        fine[0] = jnp.sin(small)
        fine[1] = jnp.cos(small)
        for a in range(window // 32):
            sa, ca = coarse[0, a : a + 1, :], coarse[1, a : a + 1, :]
            sb, cb = fine[0], fine[1]
            pos[a * 32 : (a + 1) * 32, : D // 2] = (sa * cb - ca * sb).astype(bf16)
            pos[a * 32 : (a + 1) * 32, D // 2 :] = (ca * cb + sa * sb).astype(bf16)
        never = float(LEN + 1)
        mem_at = lax.broadcasted_iota(jnp.int32, (1, MEM), 1)
        tok_at = lax.broadcasted_iota(jnp.int32, (1, LEN), 1)
        open_from = jnp.concatenate(
            [
                jnp.where(mem_at >= MEM - mem_length_ref[0], -1.0, never),
                jnp.where(
                    tok_at < length_ref[0],
                    jnp.where(tgt_ref[...] == 0, -1.0, ord_ref[...].astype(f32)),
                    never,
                ),
            ],
            axis=1,
        )
        order_col = column_of(ord_ref[...])
        seg_col = column_of(seg_ref[...])
        kaug_lane = lanes((LEN, PAIR)) % HEAD_DIM
        kaug_work[:MEM, :] = (lanes((MEM, PAIR)) % HEAD_DIM < 4).astype(f32).astype(bf16)
        kaug_work[MEM:, :] = jnp.where(
            kaug_lane < 4, 1.0, jnp.where(kaug_lane < 6, seg_col, 0.0)
        ).astype(bf16)
        kaug_t[...] = kaug_work[...].T[:HEAD_DIM]
        kaug_ref[...] = kaug_t[:16, :]
        order_work[...] = order_col
        own_order = order_work[pl.ds(first, half), :][:, :1]
        seg_work[...] = seg_col
        scol[...] = seg_work[pl.ds(first, half), :]
        seen = open_from <= own_order
        bias[:half, :] = jnp.where(seen, 0.0, -1e30)
        key_at = lax.broadcasted_iota(jnp.int32, (half, KEYS), 1)
        row_at = lax.broadcasted_iota(jnp.int32, (half, KEYS), 0)
        seen_q = seen & (key_at - MEM != row_at + first)
        bias[half:, :] = jnp.where(seen_q, 0.0, -1e30)
        seg_row[0:1, :] = seg_ref[...].astype(f32)
        srow_ref[...] = jnp.broadcast_to(seg_row[0:1, pl.ds(first, half)], srow_ref.shape)
        pos_ref[...] = pos[...]

    here = pl.ds(pl.multiple_of(step_id * QUAD, QUAD), QUAD)
    keys = mm(stack[...], wk_ref[...]).astype(bf16)
    values = mm(stack[...], wv_ref[...]).astype(bf16)
    rel = mm(pos[...], wr_ref[...]).astype(bf16)
    projection = mm(both[...], wq_ref[...])
    head_content = (projection + vectors[0:1, here]).astype(bf16)
    head_position = (projection + vectors[1:2, here]).astype(bf16)
    head_segment = projection + vectors[2:3, here]
    keys_t, values_t, rel_t = [turn(value).astype(bf16) for value in (keys, values, rel)]
    key_ref[...] = keys_t
    val_ref[...] = values_t
    rel_ref[...] = rel_t
    hs_ref[...] = head_segment
    head_content = (head_content.astype(f32) * SCALE).astype(bf16)
    head_position = (head_position.astype(f32) * SCALE).astype(bf16)
    hc_ref[...] = turn(head_content).astype(bf16)
    hp_ref[...] = turn(head_position).astype(bf16)
    row_head = lax.broadcasted_iota(jnp.int32, (QUAD, QUAD), 0) // HEAD_DIM
    at = lanes((QUAD, QUAD)) - ((row_head // 2) * PAIR + (1 - row_head % 2) * HEAD_DIM)
    place_same = jnp.where((at >= 0) & (at < 2), 1.0, 0.0).astype(bf16)
    place_step = jnp.where((at >= 2) & (at < 6), 1.0, 0.0).astype(bf16)
    same, other = se_ref[0:1, :], se_ref[1:2, :]
    terms = functools.reduce(
        jnp.add,
        [mm(part, place_same) for part in split(head_segment * same)]
        + [mm(part, place_step) for part in split(head_segment * (other - same))],
    )
    marks = jnp.concatenate([scol[...], scol[...]], axis=0)
    marks = jnp.concatenate([marks, marks], axis=1)
    lane6 = lanes((2 * half, QUAD)) % HEAD_DIM
    factor = jnp.where(lane6 < 2, 1.0, jnp.where(lane6 < 4, marks, 1.0 - 2.0 * marks))
    terms = SCALE * (terms * factor)
    high = terms.astype(bf16)
    low = (terms - high.astype(f32)).astype(bf16)
    qaug = jnp.where(lane6 % 2 == 0, high, low)
    key_x = []
    for which in range(4):
        own = keys_t[which * HEAD_DIM : (which + 1) * HEAD_DIM]
        sides = [own, kaug_t[...]] if which % 2 == 0 else [kaug_t[...], own]
        key_x.append(jnp.concatenate(sides, axis=0))
    peaks, totals, outs = {}, {}, {}
    row_first = lanes((2 * half, PAIR)) < HEAD_DIM

    def products(which):
        cols = slice(which // 2 * PAIR, (which // 2 + 1) * PAIR)
        slot = which % 2
        row_mine = row_first == (which % 2 == 0)
        query_x = jnp.where(row_mine, head_content[:, cols], qaug[:, cols])
        place_x = jnp.where(row_mine, head_position[:, cols], jnp.zeros((), bf16))

        def score(n, stop):
            scores[slot, :, n:stop] = mm(query_x, key_x[which][:, n:stop])

        def placed(n, stop):
            places[slot, :, n:stop] = mm(place_x, rel_t[cols, n:stop])

        return [functools.partial(placed, n, min(n + WIDE, window)) for n in range(0, window, WIDE)] + [
            functools.partial(score, n, min(n + WIDE, KEYS)) for n in range(0, KEYS, WIDE)
        ]

    def softmax(which):
        slot = which % 2
        tops, pieces = [], []

        def join(b):
            block = slice(b, b + BLOCK)
            shifted = pltpu.roll(
                places[slot, block, :], (KEYS + b % half) % window, 1, stride=1, stride_axis=0
            )[:, :KEYS]
            score = scores[slot, block, :] + shifted + bias[block, :]
            scores[slot, block, :] = score
            tops.append(lane_tiles(score, jnp.maximum))

        def peak():
            peaks[which] = jnp.max(jnp.concatenate(tops, axis=0), axis=1, keepdims=True)

        def power(b):
            block = slice(b, b + BLOCK)
            prob = jnp.exp(scores[slot, block, :] - peaks[which][block])
            pieces.append(lane_tiles(prob, jnp.add))
            prob_ref[which, block, :] = prob.astype(bf16)

        def finish():
            totals[which] = 1.0 / jnp.sum(
                jnp.concatenate(pieces, axis=0), axis=1, keepdims=True
            )

        blocks = range(0, 2 * half, BLOCK)
        return (
            [functools.partial(join, b) for b in blocks]
            + [peak]
            + [functools.partial(power, b) for b in blocks]
            + [finish]
        )

    def mixture(which, part):
        outs[which, part] = mm_nt(
            values_t[which * HEAD_DIM : (which + 1) * HEAD_DIM],
            prob_ref[which, part * half : (part + 1) * half, :],
        )

    interleave([], products(0))
    for which in range(4):
        tasks = products(which + 1) if which < 3 else []
        if which:
            tasks += [functools.partial(mixture, which - 1, part) for part in range(2)]
        interleave(softmax(which), tasks)
    for part in range(2):
        mixture(3, part)
    sums = [totals[which] for which in range(4)]
    mixed = jnp.concatenate(
        [jnp.concatenate([outs[which, 0], outs[which, 1]], axis=1) for which in range(4)], axis=0
    )
    mixed = functools.reduce(jnp.add, [turn(part) for part in split(mixed)])
    mine = lanes((2 * half, PAIR)) < HEAD_DIM
    for pair in range(2):
        cols = slice(pair * PAIR, (pair + 1) * PAIR)
        att_ref[:, cols] = mixed[:, cols] * jnp.where(mine, sums[2 * pair], sums[2 * pair + 1])
    lane = lanes((2 * half, TILE))
    linv_ref[...] = jnp.where(
        lane == 0, sums[0], jnp.where(lane == 1, sums[1], jnp.where(lane == 2, sums[2], sums[3]))
    )


def norm_forward(summed, gain, shift):
    center = summed - jnp.mean(summed, axis=1, keepdims=True)
    inv = lax.rsqrt(jnp.mean(center * center, axis=1, keepdims=True) + 1e-06)
    unit = center * inv
    return unit, inv, unit * gain + shift


def norm_backward(grad, unit, inv, gain):
    scaled = grad * gain
    return inv * (
        scaled
        - jnp.mean(scaled, axis=1, keepdims=True)
        - unit * jnp.mean(scaled * unit, axis=1, keepdims=True)
    )


def row_sum(value):
    return jnp.sum(value, axis=0, keepdims=True)


def gelu_parts(x):
    square = x * x
    tanh = jnp.tanh((0.7978845608028654 * x) * (1.0 + 0.044715 * square))
    rise = 0.5 * (1.0 + tanh)
    grad = rise + (0.5 * x) * (1.0 - tanh * tanh) * (
        0.7978845608028654 * (1.0 + 0.134145 * square)
    )
    return x * rise, grad


def fold_rows(value):
    return functools.reduce(jnp.add, [value[r : r + 8] for r in range(0, value.shape[0], 8)])


def middle_kernel(
    half,
    size,
    groups,
    chunk,
    att_ref,
    content_ref,
    query_ref,
    ccot_ref,
    qcot_ref,
    wo_ref,
    up_own_hbm,
    up_oth_hbm,
    down_own_hbm,
    down_oth_hbm,
    ubias_ref,
    dbias_ref,
    again_ref,
    ashift_ref,
    fgain_ref,
    fshift_ref,
    cout_ref,
    qout_ref,
    ffn_own_ref,
    ffn_oth_ref,
    sgrad_ref,
    agrad_ref,
    out_own_ref,
    out_oth_ref,
    small_ref,
    ubg_ref,
    hidden,
    slope,
    pre,
    work,
    unit,
    low,
    down_grad,
    vectors,
    up,
    down,
    low_t,
    down_t,
    turn_low,
    turn_down,
    attended_t,
    turn_work,
    sems,
):
    count = 2 * half
    member = lax.axis_index("tensor")
    first = pl.multiple_of(member * half, half)
    fetches = [
        pltpu.make_async_copy(source, target.at[side], sems.at[kind, side])
        for kind, side, source, target in (
            (0, 0, up_own_hbm, up),
            (1, 0, down_own_hbm, down),
            (0, 1, up_oth_hbm, up),
            (1, 1, down_oth_hbm, down),
        )
    ]
    for fetch in fetches:
        fetch.start()
    ups, downs = (up.at[0], up.at[1]), (down.at[0], down.at[1])
    part_cols = up.shape[2]
    chunks = part_cols // chunk
    vectors[0:1, :] = ubias_ref[...][None, :]
    attended = att_ref[...].astype(bf16)
    work[...] = mm(attended, wo_ref[...])
    attn_gain, attn_shift = again_ref[...][None, :], ashift_ref[...][None, :]
    ffn_gain, ffn_shift = fgain_ref[...][None, :], fshift_ref[...][None, :]
    down_bias = dbias_ref[...][None, :]
    inverse = []
    for b in range(0, count, BLOCK):
        block = slice(b, b + BLOCK)
        if b < half:
            rows_in = content_ref[pl.ds(pl.multiple_of(first + b, BLOCK), BLOCK), :]
        else:
            rows_in = query_ref[b - half : b - half + BLOCK, :]
        found, inv, normed = norm_forward(
            work[block, :] + rows_in.astype(f32), attn_gain, attn_shift
        )
        unit[block, :] = found
        inverse.append(inv)
        low[block, :] = normed.astype(bf16)
        work[block, :] = normed + down_bias
    for fetch in fetches:
        fetch.wait()
    pieces = [(side, at) for side in range(2) for at in range(chunks)]

    def rise(index):
        side, at = pieces[index]

        def task(n):
            pre[index % 2, :, n : n + WIDE] = mm(
                low[...], ups[side][:, at * chunk + n : at * chunk + n + WIDE]
            )

        return [functools.partial(task, n) for n in range(0, chunk, WIDE)]

    def bend(index):
        side, at = pieces[index]
        cols = slice(at * chunk, (at + 1) * chunk)
        start = lax.rem(member + side, 2) * part_cols + at * chunk
        bias = vectors[0:1, pl.ds(pl.multiple_of(start, TILE), chunk)]

        def step(b):
            block = slice(b, b + BLOCK)
            act, grad = gelu_parts(pre[index % 2, block, :] + bias)
            hidden[side, block, cols] = act.astype(bf16)
            slope[side, block, cols] = grad.astype(bf16)

        return [functools.partial(step, b) for b in range(0, count, BLOCK)]

    def fall(index):
        side, at = pieces[index]
        cols = slice(at * chunk, (at + 1) * chunk)

        def task(n):
            work[:, n : n + WIDE] += mm(hidden[side, :, cols], downs[side][cols, n : n + WIDE])

        return [functools.partial(task, n) for n in range(0, D, WIDE)]

    interleave([], rise(0))
    for index in range(len(pieces)):
        tasks = rise(index + 1) if index + 1 < len(pieces) else []
        if index:
            tasks += fall(index - 1)
        interleave(bend(index), tasks)
    interleave([], fall(len(pieces) - 1))
    sums = [jnp.zeros((8, D), f32) for _ in range(5)]
    for b in range(0, count, BLOCK):
        block = slice(b, b + BLOCK)
        found, inv, out = norm_forward(work[block, :], ffn_gain, ffn_shift)
        if b < half:
            cout_ref[block, :] = out.astype(bf16)
            cot = ccot_ref[block, :].astype(f32)
        else:
            block_q = slice(b - half, b - half + BLOCK)
            qout_ref[block_q, :] = out.astype(bf16)
            cot = qcot_ref[block_q, :].astype(f32)
        residual_grad = norm_backward(cot, found, inv, ffn_gain)
        rounded = residual_grad.astype(bf16)
        down_grad[block, :] = rounded
        work[block, :] = residual_grad
        for index, value in enumerate((cot * found, cot, rounded.astype(f32))):
            sums[index] = sums[index] + fold_rows(value)
    transpose_by_dp(low_t, low[...], turn_low, size)
    transpose_by_dp(down_t, down_grad[...], turn_down, size)
    for side in range(2):
        for at in range(chunks):
            cols = slice(at * chunk, (at + 1) * chunk)
            hidden_grad = mm_nt(down_grad[...], downs[side][cols, :])
            pre_grad = (hidden_grad * slope[side, :, cols].astype(f32)).astype(bf16)
            slope[side, :, cols] = pre_grad
            ubg_ref[side : side + 1, cols] = row_sum(pre_grad.astype(f32))
            work[...] += mm_nt(pre_grad, ups[side][:, cols])

    def settle(b):
        block = slice(b, b + BLOCK)
        grad, found = work[block, :], unit[block, :]
        summed_grad = norm_backward(grad, found, inverse[b // BLOCK], attn_gain)
        sgrad_ref[block, :] = summed_grad
        down_grad[block, :] = summed_grad.astype(bf16)
        sums[3] = sums[3] + fold_rows(grad * found)
        sums[4] = sums[4] + fold_rows(grad)

    share = D // size
    bits = size.bit_length() - 1

    def other_place(place):
        found = 0
        for step in range(bits):
            there = order_of(1, bits)[step]
            found |= ((place >> (bits - 1 - there)) & 1) << (bits - 1 - step)
        return found

    def weigh(side, kind, n):
        left, right = ((low_t, slope), (down_t, hidden))[kind]
        value = mm(left[...], right[side, :, n : n + WIDE]).astype(bf16)
        target = (ffn_own_ref, ffn_oth_ref)[side]
        cols = slice(kind * part_cols + n, kind * part_cols + n + WIDE)
        if side == 0:
            target[:, cols] = value
            return
        for place in range(size):
            to = other_place(place)
            target[to * share : (to + 1) * share, cols] = value[
                place * share : (place + 1) * share
            ]

    tasks = [
        functools.partial(weigh, side, kind, n)
        for side in (1, 0)
        for kind in range(2)
        for n in range(0, part_cols, WIDE)
    ]
    interleave([functools.partial(settle, b) for b in range(0, count, BLOCK)], tasks)
    for index, value in enumerate(sums):
        small_ref[index : index + 1, :] = row_sum(value)
    small_ref[5:8, :] = jnp.zeros((3, D), f32)
    agrad_ref[...] = mm_nt(down_grad[...], wo_ref[...]).astype(bf16)
    transpose_by_owner(attended_t, attended, turn_work, size, groups)
    out_part = mm(attended_t[...], down_grad[...]).astype(bf16)
    half_rows = D // groups
    out_own_ref[...] = out_part[:half_rows]
    out_oth_ref[...] = out_part[half_rows : 2 * half_rows]


def unshift(value, shift, window):
    whole, rest = shift // TILE, shift % TILE
    row = lax.broadcasted_iota(jnp.int32, (BLOCK, TILE), 0)
    lane = lanes((BLOCK, TILE))
    index = (lane + row - rest) & (TILE - 1)
    tiles = [
        jnp.take_along_axis(
            value[:, n : n + TILE], index, axis=1, mode="promise_in_bounds"
        )
        for n in range(0, value.shape[1], TILE)
    ]
    zero = jnp.zeros((BLOCK, TILE), f32)

    def tile(n):
        return tiles[n] if 0 <= n < len(tiles) else zero

    if rest:
        here = lane >= rest - row
        found = [
            jnp.where(here, tile(n - whole), tile(n - whole - 1)) for n in range(window // TILE)
        ]
    else:
        here = lane + row < TILE
        found = [
            jnp.where(here, tile(n - whole), tile(n - whole + 1)) for n in range(window // TILE)
        ]
    return jnp.concatenate(found, axis=1)


def backward_kernel(
    half,
    groups,
    at,
    mode,
    prob_hbm,
    key_ref,
    val_ref,
    rel_ref,
    hc_ref,
    hp_ref,
    hs_ref,
    linv_ref,
    kaug_ref,
    srow_ref,
    att_ref,
    agrad_ref,
    se_ref,
    both_t_hbm,
    stack_t_hbm,
    pos_t_hbm,
    *rest,
):
    more = rest[: {"first": 2, "middle": 0, "last": 4}[mode]]
    own_ref, oth_ref, proj_ref, tok_key_ref, tok_val_ref, small_ref = rest[len(more) :][:6]
    prob, both_t, stack_t, pos_t, spread, grads, turned, sems = rest[-8:]
    count, window = 2 * half, KEYS + half
    heads = 4
    prob_copies = [
        pltpu.make_async_copy(prob_hbm.at[at * heads + h], prob.at[h], sems.at[h])
        for h in range(heads)
    ]
    fetches = [
        pltpu.make_async_copy(source, target, sems.at[heads + index])
        for index, (source, target) in enumerate(
            ((both_t_hbm, both_t), (stack_t_hbm, stack_t), (pos_t_hbm, pos_t))
        )
    ]
    for copy in prob_copies + fetches:
        copy.start()
    share = D // groups
    if mode == "first":
        own_ref[:, 4 * QUAD :] = more[0][...]
        oth_ref[:, 4 * QUAD :] = more[1][...]
    kaug_t = kaug_ref[...]
    filler = jnp.zeros((HEAD_DIM - kaug_t.shape[0], KEYS), bf16)
    marks = jnp.concatenate([srow_ref[0:1, :], srow_ref[0:1, :]], axis=1)
    swing = 1.0 - 2.0 * marks
    key_t, val_t, rel_t = [], [], []
    lane = lanes((count, PAIR))
    agrads, grad_x, agrad_t = [], [], []
    for pair in range(2):
        cols = slice(pair * PAIR, (pair + 1) * PAIR)
        linv = jnp.where(
            lane < HEAD_DIM,
            linv_ref[:, 2 * pair : 2 * pair + 1],
            linv_ref[:, 2 * pair + 1 : 2 * pair + 2],
        )
        agrad = (agrad_ref[:, cols].astype(f32) * linv).astype(bf16).astype(f32)
        products = agrad * att_ref[:, cols]
        agrad_t.append(turn(agrad.astype(bf16)).astype(bf16))
        for head in range(2):
            base = (1 - head) * HEAD_DIM
            mine = (lane < HEAD_DIM) == (head == 0)
            weight = jnp.sum(jnp.where(mine, products, 0.0), axis=1, keepdims=True)
            high = weight.astype(bf16).astype(f32)
            grad_x.append(
                jnp.where(
                    mine,
                    agrad,
                    jnp.where(
                        lane == base, -high, jnp.where(lane == base + 1, high - weight, 0.0)
                    ),
                ).astype(bf16)
            )
    found = {}

    def head_of(ref, which):
        return ref[which * HEAD_DIM : (which + 1) * HEAD_DIM, :]

    def spreads(which):
        own = head_of(val_ref, which)
        sides = [own, kaug_t, filler] if which % 2 == 0 else [kaug_t, filler, own]
        val_x = jnp.concatenate(sides, axis=0)
        prob_copies[which].wait()

        def task(n, stop):
            spread[which % 2, :, n:stop] = mm(grad_x[which], val_x[:, n:stop])

        return [functools.partial(task, n, min(n + WIDE, KEYS)) for n in range(0, KEYS, WIDE)]

    def score_grads(which):
        buffer = which % 2

        def step(part, b):
            at_row = part * half + b
            block = slice(at_row, at_row + BLOCK)
            score_grad = prob[which, block, :].astype(f32) * spread[buffer, block, :]
            grads[buffer, block, :] = score_grad.astype(bf16)
            turned[buffer, block, :] = unshift(score_grad, half - b, window).astype(bf16)

        return [
            functools.partial(step, part, b) for part in range(2) for b in range(0, half, BLOCK)
        ]

    def gathers(which):
        buffer = which % 2
        side = slice(which % 2 * HEAD_DIM, (which % 2 + 1) * HEAD_DIM)
        key_x = jnp.concatenate([head_of(key_ref, which), kaug_t], axis=0)
        found[which] = {"value": [], "key": [], "rel": [], "content": [], "place": []}

        def down_rows(name, left, ref, n, stop):
            found[which][name].append(mm(left, ref[:, n:stop]))

        tasks = []
        for name, left, ref, end in (
            ("value", agrad_t[which // 2][side], prob.at[which], KEYS),
            ("key", head_of(hc_ref, which), grads.at[buffer], KEYS),
            ("rel", head_of(hp_ref, which), turned.at[buffer], window),
        ):
            tasks += [
                functools.partial(down_rows, name, left, ref, n, min(n + WIDE, end))
                for n in range(0, end, WIDE)
            ]

        def content(n):
            found[which]["content"].append(mm_nt(key_x, grads[buffer, n : n + half, :]))

        def placed(n):
            found[which]["place"].append(
                mm_nt(head_of(rel_ref, which), turned[buffer, n : n + half, :])
            )

        for n in (0, half):
            tasks += [functools.partial(content, n), functools.partial(placed, n)]
        return tasks

    interleave([], spreads(0))
    for which in range(heads):
        tasks = spreads(which + 1) if which + 1 < heads else []
        if which:
            tasks += gathers(which - 1)
        interleave(score_grads(which), tasks)
    interleave([], gathers(heads - 1))
    for which in range(heads):
        val_t.append(jnp.concatenate(found[which]["value"], axis=1))
        key_t.append(jnp.concatenate(found[which]["key"], axis=1))
        rel_t.append(jnp.concatenate(found[which]["rel"], axis=1))
    same, other, contents, places = [], [], [], []
    for which in range(heads):
        content_head = jnp.concatenate(found[which]["content"], axis=1)
        total = content_head[HEAD_DIM : HEAD_DIM + 1]
        marked = content_head[HEAD_DIM + 4 : HEAD_DIM + 5]
        other.append(SCALE * (marks * total + swing * marked))
        same.append(SCALE * total - other[-1])
        contents.append((SCALE * content_head[:HEAD_DIM]).astype(bf16))
        places.append((SCALE * jnp.concatenate(found[which]["place"], axis=1)).astype(bf16))
    contents, places = jnp.concatenate(contents, axis=0), jnp.concatenate(places, axis=0)
    term_high, term_low = split(jnp.concatenate(same + other, axis=0))
    line = lax.broadcasted_iota(jnp.int32, (2 * heads, QUAD), 0)
    mine = line % heads == lanes((2 * heads, QUAD)) // HEAD_DIM
    embed = jnp.where(line < heads, se_ref[0:1, :], se_ref[1:2, :])
    embed_high, embed_low = split(jnp.where(mine, embed, 0.0))
    segment_grad = mm_tn(
        jnp.concatenate([embed_high, embed_high, embed_low, embed_low], axis=0),
        jnp.concatenate([term_high, term_low, term_high, term_low], axis=0),
    )
    proj_t = (contents.astype(f32) + places.astype(f32) + segment_grad).astype(bf16)
    ones = jnp.ones((16, count), bf16)
    small_ref[0:1, :] = mm_nt(ones, contents)[0:1]
    small_ref[1:2, :] = mm_nt(ones, places)[0:1]
    small_ref[2:3, :] = functools.reduce(
        jnp.add, [mm_nt(ones, part)[0:1] for part in split(segment_grad)]
    )
    terms = jnp.concatenate([term_high, term_low], axis=0)
    embed_grad = functools.reduce(jnp.add, [mm(terms, part) for part in split(hs_ref[...])])
    embed_grad = jnp.where(mine, embed_grad[: 2 * heads] + embed_grad[2 * heads :], 0.0)
    small_ref[3:4, :] = row_sum(embed_grad[:heads])
    small_ref[4:5, :] = row_sum(embed_grad[heads:])
    small_ref[5:8, :] = jnp.zeros((3, QUAD), f32)
    key_t = jnp.concatenate(key_t, axis=0).astype(bf16)
    val_t = jnp.concatenate(val_t, axis=0).astype(bf16)
    rel_t = jnp.concatenate(rel_t, axis=0).astype(bf16)
    proj_ref[...] = turn(proj_t).astype(bf16)
    tok_key_ref[...] = turn(key_t[:, MEM:]).astype(bf16)
    tok_val_ref[...] = turn(val_t[:, MEM:]).astype(bf16)
    for fetch in fetches:
        fetch.wait()
    parts = (
        mm_nt(both_t[...], proj_t),
        mm_nt(stack_t[...], key_t),
        mm_nt(stack_t[...], val_t),
        mm_nt(pos_t[...], rel_t),
    )
    for index, value in enumerate(parts):
        cols = slice(index * QUAD, (index + 1) * QUAD)
        own_ref[:, cols] = value[:share].astype(bf16)
        oth_ref[:, cols] = value[share : 2 * share].astype(bf16)
    if mode == "last":
        vec_ref = rest[len(more) + 6]
        early, ubias, before, between = more
        core = lax.axis_index("tensor")
        rows = [early[0:5, :]]
        mine = [ubias[0:1, n : n + D] for n in range(0, ubias.shape[1], D)]
        theirs = [ubias[1:2, n : n + D] for n in range(0, ubias.shape[1], D)]
        for left, right in ((mine, theirs), (theirs, mine)):
            rows += [jnp.where(core == 0, a, b) for a, b in zip(left, right)]
        rows.append(
            jnp.concatenate([before[0:5, :], between[0:5, :], small_ref[0:5, :]], axis=1)
        )
        rows = jnp.concatenate(rows, axis=0)
        spare = jnp.zeros((VECTORS - rows.shape[0], D), f32)
        rows = jnp.concatenate([rows, spare], axis=0)
        packed = jnp.concatenate([rows[:, n : n + TILE] for n in range(0, D, TILE)], axis=0)
        vec_ref[...] = packed
        oth_ref[:VECTOR_ROWS, 4 * QUAD :] = packed.astype(bf16)
        oth_ref[VECTOR_ROWS:, 4 * QUAD :] = jnp.zeros((share - VECTOR_ROWS, TILE), bf16)


def rows_kernel(half, groups, sgrad_ref, *rest):
    proj, keys, vals = rest[:QUADS], rest[QUADS : 2 * QUADS], rest[2 * QUADS : 3 * QUADS]
    wq_ref, wk_ref, wv_ref, own_ref, query_ref, send_ref, both = rest[3 * QUADS :]
    member = lax.axis_index("tensor")
    wide = [jnp.concatenate([ref[...] for ref in refs], axis=1) for refs in (proj, keys, vals)]
    both[...] = mm_nt(wide[1], wk_ref[...]) + mm_nt(wide[2], wv_ref[...])
    rows = sgrad_ref[...] + mm_nt(wide[0], wq_ref[...])
    own = pl.multiple_of(member * half, half)
    other = pl.multiple_of(lax.rem(member + 1, groups) * half, half)
    send_ref[...] = both[pl.ds(other, half), :].astype(bf16)
    own_ref[...] = rows[:half] + both[pl.ds(own, half), :]
    query_ref[...] = rows[half:]


def summed(operands, terms, first, rows, width):
    values = []
    for index, at in terms:
        if rows % 16 == 0:
            value = operands[index][first : first + rows, at : at + width].astype(f32)
        else:
            value = operands[index][:, at : at + width].astype(f32)[first : first + rows]
        values.append(value)
    return functools.reduce(jnp.add, values)


def vector_width(rows):
    return TILE * max(1, VECTOR_ROWS // rows)


def fold_vectors(packed, rows):
    if rows > VECTOR_ROWS:
        return jnp.concatenate([packed, jnp.zeros((rows - VECTOR_ROWS, TILE), f32)], axis=0)
    return jnp.concatenate(
        [packed[n : n + rows] for n in range(0, VECTOR_ROWS, rows)], axis=1
    )


def unfold_vectors(block, rows):
    if rows >= VECTOR_ROWS:
        return block[:VECTOR_ROWS]
    return jnp.concatenate(
        [block[:, n : n + TILE] for n in range(0, vector_width(rows), TILE)], axis=0
    )


def summed_vectors(values, terms):
    return functools.reduce(
        jnp.add,
        [
            unfold_vectors(
                values(index)[:rows, at : at + vector_width(rows)].astype(f32), rows
            )
            for index, at, rows in terms
        ],
    )


def combine_kernel(plans, *refs):
    count = sum(pieces + (1 if vectors else 0) for _, pieces, _, vectors in plans)
    operands, outs = refs[:-count], list(refs[-count:])
    for rows, pieces, parts, vectors in plans:
        if vectors:
            packed = summed_vectors(lambda index: operands[index][...].astype(f32), vectors)
            outs.pop(0)[...] = packed
        for piece in range(pieces):
            out_ref = outs.pop(0)
            column = 0
            for width, terms in parts:
                value = summed(operands, terms, piece * rows, rows, width)
                out_ref[:, column : column + width] = value.astype(out_ref.dtype)
                column += width
            if piece and vectors:
                out_ref[:, column:] = fold_vectors(packed, rows).astype(out_ref.dtype)


def unpack_vectors(packed):
    return jnp.concatenate(
        [packed[n : n + VECTORS] for n in range(0, VECTOR_ROWS, VECTORS)], axis=1
    )


def finish_kernel(size, groups, count, plan, up_rows, *refs):
    operands, outs = refs[:count], refs[count:]
    weights, vec_outs, embed_out, up_out = outs[:5], outs[5:-2], outs[-2], outs[-1]
    place = lax.axis_index("dp") * groups + lax.axis_index("tensor")
    share = D // (size * groups)
    for target, at, width, terms in plan[0]:
        weights[target][:, at : at + width] = summed(operands, terms, 0, share, width)
    value = unpack_vectors(
        summed_vectors(lambda index: operands[index][...].astype(f32), plan[1])
    )
    mine = pltpu.roll(value, lax.rem(D - place * share, D), 1)[:, :TILE]
    rows = [row for row in range(5 + up_rows + 3) if not 5 <= row < 5 + up_rows]
    for row, out_ref in zip(rows, vec_outs):
        out_ref[...] = mine[row, :share]
    embed = jnp.concatenate([mine[5 + up_rows + 3 : 5 + up_rows + 5], jnp.zeros((6, TILE), f32)], axis=0)
    embed_out[...] = embed[:2, :share]
    wide = up_rows * share
    each = D // wide
    line = lax.div(place, each)
    chosen = functools.reduce(
        jnp.add,
        [jnp.where(line == r, value[5 + r : 6 + r], 0.0) for r in range(up_rows)],
    )
    chosen = jnp.broadcast_to(chosen, (8, D))
    turned = pltpu.roll(chosen, lax.rem(D - lax.rem(place, each) * wide, D), 1)[:, :TILE]
    up_out[...] = turned[0, :wide]


def whole(shape):
    return pl.BlockSpec(shape, lambda i: (0,) * len(shape))


def columns(rows, width, at=None):
    if at is None:
        return pl.BlockSpec((rows, width), lambda i: (0, i))
    return pl.BlockSpec((rows, width), lambda i: (0, at))


def row_block(rows, width, at=None):
    if at is None:
        return pl.BlockSpec((rows, width), lambda i: (i, 0))
    return pl.BlockSpec((rows, width), lambda i: (at, 0))


def scalars():
    return pl.BlockSpec(memory_space=pltpu.SMEM)


def params(size=VMEM_BYTES):
    return pltpu.CompilerParams(vmem_limit_bytes=size)


def cost(flops, bytes_accessed):
    return pl.CostEstimate(flops=flops, bytes_accessed=bytes_accessed, transcendentals=0)


def in_hbm():
    return pl.BlockSpec(memory_space=pl.ANY)


def attention_forward(
    half, ints, memory, content, query, weights, biases, segment_rows
):
    count, window = 2 * half, KEYS + half
    coarse_rows = -(-(window // 32) // 8) * 8
    outs = (
        ((count, D), f32, columns(count, QUAD)),
        ((HEADS, count, KEYS), bf16, pl.BlockSpec((4, count, KEYS), lambda i: (i, 0, 0))),
        ((D, KEYS), bf16, row_block(QUAD, KEYS)),
        ((D, KEYS), bf16, row_block(QUAD, KEYS)),
        ((D, window), bf16, row_block(QUAD, window)),
        ((D, count), bf16, row_block(QUAD, count)),
        ((D, count), bf16, row_block(QUAD, count)),
        ((count, D), f32, columns(count, QUAD)),
        ((count, QUADS * TILE), f32, columns(count, TILE)),
        ((16, KEYS), bf16, whole((16, KEYS))),
        ((8, half), f32, whole((8, half))),
        ((window, D), bf16, whole((window, D))),
    )
    return pl.pallas_call(
        functools.partial(forward_kernel, half),
        grid=(QUADS,),
        out_shape=[jax.ShapeDtypeStruct(shape, kind) for shape, kind, _ in outs],
        in_specs=[
            scalars(),
            scalars(),
            whole((1, LEN)),
            whole((1, LEN)),
            whole((1, LEN)),
            whole((MEM, D)),
            whole((LEN, D)),
            whole((half, D)),
        ]
        + [columns(D, QUAD)] * 4
        + [whole((D,))] * 3
        + [columns(2, QUAD)],
        out_specs=[spec for _, _, spec in outs],
        scratch_shapes=[
            pltpu.VMEM((KEYS, D), bf16),
            pltpu.VMEM((count, D), bf16),
            pltpu.VMEM((window, D), bf16),
            pltpu.VMEM((count, KEYS), f32),
            pltpu.VMEM((2, 32, D // 2), f32),
            pltpu.VMEM((2, coarse_rows, D // 2), f32),
            pltpu.VMEM((8, D), f32),
            pltpu.VMEM((2, count, KEYS), f32),
            pltpu.VMEM((2, count, window), f32),
            pltpu.VMEM((HEAD_DIM, KEYS), bf16),
            pltpu.VMEM((half, PAIR), f32),
            pltpu.VMEM((8, LEN), f32),
            pltpu.VMEM((KEYS, PAIR), bf16),
            pltpu.VMEM((LEN, TILE), f32),
            pltpu.VMEM((LEN, TILE), f32),
        ],
        compiler_params=params(FORWARD_BYTES),
        cost_estimate=cost(30_000_000_000, 40_000_000),
        name="attention_forward",
    )(*ints, memory, content, query, *weights, *biases, segment_rows)


def middle(half, size, groups, arrays, hidden_cols):
    count, share = 2 * half, D // groups
    chunk = min(hidden_cols, 768)
    outs = (
        ((half, D), bf16),
        ((half, D), bf16),
        ((D, 2 * hidden_cols), bf16),
        ((D, 2 * hidden_cols), bf16),
        ((count, D), f32),
        ((count, D), bf16),
        ((share, D), bf16),
        ((share, D), bf16),
        ((8, D), f32),
        ((2, hidden_cols), f32),
    )
    weights = (6, 7, 8, 9)
    return pl.pallas_call(
        functools.partial(middle_kernel, half, size, groups, chunk),
        grid=(1,),
        out_shape=[jax.ShapeDtypeStruct(shape, kind) for shape, kind in outs],
        in_specs=[
            in_hbm() if i in weights else whole(array.shape) for i, array in enumerate(arrays)
        ],
        out_specs=[whole(shape) for shape, _ in outs],
        scratch_shapes=[
            pltpu.VMEM((2, count, hidden_cols), bf16),
            pltpu.VMEM((2, count, hidden_cols), bf16),
            pltpu.VMEM((2, count, chunk), f32),
            pltpu.VMEM((count, D), f32),
            pltpu.VMEM((count, D), f32),
            pltpu.VMEM((count, D), bf16),
            pltpu.VMEM((count, D), bf16),
            pltpu.VMEM((8, FF), f32),
            pltpu.VMEM((2, D, hidden_cols), bf16),
            pltpu.VMEM((2, hidden_cols, D), bf16),
            pltpu.VMEM((D, count), bf16),
            pltpu.VMEM((D, count), bf16),
            pltpu.VMEM((D, count), bf16),
            pltpu.VMEM((D, count), bf16),
            pltpu.VMEM((D, count), bf16),
            pltpu.VMEM((D, count), f32),
            pltpu.SemaphoreType.DMA((2, 2)),
        ],
        compiler_params=params(MIDDLE_BYTES),
        cost_estimate=cost(30_000_000_000, 30_000_000),
        name="feed_forward",
    )(*arrays)


def prepare_kernel(
    half,
    size,
    groups,
    memory_ref,
    content_ref,
    query_ref,
    pos_ref,
    both_t_ref,
    stack_t_ref,
    pos_t_ref,
    both_work,
    stack_work,
    pos_work,
):
    first = pl.multiple_of(lax.axis_index("tensor") * half, half)
    both = jnp.concatenate([content_ref[pl.ds(first, half), :], query_ref[...]], axis=0)
    stack = jnp.concatenate([memory_ref[...], content_ref[...]], axis=0)
    transpose_by_owner(both_t_ref, both, both_work, size, groups)
    transpose_by_owner(stack_t_ref, stack, stack_work, size, groups)
    transpose_by_owner(pos_t_ref, pos_ref[...], pos_work, size, groups)


def transposed_rows(half, size, groups, memory, content, query, pos):
    count, window = 2 * half, KEYS + half
    arrays = (memory, content, query, pos)
    outs = ((D, count), (D, KEYS), (D, window))
    return pl.pallas_call(
        functools.partial(prepare_kernel, half, size, groups),
        grid=(1,),
        out_shape=[jax.ShapeDtypeStruct(shape, bf16) for shape in outs],
        in_specs=[whole(array.shape) for array in arrays],
        out_specs=[whole(shape) for shape in outs],
        scratch_shapes=[pltpu.VMEM(shape, f32) for shape in outs],
        compiler_params=params(BACKWARD_BYTES),
        cost_estimate=cost(6_000_000_000, 8_000_000),
        name="transposed_rows",
    )(*arrays)


def attention_backward(half, groups, at, mode, saved, agrad, segment_rows, extra):
    count, window, share = 2 * half, KEYS + half, D // groups
    att, prob, keys, values, rel, hc, hp, hs, linv, kaug, srow, _ = saved[:12]
    both_t, stack_t, pos_t = saved[12:]
    width = 4 * QUAD + (D if mode == "first" else 0)
    operands = (
        (prob, in_hbm()),
        (keys, row_block(QUAD, KEYS, at)),
        (values, row_block(QUAD, KEYS, at)),
        (rel, row_block(QUAD, window, at)),
        (hc, row_block(QUAD, count, at)),
        (hp, row_block(QUAD, count, at)),
        (hs, columns(count, QUAD, at)),
        (linv, columns(count, TILE, at)),
        (kaug, whole((16, KEYS))),
        (srow, whole((8, half))),
        (att, columns(count, QUAD, at)),
        (agrad, columns(count, QUAD, at)),
        (segment_rows, columns(2, QUAD, at)),
        (both_t, in_hbm()),
        (stack_t, in_hbm()),
        (pos_t, in_hbm()),
    ) + tuple((array, whole(array.shape)) for array in extra)
    outs = (
        ((share, width), bf16),
        ((share, width + (TILE if mode == "last" else 0)), bf16),
        ((count, QUAD), bf16),
        ((LEN, QUAD), bf16),
        ((LEN, QUAD), bf16),
        ((8, QUAD), f32),
    )
    if mode == "last":
        outs += (((VECTOR_ROWS, TILE), f32),)
    return pl.pallas_call(
        functools.partial(backward_kernel, half, groups, at, mode),
        grid=(1,),
        out_shape=[jax.ShapeDtypeStruct(shape, kind) for shape, kind in outs],
        in_specs=[spec for _, spec in operands],
        out_specs=[whole(shape) for shape, _ in outs],
        scratch_shapes=[
            pltpu.VMEM((4, count, KEYS), bf16),
            pltpu.VMEM((D, count), bf16),
            pltpu.VMEM((D, KEYS), bf16),
            pltpu.VMEM((D, window), bf16),
            pltpu.VMEM((2, count, KEYS), f32),
            pltpu.VMEM((2, count, KEYS), bf16),
            pltpu.VMEM((2, count, window), bf16),
            pltpu.SemaphoreType.DMA((7,)),
        ],
        compiler_params=params(BACKWARD_BYTES),
        cost_estimate=cost(16_000_000_000, 16_000_000),
        name="attention_backward",
    )(*[array for array, _ in operands])


def row_gradients(half, groups, summed_grad, proj, keys, vals, weights):
    count = 2 * half
    arrays = (summed_grad, *proj, *keys, *vals, *weights)
    outs = (((half, D), f32), ((half, D), f32), ((half, D), bf16))
    return pl.pallas_call(
        functools.partial(rows_kernel, half, groups),
        grid=(1,),
        out_shape=[jax.ShapeDtypeStruct(shape, kind) for shape, kind in outs],
        in_specs=[whole(array.shape) for array in arrays],
        out_specs=[whole(shape) for shape, _ in outs],
        scratch_shapes=[pltpu.VMEM((LEN, D), f32)],
        compiler_params=params(),
        cost_estimate=cost(4_000_000_000, 10_000_000),
        name="row_gradients",
    )(*arrays)


def swap(array):
    groups = lax.axis_size("tensor")
    return lax.ppermute(array, "tensor", [(i, (i + 1) % groups) for i in range(groups)])


def across(array, masks):
    size, groups = lax.axis_size("dp"), lax.axis_size("tensor")
    pairs = [
        (place * groups + core, (place ^ masks[core]) * groups + core)
        for place in range(size)
        for core in range(groups)
    ]
    return lax.ppermute(array, ("dp", "tensor"), pairs)


def total(terms):
    return functools.reduce(jnp.add, [term.astype(f32) for term in terms])


class Chain:
    def __init__(self, parts, rows, vectors=()):
        self.parts, self.rows = parts, rows
        self.vectors = list(vectors)
        self.messages = None
        self.done = 0

    def masks(self, part, bits):
        size, groups = lax.axis_size("dp"), lax.axis_size("tensor")
        found = []
        for core in range(groups):
            order = order_of(core, size.bit_length() - 1)[self.done : self.done + bits]
            found.append(
                sum(((part >> (bits - 1 - j)) & 1) << bit for j, bit in enumerate(order))
            )
        return found

    def send(self):
        if not self.bits:
            gots = [swap(self.messages[0])]
        else:
            gots = [
                across(message, self.masks(part + 1, self.bits))
                for part, message in enumerate(self.messages)
            ]
        for got in gots:
            column = 0
            for width, terms in self.parts:
                terms.append((got, column))
                column += width
            if self.vectors:
                self.vectors.append((got, column, self.rows))
        self.pending = gots
        self.done += self.bits
        self.messages = None

    def take(self, results):
        if self.vectors:
            self.vectors = [(results.pop(0), 0, VECTOR_ROWS)]
        kept, column, parts = results.pop(0), 0, []
        for width, _ in self.parts:
            parts.append((width, [(kept, column)]))
            column += width
        self.parts = parts
        self.messages = [results.pop(0) for _ in range((1 << self.bits) - 1)]

    def replace(self, old, new):
        for index, (width, terms) in enumerate(self.parts):
            self.parts[index] = (
                width,
                [(new if array is old else array, at) for array, at in terms],
            )
        self.vectors = [(new if a is old else a, at, rows) for a, at, rows in self.vectors]


def merged(chains):
    chain = Chain(
        [part for chain in chains for part in chain.parts],
        chains[0].rows,
        [term for chain in chains for term in chain.vectors],
    )
    chain.done = chains[0].done
    chain.pending = []
    return chain


class Operands:
    def __init__(self):
        self.arrays = []

    def of(self, array):
        for index, held in enumerate(self.arrays):
            if held is array:
                return index
        self.arrays.append(array)
        return len(self.arrays) - 1

    def in_specs(self):
        return [whole(array.shape) for array in self.arrays]


def prepare(requests):
    operands, plans, outs = Operands(), [], []
    plain = any(chain.rows % (8 << bits) for chain, bits in requests)
    for chain, bits in requests:
        chain.bits = bits
        chain.rows >>= bits
        rows, pieces = chain.rows, 1 << bits
        width = sum(width for width, _ in chain.parts)
        if plain:
            results = [
                jnp.concatenate(
                    [
                        total(
                            [
                                array[piece * rows : (piece + 1) * rows, at : at + width]
                                for array, at in terms
                            ]
                        )
                        for width, terms in chain.parts
                    ],
                    axis=1,
                )
                for piece in range(pieces)
            ]
            if chain.vectors:
                packed = summed_vectors(lambda array: array, chain.vectors)
                folded = fold_vectors(packed, rows)
                results = [packed, results[0]] + [
                    jnp.concatenate([result, folded], axis=1) for result in results[1:]
                ]
            chain.take([result.astype(bf16) for result in results])
            continue
        parts = [
            (width, [(operands.of(array), at) for array, at in terms])
            for width, terms in chain.parts
        ]
        vectors = [(operands.of(array), at, held) for array, at, held in chain.vectors]
        plans.append((rows, pieces, parts, vectors))
        if vectors:
            outs.append(((VECTOR_ROWS, TILE), f32))
        outs.append(((rows, width), bf16))
        wide = width + (vector_width(rows) if vectors else 0)
        outs += [((rows, wide), bf16)] * (pieces - 1)
    if plain:
        return
    results = pl.pallas_call(
        functools.partial(combine_kernel, plans),
        grid=(1,),
        out_shape=[jax.ShapeDtypeStruct(shape, kind) for shape, kind in outs],
        in_specs=operands.in_specs(),
        out_specs=[whole(shape) for shape, _ in outs],
        compiler_params=params(COMBINE_BYTES),
        cost_estimate=cost(1_000_000_000, 8_000_000),
        name="combine",
    )(*operands.arrays)
    results = list(results)
    for chain, bits in requests:
        chain.take(results)


def launch(requests, value, waits=()):
    chains = [chain for chain, bits in requests if bits is not None] + list(waits)
    olds = [got for chain in chains for got in chain.pending]
    if olds:
        value, news = lax.optimization_barrier((value, olds))
        for chain in chains + [chain for chain, _ in requests]:
            for old, new in zip(olds, news):
                chain.replace(old, new)
        for chain in chains:
            chain.pending = []
    sums = [(chain, bits) for chain, bits in requests if bits is not None]
    if sums:
        prepare(sums)
    messages = [chain.messages for chain, _ in requests]
    value, messages = lax.optimization_barrier((value, messages))
    for (chain, bits), message in zip(requests, messages):
        chain.messages = message
        if bits is None:
            chain.bits = 0
        chain.send()
    return value


def finish(size, groups, chain):
    share = D // (size * groups)
    up_rows = FF // D
    pieces = []
    for quad, (width, terms) in enumerate(chain.parts):
        for index in range(4):
            pieces.append((index, quad * QUAD, QUAD, [(a, at + index * QUAD) for a, at in terms]))
        if width > 4 * QUAD:
            pieces.append((4, 0, D, [(a, at + 4 * QUAD) for a, at in terms]))
    if share % 8:
        blocks = {}
        for target, at, width, terms in pieces:
            blocks.setdefault(target, []).append(
                total([array[:share, c : c + width] for array, c in terms])
            )
        weights = [jnp.concatenate(blocks[target], axis=1) for target in range(5)]
        vectors = unpack_vectors(summed_vectors(lambda array: array, chain.vectors))
        place = lax.axis_index("dp") * groups + lax.axis_index("tensor")
        mine = lax.dynamic_slice_in_dim(vectors, place * share, share, 1)
        ups = lax.dynamic_slice_in_dim(
            vectors[5 : 5 + up_rows].reshape(-1), place * up_rows * share, up_rows * share, 0
        )
        late = 5 + up_rows
        return weights, [mine[r] for r in (0, 1, 2, 3, 4, late, late + 1, late + 2)], mine[
            late + 3 : late + 5
        ].T, ups
    operands = Operands()
    plan = [
        (target, at, width, [(operands.of(array), c) for array, c in terms])
        for target, at, width, terms in pieces
    ]
    vectors = [(operands.of(array), at, held) for array, at, held in chain.vectors]
    outs = [(share, D)] * 5 + [(share,)] * 8 + [(2, share), (up_rows * share,)]
    found = pl.pallas_call(
        functools.partial(
            finish_kernel, size, groups, len(operands.arrays), (plan, vectors), up_rows
        ),
        grid=(1,),
        out_shape=[jax.ShapeDtypeStruct(shape, f32) for shape in outs],
        in_specs=operands.in_specs(),
        out_specs=[whole(shape) for shape in outs],
        compiler_params=params(COMBINE_BYTES),
        name="finish",
    )(*operands.arrays)
    return found[:5], found[5:13], found[13].T, found[14]


def body(
    content_in,
    query_in,
    memory,
    content_cot,
    query_cot,
    query_weight,
    key_weight,
    value_weight,
    out_weight,
    rel_weight,
    content_bias,
    position_bias,
    segment_bias,
    segment_embed,
    attn_gain,
    attn_shift,
    up_weight,
    up_bias,
    down_weight,
    down_bias,
    ffn_gain,
    ffn_shift,
    lengths,
    memory_lengths,
    segment_ids,
    orders,
    targets,
):
    groups = lax.axis_size("tensor")
    size = lax.axis_size("dp")
    steps = size.bit_length() - 1
    half = LEN // groups
    hidden_cols = up_weight.shape[1]
    up_other, down_other = swap(up_weight), swap(down_weight)
    content, query = content_in[0], query_in[0]
    segment_rows = segment_embed.T
    saved = attention_forward(
        half,
        (lengths, memory_lengths, segment_ids, orders, targets),
        memory[0],
        content,
        query,
        (query_weight, key_weight, value_weight, rel_weight),
        (content_bias, position_bias, segment_bias),
        segment_rows,
    )
    (
        content_out,
        query_out,
        ffn_own,
        ffn_other,
        summed_grad,
        attended_grad,
        out_own,
        out_other,
        early_small,
        up_bias_part,
    ) = middle(
        half,
        size,
        groups,
        (
            saved[0],
            content,
            query,
            content_cot[0],
            query_cot[0],
            out_weight,
            up_weight,
            up_other,
            down_weight,
            down_other,
            up_bias,
            down_bias,
            attn_gain,
            attn_shift,
            ffn_gain,
            ffn_shift,
        ),
        hidden_cols,
    )
    ffn = Chain([(2 * hidden_cols, [(ffn_own, 0)])], D)
    ffn.messages = [ffn_other]
    held = launch([(ffn, None)], attended_grad)
    content_late, held = lax.optimization_barrier((content, held))
    turned = transposed_rows(half, size, groups, memory[0], content_late, query, saved[11])
    turned, held = lax.optimization_barrier((turned, held))
    saved = (*saved, *turned)
    proj, tok_keys, tok_vals, small, late = [], [], [], [], []

    def backward(at, mode, grad, extra):
        own, other, proj_part, key_part, val_part, small_part, *vectors = attention_backward(
            half, groups, at, mode, saved, grad, segment_rows, extra
        )
        proj.append(proj_part)
        tok_keys.append(key_part)
        tok_vals.append(val_part)
        small.append(small_part)
        chain = Chain(
            [(own.shape[1], [(own, 0)])],
            own.shape[0],
            [(array, 0, VECTOR_ROWS) for array in vectors],
        )
        chain.messages = [other]
        late.append(chain)

    held = launch([(ffn, 1)], held)
    backward(0, "first", held, (out_own, out_other))
    held, proj[0] = launch([(late[0], None)], (attended_grad, proj[0]))
    backward(1, "middle", held, ())
    held, proj[1] = launch(
        [(ffn, 1), (late[0], 1), (late[1], None)], (attended_grad, proj[1])
    )
    backward(2, "last", held, (early_small, up_bias_part, *small))
    xy = min(2, steps)
    tok_vals[2] = launch(
        [(late[2], None), (ffn, 1), (late[0], 1), (late[1], 1)], tok_vals[2]
    )
    tok_vals[2] = launch(
        [(late[2], xy), (late[1], 1), (ffn, 1), (late[0], 1)], tok_vals[2]
    )
    pair = merged(late[1:])
    tok_vals[2] = launch(
        [(pair, min(2, steps - pair.done)), (late[0], 1)], tok_vals[2], late[1:]
    )
    own_rows, query_grad, row_send = row_gradients(
        half, groups, summed_grad, proj, tok_keys, tok_vals, (query_weight, key_weight, value_weight)
    )
    row_got = swap(row_send)
    for chain in (late[0], pair):
        while chain.done < steps:
            own_rows = launch([(chain, min(2, steps - chain.done))], own_rows)
    final = merged([late[0], pair])
    final.pending = late[0].pending + pair.pending
    while ffn.done < steps:
        own_rows = launch([(ffn, min(2, steps - ffn.done))], own_rows)
    content_grad = own_rows + row_got.astype(f32)
    ffn_sum = total([array[: ffn.rows] for array, _ in ffn.parts[0][1]])
    up_grad, down_grad_own = ffn_sum[:, :hidden_cols], ffn_sum[:, hidden_cols:].T
    (content_grad, up_grad, down_grad_own), olds = lax.optimization_barrier(
        ((content_grad, up_grad, down_grad_own), final.pending)
    )
    for old, new in zip(final.pending, olds):
        final.replace(old, new)
    weights, vectors, segment_grad, up_bias_grad = finish(size, groups, final)
    return (
        content_out[None],
        query_out[None],
        content_grad[None],
        query_grad[None],
        weights[0],
        weights[1],
        weights[2],
        weights[4],
        weights[3],
        vectors[5],
        vectors[6],
        vectors[7],
        segment_grad,
        vectors[3],
        vectors[4],
        up_grad,
        up_bias_grad,
        down_grad_own,
        vectors[2],
        vectors[0],
        vectors[1],
    )


def solution(mesh):
    in_specs = (
        P("dp", None, None),
        P("dp", "tensor", None),
        P("dp", None, None),
        P("dp", "tensor", None),
        P("dp", "tensor", None),
        P(),
        P(),
        P(),
        P(),
        P(),
        P(),
        P(),
        P(),
        P(),
        P(),
        P(),
        P(None, "tensor"),
        P(),
        P("tensor", None),
        P(),
        P(),
        P(),
        P("dp"),
        P("dp"),
        P("dp", None),
        P("dp", None),
        P("dp", None),
    )
    out_specs = (
        P("dp", "tensor", None),
        P("dp", "tensor", None),
        P("dp", "tensor", None),
        P("dp", "tensor", None),
        P(("dp", "tensor"), None),
        P(("dp", "tensor"), None),
        P(("dp", "tensor"), None),
        P(("dp", "tensor"), None),
        P(("dp", "tensor"), None),
        P(("dp", "tensor")),
        P(("dp", "tensor")),
        P(("dp", "tensor")),
        P(("dp", "tensor"), None),
        P(("dp", "tensor")),
        P(("dp", "tensor")),
        P("dp", "tensor"),
        P(("dp", "tensor")),
        P("tensor", "dp"),
        P(("dp", "tensor")),
        P(("dp", "tensor")),
        P(("dp", "tensor")),
    )
    return jax.shard_map(body, mesh=mesh, in_specs=in_specs, out_specs=out_specs, check_vma=False)
```
